32 devices in a mesh: sub: 8 (over z, core), layer: 4 (over y, x).
Axes of the slice: x: 2, y: 2, z: 4, core: 2. Of those that a mesh axis runs over, the one named last changes fastest.
Arguments:
- eigen_vectors: float32 [8, 4, 24, 4096], P('sub', 'layer'), may hold values from -4.1 to 4.1
- row_mass: float32 [8, 4, 4096], P('sub', 'layer'), may hold values from 0.1 to 0.8
- inner_weight: float32 [8, 4, 3, 4096], P('sub', 'layer'), may hold values from 0.05 to 0.4
- face_weight: float32 [8, 4, 2, 128], P('sub', 'layer'), may hold values from 80 to 10240, as said below
- margin_rows: int32 [8, 4, 4, 128], P('sub', 'layer'), may hold values from 0 to 4095, as said below
Outputs:
- applied: float32 [8, 4, 24, 4096], P('sub', 'layer')
- diag_factor: float32 [8, 96, 96], P('sub', 'layer')
- left_factor: float32 [8, 96, 96], P('sub', 'layer')
- right_factor: float32 [8, 96, 96], P('sub', 'layer')
The draws below stay inside these ranges and needn't reach their ends.
Inputs may be any that keep to these rules, and one draw needn't show every extreme that they name: Row numbers of a subdomain's own rows; a row may appear in several lists or twice in one list. Both sides of an interface list the same row numbers: margin_rows[s, j, 1] equals margin_rows[s-1, j, 0] for s >= 1, and margin_rows[s, j, 3] equals margin_rows[s, j-1, 2] for j >= 1. `face_weight`: index 0 (springs along sub) lies in 1280 to 10240, index 1 (springs along layer) in 2.5 * 32 to 640.
All inputs are finite; a program needn't handle non-finite values.
Results may differ from the reference program's by a relative error of at most 0.0003.
Values sent between devices are 32-bit elements; how exact they have to be, the bound alone decides.
No kernel may reach another device: no remote copies, remote signals or barrier semaphores. Data moves between devices by JAX's collectives and lax.ppermute only.
A program may use at most 128 MiB of HBM per device.

```python
import math
import jax
import jax.numpy as jnp
from jax import lax

NV = 24
R = 4096
H = 128
N_SUB = 8
N_LAYER = 4


def draw_eigen_vectors(key, part):
    key = jax.random.fold_in(key, 11)
    shared_key, noise_key = jax.random.split(key, 2)
    common = jax.random.truncated_normal(shared_key, -4.0, 4.0, (NV, R), jnp.float32)
    noise = 0.01 * jax.random.truncated_normal(noise_key, -4.0, 4.0, (N_SUB, N_LAYER, NV, R), jnp.float32)
    return (common[None, None] + noise).astype(jnp.float32)


def log_range(key, shape, lower, upper):
    return jnp.exp(jax.random.uniform(key, shape, jnp.float32, math.log(lower), math.log(upper)))


def draw_face_weight(key, part):
    key = jax.random.fold_in(key, 23)
    sub_key, layer_key = jax.random.split(key, 2)
    ratio = R / H
    shape = (N_SUB, N_LAYER, H)
    sub_side = log_range(sub_key, shape, 40.0 * ratio, 320.0 * ratio)
    layer_side = log_range(layer_key, shape, 2.5 * ratio, 20.0 * ratio)
    return jnp.stack([sub_side, layer_side], axis=2).astype(jnp.float32)


def draw_margin_rows(key, part):
    key = jax.random.fold_in(key, 37)
    sub_key, layer_key = jax.random.split(key, 2)
    sub_faces = jax.random.randint(sub_key, (N_SUB + 1, N_LAYER, H), 0, R, jnp.int32)
    layer_faces = jax.random.randint(layer_key, (N_SUB, N_LAYER + 1, H), 0, R, jnp.int32)
    return jnp.stack([sub_faces[1:], sub_faces[:-1], layer_faces[:, 1:], layer_faces[:, :-1]], axis=2).astype(jnp.int32)


def shard_levels(own_key, dims, cuts, smallest, top_value):
    loudness = 1.0
    for dim, blocks in cuts:
        draws = jax.random.uniform(jax.random.fold_in(jax.random.fold_in(own_key, 6), dim), (blocks,), jnp.float32, smallest / len(cuts), top_value / len(cuts))
        loudness = loudness * jnp.repeat(jnp.exp(draws), dims[dim] // blocks).reshape((-1,) + (1,) * (len(dims) - 1 - dim))
    return loudness


def setup_inputs(seed: int = 0) -> dict:
    seeds = jax.random.split(jax.random.key(seed), 6)
    return {
        "eigen_vectors": draw_eigen_vectors(jax.random.fold_in(seeds[5], 71), 0),
        "row_mass": jnp.clip(jnp.exp(math.log(0.8) - 2.0794415 * jax.random.uniform(seeds[1], (N_SUB, N_LAYER, R), jnp.float32) ** shard_levels(seeds[1], (N_SUB, N_LAYER, R), ((0, 8), (1, 4)), -0.2, 0.2)), 0.1, 0.8),
        "inner_weight": jnp.clip(jnp.exp(math.log(0.4) - 2.0794415 * jax.random.uniform(seeds[2], (N_SUB, N_LAYER, 3, R), jnp.float32) ** shard_levels(seeds[2], (N_SUB, N_LAYER, 3, R), ((0, 8), (1, 4)), -0.2, 0.2)), 0.05, 0.4),
        "face_weight": draw_face_weight(jax.random.fold_in(seeds[5], 71), 0),
        "margin_rows": draw_margin_rows(jax.random.fold_in(seeds[5], 71), 0),
    }


STRIDES = (1, 3, 27)
HIGHEST = lax.Precision.HIGHEST

def device_terms(vectors, masses, interior, row_lists, picked, springs, partners):
    row_count = vectors.shape[-1]
    places = jnp.arange(row_count, dtype=jnp.int32)
    laplace = jnp.zeros_like(vectors)
    for k, t in enumerate(STRIDES):
        edge_weight = jnp.where(places < row_count - t, interior[k], 0.0)
        fluxes = edge_weight * (vectors - jnp.roll(vectors, -t, axis=1))
        laplace = laplace + fluxes - jnp.roll(fluxes, t, axis=1)
    own_part = masses * vectors + laplace
    coupled = jnp.zeros_like(vectors)
    for k in range(4):
        onehot = (row_lists[k][:, None] == places[None, :]).astype(jnp.float32)
        own_part = own_part + jnp.dot(springs[k] * picked[k], onehot, precision=HIGHEST)
        coupled = coupled + jnp.dot(springs[k] * partners[k], onehot, precision=HIGHEST)
    applied = own_part - coupled
    inverse = 1.0 / row_count
    diag_tile = jnp.dot(vectors, own_part.T, precision=HIGHEST) * inverse
    down_tile = -jnp.dot(springs[1] * picked[1], partners[1].T, precision=HIGHEST) * inverse
    up_tile = -jnp.dot(springs[0] * partners[0], picked[0].T, precision=HIGHEST) * inverse
    side_tile = -jnp.dot(springs[3] * picked[3], partners[3].T, precision=HIGHEST) * inverse
    return (applied, jnp.stack([diag_tile, down_tile, up_tile, side_tile]))

def assemble(plane_tiles):
    layers = plane_tiles.shape[0]
    mode_count = plane_tiles.shape[-1]
    size_all = layers * mode_count
    identity = jnp.eye(layers, dtype=jnp.float32)
    subdiag = jnp.eye(layers, k=-1, dtype=jnp.float32)
    diag_block = jnp.einsum('jab,jk->jakb', plane_tiles[:, 0], identity, precision=HIGHEST) + jnp.einsum('jab,jk->jakb', plane_tiles[:, 3], subdiag, precision=HIGHEST) + jnp.einsum('jba,jk->kajb', plane_tiles[:, 3], subdiag, precision=HIGHEST)
    down_block = jnp.einsum('jab,jk->jakb', plane_tiles[:, 1], identity, precision=HIGHEST)
    up_block = jnp.einsum('jab,jk->jakb', plane_tiles[:, 2], identity, precision=HIGHEST)
    return (diag_block.reshape(size_all, size_all), down_block.reshape(size_all, size_all), up_block.reshape(size_all, size_all))

def eliminate(operands):
    diag_block, down_block, up_block = operands
    lower_factor = jnp.linalg.cholesky(diag_block)
    left_block = lax.linalg.triangular_solve(lower_factor, down_block, left_side=True, lower=True).T
    right_block = lax.linalg.triangular_solve(lower_factor, up_block.T, left_side=True, lower=True).T
    left_square = jnp.dot(left_block, left_block.T, precision=HIGHEST)
    right_square = jnp.dot(right_block, right_block.T, precision=HIGHEST)
    cross_term = -jnp.dot(right_block, left_block.T, precision=HIGHEST)
    return (lower_factor, left_block, right_block, left_square, right_square, cross_term)

def from_lower(values, axis):
    zero_edge = jnp.zeros_like(lax.slice_in_dim(values, 0, 1, axis=axis))
    return jnp.concatenate([zero_edge, lax.slice_in_dim(values, 0, values.shape[axis] - 1, axis=axis)], axis)

def from_upper(values, axis):
    zero_edge = jnp.zeros_like(lax.slice_in_dim(values, 0, 1, axis=axis))
    return jnp.concatenate([lax.slice_in_dim(values, 1, values.shape[axis], axis=axis), zero_edge], axis)

def pick_rows(vectors, row_lists):
    return jnp.stack([jnp.take(vectors, row_lists[k], axis=1) for k in range(4)])

def one_device(operands):
    return device_terms(*operands)

def reference(eigen_vectors, row_mass, inner_weight, face_weight, margin_rows):
    subs = eigen_vectors.shape[0]
    layers = eigen_vectors.shape[1]
    picked = jax.vmap(jax.vmap(pick_rows))(eigen_vectors, margin_rows)
    partners = jnp.stack([from_upper(picked[:, :, 1], 0), from_lower(picked[:, :, 0], 0), from_upper(picked[:, :, 3], 1), from_lower(picked[:, :, 2], 1)], axis=2)
    sub_places = jnp.arange(subs, dtype=jnp.int32)[:, None, None]
    lay_places = jnp.arange(layers, dtype=jnp.int32)[None, :, None]
    springs = jnp.stack([jnp.where(sub_places < subs - 1, face_weight[:, :, 0], 0.0), from_lower(face_weight[:, :, 0], 0), jnp.where(lay_places < layers - 1, face_weight[:, :, 1], 0.0), from_lower(face_weight[:, :, 1], 1)], axis=2)
    total = subs * layers

    def flat(values):
        return values.reshape((total,) + values.shape[2:])
    applied, tiles = lax.map(one_device, (flat(eigen_vectors), flat(row_mass), flat(inner_weight), flat(margin_rows), flat(picked), flat(springs), flat(partners)))
    applied = applied.reshape(eigen_vectors.shape)
    tiles = tiles.reshape((subs, layers) + tiles.shape[1:])
    diag_all, down_all, up_all = jax.vmap(assemble)(tiles)
    diag_blocks = [diag_all[s] for s in range(subs)]
    down_blocks = [down_all[s] for s in range(subs)]
    up_blocks = [up_all[s] for s in range(subs)]
    empty_block = jnp.zeros_like(diag_all[0])
    diag_out = [empty_block] * subs
    left_out = [empty_block] * subs
    right_out = [empty_block] * subs
    distance = 1
    for level_index in range(subs.bit_length() - 1):
        for plane_index in range(subs):
            if (plane_index + 1) % distance == 0 and (plane_index + 1) % (2 * distance) != 0:
                results = eliminate((diag_blocks[plane_index], down_blocks[plane_index], up_blocks[plane_index]))
                lower_factor, left_block, right_block, left_square, right_square, cross_term = results
                diag_out[plane_index] = lower_factor
                left_out[plane_index] = left_block
                right_out[plane_index] = right_block
                partner_left = plane_index - distance
                partner_right = plane_index + distance
                if partner_left >= 0:
                    diag_blocks[partner_left] = diag_blocks[partner_left] - left_square
                    up_blocks[partner_left] = cross_term
                diag_blocks[partner_right] = diag_blocks[partner_right] - right_square
                down_blocks[partner_right] = cross_term
        distance = distance * 2
    diag_out[subs - 1] = jnp.linalg.cholesky(diag_blocks[subs - 1])
    return (applied, jnp.stack(diag_out), jnp.stack(left_out), jnp.stack(right_out))
```

```python
import functools
import jax
import jax.numpy as jnp
from jax import lax
from jax.experimental import pallas as pl
from jax.experimental.pallas import tpu as pltpu
from jax.sharding import PartitionSpec as P

STRIDES = (1, 3, 27)
HIGHEST = lax.Precision.HIGHEST
LANES = 128
ROWS = 8
UNROLLED_LAYERS = 4


def padded(cells, sides, width):
    for axis, dim in sides:
        count = lax.axis_size(axis)
        ends = count - 1
        head = lax.slice_in_dim(cells, 0, width, axis=dim)
        tail = lax.slice_in_dim(cells, cells.shape[dim] - width, cells.shape[dim], axis=dim)
        cells = jnp.concatenate(
            [
                lax.ppermute(tail, axis, [(i, (i + 1) % count) for i in range(ends)]),
                cells,
                lax.ppermute(head, axis, [((i + 1) % count, i) for i in range(ends)]),
            ],
            axis=dim,
        )
    return cells


def device_terms(vectors, masses, interior, row_lists, picked, springs, partners):
    row_count = vectors.shape[-1]
    places = jnp.arange(row_count, dtype=jnp.int32)
    laplace = jnp.zeros_like(vectors)
    for k, t in enumerate(STRIDES):
        edge_weight = jnp.where(places < row_count - t, interior[k], 0.0)
        fluxes = edge_weight * (vectors - jnp.roll(vectors, -t, axis=1))
        laplace = laplace + fluxes - jnp.roll(fluxes, t, axis=1)
    own_part = masses * vectors + laplace
    inverse = 1.0 / row_count
    diag_tile = jnp.dot(vectors, own_part.T, precision=HIGHEST)
    applied = own_part
    for k in range(4):
        onehot = (row_lists[k][:, None] == places[None, :]).astype(jnp.float32)
        diag_tile = diag_tile + jnp.dot(picked[k], (springs[k] * picked[k]).T, precision=HIGHEST)
        applied = applied + jnp.dot(
            springs[k] * (picked[k] - partners[k]), onehot, precision=HIGHEST
        )
    diag_tile = diag_tile * inverse
    down_tile = -jnp.dot(springs[1] * picked[1], partners[1].T, precision=HIGHEST) * inverse
    side_turned = -jnp.dot(partners[3], (springs[3] * picked[3]).T, precision=HIGHEST) * inverse
    tiles = jnp.concatenate([diag_tile, side_turned, down_tile, down_tile.T], axis=1)
    tiles = jnp.pad(tiles, ((0, 0), (0, -tiles.shape[1] % LANES)))
    return applied, tiles


def turned_dot(left, right):
    return lax.dot_general(
        left,
        right,
        (((0,), (0,)), ((), ())),
        precision=HIGHEST,
        preferred_element_type=jnp.float32,
    )


def plain_dot(left, right):
    return lax.dot_general(
        left,
        right,
        (((1,), (0,)), ((), ())),
        precision=HIGHEST,
        preferred_element_type=jnp.float32,
    )


def factor_rows(blocks, tiles_per_part, first_row, turned):
    strip_count = len(blocks[0])
    iota = lax.broadcasted_iota(jnp.int32, (ROWS, LANES), 0)
    lane = lax.broadcasted_iota(jnp.int32, (ROWS, LANES), 1)
    blocks = [[list(strip) for strip in block] for block in blocks]
    for q in range(strip_count):
        for b, block in enumerate(blocks):
            start = q * ROWS
            source = turned(b, block, q)
            columns = [
                [
                    jnp.broadcast_to(source[r][:, start + j : start + j + 1], (ROWS, LANES))
                    for r in range(strip_count - q)
                ]
                for j in range(ROWS)
            ]
            pivots = jnp.zeros((ROWS, LANES), jnp.float32)
            for k in range(ROWS):
                pivot = columns[k][0][k : k + 1, :]
                inverse = 1.0 / pivot
                pivots = jnp.where(iota == k, pivot, pivots)
                below = [jnp.where(iota > k, columns[k][0], 0.0)] + columns[k][1:]
                below = [column * inverse for column in below]
                for j in range(k + 1, ROWS):
                    other = columns[k][0][j : j + 1, :]
                    for r in range(strip_count - q):
                        columns[j][r] = columns[j][r] - below[r] * other
                for t in range(len(block[q])):
                    row = block[q][t][k : k + 1, :]
                    for r in range(strip_count - q):
                        block[q + r][t] = block[q + r][t] - below[r] * row
            scale = lax.rsqrt(pivots)
            for t in range(len(block[q])):
                strip = block[q][t] * scale
                if t < tiles_per_part:
                    keep = lane + t * LANES >= iota + (first_row + start)
                    strip = jnp.where(keep, strip, 0.0)
                block[q][t] = strip
    return blocks


def eliminate_panel(grid_ref, planes, modes, order, part, lanes_used, panel):
    per_part = part // LANES
    first_row = panel * modes
    static = isinstance(panel, int)
    if static:
        rows = pl.ds(first_row, modes)
    else:
        rows = pl.ds(pl.multiple_of(first_row, ROWS), modes)
    blocks = []
    for plane in planes:
        panel_rows = grid_ref[plane, rows, 0:lanes_used]
        blocks.append(
            [
                [
                    panel_rows[q * ROWS : (q + 1) * ROWS, t * LANES : (t + 1) * LANES]
                    for t in range(lanes_used // LANES)
                ]
                for q in range(modes // ROWS)
            ]
        )

    def turned(b, block, q):
        found = []
        for strip in block[q:]:
            if static and first_row // LANES == (first_row + modes - 1) // LANES:
                tile = strip[first_row // LANES]
                offset = first_row % LANES
                found.append(tile if offset == 0 else tile[:, offset : offset + modes])
            else:
                wide = jnp.concatenate(strip[:per_part], axis=1)
                found.append(pltpu.roll(wide, lax.rem(part - first_row, part), 1)[:, :LANES])
        return found

    blocks = factor_rows(blocks, per_part, first_row, turned)
    for plane, block in zip(planes, blocks):
        panel_rows = jnp.concatenate([jnp.concatenate(strip, axis=1) for strip in block], axis=0)
        grid_ref[plane, rows, 0:lanes_used] = panel_rows
        if static:
            below = (panel + 1) * modes
            if below < order:
                columns = panel_rows[:, 0:part].T[below:order]
                update = plain_dot(columns, panel_rows)
                grid_ref[plane, below:order, 0:lanes_used] -= update
        else:
            lane = lax.broadcasted_iota(jnp.int32, (modes, part), 1)
            columns = jnp.where(lane >= first_row + modes, panel_rows[:, 0:part], 0.0)
            update = turned_dot(columns, panel_rows)[0:order]
            grid_ref[plane, :, 0:lanes_used] -= update


def eliminate_planes(grid_ref, planes, modes, order, part, lanes_used):
    layers = order // modes
    if layers <= UNROLLED_LAYERS:
        for panel in range(layers):
            eliminate_panel(grid_ref, planes, modes, order, part, lanes_used, panel)
    else:

        def one_panel(panel, carry):
            eliminate_panel(grid_ref, planes, modes, order, part, lanes_used, panel)
            return carry

        lax.fori_loop(0, layers, one_panel, 0)


def update_partners(grid_ref, plane, distance, part, order, has_left):
    left, right = plane - distance, plane + distance
    both = grid_ref[plane, :, part : 3 * part]
    turned = both.T
    from_right = plain_dot(turned[part : part + order], both)
    grid_ref[right, :, 0:part] -= from_right[:, part : 2 * part]
    grid_ref[right, :, part : 2 * part] = -from_right[:, 0:part]

    def to_left():
        from_left = plain_dot(turned[0:order], both)
        grid_ref[left, :, 0:part] -= from_left[:, 0:part]
        grid_ref[left, :, 2 * part : 3 * part] = -from_left[:, part : 2 * part]

    if isinstance(has_left, bool):
        if has_left:
            to_left()
    else:
        pl.when(has_left)(to_left)


def factor_kernel(place_ref, tiles_ref, diag_ref, left_ref, right_ref, grid_ref, turned_ref):
    subs, layers, modes, _ = tiles_ref.shape
    order = layers * modes
    part = grid_ref.shape[2] // 3
    unrolled = layers <= UNROLLED_LAYERS
    grid_ref[...] = jnp.zeros_like(grid_ref)

    def place_tiles(s, has_left):
        for j in range(layers):
            tile = tiles_ref[s, j]
            rows = slice(j * modes, (j + 1) * modes)
            grid_ref[s, rows, j * modes : (j + 1) * modes] = tile[:, 0:modes]
            if j > 0:
                above = slice((j - 1) * modes, j * modes)
                grid_ref[s, above, j * modes : (j + 1) * modes] = tile[:, modes : 2 * modes]
            lanes = slice(part + j * modes, part + (j + 1) * modes)
            grid_ref[s, rows, lanes] = tile[:, 2 * modes : 3 * modes]
            if has_left:
                lanes = slice(2 * part + j * modes, 2 * part + (j + 1) * modes)
                grid_ref[s - 1, rows, lanes] = tile[:, 3 * modes : 4 * modes]

    place_tiles(0, False)
    if unrolled:
        for s in range(1, subs):
            place_tiles(s, True)
    else:

        def place_one(s, carry):
            place_tiles(s, True)
            return carry

        lax.fori_loop(1, subs, place_one, 0)

    distance = 1
    while distance < subs:
        if unrolled:
            planes = list(range(distance - 1, subs, 2 * distance))
            eliminate_planes(grid_ref, planes, modes, order, part, 3 * part)
            for plane in planes:
                update_partners(grid_ref, plane, distance, part, order, plane >= distance)
        else:

            def one_plane(index, carry, distance=distance):
                plane = distance - 1 + 2 * distance * index
                eliminate_planes(grid_ref, [plane], modes, order, part, 3 * part)
                update_partners(grid_ref, plane, distance, part, order, index > 0)
                return carry

            lax.fori_loop(0, subs // (2 * distance), one_plane, 0)
        distance *= 2
    eliminate_planes(grid_ref, [subs - 1], modes, order, part, part)

    sub_here, lay_here = place_ref[0], place_ref[1]
    strip = pl.ds(pl.multiple_of(lay_here * modes, ROWS), modes)
    for k, out_ref in enumerate((diag_ref, left_ref, right_ref)):
        turned_ref[k] = grid_ref[sub_here, :, k * part : (k + 1) * part].T
        found = turned_ref[k, strip, :]
        out_ref[...] = found if k == 0 else jnp.where(sub_here < subs - 1, found, 0.0)


def factor_planes(place, plane_tiles):
    subs, layers, modes, _ = plane_tiles.shape
    order = layers * modes
    part = -(-order // LANES) * LANES
    strip = jax.ShapeDtypeStruct((modes, order), jnp.float32)
    vmem = pl.BlockSpec(memory_space=pltpu.VMEM)
    return pl.pallas_call(
        factor_kernel,
        out_shape=(strip, strip, strip),
        in_specs=[pl.BlockSpec(memory_space=pltpu.SMEM), vmem],
        out_specs=(vmem, vmem, vmem),
        scratch_shapes=[
            pltpu.VMEM((subs, order, 3 * part), jnp.float32),
            pltpu.VMEM((3, part, order), jnp.float32),
        ],
        compiler_params=pltpu.CompilerParams(vmem_limit_bytes=56 * 1024 * 1024),
        name="factor_planes",
    )(place, plane_tiles)


def per_device(eigen_vectors, row_mass, inner_weight, face_weight, margin_rows):
    vectors = eigen_vectors[0, 0]
    row_lists = margin_rows[0, 0]
    face_springs = face_weight[0, 0]
    mode_count = vectors.shape[0]
    subs = lax.axis_size("sub")
    layers = lax.axis_size("layer")
    sub_here = lax.axis_index("sub")
    lay_here = lax.axis_index("layer")
    picked = jnp.stack([jnp.take(vectors, row_lists[k], axis=1) for k in range(4)])
    zero_row = jnp.zeros((1, row_lists.shape[-1]), jnp.float32)
    sub_send = jnp.stack(
        [
            jnp.concatenate([picked[1], zero_row], 0),
            jnp.concatenate([picked[0], face_springs[0:1]], 0),
        ]
    )
    sub_rim = padded(sub_send, (("sub", 0),), 1)
    lay_send = jnp.stack(
        [
            jnp.concatenate([picked[3], zero_row], 0),
            jnp.concatenate([picked[2], face_springs[1:2]], 0),
        ]
    )
    lay_rim = padded(lay_send, (("layer", 0),), 1)
    partners = jnp.stack(
        [
            sub_rim[3, :mode_count],
            sub_rim[0, :mode_count],
            lay_rim[3, :mode_count],
            lay_rim[0, :mode_count],
        ]
    )
    springs = jnp.stack(
        [
            jnp.where(sub_here < subs - 1, face_springs[0], 0.0),
            sub_rim[0, mode_count],
            jnp.where(lay_here < layers - 1, face_springs[1], 0.0),
            lay_rim[0, mode_count],
        ]
    )
    applied, tiles = device_terms(
        vectors, row_mass[0, 0], inner_weight[0, 0], row_lists, picked, springs, partners
    )
    all_tiles = lax.all_gather(tiles, ("sub", "layer"), axis=0, tiled=False)
    all_tiles = all_tiles.reshape(subs, layers, *tiles.shape)
    place = jnp.stack([sub_here, lay_here]).astype(jnp.int32)
    diag_strip, left_strip, right_strip = factor_planes(place, all_tiles)
    return (applied[None, None], diag_strip[None], left_strip[None], right_strip[None])


def solution(mesh):
    in_specs = (
        P("sub", "layer", None, None),
        P("sub", "layer", None),
        P("sub", "layer", None, None),
        P("sub", "layer", None, None),
        P("sub", "layer", None, None),
    )
    out_specs = (
        P("sub", "layer", None, None),
        P("sub", "layer", None),
        P("sub", "layer", None),
        P("sub", "layer", None),
    )
    return jax.shard_map(
        per_device, mesh=mesh, in_specs=in_specs, out_specs=out_specs, check_vma=False
    )
```

```python
import functools
import jax
import jax.numpy as jnp
from jax import lax
from jax.experimental import pallas as pl
from jax.experimental.pallas import tpu as pltpu
from jax.sharding import PartitionSpec as P

STRIDES = (1, 3, 27)
HIGHEST = lax.Precision.HIGHEST
LANES = 128
ROWS = 8
UNROLLED_LAYERS = 4


def padded(cells, sides, width):
    for axis, dim in sides:
        count = lax.axis_size(axis)
        ends = count - 1
        head = lax.slice_in_dim(cells, 0, width, axis=dim)
        tail = lax.slice_in_dim(cells, cells.shape[dim] - width, cells.shape[dim], axis=dim)
        cells = jnp.concatenate(
            [
                lax.ppermute(tail, axis, [(i, (i + 1) % count) for i in range(ends)]),
                cells,
                lax.ppermute(head, axis, [((i + 1) % count, i) for i in range(ends)]),
            ],
            axis=dim,
        )
    return cells


def device_terms(vectors, masses, interior, row_lists, picked, springs, partners):
    row_count = vectors.shape[-1]
    places = jnp.arange(row_count, dtype=jnp.int32)
    laplace = jnp.zeros_like(vectors)
    for k, t in enumerate(STRIDES):
        edge_weight = jnp.where(places < row_count - t, interior[k], 0.0)
        fluxes = edge_weight * (vectors - jnp.roll(vectors, -t, axis=1))
        laplace = laplace + fluxes - jnp.roll(fluxes, t, axis=1)
    own_part = masses * vectors + laplace
    inverse = 1.0 / row_count
    diag_tile = jnp.dot(vectors, own_part.T, precision=HIGHEST)
    applied = own_part
    for k in range(4):
        onehot = (row_lists[k][:, None] == places[None, :]).astype(jnp.float32)
        diag_tile = diag_tile + jnp.dot(picked[k], (springs[k] * picked[k]).T, precision=HIGHEST)
        applied = applied + jnp.dot(
            springs[k] * (picked[k] - partners[k]), onehot, precision=HIGHEST
        )
    diag_tile = diag_tile * inverse
    down_tile = -jnp.dot(springs[1] * picked[1], partners[1].T, precision=HIGHEST) * inverse
    side_turned = -jnp.dot(partners[3], (springs[3] * picked[3]).T, precision=HIGHEST) * inverse
    tiles = jnp.concatenate([diag_tile, side_turned, down_tile, down_tile.T], axis=1)
    tiles = jnp.pad(tiles, ((0, 0), (0, -tiles.shape[1] % LANES)))
    return applied, tiles


def turned_dot(left, right):
    return lax.dot_general(
        left,
        right,
        (((0,), (0,)), ((), ())),
        precision=HIGHEST,
        preferred_element_type=jnp.float32,
    )


def plain_dot(left, right):
    return lax.dot_general(
        left,
        right,
        (((1,), (0,)), ((), ())),
        precision=HIGHEST,
        preferred_element_type=jnp.float32,
    )


def factor_rows(blocks, tiles_per_part, first_row, turned):
    strip_count = len(blocks[0])
    iota = lax.broadcasted_iota(jnp.int32, (ROWS, LANES), 0)
    lane = lax.broadcasted_iota(jnp.int32, (ROWS, LANES), 1)
    blocks = [[list(strip) for strip in block] for block in blocks]
    for q in range(strip_count):
        for b, block in enumerate(blocks):
            start = q * ROWS
            source = turned(b, block, q)
            columns = [
                [
                    jnp.broadcast_to(source[r][:, start + j : start + j + 1], (ROWS, LANES))
                    for r in range(strip_count - q)
                ]
                for j in range(ROWS)
            ]
            pivots = jnp.zeros((ROWS, LANES), jnp.float32)
            for k in range(ROWS):
                pivot = columns[k][0][k : k + 1, :]
                inverse = 1.0 / pivot
                pivots = jnp.where(iota == k, pivot, pivots)
                below = [jnp.where(iota > k, columns[k][0], 0.0)] + columns[k][1:]
                below = [column * inverse for column in below]
                for j in range(k + 1, ROWS):
                    other = columns[k][0][j : j + 1, :]
                    for r in range(strip_count - q):
                        columns[j][r] = columns[j][r] - below[r] * other
                for t in range(len(block[q])):
                    row = block[q][t][k : k + 1, :]
                    for r in range(strip_count - q):
                        block[q + r][t] = block[q + r][t] - below[r] * row
            scale = lax.rsqrt(pivots)
            for t in range(len(block[q])):
                strip = block[q][t] * scale
                if t < tiles_per_part:
                    keep = lane + t * LANES >= iota + (first_row + start)
                    strip = jnp.where(keep, strip, 0.0)
                block[q][t] = strip
    return blocks


def eliminate_panel(grid_ref, planes, modes, order, part, lanes_used, panel):
    per_part = part // LANES
    first_row = panel * modes
    static = isinstance(panel, int)
    if static:
        rows = pl.ds(first_row, modes)
    else:
        rows = pl.ds(pl.multiple_of(first_row, ROWS), modes)
    blocks = []
    for plane in planes:
        panel_rows = grid_ref[plane, rows, 0:lanes_used]
        blocks.append(
            [
                [
                    panel_rows[q * ROWS : (q + 1) * ROWS, t * LANES : (t + 1) * LANES]
                    for t in range(lanes_used // LANES)
                ]
                for q in range(modes // ROWS)
            ]
        )

    def turned(b, block, q):
        found = []
        for strip in block[q:]:
            if static and first_row // LANES == (first_row + modes - 1) // LANES:
                tile = strip[first_row // LANES]
                offset = first_row % LANES
                found.append(tile if offset == 0 else tile[:, offset : offset + modes])
            else:
                wide = jnp.concatenate(strip[:per_part], axis=1)
                found.append(pltpu.roll(wide, lax.rem(part - first_row, part), 1)[:, :LANES])
        return found

    blocks = factor_rows(blocks, per_part, first_row, turned)
    for plane, block in zip(planes, blocks):
        panel_rows = jnp.concatenate([jnp.concatenate(strip, axis=1) for strip in block], axis=0)
        grid_ref[plane, rows, 0:lanes_used] = panel_rows
        if static:
            below = (panel + 1) * modes
            if below < order:
                columns = panel_rows[:, 0:part].T[below:order]
                update = plain_dot(columns, panel_rows)
                grid_ref[plane, below:order, 0:lanes_used] -= update
        else:
            lane = lax.broadcasted_iota(jnp.int32, (modes, part), 1)
            columns = jnp.where(lane >= first_row + modes, panel_rows[:, 0:part], 0.0)
            update = turned_dot(columns, panel_rows)[0:order]
            grid_ref[plane, :, 0:lanes_used] -= update


def eliminate_planes(grid_ref, planes, modes, order, part, lanes_used):
    layers = order // modes
    if layers <= UNROLLED_LAYERS:
        for panel in range(layers):
            eliminate_panel(grid_ref, planes, modes, order, part, lanes_used, panel)
    else:

        def one_panel(panel, carry):
            eliminate_panel(grid_ref, planes, modes, order, part, lanes_used, panel)
            return carry

        lax.fori_loop(0, layers, one_panel, 0)


def update_partners(grid_ref, plane, distance, part, order, has_left):
    left, right = plane - distance, plane + distance
    both = grid_ref[plane, :, part : 3 * part]
    turned = both.T
    from_right = plain_dot(turned[part : part + order], both)
    grid_ref[right, :, 0:part] -= from_right[:, part : 2 * part]
    grid_ref[right, :, part : 2 * part] = -from_right[:, 0:part]

    def to_left():
        from_left = plain_dot(turned[0:order], both)
        grid_ref[left, :, 0:part] -= from_left[:, 0:part]
        grid_ref[left, :, 2 * part : 3 * part] = -from_left[:, part : 2 * part]

    if isinstance(has_left, bool):
        if has_left:
            to_left()
    else:
        pl.when(has_left)(to_left)


def factor_kernel(place_ref, tiles_ref, diag_ref, left_ref, right_ref, grid_ref, turned_ref):
    subs, layers, modes, _ = tiles_ref.shape
    order = layers * modes
    part = grid_ref.shape[2] // 3
    unrolled = layers <= UNROLLED_LAYERS
    grid_ref[...] = jnp.zeros_like(grid_ref)

    def place_tiles(s, has_left):
        for j in range(layers):
            tile = tiles_ref[s, j]
            rows = slice(j * modes, (j + 1) * modes)
            grid_ref[s, rows, j * modes : (j + 1) * modes] = tile[:, 0:modes]
            if j > 0:
                above = slice((j - 1) * modes, j * modes)
                grid_ref[s, above, j * modes : (j + 1) * modes] = tile[:, modes : 2 * modes]
            lanes = slice(part + j * modes, part + (j + 1) * modes)
            grid_ref[s, rows, lanes] = tile[:, 2 * modes : 3 * modes]
            if has_left:
                lanes = slice(2 * part + j * modes, 2 * part + (j + 1) * modes)
                grid_ref[s - 1, rows, lanes] = tile[:, 3 * modes : 4 * modes]

    place_tiles(0, False)
    if unrolled:
        for s in range(1, subs):
            place_tiles(s, True)
    else:

        def place_one(s, carry):
            place_tiles(s, True)
            return carry

        lax.fori_loop(1, subs, place_one, 0)

    distance = 1
    while distance < subs:
        if unrolled:
            planes = list(range(distance - 1, subs, 2 * distance))
            eliminate_planes(grid_ref, planes, modes, order, part, 3 * part)
            for plane in planes:
                update_partners(grid_ref, plane, distance, part, order, plane >= distance)
        else:

            def one_plane(index, carry, distance=distance):
                plane = distance - 1 + 2 * distance * index
                eliminate_planes(grid_ref, [plane], modes, order, part, 3 * part)
                update_partners(grid_ref, plane, distance, part, order, index > 0)
                return carry

            lax.fori_loop(0, subs // (2 * distance), one_plane, 0)
        distance *= 2
    eliminate_planes(grid_ref, [subs - 1], modes, order, part, part)

    sub_here, lay_here = place_ref[0], place_ref[1]
    strip = pl.ds(pl.multiple_of(lay_here * modes, ROWS), modes)
    for k, out_ref in enumerate((diag_ref, left_ref, right_ref)):
        turned_ref[k] = grid_ref[sub_here, :, k * part : (k + 1) * part].T
        found = turned_ref[k, strip, :]
        out_ref[...] = found if k == 0 else jnp.where(sub_here < subs - 1, found, 0.0)


def factor_planes(place, plane_tiles):
    subs, layers, modes, _ = plane_tiles.shape
    order = layers * modes
    part = -(-order // LANES) * LANES
    strip = jax.ShapeDtypeStruct((modes, order), jnp.float32)
    vmem = pl.BlockSpec(memory_space=pltpu.VMEM)
    return pl.pallas_call(
        factor_kernel,
        out_shape=(strip, strip, strip),
        in_specs=[pl.BlockSpec(memory_space=pltpu.SMEM), vmem],
        out_specs=(vmem, vmem, vmem),
        scratch_shapes=[
            pltpu.VMEM((subs, order, 3 * part), jnp.float32),
            pltpu.VMEM((3, part, order), jnp.float32),
        ],
        compiler_params=pltpu.CompilerParams(vmem_limit_bytes=56 * 1024 * 1024),
        name="factor_planes",
    )(place, plane_tiles)


def per_device(eigen_vectors, row_mass, inner_weight, face_weight, margin_rows):
    vectors = eigen_vectors[0, 0]
    row_lists = margin_rows[0, 0]
    face_springs = face_weight[0, 0]
    mode_count = vectors.shape[0]
    subs = lax.axis_size("sub")
    layers = lax.axis_size("layer")
    sub_here = lax.axis_index("sub")
    lay_here = lax.axis_index("layer")
    picked = jnp.stack([jnp.take(vectors, row_lists[k], axis=1) for k in range(4)])
    zero_row = jnp.zeros((1, row_lists.shape[-1]), jnp.float32)
    sub_send = jnp.stack(
        [
            jnp.concatenate([picked[1], zero_row], 0),
            jnp.concatenate([picked[0], face_springs[0:1]], 0),
        ]
    )
    sub_rim = padded(sub_send, (("sub", 0),), 1)
    lay_send = jnp.stack(
        [
            jnp.concatenate([picked[3], zero_row], 0),
            jnp.concatenate([picked[2], face_springs[1:2]], 0),
        ]
    )
    lay_rim = padded(lay_send, (("layer", 0),), 1)
    partners = jnp.stack(
        [
            sub_rim[3, :mode_count],
            sub_rim[0, :mode_count],
            lay_rim[3, :mode_count],
            lay_rim[0, :mode_count],
        ]
    )
    springs = jnp.stack(
        [
            jnp.where(sub_here < subs - 1, face_springs[0], 0.0),
            sub_rim[0, mode_count],
            jnp.where(lay_here < layers - 1, face_springs[1], 0.0),
            lay_rim[0, mode_count],
        ]
    )
    applied, tiles = device_terms(
        vectors, row_mass[0, 0], inner_weight[0, 0], row_lists, picked, springs, partners
    )
    copies = jnp.broadcast_to(tiles[None], (subs * layers,) + tiles.shape)
    all_tiles = lax.all_to_all(copies, ("sub", "layer"), split_axis=0, concat_axis=0, tiled=True)
    all_tiles = all_tiles.reshape(subs, layers, *tiles.shape)
    place = jnp.stack([sub_here, lay_here]).astype(jnp.int32)
    diag_strip, left_strip, right_strip = factor_planes(place, all_tiles)
    return (applied[None, None], diag_strip[None], left_strip[None], right_strip[None])


def solution(mesh):
    in_specs = (
        P("sub", "layer", None, None),
        P("sub", "layer", None),
        P("sub", "layer", None, None),
        P("sub", "layer", None, None),
        P("sub", "layer", None, None),
    )
    out_specs = (
        P("sub", "layer", None, None),
        P("sub", "layer", None),
        P("sub", "layer", None),
        P("sub", "layer", None),
    )
    return jax.shard_map(
        per_device, mesh=mesh, in_specs=in_specs, out_specs=out_specs, check_vma=False
    )
```

```python
import functools
import jax
import jax.numpy as jnp
from jax import lax
from jax.experimental import pallas as pl
from jax.experimental.pallas import tpu as pltpu
from jax.sharding import PartitionSpec as P

STRIDES = (1, 3, 27)
HIGHEST = lax.Precision.HIGHEST
LANES = 128
ROWS = 8
UNROLLED_LAYERS = 4


def turned_dot(left, right):
    return lax.dot_general(
        left,
        right,
        (((0,), (0,)), ((), ())),
        precision=HIGHEST,
        preferred_element_type=jnp.float32,
    )


def plain_dot(left, right):
    return lax.dot_general(
        left,
        right,
        (((1,), (0,)), ((), ())),
        precision=HIGHEST,
        preferred_element_type=jnp.float32,
    )


def factor_rows(blocks, tiles_per_part, first_row, turned):
    strip_count = len(blocks[0])
    iota = lax.broadcasted_iota(jnp.int32, (ROWS, LANES), 0)
    lane = lax.broadcasted_iota(jnp.int32, (ROWS, LANES), 1)
    blocks = [[list(strip) for strip in block] for block in blocks]
    for q in range(strip_count):
        for b, block in enumerate(blocks):
            start = q * ROWS
            source = turned(b, block, q)
            columns = [
                [
                    jnp.broadcast_to(source[r][:, start + j : start + j + 1], (ROWS, LANES))
                    for r in range(strip_count - q)
                ]
                for j in range(ROWS)
            ]
            pivots = jnp.zeros((ROWS, LANES), jnp.float32)
            for k in range(ROWS):
                pivot = columns[k][0][k : k + 1, :]
                inverse = 1.0 / pivot
                pivots = jnp.where(iota == k, pivot, pivots)
                below = [jnp.where(iota > k, columns[k][0], 0.0)] + columns[k][1:]
                below = [column * inverse for column in below]
                for j in range(k + 1, ROWS):
                    other = columns[k][0][j : j + 1, :]
                    for r in range(strip_count - q):
                        columns[j][r] = columns[j][r] - below[r] * other
                for t in range(len(block[q])):
                    row = block[q][t][k : k + 1, :]
                    for r in range(strip_count - q):
                        block[q + r][t] = block[q + r][t] - below[r] * row
            scale = lax.rsqrt(pivots)
            for t in range(len(block[q])):
                strip = block[q][t] * scale
                if t < tiles_per_part:
                    keep = lane + t * LANES >= iota + (first_row + start)
                    strip = jnp.where(keep, strip, 0.0)
                block[q][t] = strip
    return blocks


def eliminate_panel(grid_ref, planes, modes, order, part, lanes_used, panel):
    per_part = part // LANES
    first_row = panel * modes
    static = isinstance(panel, int)
    if static:
        rows = pl.ds(first_row, modes)
    else:
        rows = pl.ds(pl.multiple_of(first_row, ROWS), modes)
    blocks = []
    for plane in planes:
        panel_rows = grid_ref[plane, rows, 0:lanes_used]
        blocks.append(
            [
                [
                    panel_rows[q * ROWS : (q + 1) * ROWS, t * LANES : (t + 1) * LANES]
                    for t in range(lanes_used // LANES)
                ]
                for q in range(modes // ROWS)
            ]
        )

    def turned(b, block, q):
        found = []
        for strip in block[q:]:
            if static and first_row // LANES == (first_row + modes - 1) // LANES:
                tile = strip[first_row // LANES]
                offset = first_row % LANES
                found.append(tile if offset == 0 else tile[:, offset : offset + modes])
            else:
                wide = jnp.concatenate(strip[:per_part], axis=1)
                found.append(pltpu.roll(wide, lax.rem(part - first_row, part), 1)[:, :LANES])
        return found

    blocks = factor_rows(blocks, per_part, first_row, turned)
    for plane, block in zip(planes, blocks):
        panel_rows = jnp.concatenate([jnp.concatenate(strip, axis=1) for strip in block], axis=0)
        grid_ref[plane, rows, 0:lanes_used] = panel_rows
        if static:
            below = (panel + 1) * modes
            if below < order:
                columns = panel_rows[:, 0:part].T[below:order]
                update = plain_dot(columns, panel_rows)
                grid_ref[plane, below:order, 0:lanes_used] -= update
        else:
            lane = lax.broadcasted_iota(jnp.int32, (modes, part), 1)
            columns = jnp.where(lane >= first_row + modes, panel_rows[:, 0:part], 0.0)
            update = turned_dot(columns, panel_rows)[0:order]
            grid_ref[plane, :, 0:lanes_used] -= update


def eliminate_planes(grid_ref, planes, modes, order, part, lanes_used):
    layers = order // modes
    if layers <= UNROLLED_LAYERS:
        for panel in range(layers):
            eliminate_panel(grid_ref, planes, modes, order, part, lanes_used, panel)
    else:

        def one_panel(panel, carry):
            eliminate_panel(grid_ref, planes, modes, order, part, lanes_used, panel)
            return carry

        lax.fori_loop(0, layers, one_panel, 0)


def update_partners(grid_ref, plane, distance, part, order, has_left):
    left, right = plane - distance, plane + distance
    both = grid_ref[plane, :, part : 3 * part]
    turned = both.T
    from_right = plain_dot(turned[part : part + order], both)
    grid_ref[right, :, 0:part] -= from_right[:, part : 2 * part]
    grid_ref[right, :, part : 2 * part] = -from_right[:, 0:part]

    def to_left():
        from_left = plain_dot(turned[0:order], both)
        grid_ref[left, :, 0:part] -= from_left[:, 0:part]
        grid_ref[left, :, 2 * part : 3 * part] = -from_left[:, part : 2 * part]

    if isinstance(has_left, bool):
        if has_left:
            to_left()
    else:
        pl.when(has_left)(to_left)


def unpack_tile(packed, modes):
    half = 3 * modes // 2
    upper = packed[:, 0 : 3 * modes]
    lower = jnp.concatenate(
        [packed[0:ROWS, 3 * modes : 3 * modes + half], packed[ROWS:, 3 * modes : 3 * modes + half]],
        axis=1,
    )
    return jnp.concatenate([upper, lower], axis=0)


def pack_tile(tile):
    modes = tile.shape[0]
    half = 3 * modes // 2
    top = modes - ROWS
    upper = tile[0:top]
    lower = jnp.concatenate([tile[top:, 0:half], tile[top:, half:]], axis=0)
    spare = jnp.zeros((top, LANES - 3 * modes - half), jnp.float32)
    return jnp.concatenate([upper, lower, spare], axis=1)


def factor_kernel(place_ref, tiles_ref, diag_ref, left_ref, right_ref, grid_ref, turned_ref):
    layers, subs, _, _ = tiles_ref.shape
    modes, order = diag_ref.shape
    part = grid_ref.shape[2] // 3
    unrolled = layers <= UNROLLED_LAYERS
    grid_ref[...] = jnp.zeros_like(grid_ref)

    def place_tiles(s, has_left):
        for j in range(layers):
            tile = unpack_tile(tiles_ref[j, s], modes)
            rows = slice(j * modes, (j + 1) * modes)
            grid_ref[s, rows, j * modes : (j + 1) * modes] = tile[:, 0:modes]
            if j > 0:
                above = slice((j - 1) * modes, j * modes)
                grid_ref[s, above, j * modes : (j + 1) * modes] = tile[:, modes : 2 * modes]
            if has_left:
                down_turned = tile[:, 2 * modes : 3 * modes]
                lanes = slice(part + j * modes, part + (j + 1) * modes)
                grid_ref[s, rows, lanes] = down_turned.T
                lanes = slice(2 * part + j * modes, 2 * part + (j + 1) * modes)
                grid_ref[s - 1, rows, lanes] = down_turned

    place_tiles(0, False)
    if unrolled:
        for s in range(1, subs):
            place_tiles(s, True)
    else:

        def place_one(s, carry):
            place_tiles(s, True)
            return carry

        lax.fori_loop(1, subs, place_one, 0)

    distance = 1
    while distance < subs:
        if unrolled:
            planes = list(range(distance - 1, subs, 2 * distance))
            eliminate_planes(grid_ref, planes, modes, order, part, 3 * part)
            for plane in planes:
                update_partners(grid_ref, plane, distance, part, order, plane >= distance)
        else:

            def one_plane(index, carry, distance=distance):
                plane = distance - 1 + 2 * distance * index
                eliminate_planes(grid_ref, [plane], modes, order, part, 3 * part)
                update_partners(grid_ref, plane, distance, part, order, index > 0)
                return carry

            lax.fori_loop(0, subs // (2 * distance), one_plane, 0)
        distance *= 2
    eliminate_planes(grid_ref, [subs - 1], modes, order, part, part)

    sub_here, lay_here = place_ref[0], place_ref[1]
    strip = pl.ds(pl.multiple_of(lay_here * modes, ROWS), modes)
    for k, out_ref in enumerate((diag_ref, left_ref, right_ref)):
        turned_ref[k] = grid_ref[sub_here, :, k * part : (k + 1) * part].T
        found = turned_ref[k, strip, :]
        out_ref[...] = found if k == 0 else jnp.where(sub_here < subs - 1, found, 0.0)


VMEM_BLOCK = pl.BlockSpec(memory_space=pltpu.VMEM)
SMEM_BLOCK = pl.BlockSpec(memory_space=pltpu.SMEM)
PARAMS = pltpu.CompilerParams(vmem_limit_bytes=56 * 1024 * 1024)


def factor_planes(place, plane_tiles, modes):
    layers, subs, _, _ = plane_tiles.shape
    order = layers * modes
    part = -(-order // LANES) * LANES
    strip = jax.ShapeDtypeStruct((modes, order), jnp.float32)
    return pl.pallas_call(
        factor_kernel,
        out_shape=(strip, strip, strip),
        in_specs=[SMEM_BLOCK, VMEM_BLOCK],
        out_specs=(VMEM_BLOCK, VMEM_BLOCK, VMEM_BLOCK),
        scratch_shapes=[
            pltpu.VMEM((subs, order, 3 * part), jnp.float32),
            pltpu.VMEM((3, part, order), jnp.float32),
        ],
        compiler_params=PARAMS,
        name="factor_planes",
    )(place, plane_tiles)


def across_dot(left, right):
    return lax.dot_general(
        left,
        right,
        (((1,), (1,)), ((), ())),
        precision=HIGHEST,
        preferred_element_type=jnp.float32,
    )


def pick_kernel(place_ref, vectors_ref, lists_ref, face_ref, picked_ref, sub_ref, layer_ref):
    lay_here, layers = place_ref[1], layer_ref.shape[0]
    modes, row_count = vectors_ref.shape
    layer_ref[...] = jnp.zeros_like(layer_ref)
    sub_ref[...] = jnp.zeros_like(sub_ref)
    for k in range(4):
        rows = jnp.broadcast_to(lists_ref[k : k + 1, :], (ROWS, LANES))
        tile_of, lane_of = rows // LANES, rows % LANES
        found = [jnp.zeros((ROWS, LANES), jnp.float32) for _ in range(modes // ROWS)]
        for c in range(row_count // LANES):
            here = tile_of == c
            for r in range(modes // ROWS):
                tile = vectors_ref[r * ROWS : (r + 1) * ROWS, c * LANES : (c + 1) * LANES]
                moved = jnp.take_along_axis(tile, lane_of, axis=1, mode="promise_in_bounds")
                found[r] = jnp.where(here, moved, found[r])
        picked_ref[k] = jnp.concatenate(found, axis=0)
    sub_ref[0:modes] = picked_ref[0]
    sub_ref[modes : modes + 1] = face_ref[0:1]

    @pl.when(lay_here < layers - 1)
    def _():
        layer_ref[lay_here + 1, 0:modes] = picked_ref[2]
        layer_ref[lay_here + 1, modes : modes + 1] = face_ref[1:2]

    @pl.when(lay_here > 0)
    def _():
        layer_ref[lay_here - 1, 0:modes] = picked_ref[3]


def own_kernel(place_ref, vectors_ref, mass_ref, inner_ref, face_ref, picked_ref, base_ref, own_ref, *, subs, layers):
    vectors = vectors_ref[...]
    row_count = vectors.shape[1]
    places = lax.broadcasted_iota(jnp.int32, (1, row_count), 1)
    base = mass_ref[...] * vectors
    for k, t in enumerate(STRIDES):
        edge_weight = jnp.where(places < row_count - t, inner_ref[k : k + 1, :], 0.0)
        fluxes = edge_weight * (vectors - pltpu.roll(vectors, row_count - t, 1))
        base = base + fluxes - pltpu.roll(fluxes, t, 1)
    base_ref[...] = base
    own = across_dot(vectors, base)
    for k, has_next in ((0, place_ref[0] < subs - 1), (2, place_ref[1] < layers - 1)):
        springs = jnp.where(has_next, face_ref[k // 2 : k // 2 + 1, :], 0.0)
        own = own + across_dot(picked_ref[k], springs * picked_ref[k])
    own_ref[...] = own


def partner_from(layer_ref, position, exists):
    clamped = jnp.clip(position, 0, layer_ref.shape[0] - 1)
    return jnp.where(exists, layer_ref[clamped], 0.0)


def tile_kernel(place_ref, own_ref, picked_ref, sub_ref, layer_ref, copies_ref, *, row_count):
    modes = own_ref.shape[0]
    lay_here = place_ref[1]
    inverse = 1.0 / row_count
    before = partner_from(layer_ref, lay_here - 1, lay_here > 0)
    pairs = []
    for mine, theirs in ((picked_ref[1], sub_ref[...]), (picked_ref[3], before)):
        sprung = theirs[modes : modes + 1] * mine
        stacked = jnp.concatenate([mine, theirs[0:modes]], axis=0)
        pairs.append(across_dot(stacked, sprung))
    down, side = pairs
    diag_tile = (own_ref[...] + down[0:modes] + side[0:modes]) * inverse
    side_turned = -side[modes:] * inverse
    down_turned = -down[modes:] * inverse
    packed = pack_tile(jnp.concatenate([diag_tile, side_turned, down_turned], axis=1))
    for s in range(copies_ref.shape[0]):
        copies_ref[s] = packed


def scatter_kernel(place_ref, base_ref, lists_ref, face_ref, picked_ref, sub_ref, next_ref, layer_ref, applied_ref, *, subs):
    modes, row_count = base_ref.shape
    sub_here, lay_here = place_ref[0], place_ref[1]
    layers = layer_ref.shape[0]
    width = 2 * LANES
    after = partner_from(layer_ref, lay_here + 1, lay_here < layers - 1)
    before = partner_from(layer_ref, lay_here - 1, lay_here > 0)
    springs = [
        jnp.where(sub_here < subs - 1, face_ref[0:1, :], 0.0),
        sub_ref[modes : modes + 1, :],
        jnp.where(lay_here < layers - 1, face_ref[1:2, :], 0.0),
        before[modes : modes + 1],
    ]
    partners = [next_ref[...], sub_ref[0:modes, :], after[0:modes], before[0:modes]]
    pulls = jnp.concatenate(
        [springs[k] * (picked_ref[k] - partners[k]) for k in range(4)], axis=1
    )
    rows = jnp.concatenate([lists_ref[k : k + 1, :] for k in range(4)], axis=1)
    block_of, lane_of = rows // width, rows % width
    lanes = lax.broadcasted_iota(jnp.int32, (width, rows.shape[1]), 0)
    onehot = jnp.where(lanes == lane_of, 1.0, 0.0).astype(jnp.bfloat16)
    total = None
    rest = pulls
    for _ in range(3):
        piece = rest.astype(jnp.bfloat16).astype(jnp.float32)
        rest = rest - piece
        spread = jnp.concatenate(
            [jnp.where(block_of == h, piece, 0.0) for h in range(row_count // width)], axis=0
        ).astype(jnp.bfloat16)
        moved = lax.dot_general(
            spread, onehot, (((1,), (1,)), ((), ())), preferred_element_type=jnp.float32
        )
        total = moved if total is None else total + moved
    for h in range(row_count // width):
        lanes = slice(h * width, (h + 1) * width)
        applied_ref[:, lanes] = base_ref[:, lanes] + total[h * modes : (h + 1) * modes]


def local_call(body, outputs, operands, name):
    shapes = tuple(jax.ShapeDtypeStruct(shape, jnp.float32) for shape in outputs)
    return pl.pallas_call(
        body,
        out_shape=shapes,
        in_specs=[SMEM_BLOCK] + [VMEM_BLOCK] * (len(operands) - 1),
        out_specs=tuple(VMEM_BLOCK for _ in shapes),
        compiler_params=PARAMS,
        name=name,
    )(*operands)


def per_device(eigen_vectors, row_mass, inner_weight, face_weight, margin_rows):
    vectors = eigen_vectors[0, 0]
    row_lists = margin_rows[0, 0]
    face_springs = face_weight[0, 0]
    modes, row_count = vectors.shape
    width = row_lists.shape[-1]
    subs = lax.axis_size("sub")
    layers = lax.axis_size("layer")
    place = jnp.stack([lax.axis_index("sub"), lax.axis_index("layer")]).astype(jnp.int32)
    picked, sub_send, layer_send = local_call(
        pick_kernel,
        [(4, modes, width), (modes + ROWS, width), (layers, modes + ROWS, width)],
        (place, vectors, row_lists, face_springs),
        "pick_rows",
    )
    layer_rim = lax.all_to_all(layer_send, "layer", split_axis=0, concat_axis=0, tiled=True)
    sub_rim = lax.ppermute(sub_send, "sub", [(i, i + 1) for i in range(subs - 1)])
    next_rim = lax.ppermute(picked[1], "sub", [(i + 1, i) for i in range(subs - 1)])
    base, own = local_call(
        functools.partial(own_kernel, subs=subs, layers=layers),
        [(modes, row_count), (modes, modes)],
        (place, vectors, row_mass[0], inner_weight[0, 0], face_springs, picked),
        "own_rows",
    )
    (copies,) = local_call(
        functools.partial(tile_kernel, row_count=row_count),
        [(subs, modes - ROWS, LANES)],
        (place, own, picked, sub_rim, layer_rim),
        "coarse_tiles",
    )
    column = lax.all_to_all(copies, "sub", split_axis=0, concat_axis=0, tiled=True)
    columns = jnp.broadcast_to(column[None], (layers,) + column.shape)
    plane_tiles = lax.all_to_all(columns, "layer", split_axis=0, concat_axis=0, tiled=True)
    (applied,) = local_call(
        functools.partial(scatter_kernel, subs=subs),
        [(modes, row_count)],
        (place, base, row_lists, face_springs, picked, sub_rim, next_rim, layer_rim),
        "spread_rows",
    )
    diag_strip, left_strip, right_strip = factor_planes(place, plane_tiles, modes)
    return (applied[None, None], diag_strip[None], left_strip[None], right_strip[None])


def solution(mesh):
    in_specs = (
        P("sub", "layer", None, None),
        P("sub", "layer", None),
        P("sub", "layer", None, None),
        P("sub", "layer", None, None),
        P("sub", "layer", None, None),
    )
    out_specs = (
        P("sub", "layer", None, None),
        P("sub", "layer", None),
        P("sub", "layer", None),
        P("sub", "layer", None),
    )
    return jax.shard_map(
        per_device, mesh=mesh, in_specs=in_specs, out_specs=out_specs, check_vma=False
    )
```

```python
import functools
import math
import jax
import jax.numpy as jnp
from jax import lax
from jax.experimental import pallas as pl
from jax.experimental.pallas import tpu as pltpu
from jax.sharding import PartitionSpec as P

STRIDES = (1, 3, 27)
HIGHEST = lax.Precision.HIGHEST
LANES = 128
ROWS = 8
UNROLLED_LAYERS = 4


def turned_dot(left, right):
    return lax.dot_general(
        left,
        right,
        (((0,), (0,)), ((), ())),
        precision=HIGHEST,
        preferred_element_type=jnp.float32,
    )


def plain_dot(left, right):
    return lax.dot_general(
        left,
        right,
        (((1,), (0,)), ((), ())),
        precision=HIGHEST,
        preferred_element_type=jnp.float32,
    )


def factor_rows(blocks, tiles_per_part, first_row, turned):
    strip_count = len(blocks[0])
    iota = lax.broadcasted_iota(jnp.int32, (ROWS, LANES), 0)
    lane = lax.broadcasted_iota(jnp.int32, (ROWS, LANES), 1)
    blocks = [[list(strip) for strip in block] for block in blocks]
    for q in range(strip_count):
        for b, block in enumerate(blocks):
            start = q * ROWS
            source = turned(b, block, q)
            columns = [
                [
                    jnp.broadcast_to(source[r][:, start + j : start + j + 1], (ROWS, LANES))
                    for r in range(strip_count - q)
                ]
                for j in range(ROWS)
            ]
            pivots = jnp.zeros((ROWS, LANES), jnp.float32)
            for k in range(ROWS):
                pivot = columns[k][0][k : k + 1, :]
                inverse = 1.0 / pivot
                pivots = jnp.where(iota == k, pivot, pivots)
                below = [jnp.where(iota > k, columns[k][0], 0.0)] + columns[k][1:]
                below = [column * inverse for column in below]
                for j in range(k + 1, ROWS):
                    other = columns[k][0][j : j + 1, :]
                    for r in range(strip_count - q):
                        columns[j][r] = columns[j][r] - below[r] * other
                for t in range(len(block[q])):
                    row = block[q][t][k : k + 1, :]
                    for r in range(strip_count - q):
                        block[q + r][t] = block[q + r][t] - below[r] * row
            scale = lax.rsqrt(pivots)
            for t in range(len(block[q])):
                strip = block[q][t] * scale
                if t < tiles_per_part:
                    keep = lane + t * LANES >= iota + (first_row + start)
                    strip = jnp.where(keep, strip, 0.0)
                block[q][t] = strip
    return blocks


def eliminate_panel(grid_ref, planes, modes, order, part, lanes_used, panel):
    per_part = part // LANES
    first_row = panel * modes
    static = isinstance(panel, int)
    if static:
        rows = pl.ds(first_row, modes)
    else:
        rows = pl.ds(pl.multiple_of(first_row, ROWS), modes)
    blocks = []
    for plane in planes:
        panel_rows = grid_ref[plane, rows, 0:lanes_used]
        blocks.append(
            [
                [
                    panel_rows[q * ROWS : (q + 1) * ROWS, t * LANES : (t + 1) * LANES]
                    for t in range(lanes_used // LANES)
                ]
                for q in range(modes // ROWS)
            ]
        )

    def turned(b, block, q):
        found = []
        for strip in block[q:]:
            if static and first_row // LANES == (first_row + modes - 1) // LANES:
                tile = strip[first_row // LANES]
                offset = first_row % LANES
                found.append(tile if offset == 0 else tile[:, offset : offset + modes])
            else:
                wide = jnp.concatenate(strip[:per_part], axis=1)
                found.append(pltpu.roll(wide, lax.rem(part - first_row, part), 1)[:, :LANES])
        return found

    blocks = factor_rows(blocks, per_part, first_row, turned)
    for plane, block in zip(planes, blocks):
        panel_rows = jnp.concatenate([jnp.concatenate(strip, axis=1) for strip in block], axis=0)
        grid_ref[plane, rows, 0:lanes_used] = panel_rows
        if static:
            below = (panel + 1) * modes
            if below < order:
                columns = panel_rows[:, 0:part].T[below:order]
                update = plain_dot(columns, panel_rows)
                grid_ref[plane, below:order, 0:lanes_used] -= update
        else:
            lane = lax.broadcasted_iota(jnp.int32, (modes, part), 1)
            columns = jnp.where(lane >= first_row + modes, panel_rows[:, 0:part], 0.0)
            update = turned_dot(columns, panel_rows)[0:order]
            grid_ref[plane, :, 0:lanes_used] -= update


def eliminate_planes(grid_ref, planes, modes, order, part, lanes_used):
    layers = order // modes
    if layers <= UNROLLED_LAYERS:
        for panel in range(layers):
            eliminate_panel(grid_ref, planes, modes, order, part, lanes_used, panel)
    else:

        def one_panel(panel, carry):
            eliminate_panel(grid_ref, planes, modes, order, part, lanes_used, panel)
            return carry

        lax.fori_loop(0, layers, one_panel, 0)


def update_partners(grid_ref, plane, distance, part, order, has_left):
    left, right = plane - distance, plane + distance
    both = grid_ref[plane, :, part : 3 * part]
    turned = both.T
    from_right = plain_dot(turned[part : part + order], both)
    grid_ref[right, :, 0:part] -= from_right[:, part : 2 * part]
    grid_ref[right, :, part : 2 * part] = -from_right[:, 0:part]

    def to_left():
        from_left = plain_dot(turned[0:order], both)
        grid_ref[left, :, 0:part] -= from_left[:, 0:part]
        grid_ref[left, :, 2 * part : 3 * part] = -from_left[:, part : 2 * part]

    if isinstance(has_left, bool):
        if has_left:
            to_left()
    else:
        pl.when(has_left)(to_left)


def unpack_tile(packed, modes):
    half = 3 * modes // 2
    upper = packed[:, 0 : 3 * modes]
    lower = jnp.concatenate(
        [packed[0:ROWS, 3 * modes : 3 * modes + half], packed[ROWS:, 3 * modes : 3 * modes + half]],
        axis=1,
    )
    return jnp.concatenate([upper, lower], axis=0)


def pack_tile(tile):
    modes = tile.shape[0]
    half = 3 * modes // 2
    top = modes - ROWS
    upper = tile[0:top]
    lower = jnp.concatenate([tile[top:, 0:half], tile[top:, half:]], axis=0)
    spare = jnp.zeros((top, LANES - 3 * modes - half), jnp.float32)
    return jnp.concatenate([upper, lower, spare], axis=1)


def factor_kernel(tiles_ref, after_ref, diag_ref, left_ref, right_ref, grid_ref, turned_ref):
    subs, layers, _, _ = tiles_ref.shape
    modes, order = diag_ref.shape
    part = grid_ref.shape[2] // 3
    unrolled = layers <= UNROLLED_LAYERS
    del after_ref
    grid_ref[...] = jnp.zeros_like(grid_ref)

    def place_tiles(s, has_left):
        for j in range(layers):
            tile = unpack_tile(tiles_ref[s, j], modes)
            rows = slice(j * modes, (j + 1) * modes)
            grid_ref[s, rows, j * modes : (j + 1) * modes] = tile[:, 0:modes]
            if j > 0:
                above = slice((j - 1) * modes, j * modes)
                grid_ref[s, above, j * modes : (j + 1) * modes] = tile[:, modes : 2 * modes]
            if has_left:
                down_turned = tile[:, 2 * modes : 3 * modes]
                lanes = slice(part + j * modes, part + (j + 1) * modes)
                grid_ref[s, rows, lanes] = down_turned.T
                lanes = slice(2 * part + j * modes, 2 * part + (j + 1) * modes)
                grid_ref[s - 1, rows, lanes] = down_turned

    place_tiles(0, False)
    if unrolled:
        for s in range(1, subs):
            place_tiles(s, True)
    else:

        def place_one(s, carry):
            place_tiles(s, True)
            return carry

        lax.fori_loop(1, subs, place_one, 0)

    distance = 1
    while distance < subs:
        if unrolled:
            planes = list(range(distance - 1, subs, 2 * distance))
            eliminate_planes(grid_ref, planes, modes, order, part, 3 * part)
            for plane in planes:
                update_partners(grid_ref, plane, distance, part, order, plane >= distance)
        else:

            def one_plane(index, carry, distance=distance):
                plane = distance - 1 + 2 * distance * index
                eliminate_planes(grid_ref, [plane], modes, order, part, 3 * part)
                update_partners(grid_ref, plane, distance, part, order, index > 0)
                return carry

            lax.fori_loop(0, subs // (2 * distance), one_plane, 0)
        distance *= 2
    eliminate_planes(grid_ref, [subs - 1], modes, order, part, part)

    sub_here, lay_here = lax.axis_index("sub"), lax.axis_index("layer")
    strip = pl.ds(pl.multiple_of(lay_here * modes, ROWS), modes)
    for k, out_ref in enumerate((diag_ref, left_ref, right_ref)):
        turned_ref[k] = grid_ref[sub_here, :, k * part : (k + 1) * part].T
        found = turned_ref[k, strip, :]
        out_ref[...] = found if k == 0 else jnp.where(sub_here < subs - 1, found, 0.0)


VMEM_BLOCK = pl.BlockSpec(memory_space=pltpu.VMEM)
SPARE_BYTES = 4 * 1024 * 1024


def kernel_params(shapes):
    held = sum(4 * math.prod(shape) for shape in shapes)
    return pltpu.CompilerParams(vmem_limit_bytes=min(2 * held + SPARE_BYTES, 60 * 1024 * 1024))


def factor_planes(plane_tiles, modes, after):
    subs, layers, _, _ = plane_tiles.shape
    order = layers * modes
    part = -(-order // LANES) * LANES
    strip = jax.ShapeDtypeStruct((modes, order), jnp.float32)
    scratch = ((subs, order, 3 * part), (3, part, order))
    return pl.pallas_call(
        factor_kernel,
        out_shape=(strip, strip, strip),
        in_specs=[VMEM_BLOCK, pl.BlockSpec(memory_space=pl.ANY)],
        out_specs=(VMEM_BLOCK, VMEM_BLOCK, VMEM_BLOCK),
        scratch_shapes=[pltpu.VMEM(shape, jnp.float32) for shape in scratch],
        compiler_params=kernel_params((plane_tiles.shape,) + scratch),
        name="factor_planes",
    )(plane_tiles, after)


def across_dot(left, right):
    return lax.dot_general(
        left,
        right,
        (((1,), (1,)), ((), ())),
        precision=HIGHEST,
        preferred_element_type=jnp.float32,
    )


def pick_kernel(vectors_ref, lists_ref, face_ref, picked_ref, sub_ref, layer_ref):
    modes, row_count = vectors_ref.shape
    for k in range(4):
        rows = jnp.broadcast_to(lists_ref[k : k + 1, :], (ROWS, LANES))
        tile_of, lane_of = rows // LANES, rows % LANES
        found = [jnp.zeros((ROWS, LANES), jnp.float32) for _ in range(modes // ROWS)]
        for c in range(row_count // LANES):
            here = tile_of == c
            for r in range(modes // ROWS):
                tile = vectors_ref[r * ROWS : (r + 1) * ROWS, c * LANES : (c + 1) * LANES]
                moved = jnp.take_along_axis(tile, lane_of, axis=1, mode="promise_in_bounds")
                found[r] = jnp.where(here, moved, found[r])
        picked_ref[k] = jnp.concatenate(found, axis=0)
    for k, send_ref in ((0, sub_ref), (2, layer_ref)):
        send_ref[0:modes] = picked_ref[k]
        send_ref[modes:] = jnp.broadcast_to(face_ref[k // 2 : k // 2 + 1, :], (ROWS, LANES))


def own_kernel(
    vectors_ref, mass_ref, inner_ref, face_ref, picked_ref, base_ref, own_ref, *, subs, layers
):
    vectors = vectors_ref[...]
    row_count = vectors.shape[1]
    places = lax.broadcasted_iota(jnp.int32, (1, row_count), 1)
    base = mass_ref[...] * vectors
    for k, t in enumerate(STRIDES):
        edge_weight = jnp.where(places < row_count - t, inner_ref[k], 0.0)
        fluxes = edge_weight * (vectors - pltpu.roll(vectors, row_count - t, 1))
        base = base + fluxes - pltpu.roll(fluxes, t, 1)
    base_ref[...] = base
    own = across_dot(vectors, base)
    for k, axis, ends in ((0, "sub", subs - 1), (2, "layer", layers - 1)):
        springs = jnp.where(lax.axis_index(axis) < ends, face_ref[k // 2 : k // 2 + 1, :], 0.0)
        own = own + across_dot(picked_ref[k], springs * picked_ref[k])
    own_ref[...] = own


def tile_kernel(
    own_ref, picked_ref, sub_ref, layer_ref, copies_ref, sub_send_ref, layer_send_ref, *, row_count
):
    modes = own_ref.shape[0]
    inverse = 1.0 / row_count
    pairs = []
    for k, theirs_ref in ((1, sub_ref), (3, layer_ref)):
        mine = picked_ref[k]
        sprung = theirs_ref[modes : modes + 1] * mine
        stacked = jnp.concatenate([mine, theirs_ref[0:modes]], axis=0)
        pairs.append(across_dot(stacked, sprung))
    down, side = pairs
    diag_tile = (own_ref[...] + down[0:modes] + side[0:modes]) * inverse
    side_turned = -side[modes:] * inverse
    down_turned = -down[modes:] * inverse
    packed = pack_tile(jnp.concatenate([diag_tile, side_turned, down_turned], axis=1))
    for s in range(copies_ref.shape[0]):
        copies_ref[s] = packed
    sub_send_ref[...] = picked_ref[1]
    layer_send_ref[...] = picked_ref[3]


def scatter_kernel(
    base_ref, lists_ref, face_ref, picked_ref, before_sub_ref, after_sub_ref,
    before_layer_ref, after_layer_ref, applied_ref, *, subs, layers
):
    modes, row_count = base_ref.shape
    width = 2 * LANES
    springs = [
        jnp.where(lax.axis_index("sub") < subs - 1, face_ref[0:1, :], 0.0),
        before_sub_ref[modes : modes + 1, :],
        jnp.where(lax.axis_index("layer") < layers - 1, face_ref[1:2, :], 0.0),
        before_layer_ref[modes : modes + 1, :],
    ]
    partners = [
        after_sub_ref[...],
        before_sub_ref[0:modes, :],
        after_layer_ref[...],
        before_layer_ref[0:modes, :],
    ]
    pulls = jnp.concatenate(
        [springs[k] * (picked_ref[k] - partners[k]) for k in range(4)], axis=1
    )
    rows = jnp.concatenate([lists_ref[k : k + 1, :] for k in range(4)], axis=1)
    block_of, lane_of = rows // width, rows % width
    lanes = lax.broadcasted_iota(jnp.int32, (width, rows.shape[1]), 0)
    onehot = jnp.where(lanes == lane_of, 1.0, 0.0).astype(jnp.bfloat16)
    total = None
    rest = pulls
    for _ in range(3):
        piece = rest.astype(jnp.bfloat16).astype(jnp.float32)
        rest = rest - piece
        spread = jnp.concatenate(
            [jnp.where(block_of == h, piece, 0.0) for h in range(row_count // width)], axis=0
        ).astype(jnp.bfloat16)
        moved = lax.dot_general(
            spread, onehot, (((1,), (1,)), ((), ())), preferred_element_type=jnp.float32
        )
        total = moved if total is None else total + moved
    for h in range(row_count // width):
        lanes = slice(h * width, (h + 1) * width)
        applied_ref[:, lanes] = base_ref[:, lanes] + total[h * modes : (h + 1) * modes]


def local_call(body, outputs, operands, name):
    shapes = tuple(jax.ShapeDtypeStruct(shape, jnp.float32) for shape in outputs)
    return pl.pallas_call(
        body,
        out_shape=shapes,
        in_specs=[VMEM_BLOCK] * len(operands),
        out_specs=tuple(VMEM_BLOCK for _ in shapes),
        compiler_params=kernel_params([x.shape for x in operands] + list(outputs)),
        name=name,
    )(*operands)


def per_device(eigen_vectors, row_mass, inner_weight, face_weight, margin_rows):
    vectors = eigen_vectors[0, 0]
    row_lists = margin_rows[0, 0]
    face_springs = face_weight[0, 0]
    modes, row_count = vectors.shape
    width = row_lists.shape[-1]
    subs = lax.axis_size("sub")
    layers = lax.axis_size("layer")
    up_sub = [(i, i + 1) for i in range(subs - 1)]
    up_layer = [(i, i + 1) for i in range(layers - 1)]
    down_sub = [(i + 1, i) for i in range(subs - 1)]
    down_layer = [(i + 1, i) for i in range(layers - 1)]
    picked, sub_send, layer_send = local_call(
        pick_kernel,
        [(4, modes, width), (modes + ROWS, width), (modes + ROWS, width)],
        (vectors, row_lists, face_springs),
        "pick_rows",
    )
    before_sub = lax.ppermute(sub_send, "sub", up_sub)
    before_layer = lax.ppermute(layer_send, "layer", up_layer)
    base, own = local_call(
        functools.partial(own_kernel, subs=subs, layers=layers),
        [(modes, row_count), (modes, modes)],
        (vectors, row_mass[0], inner_weight[0].reshape(-1, 1, row_count), face_springs, picked),
        "own_rows",
    )
    copies, sub_send, layer_send = local_call(
        functools.partial(tile_kernel, row_count=row_count),
        [(subs * layers, modes - ROWS, LANES), (modes, width), (modes, width)],
        (own, picked, before_sub, before_layer),
        "coarse_tiles",
    )
    tiles = lax.all_to_all(copies, ("sub", "layer"), split_axis=0, concat_axis=0, tiled=True)
    after_sub = lax.ppermute(sub_send, "sub", down_sub)
    after_layer = lax.ppermute(layer_send, "layer", down_layer)
    (applied,) = local_call(
        functools.partial(scatter_kernel, subs=subs, layers=layers),
        [(modes, row_count)],
        (base, row_lists, face_springs, picked, before_sub, after_sub, before_layer, after_layer),
        "spread_rows",
    )
    diag_strip, left_strip, right_strip = factor_planes(
        tiles.reshape(subs, layers, *tiles.shape[1:]), modes, applied
    )
    return (applied[None, None], diag_strip[None], left_strip[None], right_strip[None])


def solution(mesh):
    in_specs = (
        P("sub", "layer", None, None),
        P("sub", "layer", None),
        P("sub", "layer", None, None),
        P("sub", "layer", None, None),
        P("sub", "layer", None, None),
    )
    out_specs = (
        P("sub", "layer", None, None),
        P("sub", "layer", None),
        P("sub", "layer", None),
        P("sub", "layer", None),
    )
    return jax.shard_map(
        per_device, mesh=mesh, in_specs=in_specs, out_specs=out_specs, check_vma=False
    )
```

```python
import functools
import math
import jax
import jax.numpy as jnp
from jax import lax
from jax.experimental import pallas as pl
from jax.experimental.pallas import tpu as pltpu
from jax.sharding import PartitionSpec as P

STRIDES = (1, 3, 27)
HIGHEST = lax.Precision.HIGHEST
LANES = 128
ROWS = 8
UNROLLED_LAYERS = 4


def turned_dot(left, right):
    return lax.dot_general(
        left,
        right,
        (((0,), (0,)), ((), ())),
        precision=HIGHEST,
        preferred_element_type=jnp.float32,
    )


def plain_dot(left, right):
    return lax.dot_general(
        left,
        right,
        (((1,), (0,)), ((), ())),
        precision=HIGHEST,
        preferred_element_type=jnp.float32,
    )


def spread_row(strip, k):
    return jnp.broadcast_to(strip[k : k + 1, :], strip.shape)


def factor_rows(blocks, tiles_per_part, first_row, turned):
    strip_count = len(blocks[0])
    iota = lax.broadcasted_iota(jnp.int32, (ROWS, LANES), 0)
    lane = lax.broadcasted_iota(jnp.int32, (ROWS, LANES), 1)
    blocks = [[list(strip) for strip in block] for block in blocks]
    for q in range(strip_count):
        for b, block in enumerate(blocks):
            start = q * ROWS
            source = turned(b, block, q)
            columns = [
                [
                    jnp.broadcast_to(source[r][:, start + j : start + j + 1], (ROWS, LANES))
                    for r in range(strip_count - q)
                ]
                for j in range(ROWS)
            ]
            pivots = jnp.zeros((ROWS, LANES), jnp.float32)
            for k in range(0, ROWS, 2):
                first, second = columns[k], columns[k + 1]
                corner, joint = spread_row(first[0], k), spread_row(first[0], k + 1)
                other_corner = spread_row(second[0], k + 1)
                minor = corner * other_corner - joint * joint
                inverse = pl.reciprocal(corner, approx=True)
                other_inverse = corner * pl.reciprocal(minor, approx=True)
                pivots = jnp.where(iota == k, corner, pivots)
                pivots = jnp.where(iota == k + 1, minor * inverse, pivots)
                below = [column * inverse for column in first]
                second = [second[r] - below[r] * joint for r in range(len(second))]
                other_below = [column * other_inverse for column in second]
                below[0] = jnp.where(iota > k, below[0], 0.0)
                other_below[0] = jnp.where(iota > k + 1, other_below[0], 0.0)
                for j in range(k + 2, ROWS):
                    head, other_head = spread_row(first[0], j), spread_row(second[0], j)
                    for r in range(strip_count - q):
                        columns[j][r] = columns[j][r] - below[r] * head - other_below[r] * other_head
                for t in range(len(block[q])):
                    row = spread_row(block[q][t], k)
                    for r in range(strip_count - q):
                        block[q + r][t] = block[q + r][t] - below[r] * row
                    row = spread_row(block[q][t], k + 1)
                    for r in range(strip_count - q):
                        block[q + r][t] = block[q + r][t] - other_below[r] * row
            scale = lax.rsqrt(pivots)
            for t in range(len(block[q])):
                strip = block[q][t] * scale
                if t < tiles_per_part:
                    keep = lane + t * LANES >= iota + (first_row + start)
                    strip = jnp.where(keep, strip, 0.0)
                block[q][t] = strip
    return blocks


def eliminate_panel(grid_ref, planes, modes, order, part, lanes_used, panel, banded):
    per_part = part // LANES
    first_row = panel * modes
    static = isinstance(panel, int)
    if static:
        rows = pl.ds(first_row, modes)
    else:
        rows = pl.ds(pl.multiple_of(first_row, ROWS), modes)
    blocks = []
    for plane in planes:
        panel_rows = grid_ref[plane, rows, 0:lanes_used]
        blocks.append(
            [
                [
                    panel_rows[q * ROWS : (q + 1) * ROWS, t * LANES : (t + 1) * LANES]
                    for t in range(lanes_used // LANES)
                ]
                for q in range(modes // ROWS)
            ]
        )

    def turned(b, block, q):
        found = []
        for strip in block[q:]:
            if static and first_row // LANES == (first_row + modes - 1) // LANES:
                tile = strip[first_row // LANES]
                offset = first_row % LANES
                found.append(tile if offset == 0 else tile[:, offset : offset + modes])
            else:
                wide = jnp.concatenate(strip[:per_part], axis=1)
                found.append(pltpu.roll(wide, lax.rem(part - first_row, part), 1)[:, :LANES])
        return found

    blocks = factor_rows(blocks, per_part, first_row, turned)
    for plane, block in zip(planes, blocks):
        panel_rows = jnp.concatenate([jnp.concatenate(strip, axis=1) for strip in block], axis=0)
        grid_ref[plane, rows, 0:lanes_used] = panel_rows
        if static:
            below = (panel + 1) * modes
            end = min(below + modes, order) if banded else order
            if below < order:
                columns = panel_rows[:, 0:part].T[below:end]
                update = plain_dot(columns, panel_rows)
                grid_ref[plane, below:end, 0:lanes_used] -= update
        else:
            lane = lax.broadcasted_iota(jnp.int32, (modes, part), 1)
            columns = jnp.where(lane >= first_row + modes, panel_rows[:, 0:part], 0.0)
            update = turned_dot(columns, panel_rows)[0:order]
            grid_ref[plane, :, 0:lanes_used] -= update


def eliminate_planes(grid_ref, planes, modes, order, part, lanes_used, banded=False):
    layers = order // modes
    if layers <= UNROLLED_LAYERS:
        for panel in range(layers):
            eliminate_panel(grid_ref, planes, modes, order, part, lanes_used, panel, banded)
    else:

        def one_panel(panel, carry):
            eliminate_panel(grid_ref, planes, modes, order, part, lanes_used, panel, banded)
            return carry

        lax.fori_loop(0, layers, one_panel, 0)


def update_partners(grid_ref, plane, distance, part, order, has_left):
    left, right = plane - distance, plane + distance
    both = grid_ref[plane, :, part : 3 * part]
    turned = both.T
    from_right = plain_dot(turned[part : part + order], both)
    grid_ref[right, :, 0:part] -= from_right[:, part : 2 * part]
    grid_ref[right, :, part : 2 * part] = -from_right[:, 0:part]

    def to_left():
        from_left = plain_dot(turned[0:order], both)
        grid_ref[left, :, 0:part] -= from_left[:, 0:part]
        grid_ref[left, :, 2 * part : 3 * part] = -from_left[:, part : 2 * part]

    if isinstance(has_left, bool):
        if has_left:
            to_left()
    else:
        pl.when(has_left)(to_left)


def unpack_tile(packed, modes):
    half = 3 * modes // 2
    upper = packed[:, 0 : 3 * modes]
    lower = jnp.concatenate(
        [packed[0:ROWS, 3 * modes : 3 * modes + half], packed[ROWS:, 3 * modes : 3 * modes + half]],
        axis=1,
    )
    return jnp.concatenate([upper, lower], axis=0)


def pack_tile(tile):
    modes = tile.shape[0]
    half = 3 * modes // 2
    top = modes - ROWS
    upper = tile[0:top]
    lower = jnp.concatenate([tile[top:, 0:half], tile[top:, half:]], axis=0)
    spare = jnp.zeros((top, LANES - 3 * modes - half), jnp.float32)
    return jnp.concatenate([upper, lower, spare], axis=1)


def factor_kernel(tiles_ref, after_ref, diag_ref, left_ref, right_ref, grid_ref, turned_ref):
    subs, layers, _, _ = tiles_ref.shape
    modes, order = diag_ref.shape
    part = grid_ref.shape[2] // 3
    unrolled = layers <= UNROLLED_LAYERS
    del after_ref
    grid_ref[...] = jnp.zeros_like(grid_ref)

    def place_tiles(s, has_left):
        for j in range(layers):
            tile = unpack_tile(tiles_ref[s, j], modes)
            rows = slice(j * modes, (j + 1) * modes)
            grid_ref[s, rows, j * modes : (j + 1) * modes] = tile[:, 0:modes]
            if j > 0:
                above = slice((j - 1) * modes, j * modes)
                grid_ref[s, above, j * modes : (j + 1) * modes] = tile[:, modes : 2 * modes]
            if has_left:
                down_turned = tile[:, 2 * modes : 3 * modes]
                lanes = slice(part + j * modes, part + (j + 1) * modes)
                grid_ref[s, rows, lanes] = down_turned.T
                lanes = slice(2 * part + j * modes, 2 * part + (j + 1) * modes)
                grid_ref[s - 1, rows, lanes] = down_turned

    place_tiles(0, False)
    if unrolled:
        for s in range(1, subs):
            place_tiles(s, True)
    else:

        def place_one(s, carry):
            place_tiles(s, True)
            return carry

        lax.fori_loop(1, subs, place_one, 0)

    distance = 1
    while distance < subs:
        if unrolled:
            planes = list(range(distance - 1, subs, 2 * distance))
            eliminate_planes(grid_ref, planes, modes, order, part, 3 * part, distance == 1)
            for plane in planes:
                update_partners(grid_ref, plane, distance, part, order, plane >= distance)
        else:

            def one_plane(index, carry, distance=distance):
                plane = distance - 1 + 2 * distance * index
                eliminate_planes(grid_ref, [plane], modes, order, part, 3 * part)
                update_partners(grid_ref, plane, distance, part, order, index > 0)
                return carry

            lax.fori_loop(0, subs // (2 * distance), one_plane, 0)
        distance *= 2
    eliminate_planes(grid_ref, [subs - 1], modes, order, part, part)

    sub_here, lay_here = lax.axis_index("sub"), lax.axis_index("layer")
    strip = pl.ds(pl.multiple_of(lay_here * modes, ROWS), modes)
    for k, out_ref in enumerate((diag_ref, left_ref, right_ref)):
        turned_ref[k] = grid_ref[sub_here, :, k * part : (k + 1) * part].T
        found = turned_ref[k, strip, :]
        out_ref[...] = found if k == 0 else jnp.where(sub_here < subs - 1, found, 0.0)


VMEM_BLOCK = pl.BlockSpec(memory_space=pltpu.VMEM)
SPARE_BYTES = 4 * 1024 * 1024


def kernel_params(shapes):
    held = sum(4 * math.prod(shape) for shape in shapes)
    return pltpu.CompilerParams(vmem_limit_bytes=min(2 * held + SPARE_BYTES, 60 * 1024 * 1024))


def factor_planes(plane_tiles, modes, after):
    subs, layers, _, _ = plane_tiles.shape
    order = layers * modes
    part = -(-order // LANES) * LANES
    strip = jax.ShapeDtypeStruct((modes, order), jnp.float32)
    scratch = ((subs, order, 3 * part), (3, part, order))
    return pl.pallas_call(
        factor_kernel,
        out_shape=(strip, strip, strip),
        in_specs=[VMEM_BLOCK, VMEM_BLOCK],
        out_specs=(VMEM_BLOCK, VMEM_BLOCK, VMEM_BLOCK),
        scratch_shapes=[pltpu.VMEM(shape, jnp.float32) for shape in scratch],
        compiler_params=kernel_params((plane_tiles.shape,) + scratch),
        name="factor_planes",
    )(plane_tiles, after)


def across_dot(left, right):
    return lax.dot_general(
        left,
        right,
        (((1,), (1,)), ((), ())),
        precision=HIGHEST,
        preferred_element_type=jnp.float32,
    )


def pick_kernel(
    vectors_in, lists_in, face_in, mass_in, inner_in,
    vectors_ref, lists_ref, face_ref, mass_ref, inner_ref, picked_ref, sub_ref, layer_ref, sems
):
    modes, row_count = vectors_ref.shape
    strips = modes // ROWS
    pairs = [(lists_in, lists_ref)]
    pairs += [
        (vectors_in.at[pl.ds(r * ROWS, ROWS)], vectors_ref.at[pl.ds(r * ROWS, ROWS)])
        for r in range(strips)
    ]
    pairs += [(face_in, face_ref), (mass_in, mass_ref), (inner_in, inner_ref)]
    copies = [pltpu.make_async_copy(a, b, sems.at[i]) for i, (a, b) in enumerate(pairs)]
    for copy in copies:
        copy.start()
    copies[0].wait()
    lists = []
    for k in range(4):
        rows = jnp.broadcast_to(lists_ref[k : k + 1, :], (ROWS, LANES))
        lists.append((rows // LANES, rows % LANES))
    for r in range(strips):
        copies[1 + r].wait()
        strip = slice(r * ROWS, (r + 1) * ROWS)
        found = [jnp.zeros((ROWS, LANES), jnp.float32) for _ in range(4)]
        for c in range(row_count // LANES):
            tile = vectors_ref[strip, c * LANES : (c + 1) * LANES]
            for k, (tile_of, lane_of) in enumerate(lists):
                moved = jnp.take_along_axis(tile, lane_of, axis=1, mode="promise_in_bounds")
                found[k] = jnp.where(tile_of == c, moved, found[k])
        for k in range(4):
            picked_ref[k, strip] = found[k]
    for copy in copies[1 + strips :]:
        copy.wait()
    for k, send_ref in ((0, sub_ref), (2, layer_ref)):
        send_ref[0:modes] = picked_ref[k]
        send_ref[modes:] = jnp.broadcast_to(face_ref[k // 2 : k // 2 + 1, :], (ROWS, LANES))


def own_kernel(
    vectors_ref, mass_ref, inner_ref, face_ref, picked_ref, base_ref, own_ref, *, subs, layers
):
    vectors = vectors_ref[...]
    row_count = vectors.shape[1]
    places = lax.broadcasted_iota(jnp.int32, (1, row_count), 1)
    base = mass_ref[...] * vectors
    for k, t in enumerate(STRIDES):
        edge_weight = jnp.where(places < row_count - t, inner_ref[k], 0.0)
        fluxes = edge_weight * (vectors - pltpu.roll(vectors, row_count - t, 1))
        base = base + fluxes - pltpu.roll(fluxes, t, 1)
    base_ref[...] = base
    own = across_dot(vectors, base)
    for k, axis, ends in ((0, "sub", subs - 1), (2, "layer", layers - 1)):
        springs = jnp.where(lax.axis_index(axis) < ends, face_ref[k // 2 : k // 2 + 1, :], 0.0)
        own = own + across_dot(picked_ref[k], springs * picked_ref[k])
    own_ref[...] = own


def tile_kernel(
    own_ref, picked_ref, sub_ref, layer_ref, copies_ref, sub_send_ref, layer_send_ref, *, row_count
):
    modes = own_ref.shape[0]
    inverse = 1.0 / row_count
    pairs = []
    for k, theirs_ref in ((1, sub_ref), (3, layer_ref)):
        mine = picked_ref[k]
        sprung = theirs_ref[modes : modes + 1] * mine
        stacked = jnp.concatenate([mine, theirs_ref[0:modes]], axis=0)
        pairs.append(across_dot(stacked, sprung))
    down, side = pairs
    diag_tile = (own_ref[...] + down[0:modes] + side[0:modes]) * inverse
    side_turned = -side[modes:] * inverse
    down_turned = -down[modes:] * inverse
    packed = pack_tile(jnp.concatenate([diag_tile, side_turned, down_turned], axis=1))
    for s in range(copies_ref.shape[0]):
        copies_ref[s] = packed
    sub_send_ref[...] = picked_ref[1]
    layer_send_ref[...] = picked_ref[3]


def scatter_kernel(
    base_ref, lists_ref, face_ref, picked_ref, before_sub_ref, after_sub_ref,
    before_layer_ref, after_layer_ref, applied_ref, token_ref, *, subs, layers
):
    modes, row_count = base_ref.shape
    width = 2 * LANES
    springs = [
        jnp.where(lax.axis_index("sub") < subs - 1, face_ref[0:1, :], 0.0),
        before_sub_ref[modes : modes + 1, :],
        jnp.where(lax.axis_index("layer") < layers - 1, face_ref[1:2, :], 0.0),
        before_layer_ref[modes : modes + 1, :],
    ]
    partners = [
        after_sub_ref[...],
        before_sub_ref[0:modes, :],
        after_layer_ref[...],
        before_layer_ref[0:modes, :],
    ]
    pulls = jnp.concatenate(
        [springs[k] * (picked_ref[k] - partners[k]) for k in range(4)], axis=1
    )
    rows = jnp.concatenate([lists_ref[k : k + 1, :] for k in range(4)], axis=1)
    block_of, lane_of = rows // width, rows % width
    lanes = lax.broadcasted_iota(jnp.int32, (width, rows.shape[1]), 0)
    onehot = jnp.where(lanes == lane_of, 1.0, 0.0).astype(jnp.bfloat16)
    total = None
    rest = pulls
    for _ in range(3):
        piece = rest.astype(jnp.bfloat16).astype(jnp.float32)
        rest = rest - piece
        spread = jnp.concatenate(
            [jnp.where(block_of == h, piece, 0.0) for h in range(row_count // width)], axis=0
        ).astype(jnp.bfloat16)
        moved = lax.dot_general(
            spread, onehot, (((1,), (1,)), ((), ())), preferred_element_type=jnp.float32
        )
        total = moved if total is None else total + moved
    for h in range(row_count // width):
        lanes = slice(h * width, (h + 1) * width)
        applied_ref[:, lanes] = base_ref[:, lanes] + total[h * modes : (h + 1) * modes]
    token_ref[...] = jnp.zeros_like(token_ref)


def local_call(body, outputs, operands, name):
    shapes = tuple(jax.ShapeDtypeStruct(shape, jnp.float32) for shape in outputs)
    return pl.pallas_call(
        body,
        out_shape=shapes,
        in_specs=[VMEM_BLOCK] * len(operands),
        out_specs=tuple(VMEM_BLOCK for _ in shapes),
        compiler_params=kernel_params([x.shape for x in operands] + list(outputs)),
        name=name,
    )(*operands)


def per_device(eigen_vectors, row_mass, inner_weight, face_weight, margin_rows):
    vectors = eigen_vectors[0, 0]
    row_lists = margin_rows[0, 0]
    face_springs = face_weight[0, 0]
    modes, row_count = vectors.shape
    width = row_lists.shape[-1]
    subs = lax.axis_size("sub")
    layers = lax.axis_size("layer")
    up_sub = [(i, i + 1) for i in range(subs - 1)]
    up_layer = [(i, i + 1) for i in range(layers - 1)]
    down_sub = [(i + 1, i) for i in range(subs - 1)]
    down_layer = [(i + 1, i) for i in range(layers - 1)]
    taken = (vectors, row_lists, face_springs, row_mass[0], inner_weight[0].reshape(-1, 1, row_count))
    held = [(x.shape, x.dtype) for x in taken]
    made = [(4, modes, width), (modes + ROWS, width), (modes + ROWS, width)]
    held += [(shape, jnp.float32) for shape in made]
    vectors, row_lists, face_springs, masses, interior, picked, sub_send, layer_send = pl.pallas_call(
        pick_kernel,
        out_shape=tuple(jax.ShapeDtypeStruct(*pair) for pair in held),
        in_specs=[pl.BlockSpec(memory_space=pltpu.HBM)] * len(taken),
        out_specs=(VMEM_BLOCK,) * len(held),
        scratch_shapes=[pltpu.SemaphoreType.DMA((len(taken) + modes // ROWS - 1,))],
        compiler_params=kernel_params([shape for shape, _ in held]),
        name="pick_rows",
    )(*(pltpu.with_memory_space_constraint(x, pltpu.HBM) for x in taken))
    before_sub = lax.ppermute(sub_send, "sub", up_sub)
    before_layer = lax.ppermute(layer_send, "layer", up_layer)
    base, own = local_call(
        functools.partial(own_kernel, subs=subs, layers=layers),
        [(modes, row_count), (modes, modes)],
        (vectors, masses, interior, face_springs, picked),
        "own_rows",
    )
    copies, sub_send, layer_send = local_call(
        functools.partial(tile_kernel, row_count=row_count),
        [(subs * layers, modes - ROWS, LANES), (modes, width), (modes, width)],
        (own, picked, before_sub, before_layer),
        "coarse_tiles",
    )
    tiles = lax.all_to_all(copies, ("sub", "layer"), split_axis=0, concat_axis=0, tiled=True)
    after_sub = lax.ppermute(sub_send, "sub", down_sub)
    after_layer = lax.ppermute(layer_send, "layer", down_layer)
    applied, token = local_call(
        functools.partial(scatter_kernel, subs=subs, layers=layers),
        [(modes, row_count), (ROWS, LANES)],
        (base, row_lists, face_springs, picked, before_sub, after_sub, before_layer, after_layer),
        "spread_rows",
    )
    diag_strip, left_strip, right_strip = factor_planes(
        tiles.reshape(subs, layers, *tiles.shape[1:]), modes, token
    )
    return (applied[None, None], diag_strip[None], left_strip[None], right_strip[None])


def solution(mesh):
    in_specs = (
        P("sub", "layer", None, None),
        P("sub", "layer", None),
        P("sub", "layer", None, None),
        P("sub", "layer", None, None),
        P("sub", "layer", None, None),
    )
    out_specs = (
        P("sub", "layer", None, None),
        P("sub", "layer", None),
        P("sub", "layer", None),
        P("sub", "layer", None),
    )
    return jax.shard_map(
        per_device, mesh=mesh, in_specs=in_specs, out_specs=out_specs, check_vma=False
    )
```

```python
import functools
import math
import jax
import jax.numpy as jnp
from jax import lax
from jax.experimental import pallas as pl
from jax.experimental.pallas import tpu as pltpu
from jax.sharding import PartitionSpec as P

STRIDES = (1, 3, 27)
HIGHEST = lax.Precision.HIGHEST
LANES = 128
ROWS = 8
UNROLLED_LAYERS = 4


def turned_dot(left, right):
    return lax.dot_general(
        left,
        right,
        (((0,), (0,)), ((), ())),
        precision=HIGHEST,
        preferred_element_type=jnp.float32,
    )


def plain_dot(left, right):
    return lax.dot_general(
        left,
        right,
        (((1,), (0,)), ((), ())),
        precision=HIGHEST,
        preferred_element_type=jnp.float32,
    )


def spread_row(strip, k):
    return jnp.broadcast_to(strip[k : k + 1, :], strip.shape)


def factor_rows(blocks, tiles_per_part, first_row, turned):
    strip_count = len(blocks[0])
    iota = lax.broadcasted_iota(jnp.int32, (ROWS, LANES), 0)
    lane = lax.broadcasted_iota(jnp.int32, (ROWS, LANES), 1)
    blocks = [[list(strip) for strip in block] for block in blocks]
    for q in range(strip_count):
        for b, block in enumerate(blocks):
            start = q * ROWS
            source = turned(b, block, q)
            columns = [
                [
                    jnp.broadcast_to(source[r][:, start + j : start + j + 1], (ROWS, LANES))
                    for r in range(strip_count - q)
                ]
                for j in range(ROWS)
            ]
            pivots = jnp.zeros((ROWS, LANES), jnp.float32)
            for k in range(0, ROWS, 2):
                first, second = columns[k], columns[k + 1]
                corner, joint = spread_row(first[0], k), spread_row(first[0], k + 1)
                other_corner = spread_row(second[0], k + 1)
                minor = corner * other_corner - joint * joint
                inverse = pl.reciprocal(corner, approx=True)
                other_inverse = corner * pl.reciprocal(minor, approx=True)
                pivots = jnp.where(iota == k, corner, pivots)
                pivots = jnp.where(iota == k + 1, minor * inverse, pivots)
                below = [column * inverse for column in first]
                second = [second[r] - below[r] * joint for r in range(len(second))]
                other_below = [column * other_inverse for column in second]
                below[0] = jnp.where(iota > k, below[0], 0.0)
                other_below[0] = jnp.where(iota > k + 1, other_below[0], 0.0)
                for j in range(k + 2, ROWS):
                    head, other_head = spread_row(first[0], j), spread_row(second[0], j)
                    for r in range(strip_count - q):
                        columns[j][r] = columns[j][r] - below[r] * head - other_below[r] * other_head
                for t in range(len(block[q])):
                    row = spread_row(block[q][t], k)
                    for r in range(strip_count - q):
                        block[q + r][t] = block[q + r][t] - below[r] * row
                    row = spread_row(block[q][t], k + 1)
                    for r in range(strip_count - q):
                        block[q + r][t] = block[q + r][t] - other_below[r] * row
            scale = lax.rsqrt(pivots)
            for t in range(len(block[q])):
                strip = block[q][t] * scale
                if t < tiles_per_part:
                    keep = lane + t * LANES >= iota + (first_row + start)
                    strip = jnp.where(keep, strip, 0.0)
                block[q][t] = strip
    return blocks


def eliminate_panel(grid_ref, planes, modes, order, part, lanes_used, panel, banded):
    per_part = part // LANES
    first_row = panel * modes
    static = isinstance(panel, int)
    if static:
        rows = pl.ds(first_row, modes)
    else:
        rows = pl.ds(pl.multiple_of(first_row, ROWS), modes)
    blocks = []
    for plane in planes:
        panel_rows = grid_ref[plane, rows, 0:lanes_used]
        blocks.append(
            [
                [
                    panel_rows[q * ROWS : (q + 1) * ROWS, t * LANES : (t + 1) * LANES]
                    for t in range(lanes_used // LANES)
                ]
                for q in range(modes // ROWS)
            ]
        )

    def turned(b, block, q):
        found = []
        for strip in block[q:]:
            if static and first_row // LANES == (first_row + modes - 1) // LANES:
                tile = strip[first_row // LANES]
                offset = first_row % LANES
                found.append(tile if offset == 0 else tile[:, offset : offset + modes])
            else:
                wide = jnp.concatenate(strip[:per_part], axis=1)
                found.append(pltpu.roll(wide, lax.rem(part - first_row, part), 1)[:, :LANES])
        return found

    blocks = factor_rows(blocks, per_part, first_row, turned)
    for plane, block in zip(planes, blocks):
        panel_rows = jnp.concatenate([jnp.concatenate(strip, axis=1) for strip in block], axis=0)
        grid_ref[plane, rows, 0:lanes_used] = panel_rows
        if static:
            below = (panel + 1) * modes
            end = min(below + modes, order) if banded else order
            if below < order:
                columns = panel_rows[:, 0:part].T[below:end]
                update = plain_dot(columns, panel_rows)
                grid_ref[plane, below:end, 0:lanes_used] -= update
        else:
            lane = lax.broadcasted_iota(jnp.int32, (modes, part), 1)
            columns = jnp.where(lane >= first_row + modes, panel_rows[:, 0:part], 0.0)
            update = turned_dot(columns, panel_rows)[0:order]
            grid_ref[plane, :, 0:lanes_used] -= update


def eliminate_planes(grid_ref, planes, modes, order, part, lanes_used, banded=False):
    layers = order // modes
    if layers <= UNROLLED_LAYERS:
        height = modes if banded else modes * max(1, layers // len(planes))
        for panel in range(order // height):
            eliminate_panel(grid_ref, planes, height, order, part, lanes_used, panel, banded)
    else:

        def one_panel(panel, carry):
            eliminate_panel(grid_ref, planes, modes, order, part, lanes_used, panel, banded)
            return carry

        lax.fori_loop(0, layers, one_panel, 0)


def update_partners(grid_ref, plane, distance, part, order, has_left):
    left, right = plane - distance, plane + distance
    both = grid_ref[plane, :, part : 3 * part]
    turned = both.T
    from_right = plain_dot(turned[part : part + order], both)
    grid_ref[right, :, 0:part] -= from_right[:, part : 2 * part]
    grid_ref[right, :, part : 2 * part] = -from_right[:, 0:part]

    def to_left():
        from_left = plain_dot(turned[0:order], both)
        grid_ref[left, :, 0:part] -= from_left[:, 0:part]
        grid_ref[left, :, 2 * part : 3 * part] = -from_left[:, part : 2 * part]

    if isinstance(has_left, bool):
        if has_left:
            to_left()
    else:
        pl.when(has_left)(to_left)


def unpack_tile(packed, modes):
    half = 3 * modes // 2
    upper = packed[:, 0 : 3 * modes]
    lower = jnp.concatenate(
        [packed[0:ROWS, 3 * modes : 3 * modes + half], packed[ROWS:, 3 * modes : 3 * modes + half]],
        axis=1,
    )
    return jnp.concatenate([upper, lower], axis=0)


def pack_tile(tile):
    modes = tile.shape[0]
    half = 3 * modes // 2
    top = modes - ROWS
    upper = tile[0:top]
    lower = jnp.concatenate([tile[top:, 0:half], tile[top:, half:]], axis=0)
    spare = jnp.zeros((top, LANES - 3 * modes - half), jnp.float32)
    return jnp.concatenate([upper, lower, spare], axis=1)


def factor_kernel(tiles_ref, after_ref, diag_ref, left_ref, right_ref, grid_ref, turned_ref):
    subs, layers, _, _ = tiles_ref.shape
    modes, order = diag_ref.shape
    part = grid_ref.shape[2] // 3
    unrolled = layers <= UNROLLED_LAYERS
    del after_ref
    grid_ref[...] = jnp.zeros_like(grid_ref)

    def place_tiles(s, has_left):
        for j in range(layers):
            tile = unpack_tile(tiles_ref[s, j], modes)
            turned = tile.T
            rows = slice(j * modes, (j + 1) * modes)
            grid_ref[s, rows, j * modes : (j + 1) * modes] = tile[:, 0:modes]
            if j > 0:
                above = slice((j - 1) * modes, j * modes)
                grid_ref[s, above, j * modes : (j + 1) * modes] = tile[:, modes : 2 * modes]
                grid_ref[s, rows, (j - 1) * modes : j * modes] = turned[modes : 2 * modes]
            if has_left:
                lanes = slice(part + j * modes, part + (j + 1) * modes)
                grid_ref[s, rows, lanes] = turned[2 * modes : 3 * modes]
                lanes = slice(2 * part + j * modes, 2 * part + (j + 1) * modes)
                grid_ref[s - 1, rows, lanes] = tile[:, 2 * modes : 3 * modes]

    place_tiles(0, False)
    if unrolled:
        for s in range(1, subs):
            place_tiles(s, True)
    else:

        def place_one(s, carry):
            place_tiles(s, True)
            return carry

        lax.fori_loop(1, subs, place_one, 0)

    distance = 1
    while distance < subs:
        if unrolled:
            planes = list(range(distance - 1, subs, 2 * distance))
            eliminate_planes(grid_ref, planes, modes, order, part, 3 * part, distance == 1)
            for plane in planes:
                update_partners(grid_ref, plane, distance, part, order, plane >= distance)
        else:

            def one_plane(index, carry, distance=distance):
                plane = distance - 1 + 2 * distance * index
                eliminate_planes(grid_ref, [plane], modes, order, part, 3 * part)
                update_partners(grid_ref, plane, distance, part, order, index > 0)
                return carry

            lax.fori_loop(0, subs // (2 * distance), one_plane, 0)
        distance *= 2
    eliminate_planes(grid_ref, [subs - 1], modes, order, part, part)

    sub_here, lay_here = lax.axis_index("sub"), lax.axis_index("layer")
    strip = pl.ds(pl.multiple_of(lay_here * modes, ROWS), modes)
    for k, out_ref in enumerate((diag_ref, left_ref, right_ref)):
        turned_ref[k] = grid_ref[sub_here, :, k * part : (k + 1) * part].T
        found = turned_ref[k, strip, :]
        out_ref[...] = found if k == 0 else jnp.where(sub_here < subs - 1, found, 0.0)


VMEM_BLOCK = pl.BlockSpec(memory_space=pltpu.VMEM)
SPARE_BYTES = 4 * 1024 * 1024


def kernel_params(shapes):
    held = sum(4 * math.prod(shape) for shape in shapes)
    return pltpu.CompilerParams(vmem_limit_bytes=min(2 * held + SPARE_BYTES, 60 * 1024 * 1024))


def factor_planes(plane_tiles, modes, after):
    subs, layers, _, _ = plane_tiles.shape
    order = layers * modes
    part = -(-order // LANES) * LANES
    strip = jax.ShapeDtypeStruct((modes, order), jnp.float32)
    scratch = ((subs, order, 3 * part), (3, part, order))
    return pl.pallas_call(
        factor_kernel,
        out_shape=(strip, strip, strip),
        in_specs=[VMEM_BLOCK, VMEM_BLOCK],
        out_specs=(VMEM_BLOCK, VMEM_BLOCK, VMEM_BLOCK),
        scratch_shapes=[pltpu.VMEM(shape, jnp.float32) for shape in scratch],
        compiler_params=kernel_params((plane_tiles.shape,) + scratch),
        name="factor_planes",
    )(plane_tiles, after)


def across_dot(left, right):
    return lax.dot_general(
        left,
        right,
        (((1,), (1,)), ((), ())),
        precision=HIGHEST,
        preferred_element_type=jnp.float32,
    )


def pick_kernel(
    vectors_in, lists_in, face_in, mass_in, inner_in,
    vectors_ref, lists_ref, face_ref, mass_ref, inner_ref, picked_ref, sub_ref, layer_ref, sems
):
    modes, row_count = vectors_ref.shape
    strips = modes // ROWS
    pairs = [(lists_in, lists_ref)]
    pairs += [
        (vectors_in.at[pl.ds(r * ROWS, ROWS)], vectors_ref.at[pl.ds(r * ROWS, ROWS)])
        for r in range(strips)
    ]
    pairs += [(face_in, face_ref), (mass_in, mass_ref), (inner_in, inner_ref)]
    copies = [pltpu.make_async_copy(a, b, sems.at[i]) for i, (a, b) in enumerate(pairs)]
    for copy in copies:
        copy.start()
    copies[0].wait()
    lists = []
    for k in range(4):
        rows = jnp.broadcast_to(lists_ref[k : k + 1, :], (ROWS, LANES))
        lists.append((rows // LANES, rows % LANES))
    for r in range(strips):
        copies[1 + r].wait()
        strip = slice(r * ROWS, (r + 1) * ROWS)
        found = [jnp.zeros((ROWS, LANES), jnp.float32) for _ in range(4)]
        for c in range(row_count // LANES):
            tile = vectors_ref[strip, c * LANES : (c + 1) * LANES]
            for k, (tile_of, lane_of) in enumerate(lists):
                moved = jnp.take_along_axis(tile, lane_of, axis=1, mode="promise_in_bounds")
                found[k] = jnp.where(tile_of == c, moved, found[k])
        for k in range(4):
            picked_ref[k, strip] = found[k]
    for copy in copies[1 + strips :]:
        copy.wait()
    for k, send_ref in ((0, sub_ref), (2, layer_ref)):
        send_ref[0:modes] = picked_ref[k]
        send_ref[modes:] = jnp.broadcast_to(face_ref[k // 2 : k // 2 + 1, :], (ROWS, LANES))


def own_kernel(
    vectors_ref, mass_ref, inner_ref, face_ref, picked_ref, base_ref, own_ref, *, subs, layers
):
    vectors = vectors_ref[...]
    row_count = vectors.shape[1]
    places = lax.broadcasted_iota(jnp.int32, (1, row_count), 1)
    base = mass_ref[...] * vectors
    for k, t in enumerate(STRIDES):
        edge_weight = jnp.where(places < row_count - t, inner_ref[k], 0.0)
        fluxes = edge_weight * (vectors - pltpu.roll(vectors, row_count - t, 1))
        base = base + fluxes - pltpu.roll(fluxes, t, 1)
    base_ref[...] = base
    own = across_dot(vectors, base)
    for k, axis, ends in ((0, "sub", subs - 1), (2, "layer", layers - 1)):
        springs = jnp.where(lax.axis_index(axis) < ends, face_ref[k // 2 : k // 2 + 1, :], 0.0)
        own = own + across_dot(picked_ref[k], springs * picked_ref[k])
    own_ref[...] = own


def tile_kernel(
    own_ref, picked_ref, sub_ref, layer_ref, copies_ref, sub_send_ref, layer_send_ref, *, row_count
):
    modes = own_ref.shape[0]
    inverse = 1.0 / row_count
    pairs = []
    for k, theirs_ref in ((1, sub_ref), (3, layer_ref)):
        mine = picked_ref[k]
        sprung = theirs_ref[modes : modes + 1] * mine
        stacked = jnp.concatenate([mine, theirs_ref[0:modes]], axis=0)
        pairs.append(across_dot(stacked, sprung))
    down, side = pairs
    diag_tile = (own_ref[...] + down[0:modes] + side[0:modes]) * inverse
    side_turned = -side[modes:] * inverse
    down_turned = -down[modes:] * inverse
    packed = pack_tile(jnp.concatenate([diag_tile, side_turned, down_turned], axis=1))
    for s in range(copies_ref.shape[0]):
        copies_ref[s] = packed
    sub_send_ref[...] = picked_ref[1]
    layer_send_ref[...] = picked_ref[3]


def scatter_kernel(
    base_ref, lists_ref, face_ref, picked_ref, before_sub_ref, after_sub_ref,
    before_layer_ref, after_layer_ref, applied_ref, token_ref, *, subs, layers
):
    modes, row_count = base_ref.shape
    width = 2 * LANES
    springs = [
        jnp.where(lax.axis_index("sub") < subs - 1, face_ref[0:1, :], 0.0),
        before_sub_ref[modes : modes + 1, :],
        jnp.where(lax.axis_index("layer") < layers - 1, face_ref[1:2, :], 0.0),
        before_layer_ref[modes : modes + 1, :],
    ]
    partners = [
        after_sub_ref[...],
        before_sub_ref[0:modes, :],
        after_layer_ref[...],
        before_layer_ref[0:modes, :],
    ]
    pulls = jnp.concatenate(
        [springs[k] * (picked_ref[k] - partners[k]) for k in range(4)], axis=1
    )
    rows = jnp.concatenate([lists_ref[k : k + 1, :] for k in range(4)], axis=1)
    block_of, lane_of = rows // width, rows % width
    lanes = lax.broadcasted_iota(jnp.int32, (width, rows.shape[1]), 0)
    onehot = jnp.where(lanes == lane_of, 1.0, 0.0).astype(jnp.bfloat16)
    total = None
    rest = pulls
    for _ in range(3):
        piece = rest.astype(jnp.bfloat16).astype(jnp.float32)
        rest = rest - piece
        spread = jnp.concatenate(
            [jnp.where(block_of == h, piece, 0.0) for h in range(row_count // width)], axis=0
        ).astype(jnp.bfloat16)
        moved = lax.dot_general(
            spread, onehot, (((1,), (1,)), ((), ())), preferred_element_type=jnp.float32
        )
        total = moved if total is None else total + moved
    for h in range(row_count // width):
        lanes = slice(h * width, (h + 1) * width)
        applied_ref[:, lanes] = base_ref[:, lanes] + total[h * modes : (h + 1) * modes]
    token_ref[...] = jnp.zeros_like(token_ref)


def local_call(body, outputs, operands, name):
    shapes = tuple(jax.ShapeDtypeStruct(shape, jnp.float32) for shape in outputs)
    return pl.pallas_call(
        body,
        out_shape=shapes,
        in_specs=[VMEM_BLOCK] * len(operands),
        out_specs=tuple(VMEM_BLOCK for _ in shapes),
        compiler_params=kernel_params([x.shape for x in operands] + list(outputs)),
        name=name,
    )(*operands)


def per_device(eigen_vectors, row_mass, inner_weight, face_weight, margin_rows):
    vectors = eigen_vectors[0, 0]
    row_lists = margin_rows[0, 0]
    face_springs = face_weight[0, 0]
    modes, row_count = vectors.shape
    width = row_lists.shape[-1]
    subs = lax.axis_size("sub")
    layers = lax.axis_size("layer")
    up_sub = [(i, i + 1) for i in range(subs - 1)]
    up_layer = [(i, i + 1) for i in range(layers - 1)]
    down_sub = [(i + 1, i) for i in range(subs - 1)]
    down_layer = [(i + 1, i) for i in range(layers - 1)]
    taken = (vectors, row_lists, face_springs, row_mass[0], inner_weight[0].reshape(-1, 1, row_count))
    held = [(x.shape, x.dtype) for x in taken]
    made = [(4, modes, width), (modes + ROWS, width), (modes + ROWS, width)]
    held += [(shape, jnp.float32) for shape in made]
    vectors, row_lists, face_springs, masses, interior, picked, sub_send, layer_send = pl.pallas_call(
        pick_kernel,
        out_shape=tuple(jax.ShapeDtypeStruct(*pair) for pair in held),
        in_specs=[pl.BlockSpec(memory_space=pltpu.HBM)] * len(taken),
        out_specs=(VMEM_BLOCK,) * len(held),
        scratch_shapes=[pltpu.SemaphoreType.DMA((len(taken) + modes // ROWS - 1,))],
        compiler_params=kernel_params([shape for shape, _ in held]),
        name="pick_rows",
    )(*(pltpu.with_memory_space_constraint(x, pltpu.HBM) for x in taken))
    before_sub = lax.ppermute(sub_send, "sub", up_sub)
    before_layer = lax.ppermute(layer_send, "layer", up_layer)
    base, own = local_call(
        functools.partial(own_kernel, subs=subs, layers=layers),
        [(modes, row_count), (modes, modes)],
        (vectors, masses, interior, face_springs, picked),
        "own_rows",
    )
    copies, sub_send, layer_send = local_call(
        functools.partial(tile_kernel, row_count=row_count),
        [(subs * layers, modes - ROWS, LANES), (modes, width), (modes, width)],
        (own, picked, before_sub, before_layer),
        "coarse_tiles",
    )
    tiles = lax.all_to_all(copies, ("sub", "layer"), split_axis=0, concat_axis=0, tiled=True)
    after_sub = lax.ppermute(sub_send, "sub", down_sub)
    after_layer = lax.ppermute(layer_send, "layer", down_layer)
    applied, token = local_call(
        functools.partial(scatter_kernel, subs=subs, layers=layers),
        [(modes, row_count), (ROWS, LANES)],
        (base, row_lists, face_springs, picked, before_sub, after_sub, before_layer, after_layer),
        "spread_rows",
    )
    diag_strip, left_strip, right_strip = factor_planes(
        tiles.reshape(subs, layers, *tiles.shape[1:]), modes, token
    )
    return (applied[None, None], diag_strip[None], left_strip[None], right_strip[None])


def solution(mesh):
    in_specs = (
        P("sub", "layer", None, None),
        P("sub", "layer", None),
        P("sub", "layer", None, None),
        P("sub", "layer", None, None),
        P("sub", "layer", None, None),
    )
    out_specs = (
        P("sub", "layer", None, None),
        P("sub", "layer", None),
        P("sub", "layer", None),
        P("sub", "layer", None),
    )
    return jax.shard_map(
        per_device, mesh=mesh, in_specs=in_specs, out_specs=out_specs, check_vma=False
    )
```

```python
import functools
import math
import jax
import jax.numpy as jnp
from jax import lax
from jax.experimental import pallas as pl
from jax.experimental.pallas import tpu as pltpu
from jax.sharding import PartitionSpec as P

STRIDES = (1, 3, 27)
HIGHEST = lax.Precision.HIGHEST
LANES = 128
ROWS = 8
UNROLLED_LAYERS = 4


def turned_dot(left, right):
    return lax.dot_general(
        left,
        right,
        (((0,), (0,)), ((), ())),
        precision=HIGHEST,
        preferred_element_type=jnp.float32,
    )


def plain_dot(left, right):
    return lax.dot_general(
        left,
        right,
        (((1,), (0,)), ((), ())),
        precision=HIGHEST,
        preferred_element_type=jnp.float32,
    )


def spread_row(strip, k):
    return jnp.broadcast_to(strip[k : k + 1, :], strip.shape)


def eliminate_pair(block, columns, pivots, iota, q, k):
    first, second = columns[k], columns[k + 1]
    corner, joint = spread_row(first[0], k), spread_row(first[0], k + 1)
    other_corner = spread_row(second[0], k + 1)
    minor = corner * other_corner - joint * joint
    inverse = pl.reciprocal(corner, approx=True)
    other_inverse = corner * pl.reciprocal(minor, approx=True)
    below = [column * inverse for column in first]
    second = [column - below[r] * joint for r, column in enumerate(second)]
    other_below = [column * other_inverse for column in second]
    below[0] = jnp.where(iota > k, below[0], 0.0)
    other_below[0] = jnp.where(iota > k + 1, other_below[0], 0.0)
    for j in range(k + 2, ROWS):
        head, other_head = spread_row(first[0], j), spread_row(second[0], j)
        columns[j] = [
            column - below[r] * head - other_below[r] * other_head
            for r, column in enumerate(columns[j])
        ]
    for t in range(len(block[q])):
        row = spread_row(block[q][t], k)
        for r, lower in enumerate(below):
            block[q + r][t] = block[q + r][t] - lower * row
        row = spread_row(block[q][t], k + 1)
        for r, lower in enumerate(other_below):
            block[q + r][t] = block[q + r][t] - lower * row
    return jnp.where(iota == k, corner, jnp.where(iota == k + 1, minor * inverse, pivots))


def factor_rows(blocks, tiles_per_part, first_row, turned):
    strip_count = len(blocks[0])
    iota = lax.broadcasted_iota(jnp.int32, (ROWS, LANES), 0)
    lane = lax.broadcasted_iota(jnp.int32, (ROWS, LANES), 1)
    blocks = [[list(strip) for strip in block] for block in blocks]
    for q in range(strip_count):
        start = q * ROWS
        held = []
        for b, block in enumerate(blocks):
            source = turned(b, block, q)
            held.append(
                [
                    [
                        jnp.broadcast_to(strip[:, start + j : start + j + 1], (ROWS, LANES))
                        for strip in source
                    ]
                    for j in range(ROWS)
                ]
            )
        pivots = [jnp.zeros((ROWS, LANES), jnp.float32) for _ in blocks]
        for k in range(0, ROWS, 2):
            for b, block in enumerate(blocks):
                pivots[b] = eliminate_pair(block, held[b], pivots[b], iota, q, k)
        for b, block in enumerate(blocks):
            scale = lax.rsqrt(pivots[b])
            for t in range(len(block[q])):
                strip = block[q][t] * scale
                if t < tiles_per_part:
                    keep = lane + t * LANES >= iota + (first_row + start)
                    strip = jnp.where(keep, strip, 0.0)
                block[q][t] = strip
    return blocks


def eliminate_panel(grid_ref, planes, modes, order, part, lanes_used, panel, banded):
    per_part = part // LANES
    first_row = panel * modes
    static = isinstance(panel, int)
    if static:
        rows = pl.ds(first_row, modes)
    else:
        rows = pl.ds(pl.multiple_of(first_row, ROWS), modes)
    blocks = []
    for plane in planes:
        panel_rows = grid_ref[plane, rows, 0:lanes_used]
        blocks.append(
            [
                [
                    panel_rows[q * ROWS : (q + 1) * ROWS, t * LANES : (t + 1) * LANES]
                    for t in range(lanes_used // LANES)
                ]
                for q in range(modes // ROWS)
            ]
        )

    def turned(b, block, q):
        found = []
        for strip in block[q:]:
            if static and first_row // LANES == (first_row + modes - 1) // LANES:
                tile = strip[first_row // LANES]
                offset = first_row % LANES
                found.append(tile if offset == 0 else tile[:, offset : offset + modes])
            else:
                wide = jnp.concatenate(strip[:per_part], axis=1)
                found.append(pltpu.roll(wide, lax.rem(part - first_row, part), 1)[:, :LANES])
        return found

    blocks = factor_rows(blocks, per_part, first_row, turned)
    for plane, block in zip(planes, blocks):
        panel_rows = jnp.concatenate([jnp.concatenate(strip, axis=1) for strip in block], axis=0)
        grid_ref[plane, rows, 0:lanes_used] = panel_rows
        if static:
            below = (panel + 1) * modes
            end = min(below + modes, order) if banded else order
            if below < order:
                columns = panel_rows[:, 0:part].T[below:end]
                update = plain_dot(columns, panel_rows)
                grid_ref[plane, below:end, 0:lanes_used] -= update
        else:
            lane = lax.broadcasted_iota(jnp.int32, (modes, part), 1)
            columns = jnp.where(lane >= first_row + modes, panel_rows[:, 0:part], 0.0)
            update = turned_dot(columns, panel_rows)[0:order]
            grid_ref[plane, :, 0:lanes_used] -= update


def eliminate_planes(grid_ref, planes, modes, order, part, lanes_used, banded=False):
    layers = order // modes
    if layers <= UNROLLED_LAYERS:
        for panel in range(layers):
            eliminate_panel(grid_ref, planes, modes, order, part, lanes_used, panel, banded)
    else:

        def one_panel(panel, carry):
            eliminate_panel(grid_ref, planes, modes, order, part, lanes_used, panel, banded)
            return carry

        lax.fori_loop(0, layers, one_panel, 0)


def update_partners(grid_ref, plane, distance, part, order, has_left):
    left, right = plane - distance, plane + distance
    both = grid_ref[plane, :, part : 3 * part]
    turned = both.T
    from_right = plain_dot(turned[part : part + order], both)
    grid_ref[right, :, 0:part] -= from_right[:, part : 2 * part]
    grid_ref[right, :, part : 2 * part] = -from_right[:, 0:part]

    def to_left():
        from_left = plain_dot(turned[0:order], both)
        grid_ref[left, :, 0:part] -= from_left[:, 0:part]
        grid_ref[left, :, 2 * part : 3 * part] = -from_left[:, part : 2 * part]

    if isinstance(has_left, bool):
        if has_left:
            to_left()
    else:
        pl.when(has_left)(to_left)


def unpack_tile(packed, modes):
    half = 3 * modes // 2
    upper = packed[:, 0 : 3 * modes]
    lower = jnp.concatenate(
        [packed[0:ROWS, 3 * modes : 3 * modes + half], packed[ROWS:, 3 * modes : 3 * modes + half]],
        axis=1,
    )
    return jnp.concatenate([upper, lower], axis=0)


def pack_tile(tile):
    modes = tile.shape[0]
    half = 3 * modes // 2
    top = modes - ROWS
    upper = tile[0:top]
    lower = jnp.concatenate([tile[top:, 0:half], tile[top:, half:]], axis=0)
    spare = jnp.zeros((top, LANES - 3 * modes - half), jnp.float32)
    return jnp.concatenate([upper, lower, spare], axis=1)


def factor_kernel(tiles_ref, after_ref, diag_ref, left_ref, right_ref, grid_ref, turned_ref):
    subs, layers, _, _ = tiles_ref.shape
    modes, order = diag_ref.shape
    part = grid_ref.shape[2] // 3
    unrolled = layers <= UNROLLED_LAYERS
    del after_ref
    grid_ref[...] = jnp.zeros_like(grid_ref)

    def place_tiles(s, has_left):
        for j in range(layers):
            tile = unpack_tile(tiles_ref[s, j], modes)
            turned = tile.T
            rows = slice(j * modes, (j + 1) * modes)
            grid_ref[s, rows, j * modes : (j + 1) * modes] = tile[:, 0:modes]
            if j > 0:
                above = slice((j - 1) * modes, j * modes)
                grid_ref[s, above, j * modes : (j + 1) * modes] = tile[:, modes : 2 * modes]
            if has_left:
                lanes = slice(part + j * modes, part + (j + 1) * modes)
                grid_ref[s, rows, lanes] = turned[2 * modes : 3 * modes]
                lanes = slice(2 * part + j * modes, 2 * part + (j + 1) * modes)
                grid_ref[s - 1, rows, lanes] = tile[:, 2 * modes : 3 * modes]

    place_tiles(0, False)
    if unrolled:
        for s in range(1, subs):
            place_tiles(s, True)
    else:

        def place_one(s, carry):
            place_tiles(s, True)
            return carry

        lax.fori_loop(1, subs, place_one, 0)

    distance = 1
    while distance < subs:
        if unrolled:
            planes = list(range(distance - 1, subs, 2 * distance))
            eliminate_planes(grid_ref, planes, modes, order, part, 3 * part, distance == 1)
            for plane in planes:
                update_partners(grid_ref, plane, distance, part, order, plane >= distance)
        else:

            def one_plane(index, carry, distance=distance):
                plane = distance - 1 + 2 * distance * index
                eliminate_planes(grid_ref, [plane], modes, order, part, 3 * part)
                update_partners(grid_ref, plane, distance, part, order, index > 0)
                return carry

            lax.fori_loop(0, subs // (2 * distance), one_plane, 0)
        distance *= 2
    eliminate_planes(grid_ref, [subs - 1], modes, order, part, part)

    sub_here, lay_here = lax.axis_index("sub"), lax.axis_index("layer")
    strip = pl.ds(pl.multiple_of(lay_here * modes, ROWS), modes)
    for k, out_ref in enumerate((diag_ref, left_ref, right_ref)):
        turned_ref[k] = grid_ref[sub_here, :, k * part : (k + 1) * part].T
        found = turned_ref[k, strip, :]
        out_ref[...] = found if k == 0 else jnp.where(sub_here < subs - 1, found, 0.0)


VMEM_BLOCK = pl.BlockSpec(memory_space=pltpu.VMEM)
SPARE_BYTES = 4 * 1024 * 1024


def kernel_params(shapes):
    held = sum(4 * math.prod(shape) for shape in shapes)
    return pltpu.CompilerParams(vmem_limit_bytes=min(2 * held + SPARE_BYTES, 60 * 1024 * 1024))


def factor_planes(plane_tiles, modes, after):
    subs, layers, _, _ = plane_tiles.shape
    order = layers * modes
    part = -(-order // LANES) * LANES
    strip = jax.ShapeDtypeStruct((modes, order), jnp.float32)
    scratch = ((subs, order, 3 * part), (3, part, order))
    return pl.pallas_call(
        factor_kernel,
        out_shape=(strip, strip, strip),
        in_specs=[VMEM_BLOCK, VMEM_BLOCK],
        out_specs=(VMEM_BLOCK, VMEM_BLOCK, VMEM_BLOCK),
        scratch_shapes=[pltpu.VMEM(shape, jnp.float32) for shape in scratch],
        compiler_params=kernel_params((plane_tiles.shape,) + scratch),
        name="factor_planes",
    )(plane_tiles, after)


def across_dot(left, right):
    return lax.dot_general(
        left,
        right,
        (((1,), (1,)), ((), ())),
        precision=HIGHEST,
        preferred_element_type=jnp.float32,
    )


def pick_kernel(
    vectors_in, lists_in, face_in, mass_in, inner_in,
    vectors_ref, lists_ref, face_ref, mass_ref, inner_ref, picked_ref, sub_ref, layer_ref, sems
):
    modes, row_count = vectors_ref.shape
    strips = modes // ROWS
    pairs = [(lists_in, lists_ref)]
    pairs += [
        (vectors_in.at[pl.ds(r * ROWS, ROWS)], vectors_ref.at[pl.ds(r * ROWS, ROWS)])
        for r in range(strips)
    ]
    pairs += [(face_in, face_ref), (mass_in, mass_ref), (inner_in, inner_ref)]
    copies = [pltpu.make_async_copy(a, b, sems.at[i]) for i, (a, b) in enumerate(pairs)]
    for copy in copies:
        copy.start()
    copies[0].wait()
    lists = []
    for k in range(4):
        rows = jnp.broadcast_to(lists_ref[k : k + 1, :], (ROWS, LANES))
        lists.append((rows // LANES, rows % LANES))
    for r in range(strips):
        copies[1 + r].wait()
        strip = slice(r * ROWS, (r + 1) * ROWS)
        found = [jnp.zeros((ROWS, LANES), jnp.float32) for _ in range(4)]
        for c in range(row_count // LANES):
            tile = vectors_ref[strip, c * LANES : (c + 1) * LANES]
            for k, (tile_of, lane_of) in enumerate(lists):
                moved = jnp.take_along_axis(tile, lane_of, axis=1, mode="promise_in_bounds")
                found[k] = jnp.where(tile_of == c, moved, found[k])
        for k in range(4):
            picked_ref[k, strip] = found[k]
    for copy in copies[1 + strips :]:
        copy.wait()
    for k, send_ref in ((0, sub_ref), (2, layer_ref)):
        send_ref[0:modes] = picked_ref[k]
        send_ref[modes:] = jnp.broadcast_to(face_ref[k // 2 : k // 2 + 1, :], (ROWS, LANES))


def own_kernel(
    vectors_ref, mass_ref, inner_ref, face_ref, picked_ref, base_ref, own_ref, *, subs, layers
):
    vectors = vectors_ref[...]
    row_count = vectors.shape[1]
    places = lax.broadcasted_iota(jnp.int32, (1, row_count), 1)
    base = mass_ref[...] * vectors
    for k, t in enumerate(STRIDES):
        edge_weight = jnp.where(places < row_count - t, inner_ref[k], 0.0)
        fluxes = edge_weight * (vectors - pltpu.roll(vectors, row_count - t, 1))
        base = base + fluxes - pltpu.roll(fluxes, t, 1)
    base_ref[...] = base
    own = across_dot(vectors, base)
    for k, axis, ends in ((0, "sub", subs - 1), (2, "layer", layers - 1)):
        springs = jnp.where(lax.axis_index(axis) < ends, face_ref[k // 2 : k // 2 + 1, :], 0.0)
        own = own + across_dot(picked_ref[k], springs * picked_ref[k])
    own_ref[...] = own


def tile_kernel(
    own_ref, picked_ref, sub_ref, layer_ref, copies_ref, sub_send_ref, layer_send_ref, *, row_count
):
    modes = own_ref.shape[0]
    inverse = 1.0 / row_count
    pairs = []
    for k, theirs_ref in ((1, sub_ref), (3, layer_ref)):
        mine = picked_ref[k]
        sprung = theirs_ref[modes : modes + 1] * mine
        stacked = jnp.concatenate([mine, theirs_ref[0:modes]], axis=0)
        pairs.append(across_dot(stacked, sprung))
    down, side = pairs
    diag_tile = (own_ref[...] + down[0:modes] + side[0:modes]) * inverse
    side_turned = -side[modes:] * inverse
    down_turned = -down[modes:] * inverse
    packed = pack_tile(jnp.concatenate([diag_tile, side_turned, down_turned], axis=1))
    for s in range(copies_ref.shape[0]):
        copies_ref[s] = packed
    sub_send_ref[...] = picked_ref[1]
    layer_send_ref[...] = picked_ref[3]


def scatter_kernel(
    base_ref, lists_ref, face_ref, picked_ref, before_sub_ref, after_sub_ref,
    before_layer_ref, after_layer_ref, applied_ref, token_ref, *, subs, layers
):
    modes, row_count = base_ref.shape
    width = 2 * LANES
    springs = [
        jnp.where(lax.axis_index("sub") < subs - 1, face_ref[0:1, :], 0.0),
        before_sub_ref[modes : modes + 1, :],
        jnp.where(lax.axis_index("layer") < layers - 1, face_ref[1:2, :], 0.0),
        before_layer_ref[modes : modes + 1, :],
    ]
    partners = [
        after_sub_ref[...],
        before_sub_ref[0:modes, :],
        after_layer_ref[...],
        before_layer_ref[0:modes, :],
    ]
    pulls = jnp.concatenate(
        [springs[k] * (picked_ref[k] - partners[k]) for k in range(4)], axis=1
    )
    rows = jnp.concatenate([lists_ref[k : k + 1, :] for k in range(4)], axis=1)
    block_of, lane_of = rows // width, rows % width
    lanes = lax.broadcasted_iota(jnp.int32, (width, rows.shape[1]), 0)
    onehot = jnp.where(lanes == lane_of, 1.0, 0.0).astype(jnp.bfloat16)
    total = None
    rest = pulls
    for _ in range(3):
        piece = rest.astype(jnp.bfloat16).astype(jnp.float32)
        rest = rest - piece
        spread = jnp.concatenate(
            [jnp.where(block_of == h, piece, 0.0) for h in range(row_count // width)], axis=0
        ).astype(jnp.bfloat16)
        moved = lax.dot_general(
            spread, onehot, (((1,), (1,)), ((), ())), preferred_element_type=jnp.float32
        )
        total = moved if total is None else total + moved
    for h in range(row_count // width):
        lanes = slice(h * width, (h + 1) * width)
        applied_ref[:, lanes] = base_ref[:, lanes] + total[h * modes : (h + 1) * modes]
    token_ref[...] = jnp.zeros_like(token_ref)


def local_call(body, outputs, operands, name):
    shapes = tuple(jax.ShapeDtypeStruct(shape, jnp.float32) for shape in outputs)
    return pl.pallas_call(
        body,
        out_shape=shapes,
        in_specs=[VMEM_BLOCK] * len(operands),
        out_specs=tuple(VMEM_BLOCK for _ in shapes),
        compiler_params=kernel_params([x.shape for x in operands] + list(outputs)),
        name=name,
    )(*operands)


def per_device(eigen_vectors, row_mass, inner_weight, face_weight, margin_rows):
    vectors = eigen_vectors[0, 0]
    row_lists = margin_rows[0, 0]
    face_springs = face_weight[0, 0]
    modes, row_count = vectors.shape
    width = row_lists.shape[-1]
    subs = lax.axis_size("sub")
    layers = lax.axis_size("layer")
    up_sub = [(i, i + 1) for i in range(subs - 1)]
    up_layer = [(i, i + 1) for i in range(layers - 1)]
    down_sub = [(i + 1, i) for i in range(subs - 1)]
    down_layer = [(i + 1, i) for i in range(layers - 1)]
    taken = (vectors, row_lists, face_springs, row_mass[0], inner_weight[0].reshape(-1, 1, row_count))
    held = [(x.shape, x.dtype) for x in taken]
    made = [(4, modes, width), (modes + ROWS, width), (modes + ROWS, width)]
    held += [(shape, jnp.float32) for shape in made]
    vectors, row_lists, face_springs, masses, interior, picked, sub_send, layer_send = pl.pallas_call(
        pick_kernel,
        out_shape=tuple(jax.ShapeDtypeStruct(*pair) for pair in held),
        in_specs=[pl.BlockSpec(memory_space=pltpu.HBM)] * len(taken),
        out_specs=(VMEM_BLOCK,) * len(held),
        scratch_shapes=[pltpu.SemaphoreType.DMA((len(taken) + modes // ROWS - 1,))],
        compiler_params=kernel_params([shape for shape, _ in held]),
        name="pick_rows",
    )(*(pltpu.with_memory_space_constraint(x, pltpu.HBM) for x in taken))
    before_sub = lax.ppermute(sub_send, "sub", up_sub)
    before_layer = lax.ppermute(layer_send, "layer", up_layer)
    base, own = local_call(
        functools.partial(own_kernel, subs=subs, layers=layers),
        [(modes, row_count), (modes, modes)],
        (vectors, masses, interior, face_springs, picked),
        "own_rows",
    )
    copies, sub_send, layer_send = local_call(
        functools.partial(tile_kernel, row_count=row_count),
        [(subs * layers, modes - ROWS, LANES), (modes, width), (modes, width)],
        (own, picked, before_sub, before_layer),
        "coarse_tiles",
    )
    tiles = lax.all_to_all(copies, ("sub", "layer"), split_axis=0, concat_axis=0, tiled=True)
    after_sub = lax.ppermute(sub_send, "sub", down_sub)
    after_layer = lax.ppermute(layer_send, "layer", down_layer)
    applied, token = local_call(
        functools.partial(scatter_kernel, subs=subs, layers=layers),
        [(modes, row_count), (ROWS, LANES)],
        (base, row_lists, face_springs, picked, before_sub, after_sub, before_layer, after_layer),
        "spread_rows",
    )
    diag_strip, left_strip, right_strip = factor_planes(
        tiles.reshape(subs, layers, *tiles.shape[1:]), modes, token
    )
    return (applied[None, None], diag_strip[None], left_strip[None], right_strip[None])


def solution(mesh):
    in_specs = (
        P("sub", "layer", None, None),
        P("sub", "layer", None),
        P("sub", "layer", None, None),
        P("sub", "layer", None, None),
        P("sub", "layer", None, None),
    )
    out_specs = (
        P("sub", "layer", None, None),
        P("sub", "layer", None),
        P("sub", "layer", None),
        P("sub", "layer", None),
    )
    return jax.shard_map(
        per_device, mesh=mesh, in_specs=in_specs, out_specs=out_specs, check_vma=False
    )
```

```python
import functools
import math
import jax
import jax.numpy as jnp
from jax import lax
from jax.experimental import pallas as pl
from jax.experimental.pallas import tpu as pltpu
from jax.sharding import PartitionSpec as P

STRIDES = (1, 3, 27)
HIGHEST = lax.Precision.HIGHEST
LANES = 128
ROWS = 8
PLANES_AT_ONCE = 4
BLOCKS_AT_ONCE = 3


def plain_dot(left, right):
    return lax.dot_general(
        left,
        right,
        (((1,), (0,)), ((), ())),
        precision=HIGHEST,
        preferred_element_type=jnp.float32,
    )


def spread_row(strip, k):
    return jnp.broadcast_to(strip[k : k + 1, :], strip.shape)


def eliminate_pair(block, columns, pivots, iota, q, k):
    first, second = columns[k], columns[k + 1]
    corner, joint = spread_row(first[0], k), spread_row(first[0], k + 1)
    other_corner = spread_row(second[0], k + 1)
    minor = corner * other_corner - joint * joint
    inverse = pl.reciprocal(corner, approx=True)
    other_inverse = corner * pl.reciprocal(minor, approx=True)
    below = [column * inverse for column in first]
    second = [column - below[r] * joint for r, column in enumerate(second)]
    other_below = [column * other_inverse for column in second]
    below[0] = jnp.where(iota > k, below[0], 0.0)
    other_below[0] = jnp.where(iota > k + 1, other_below[0], 0.0)
    for j in range(k + 2, ROWS):
        head, other_head = spread_row(first[0], j), spread_row(second[0], j)
        columns[j] = [
            column - below[r] * head - other_below[r] * other_head
            for r, column in enumerate(columns[j])
        ]
    for t in range(len(block[q])):
        row = spread_row(block[q][t], k)
        for r, lower in enumerate(below):
            block[q + r][t] = block[q + r][t] - lower * row
        row = spread_row(block[q][t], k + 1)
        for r, lower in enumerate(other_below):
            block[q + r][t] = block[q + r][t] - lower * row
    return jnp.where(iota == k, corner, jnp.where(iota == k + 1, minor * inverse, pivots))


def factor_rows(blocks, tiles_per_part, columns_left):
    strip_count = len(blocks[0])
    iota = lax.broadcasted_iota(jnp.int32, (ROWS, LANES), 0)
    lane = lax.broadcasted_iota(jnp.int32, (ROWS, LANES), 1)
    blocks = [[list(strip) for strip in block] for block in blocks]
    for q in range(strip_count):
        start = q * ROWS
        held = [
            [
                [
                    jnp.broadcast_to(strip[0][:, start + j : start + j + 1], (ROWS, LANES))
                    for strip in block[q:]
                ]
                for j in range(ROWS)
            ]
            for block in blocks
        ]
        pivots = [jnp.zeros((ROWS, LANES), jnp.float32) for _ in blocks]
        for k in range(0, ROWS, 2):
            for b, block in enumerate(blocks):
                pivots[b] = eliminate_pair(block, held[b], pivots[b], iota, q, k)
        for b, block in enumerate(blocks):
            scale = lax.rsqrt(pivots[b])
            for t in range(len(block[q])):
                strip = block[q][t] * scale
                if t < tiles_per_part:
                    place = lane + t * LANES
                    keep = (place >= iota + start) & (place < columns_left)
                    strip = jnp.where(keep, strip, 0.0)
                block[q][t] = strip
    return blocks


def eliminate_panel(grid_ref, turned_ref, planes, modes, order, part, panel, banded):
    first_row = pl.multiple_of(panel * modes, ROWS)
    rows = pl.ds(first_row, modes)
    reach = modes if banded else min(order - modes, BLOCKS_AT_ONCE * modes)
    chunks = 1
    if not banded and reach < order - modes:
        chunks = lax.div(order - first_row - modes + reach - 1, reach)
    blocks = []
    for plane in planes:
        panel_rows = grid_ref[plane, rows, :]
        blocks.append(
            [
                [
                    panel_rows[q * ROWS : (q + 1) * ROWS, t * LANES : (t + 1) * LANES]
                    for t in range(3 * part // LANES)
                ]
                for q in range(modes // ROWS)
            ]
        )
    blocks = factor_rows(blocks, part // LANES, order - first_row)
    for plane, block in zip(planes, blocks):
        panel_rows = jnp.concatenate([jnp.concatenate(strip, axis=1) for strip in block], axis=0)
        grid_ref[plane, rows, :] = panel_rows
        own = panel_rows[:, 0:part]
        if banded:
            panel_rows = jnp.concatenate(
                [pltpu.roll(own, part - modes, 1), panel_rows[:, part:]], axis=1
            )

        def update_rows(first, columns, plane=plane, panel_rows=panel_rows):
            below = pl.ds(pl.multiple_of(first_row + first, ROWS), reach)
            rest = grid_ref[plane, below, :] - plain_dot(columns, panel_rows)
            if banded:
                grid_ref[plane, below, :] = rest
            else:
                grid_ref[plane, below, 0:part] = pltpu.roll(rest[:, 0:part], part - modes, 1)
                grid_ref[plane, below, part:] = rest[:, part:]

        if isinstance(chunks, int):
            update_rows(modes, own.T[modes : modes + reach])
        else:
            turned_ref[0, :, 0:modes] = own.T

            def one_chunk(chunk, carry):
                first = pl.multiple_of(modes + chunk * reach, ROWS)
                update_rows(first, turned_ref[0, pl.ds(first, reach), 0:modes])
                return carry

            lax.fori_loop(0, chunks, one_chunk, 0)


def eliminate_planes(grid_ref, turned_ref, planes, modes, order, part, banded=False):
    def one_panel(panel, carry):
        eliminate_panel(grid_ref, turned_ref, planes, modes, order, part, panel, banded)
        return carry

    lax.fori_loop(0, order // modes, one_panel, 0)


def update_partners(grid_ref, plane, distance, part, order, has_left):
    left, right = plane - distance, plane + distance
    both = grid_ref[plane, 0:order, part : 3 * part]
    turned = both.T
    from_right = plain_dot(turned[part : part + order], both)
    grid_ref[right, 0:order, 0:part] -= from_right[:, part : 2 * part]
    grid_ref[right, 0:order, part : 2 * part] = -from_right[:, 0:part]
    if has_left is False:
        return

    @pl.when(has_left)
    def _():
        from_left = plain_dot(turned[0:order], both)
        grid_ref[left, 0:order, 0:part] -= from_left[:, 0:part]
        grid_ref[left, 0:order, 2 * part : 3 * part] = -from_left[:, part : 2 * part]


def unpack_tile(packed, modes):
    half = 3 * modes // 2
    upper = packed[:, 0 : 3 * modes]
    lower = jnp.concatenate(
        [packed[0:ROWS, 3 * modes : 3 * modes + half], packed[ROWS:, 3 * modes : 3 * modes + half]],
        axis=1,
    )
    return jnp.concatenate([upper, lower], axis=0)


def pack_tile(tile):
    modes = tile.shape[0]
    half = 3 * modes // 2
    top = modes - ROWS
    upper = tile[0:top]
    lower = jnp.concatenate([tile[top:, 0:half], tile[top:, half:]], axis=0)
    spare = jnp.zeros((top, LANES - 3 * modes - half), jnp.float32)
    return jnp.concatenate([upper, lower, spare], axis=1)


def factor_kernel(tiles_ref, after_ref, diag_ref, left_ref, right_ref, grid_ref, turned_ref):
    subs, layers, _, _ = tiles_ref.shape
    modes, order = diag_ref.shape
    part = grid_ref.shape[2] // 3
    del after_ref

    def place_plane(s, banded):
        grid_ref[s] = jnp.zeros(grid_ref.shape[1:], jnp.float32)
        before = jnp.maximum(s - 1, 0)
        for j in range(layers):
            tile = unpack_tile(tiles_ref[s, j], modes)
            turned = tile.T
            rows = slice(j * modes, (j + 1) * modes)
            first = 0 if banded else j * modes
            grid_ref[s, rows, first : first + modes] = tile[:, 0:modes]
            if j > 0:
                above = slice((j - 1) * modes, j * modes)
                first = modes if banded else j * modes
                grid_ref[s, above, first : first + modes] = tile[:, modes : 2 * modes]
            lanes = slice(part + j * modes, part + (j + 1) * modes)
            grid_ref[s, rows, lanes] = turned[2 * modes : 3 * modes]
            lanes = slice(2 * part + j * modes, 2 * part + (j + 1) * modes)
            grid_ref[before, rows, lanes] = tile[:, 2 * modes : 3 * modes]

    def place_pair(i, carry):
        place_plane(2 * i, True)
        place_plane(2 * i + 1, False)
        return carry

    lax.fori_loop(0, subs // 2, place_pair, 0)

    distance = 1
    while distance < subs // 2:
        count = subs // (2 * distance)
        planes = [distance - 1 + 2 * distance * i for i in range(count)]
        taken = min(count, PLANES_AT_ONCE)
        for first in range(0, count, taken):
            some = planes[first : first + taken]
            eliminate_planes(grid_ref, turned_ref, some, modes, order, part, distance == 1)

        def one_plane(index, carry, distance=distance):
            plane = distance - 1 + 2 * distance * index
            update_partners(grid_ref, plane, distance, part, order, index > 0)
            return carry

        lax.fori_loop(0, count, one_plane, 0)
        distance *= 2

    def last_planes(index, carry):
        plane = distance - 1 + distance * index
        eliminate_planes(grid_ref, turned_ref, [plane], modes, order, part)

        @pl.when(index == 0)
        def _():
            update_partners(grid_ref, plane, distance, part, order, False)

        return carry

    lax.fori_loop(0, 2, last_planes, 0)

    sub_here, lay_here = lax.axis_index("sub"), lax.axis_index("layer")
    strip = pl.ds(pl.multiple_of(lay_here * modes, ROWS), modes)
    for j in range(layers):
        rows = slice(j * modes, (j + 1) * modes)
        own = grid_ref[sub_here, rows, 0:part]
        grid_ref[sub_here, rows, 0:part] = pltpu.roll(own, j * modes, 1) if j else own
    for k, out_ref in enumerate((diag_ref, left_ref, right_ref)):
        turned_ref[k] = grid_ref[sub_here, 0:order, k * part : (k + 1) * part].T
        found = turned_ref[k, strip, :]
        out_ref[...] = found if k == 0 else jnp.where(sub_here < subs - 1, found, 0.0)


VMEM_BLOCK = pl.BlockSpec(memory_space=pltpu.VMEM)
SPARE_BYTES = 4 * 1024 * 1024


def kernel_params(shapes):
    held = sum(4 * math.prod(shape) for shape in shapes)
    return pltpu.CompilerParams(vmem_limit_bytes=min(2 * held + SPARE_BYTES, 60 * 1024 * 1024))


def factor_planes(plane_tiles, modes, after):
    subs, layers, _, _ = plane_tiles.shape
    order = layers * modes
    part = -(-order // LANES) * LANES
    strip = jax.ShapeDtypeStruct((modes, order), jnp.float32)
    spare = modes * min(layers - 1, BLOCKS_AT_ONCE)
    scratch = ((subs, order + spare, 3 * part), (3, part, order))
    return pl.pallas_call(
        factor_kernel,
        out_shape=(strip, strip, strip),
        in_specs=[VMEM_BLOCK, VMEM_BLOCK],
        out_specs=(VMEM_BLOCK, VMEM_BLOCK, VMEM_BLOCK),
        scratch_shapes=[pltpu.VMEM(shape, jnp.float32) for shape in scratch],
        compiler_params=kernel_params((plane_tiles.shape,) + scratch),
        name="factor_planes",
    )(plane_tiles, after)


def across_dot(left, right):
    return lax.dot_general(
        left,
        right,
        (((1,), (1,)), ((), ())),
        precision=HIGHEST,
        preferred_element_type=jnp.float32,
    )


def pick_kernel(
    vectors_in, lists_in, face_in, mass_in, inner_in,
    vectors_ref, lists_ref, face_ref, mass_ref, inner_ref, picked_ref, sub_ref, layer_ref, sems
):
    modes, row_count = vectors_ref.shape
    strips = modes // ROWS
    pairs = [(lists_in, lists_ref)]
    pairs += [
        (vectors_in.at[pl.ds(r * ROWS, ROWS)], vectors_ref.at[pl.ds(r * ROWS, ROWS)])
        for r in range(strips)
    ]
    pairs += [(face_in, face_ref), (mass_in, mass_ref), (inner_in, inner_ref)]
    copies = [pltpu.make_async_copy(a, b, sems.at[i]) for i, (a, b) in enumerate(pairs)]
    for copy in copies:
        copy.start()
    copies[0].wait()
    lists = []
    for k in range(4):
        rows = jnp.broadcast_to(lists_ref[k : k + 1, :], (ROWS, LANES))
        lists.append((rows // LANES, rows % LANES))
    for r in range(strips):
        copies[1 + r].wait()
        strip = slice(r * ROWS, (r + 1) * ROWS)
        found = [jnp.zeros((ROWS, LANES), jnp.float32) for _ in range(4)]
        for c in range(row_count // LANES):
            tile = vectors_ref[strip, c * LANES : (c + 1) * LANES]
            for k, (tile_of, lane_of) in enumerate(lists):
                moved = jnp.take_along_axis(tile, lane_of, axis=1, mode="promise_in_bounds")
                found[k] = jnp.where(tile_of == c, moved, found[k])
        for k in range(4):
            picked_ref[k, strip] = found[k]
    for copy in copies[1 + strips :]:
        copy.wait()
    for k, send_ref in ((0, sub_ref), (2, layer_ref)):
        send_ref[0:modes] = picked_ref[k]
        send_ref[modes:] = jnp.broadcast_to(face_ref[k // 2 : k // 2 + 1, :], (ROWS, LANES))


def own_kernel(
    vectors_ref, mass_ref, inner_ref, face_ref, picked_ref, base_ref, own_ref, *, subs, layers
):
    vectors = vectors_ref[...]
    row_count = vectors.shape[1]
    places = lax.broadcasted_iota(jnp.int32, (1, row_count), 1)
    base = mass_ref[...] * vectors
    for k, t in enumerate(STRIDES):
        edge_weight = jnp.where(places < row_count - t, inner_ref[k], 0.0)
        fluxes = edge_weight * (vectors - pltpu.roll(vectors, row_count - t, 1))
        base = base + fluxes - pltpu.roll(fluxes, t, 1)
    base_ref[...] = base
    own = across_dot(vectors, base)
    for k, axis, ends in ((0, "sub", subs - 1), (2, "layer", layers - 1)):
        springs = jnp.where(lax.axis_index(axis) < ends, face_ref[k // 2 : k // 2 + 1, :], 0.0)
        own = own + across_dot(picked_ref[k], springs * picked_ref[k])
    own_ref[...] = own


def tile_kernel(
    own_ref, picked_ref, sub_ref, layer_ref, copies_ref, sub_send_ref, layer_send_ref, *, row_count
):
    modes = own_ref.shape[0]
    inverse = 1.0 / row_count
    pairs = []
    for k, theirs_ref in ((1, sub_ref), (3, layer_ref)):
        mine = picked_ref[k]
        sprung = theirs_ref[modes : modes + 1] * mine
        stacked = jnp.concatenate([mine, theirs_ref[0:modes]], axis=0)
        pairs.append(across_dot(stacked, sprung))
    down, side = pairs
    diag_tile = (own_ref[...] + down[0:modes] + side[0:modes]) * inverse
    side_turned = -side[modes:] * inverse
    down_turned = -down[modes:] * inverse
    packed = pack_tile(jnp.concatenate([diag_tile, side_turned, down_turned], axis=1))
    for s in range(copies_ref.shape[0]):
        copies_ref[s] = packed
    sub_send_ref[...] = picked_ref[1]
    layer_send_ref[...] = picked_ref[3]


def scatter_kernel(
    base_ref, lists_ref, face_ref, picked_ref, before_sub_ref, after_sub_ref,
    before_layer_ref, after_layer_ref, applied_ref, token_ref, *, subs, layers
):
    modes, row_count = base_ref.shape
    width = 2 * LANES
    springs = [
        jnp.where(lax.axis_index("sub") < subs - 1, face_ref[0:1, :], 0.0),
        before_sub_ref[modes : modes + 1, :],
        jnp.where(lax.axis_index("layer") < layers - 1, face_ref[1:2, :], 0.0),
        before_layer_ref[modes : modes + 1, :],
    ]
    partners = [
        after_sub_ref[...],
        before_sub_ref[0:modes, :],
        after_layer_ref[...],
        before_layer_ref[0:modes, :],
    ]
    pulls = jnp.concatenate(
        [springs[k] * (picked_ref[k] - partners[k]) for k in range(4)], axis=1
    )
    rows = jnp.concatenate([lists_ref[k : k + 1, :] for k in range(4)], axis=1)
    block_of, lane_of = rows // width, rows % width
    lanes = lax.broadcasted_iota(jnp.int32, (width, rows.shape[1]), 0)
    onehot = jnp.where(lanes == lane_of, 1.0, 0.0).astype(jnp.bfloat16)
    total = None
    rest = pulls
    for _ in range(3):
        piece = rest.astype(jnp.bfloat16).astype(jnp.float32)
        rest = rest - piece
        spread = jnp.concatenate(
            [jnp.where(block_of == h, piece, 0.0) for h in range(row_count // width)], axis=0
        ).astype(jnp.bfloat16)
        moved = lax.dot_general(
            spread, onehot, (((1,), (1,)), ((), ())), preferred_element_type=jnp.float32
        )
        total = moved if total is None else total + moved
    for h in range(row_count // width):
        lanes = slice(h * width, (h + 1) * width)
        applied_ref[:, lanes] = base_ref[:, lanes] + total[h * modes : (h + 1) * modes]
    token_ref[...] = jnp.zeros_like(token_ref)


def local_call(body, outputs, operands, name):
    shapes = tuple(jax.ShapeDtypeStruct(shape, jnp.float32) for shape in outputs)
    return pl.pallas_call(
        body,
        out_shape=shapes,
        in_specs=[VMEM_BLOCK] * len(operands),
        out_specs=tuple(VMEM_BLOCK for _ in shapes),
        compiler_params=kernel_params([x.shape for x in operands] + list(outputs)),
        name=name,
    )(*operands)


def per_device(eigen_vectors, row_mass, inner_weight, face_weight, margin_rows):
    vectors = eigen_vectors[0, 0]
    row_lists = margin_rows[0, 0]
    face_springs = face_weight[0, 0]
    modes, row_count = vectors.shape
    width = row_lists.shape[-1]
    subs = lax.axis_size("sub")
    layers = lax.axis_size("layer")
    up_sub = [(i, i + 1) for i in range(subs - 1)]
    up_layer = [(i, i + 1) for i in range(layers - 1)]
    down_sub = [(i + 1, i) for i in range(subs - 1)]
    down_layer = [(i + 1, i) for i in range(layers - 1)]
    taken = (vectors, row_lists, face_springs, row_mass[0], inner_weight[0].reshape(-1, 1, row_count))
    held = [(x.shape, x.dtype) for x in taken]
    made = [(4, modes, width), (modes + ROWS, width), (modes + ROWS, width)]
    held += [(shape, jnp.float32) for shape in made]
    vectors, row_lists, face_springs, masses, interior, picked, sub_send, layer_send = pl.pallas_call(
        pick_kernel,
        out_shape=tuple(jax.ShapeDtypeStruct(*pair) for pair in held),
        in_specs=[pl.BlockSpec(memory_space=pltpu.HBM)] * len(taken),
        out_specs=(VMEM_BLOCK,) * len(held),
        scratch_shapes=[pltpu.SemaphoreType.DMA((len(taken) + modes // ROWS - 1,))],
        compiler_params=kernel_params([shape for shape, _ in held]),
        name="pick_rows",
    )(*(pltpu.with_memory_space_constraint(x, pltpu.HBM) for x in taken))
    before_sub = lax.ppermute(sub_send, "sub", up_sub)
    before_layer = lax.ppermute(layer_send, "layer", up_layer)
    base, own = local_call(
        functools.partial(own_kernel, subs=subs, layers=layers),
        [(modes, row_count), (modes, modes)],
        (vectors, masses, interior, face_springs, picked),
        "own_rows",
    )
    copies, sub_send, layer_send = local_call(
        functools.partial(tile_kernel, row_count=row_count),
        [(subs * layers, modes - ROWS, LANES), (modes, width), (modes, width)],
        (own, picked, before_sub, before_layer),
        "coarse_tiles",
    )
    tiles = lax.all_to_all(copies, ("sub", "layer"), split_axis=0, concat_axis=0, tiled=True)
    after_sub = lax.ppermute(sub_send, "sub", down_sub)
    after_layer = lax.ppermute(layer_send, "layer", down_layer)
    applied, token = local_call(
        functools.partial(scatter_kernel, subs=subs, layers=layers),
        [(modes, row_count), (ROWS, LANES)],
        (base, row_lists, face_springs, picked, before_sub, after_sub, before_layer, after_layer),
        "spread_rows",
    )
    diag_strip, left_strip, right_strip = factor_planes(
        tiles.reshape(subs, layers, *tiles.shape[1:]), modes, token
    )
    return (applied[None, None], diag_strip[None], left_strip[None], right_strip[None])


def solution(mesh):
    in_specs = (
        P("sub", "layer", None, None),
        P("sub", "layer", None),
        P("sub", "layer", None, None),
        P("sub", "layer", None, None),
        P("sub", "layer", None, None),
    )
    out_specs = (
        P("sub", "layer", None, None),
        P("sub", "layer", None),
        P("sub", "layer", None),
        P("sub", "layer", None),
    )
    return jax.shard_map(
        per_device, mesh=mesh, in_specs=in_specs, out_specs=out_specs, check_vma=False
    )
```

```python
import functools
import math
import jax
import jax.numpy as jnp
from jax import lax
from jax.experimental import pallas as pl
from jax.experimental.pallas import tpu as pltpu
from jax.sharding import PartitionSpec as P

STRIDES = (1, 3, 27)
HIGHEST = lax.Precision.HIGHEST
LANES = 128
ROWS = 8
UNROLLED_LAYERS = 4


def turned_dot(left, right):
    return lax.dot_general(
        left,
        right,
        (((0,), (0,)), ((), ())),
        precision=HIGHEST,
        preferred_element_type=jnp.float32,
    )


PRODUCTS = ((0, 0), (1, 0), (2, 0), (0, 1), (1, 1), (0, 2))


def pieces_of(values):
    first = values.astype(jnp.bfloat16).astype(jnp.float32)
    rest = values - first
    second = rest.astype(jnp.bfloat16).astype(jnp.float32)
    return first, second, rest - second


def single_dot(left, right):
    return lax.dot_general(
        left, right, (((1,), (0,)), ((), ())), preferred_element_type=jnp.float32
    )


def narrow_product(panel_rows, part, below, end):
    modes = panel_rows.shape[0]
    first, second, third = pieces_of(panel_rows)
    stacked = jnp.concatenate([x[:, 0:part] for x in (first, second, third)], axis=0)
    turned = stacked.T[below:end]
    lane = lax.broadcasted_iota(jnp.int32, (end - below, LANES), 1)
    wide = jnp.concatenate(
        [turned, jnp.zeros((end - below, LANES - 3 * modes), jnp.float32)], axis=1
    )
    again = pltpu.roll(wide, 3 * modes, 1)
    left = jnp.where(lane < 3 * modes, wide, jnp.where(lane < 5 * modes, again, 0.0))
    last = jnp.where(lane < modes, wide, 0.0)
    depth = LANES + 2 * LANES // 8
    columns = jnp.concatenate([left, last], axis=1)[:, 0:depth]
    gap = jnp.zeros((LANES - 5 * modes, panel_rows.shape[1]), jnp.float32)
    tail = jnp.zeros((depth - LANES - modes, panel_rows.shape[1]), jnp.float32)
    rows = jnp.concatenate([first] * 3 + [second] * 2 + [gap, third, tail], axis=0)
    return single_dot(columns.astype(jnp.bfloat16), rows.astype(jnp.bfloat16))


def plain_dot(left, right):
    return lax.dot_general(
        left,
        right,
        (((1,), (0,)), ((), ())),
        precision=HIGHEST,
        preferred_element_type=jnp.float32,
    )


def spread_row(strip, k):
    return jnp.broadcast_to(strip[k : k + 1, :], strip.shape)


def eliminate_pair(block, columns, pivots, iota, q, k):
    first, second = columns[k], columns[k + 1]
    corner, joint = spread_row(first[0], k), spread_row(first[0], k + 1)
    other_corner = spread_row(second[0], k + 1)
    minor = corner * other_corner - joint * joint
    inverse = pl.reciprocal(corner, approx=True)
    other_inverse = corner * pl.reciprocal(minor, approx=True)
    below = [column * inverse for column in first]
    second = [column - below[r] * joint for r, column in enumerate(second)]
    other_below = [column * other_inverse for column in second]
    below[0] = jnp.where(iota > k, below[0], 0.0)
    other_below[0] = jnp.where(iota > k + 1, other_below[0], 0.0)
    for j in range(k + 2, ROWS):
        head, other_head = spread_row(first[0], j), spread_row(second[0], j)
        columns[j] = [
            column - below[r] * head - other_below[r] * other_head
            for r, column in enumerate(columns[j])
        ]
    for t in range(len(block[q])):
        row = spread_row(block[q][t], k)
        for r, lower in enumerate(below):
            block[q + r][t] = block[q + r][t] - lower * row
        row = spread_row(block[q][t], k + 1)
        for r, lower in enumerate(other_below):
            block[q + r][t] = block[q + r][t] - lower * row
    return jnp.where(iota == k, corner, jnp.where(iota == k + 1, minor * inverse, pivots))


def factor_rows(blocks, tiles_per_part, first_row, turned):
    strip_count = len(blocks[0])
    iota = lax.broadcasted_iota(jnp.int32, (ROWS, LANES), 0)
    lane = lax.broadcasted_iota(jnp.int32, (ROWS, LANES), 1)
    blocks = [[list(strip) for strip in block] for block in blocks]
    for q in range(strip_count):
        start = q * ROWS
        held = []
        for b, block in enumerate(blocks):
            source = turned(b, block, q)
            held.append(
                [
                    [
                        jnp.broadcast_to(strip[:, start + j : start + j + 1], (ROWS, LANES))
                        for strip in source
                    ]
                    for j in range(ROWS)
                ]
            )
        pivots = [jnp.zeros((ROWS, LANES), jnp.float32) for _ in blocks]
        for k in range(0, ROWS, 2):
            for b, block in enumerate(blocks):
                pivots[b] = eliminate_pair(block, held[b], pivots[b], iota, q, k)
        for b, block in enumerate(blocks):
            scale = lax.rsqrt(pivots[b])
            for t in range(len(block[q])):
                strip = block[q][t] * scale
                if t < tiles_per_part:
                    keep = lane + t * LANES >= iota + (first_row + start)
                    strip = jnp.where(keep, strip, 0.0)
                block[q][t] = strip
    return blocks


def eliminate_panel(grid_ref, planes, modes, order, part, lanes_used, panel, banded):
    per_part = part // LANES
    first_row = panel * modes
    static = isinstance(panel, int)
    if static:
        rows = pl.ds(first_row, modes)
    else:
        rows = pl.ds(pl.multiple_of(first_row, ROWS), modes)
    blocks = []
    for plane in planes:
        panel_rows = grid_ref[plane, rows, 0:lanes_used]
        blocks.append(
            [
                [
                    panel_rows[q * ROWS : (q + 1) * ROWS, t * LANES : (t + 1) * LANES]
                    for t in range(lanes_used // LANES)
                ]
                for q in range(modes // ROWS)
            ]
        )

    def turned(b, block, q):
        found = []
        for strip in block[q:]:
            if static and first_row // LANES == (first_row + modes - 1) // LANES:
                tile = strip[first_row // LANES]
                offset = first_row % LANES
                found.append(tile if offset == 0 else tile[:, offset : offset + modes])
            else:
                wide = jnp.concatenate(strip[:per_part], axis=1)
                found.append(pltpu.roll(wide, lax.rem(part - first_row, part), 1)[:, :LANES])
        return found

    blocks = factor_rows(blocks, per_part, first_row, turned)
    for plane, block in zip(planes, blocks):
        panel_rows = jnp.concatenate([jnp.concatenate(strip, axis=1) for strip in block], axis=0)
        grid_ref[plane, rows, 0:lanes_used] = panel_rows
        if static:
            below = (panel + 1) * modes
            end = min(below + modes, order) if banded else order
            if below < order:
                update = narrow_product(panel_rows, part, below, end)
                grid_ref[plane, below:end, 0:lanes_used] -= update
        else:
            lane = lax.broadcasted_iota(jnp.int32, (modes, part), 1)
            columns = jnp.where(lane >= first_row + modes, panel_rows[:, 0:part], 0.0)
            update = turned_dot(columns, panel_rows)[0:order]
            grid_ref[plane, :, 0:lanes_used] -= update


def eliminate_planes(grid_ref, planes, modes, order, part, lanes_used, banded=False):
    layers = order // modes
    if layers <= UNROLLED_LAYERS:
        for panel in range(layers):
            eliminate_panel(grid_ref, planes, modes, order, part, lanes_used, panel, banded)
    else:

        def one_panel(panel, carry):
            eliminate_panel(grid_ref, planes, modes, order, part, lanes_used, panel, banded)
            return carry

        lax.fori_loop(0, layers, one_panel, 0)


def update_partners(grid_ref, plane, distance, part, order, has_left):
    left, right = plane - distance, plane + distance
    both = grid_ref[plane, :, part : 3 * part]
    if part > order:
        spare = jnp.zeros((part - order, 2 * part), jnp.float32)
        both = jnp.concatenate([both, spare], axis=0)
    turned = [piece.astype(jnp.bfloat16) for piece in pieces_of(both.T)]
    held = [piece.astype(jnp.bfloat16) for piece in pieces_of(both)]
    held = jnp.concatenate([held[right] for _, right in PRODUCTS], axis=0)

    def product(rows):
        columns = jnp.concatenate([turned[left][rows] for left, _ in PRODUCTS], axis=1)
        return single_dot(columns, held)

    from_right = product(slice(part, part + order))
    grid_ref[right, :, 0:part] -= from_right[:, part : 2 * part]
    grid_ref[right, :, part : 2 * part] = -from_right[:, 0:part]

    def to_left():
        from_left = product(slice(0, order))
        grid_ref[left, :, 0:part] -= from_left[:, 0:part]
        grid_ref[left, :, 2 * part : 3 * part] = -from_left[:, part : 2 * part]

    if isinstance(has_left, bool):
        if has_left:
            to_left()
    else:
        pl.when(has_left)(to_left)


def unpack_tile(packed, modes):
    half = 3 * modes // 2
    upper = packed[:, 0 : 3 * modes]
    lower = jnp.concatenate(
        [packed[0:ROWS, 3 * modes : 3 * modes + half], packed[ROWS:, 3 * modes : 3 * modes + half]],
        axis=1,
    )
    return jnp.concatenate([upper, lower], axis=0)


def pack_tile(tile):
    modes = tile.shape[0]
    half = 3 * modes // 2
    top = modes - ROWS
    upper = tile[0:top]
    lower = jnp.concatenate([tile[top:, 0:half], tile[top:, half:]], axis=0)
    spare = jnp.zeros((top, LANES - 3 * modes - half), jnp.float32)
    return jnp.concatenate([upper, lower, spare], axis=1)


def factor_kernel(tiles_ref, after_ref, diag_ref, left_ref, right_ref, grid_ref, turned_ref):
    subs, layers, _, _ = tiles_ref.shape
    modes, order = diag_ref.shape
    part = grid_ref.shape[2] // 3
    unrolled = layers <= UNROLLED_LAYERS
    del after_ref
    grid_ref[...] = jnp.zeros_like(grid_ref)

    def place_tiles(s, has_left):
        for j in range(layers):
            tile = unpack_tile(tiles_ref[s, j], modes)
            turned = tile.T
            rows = slice(j * modes, (j + 1) * modes)
            grid_ref[s, rows, j * modes : (j + 1) * modes] = tile[:, 0:modes]
            if j > 0:
                above = slice((j - 1) * modes, j * modes)
                grid_ref[s, above, j * modes : (j + 1) * modes] = tile[:, modes : 2 * modes]
            if has_left:
                lanes = slice(part + j * modes, part + (j + 1) * modes)
                grid_ref[s, rows, lanes] = turned[2 * modes : 3 * modes]
                lanes = slice(2 * part + j * modes, 2 * part + (j + 1) * modes)
                grid_ref[s - 1, rows, lanes] = tile[:, 2 * modes : 3 * modes]

    place_tiles(0, False)
    if unrolled:
        for s in range(1, subs):
            place_tiles(s, True)
    else:

        def place_one(s, carry):
            place_tiles(s, True)
            return carry

        lax.fori_loop(1, subs, place_one, 0)

    distance = 1
    while distance < subs:
        if unrolled:
            planes = list(range(distance - 1, subs, 2 * distance))
            eliminate_planes(grid_ref, planes, modes, order, part, 3 * part, distance == 1)
            for plane in planes:
                update_partners(grid_ref, plane, distance, part, order, plane >= distance)
        else:

            def one_plane(index, carry, distance=distance):
                plane = distance - 1 + 2 * distance * index
                eliminate_planes(grid_ref, [plane], modes, order, part, 3 * part)
                update_partners(grid_ref, plane, distance, part, order, index > 0)
                return carry

            lax.fori_loop(0, subs // (2 * distance), one_plane, 0)
        distance *= 2
    eliminate_planes(grid_ref, [subs - 1], modes, order, part, part)

    sub_here, lay_here = lax.axis_index("sub"), lax.axis_index("layer")
    strip = pl.ds(pl.multiple_of(lay_here * modes, ROWS), modes)
    for k, out_ref in enumerate((diag_ref, left_ref, right_ref)):
        turned_ref[k] = grid_ref[sub_here, :, k * part : (k + 1) * part].T
        found = turned_ref[k, strip, :]
        out_ref[...] = found if k == 0 else jnp.where(sub_here < subs - 1, found, 0.0)


VMEM_BLOCK = pl.BlockSpec(memory_space=pltpu.VMEM)
SPARE_BYTES = 4 * 1024 * 1024


def kernel_params(shapes):
    held = sum(4 * math.prod(shape) for shape in shapes)
    return pltpu.CompilerParams(vmem_limit_bytes=min(2 * held + SPARE_BYTES, 60 * 1024 * 1024))


def factor_planes(plane_tiles, modes, after):
    subs, layers, _, _ = plane_tiles.shape
    order = layers * modes
    part = -(-order // LANES) * LANES
    strip = jax.ShapeDtypeStruct((modes, order), jnp.float32)
    scratch = ((subs, order, 3 * part), (3, part, order))
    return pl.pallas_call(
        factor_kernel,
        out_shape=(strip, strip, strip),
        in_specs=[VMEM_BLOCK, VMEM_BLOCK],
        out_specs=(VMEM_BLOCK, VMEM_BLOCK, VMEM_BLOCK),
        scratch_shapes=[pltpu.VMEM(shape, jnp.float32) for shape in scratch],
        compiler_params=kernel_params((plane_tiles.shape,) + scratch),
        name="factor_planes",
    )(plane_tiles, after)


def across_dot(left, right):
    return lax.dot_general(
        left,
        right,
        (((1,), (1,)), ((), ())),
        precision=HIGHEST,
        preferred_element_type=jnp.float32,
    )


def pick_kernel(
    vectors_in, lists_in, face_in, mass_in, inner_in,
    vectors_ref, lists_ref, face_ref, mass_ref, inner_ref, picked_ref, sub_ref, layer_ref, sems
):
    modes, row_count = vectors_ref.shape
    strips = modes // ROWS
    pairs = [(lists_in, lists_ref)]
    pairs += [
        (vectors_in.at[pl.ds(r * ROWS, ROWS)], vectors_ref.at[pl.ds(r * ROWS, ROWS)])
        for r in range(strips)
    ]
    pairs += [(face_in, face_ref), (mass_in, mass_ref), (inner_in, inner_ref)]
    copies = [pltpu.make_async_copy(a, b, sems.at[i]) for i, (a, b) in enumerate(pairs)]
    for copy in copies:
        copy.start()
    copies[0].wait()
    lists = []
    for k in range(4):
        rows = jnp.broadcast_to(lists_ref[k : k + 1, :], (ROWS, LANES))
        lists.append((rows // LANES, rows % LANES))
    for r in range(strips):
        copies[1 + r].wait()
        strip = slice(r * ROWS, (r + 1) * ROWS)
        found = [jnp.zeros((ROWS, LANES), jnp.float32) for _ in range(4)]
        for c in range(row_count // LANES):
            tile = vectors_ref[strip, c * LANES : (c + 1) * LANES]
            for k, (tile_of, lane_of) in enumerate(lists):
                moved = jnp.take_along_axis(tile, lane_of, axis=1, mode="promise_in_bounds")
                found[k] = jnp.where(tile_of == c, moved, found[k])
        for k in range(4):
            picked_ref[k, strip] = found[k]
    for copy in copies[1 + strips :]:
        copy.wait()
    for k, send_ref in ((0, sub_ref), (2, layer_ref)):
        send_ref[0:modes] = picked_ref[k]
        send_ref[modes:] = jnp.broadcast_to(face_ref[k // 2 : k // 2 + 1, :], (ROWS, LANES))


def own_kernel(
    vectors_ref, mass_ref, inner_ref, face_ref, picked_ref, base_ref, own_ref, *, subs, layers
):
    vectors = vectors_ref[...]
    row_count = vectors.shape[1]
    places = lax.broadcasted_iota(jnp.int32, (1, row_count), 1)
    base = mass_ref[...] * vectors
    for k, t in enumerate(STRIDES):
        edge_weight = jnp.where(places < row_count - t, inner_ref[k], 0.0)
        fluxes = edge_weight * (vectors - pltpu.roll(vectors, row_count - t, 1))
        base = base + fluxes - pltpu.roll(fluxes, t, 1)
    base_ref[...] = base
    own = across_dot(vectors, base)
    for k, axis, ends in ((0, "sub", subs - 1), (2, "layer", layers - 1)):
        springs = jnp.where(lax.axis_index(axis) < ends, face_ref[k // 2 : k // 2 + 1, :], 0.0)
        own = own + across_dot(picked_ref[k], springs * picked_ref[k])
    own_ref[...] = own


def tile_kernel(
    own_ref, picked_ref, sub_ref, layer_ref, copies_ref, sub_send_ref, layer_send_ref, *, row_count
):
    modes = own_ref.shape[0]
    inverse = 1.0 / row_count
    pairs = []
    for k, theirs_ref in ((1, sub_ref), (3, layer_ref)):
        mine = picked_ref[k]
        sprung = theirs_ref[modes : modes + 1] * mine
        stacked = jnp.concatenate([mine, theirs_ref[0:modes]], axis=0)
        pairs.append(across_dot(stacked, sprung))
    down, side = pairs
    diag_tile = (own_ref[...] + down[0:modes] + side[0:modes]) * inverse
    side_turned = -side[modes:] * inverse
    down_turned = -down[modes:] * inverse
    packed = pack_tile(jnp.concatenate([diag_tile, side_turned, down_turned], axis=1))
    for s in range(copies_ref.shape[0]):
        copies_ref[s] = packed
    sub_send_ref[...] = picked_ref[1]
    layer_send_ref[...] = picked_ref[3]


def scatter_kernel(
    base_ref, lists_ref, face_ref, picked_ref, before_sub_ref, after_sub_ref,
    before_layer_ref, after_layer_ref, applied_ref, token_ref, *, subs, layers
):
    modes, row_count = base_ref.shape
    width = 2 * LANES
    springs = [
        jnp.where(lax.axis_index("sub") < subs - 1, face_ref[0:1, :], 0.0),
        before_sub_ref[modes : modes + 1, :],
        jnp.where(lax.axis_index("layer") < layers - 1, face_ref[1:2, :], 0.0),
        before_layer_ref[modes : modes + 1, :],
    ]
    partners = [
        after_sub_ref[...],
        before_sub_ref[0:modes, :],
        after_layer_ref[...],
        before_layer_ref[0:modes, :],
    ]
    pulls = jnp.concatenate(
        [springs[k] * (picked_ref[k] - partners[k]) for k in range(4)], axis=1
    )
    rows = jnp.concatenate([lists_ref[k : k + 1, :] for k in range(4)], axis=1)
    block_of, lane_of = rows // width, rows % width
    lanes = lax.broadcasted_iota(jnp.int32, (width, rows.shape[1]), 0)
    onehot = jnp.where(lanes == lane_of, 1.0, 0.0).astype(jnp.bfloat16)
    total = None
    rest = pulls
    for _ in range(3):
        piece = rest.astype(jnp.bfloat16).astype(jnp.float32)
        rest = rest - piece
        spread = jnp.concatenate(
            [jnp.where(block_of == h, piece, 0.0) for h in range(row_count // width)], axis=0
        ).astype(jnp.bfloat16)
        moved = lax.dot_general(
            spread, onehot, (((1,), (1,)), ((), ())), preferred_element_type=jnp.float32
        )
        total = moved if total is None else total + moved
    for h in range(row_count // width):
        lanes = slice(h * width, (h + 1) * width)
        applied_ref[:, lanes] = base_ref[:, lanes] + total[h * modes : (h + 1) * modes]
    token_ref[...] = jnp.zeros_like(token_ref)


def local_call(body, outputs, operands, name):
    shapes = tuple(jax.ShapeDtypeStruct(shape, jnp.float32) for shape in outputs)
    return pl.pallas_call(
        body,
        out_shape=shapes,
        in_specs=[VMEM_BLOCK] * len(operands),
        out_specs=tuple(VMEM_BLOCK for _ in shapes),
        compiler_params=kernel_params([x.shape for x in operands] + list(outputs)),
        name=name,
    )(*operands)


def per_device(eigen_vectors, row_mass, inner_weight, face_weight, margin_rows):
    vectors = eigen_vectors[0, 0]
    row_lists = margin_rows[0, 0]
    face_springs = face_weight[0, 0]
    modes, row_count = vectors.shape
    width = row_lists.shape[-1]
    subs = lax.axis_size("sub")
    layers = lax.axis_size("layer")
    up_sub = [(i, i + 1) for i in range(subs - 1)]
    up_layer = [(i, i + 1) for i in range(layers - 1)]
    down_sub = [(i + 1, i) for i in range(subs - 1)]
    down_layer = [(i + 1, i) for i in range(layers - 1)]
    taken = (vectors, row_lists, face_springs, row_mass[0], inner_weight[0].reshape(-1, 1, row_count))
    held = [(x.shape, x.dtype) for x in taken]
    made = [(4, modes, width), (modes + ROWS, width), (modes + ROWS, width)]
    held += [(shape, jnp.float32) for shape in made]
    vectors, row_lists, face_springs, masses, interior, picked, sub_send, layer_send = pl.pallas_call(
        pick_kernel,
        out_shape=tuple(jax.ShapeDtypeStruct(*pair) for pair in held),
        in_specs=[pl.BlockSpec(memory_space=pltpu.HBM)] * len(taken),
        out_specs=(VMEM_BLOCK,) * len(held),
        scratch_shapes=[pltpu.SemaphoreType.DMA((len(taken) + modes // ROWS - 1,))],
        compiler_params=kernel_params([shape for shape, _ in held]),
        name="pick_rows",
    )(*(pltpu.with_memory_space_constraint(x, pltpu.HBM) for x in taken))
    before_sub = lax.ppermute(sub_send, "sub", up_sub)
    before_layer = lax.ppermute(layer_send, "layer", up_layer)
    base, own = local_call(
        functools.partial(own_kernel, subs=subs, layers=layers),
        [(modes, row_count), (modes, modes)],
        (vectors, masses, interior, face_springs, picked),
        "own_rows",
    )
    copies, sub_send, layer_send = local_call(
        functools.partial(tile_kernel, row_count=row_count),
        [(subs * layers, modes - ROWS, LANES), (modes, width), (modes, width)],
        (own, picked, before_sub, before_layer),
        "coarse_tiles",
    )
    tiles = lax.all_to_all(copies, ("sub", "layer"), split_axis=0, concat_axis=0, tiled=True)
    after_sub = lax.ppermute(sub_send, "sub", down_sub)
    after_layer = lax.ppermute(layer_send, "layer", down_layer)
    applied, token = local_call(
        functools.partial(scatter_kernel, subs=subs, layers=layers),
        [(modes, row_count), (ROWS, LANES)],
        (base, row_lists, face_springs, picked, before_sub, after_sub, before_layer, after_layer),
        "spread_rows",
    )
    diag_strip, left_strip, right_strip = factor_planes(
        tiles.reshape(subs, layers, *tiles.shape[1:]), modes, token
    )
    return (applied[None, None], diag_strip[None], left_strip[None], right_strip[None])


def solution(mesh):
    in_specs = (
        P("sub", "layer", None, None),
        P("sub", "layer", None),
        P("sub", "layer", None, None),
        P("sub", "layer", None, None),
        P("sub", "layer", None, None),
    )
    out_specs = (
        P("sub", "layer", None, None),
        P("sub", "layer", None),
        P("sub", "layer", None),
        P("sub", "layer", None),
    )
    return jax.shard_map(
        per_device, mesh=mesh, in_specs=in_specs, out_specs=out_specs, check_vma=False
    )
```

```python
import functools
import math
import jax
import jax.numpy as jnp
from jax import lax
from jax.experimental import pallas as pl
from jax.experimental.pallas import tpu as pltpu
from jax.sharding import PartitionSpec as P

STRIDES = (1, 3, 27)
HIGHEST = lax.Precision.HIGHEST
LANES = 128
ROWS = 8
UNROLLED_LAYERS = 4
PLANES_AT_ONCE = 2
CUTS = 4


def turned_dot(left, right):
    return lax.dot_general(
        left,
        right,
        (((0,), (0,)), ((), ())),
        precision=HIGHEST,
        preferred_element_type=jnp.float32,
    )


PRODUCTS = ((0, 0), (1, 0), (2, 0), (0, 1), (1, 1), (0, 2))


def pieces_of(values):
    first = values.astype(jnp.bfloat16).astype(jnp.float32)
    rest = values - first
    second = rest.astype(jnp.bfloat16).astype(jnp.float32)
    return first, second, rest - second


def single_dot(left, right):
    return lax.dot_general(
        left, right, (((1,), (0,)), ((), ())), preferred_element_type=jnp.float32
    )


def narrow_product(panel_rows, part, below, end):
    modes = panel_rows.shape[0]
    first, second, third = pieces_of(panel_rows)
    stacked = jnp.concatenate([x[:, 0:part] for x in (first, second, third)], axis=0)
    turned = stacked.T[below:end]
    lane = lax.broadcasted_iota(jnp.int32, (end - below, LANES), 1)
    wide = jnp.concatenate(
        [turned, jnp.zeros((end - below, LANES - 3 * modes), jnp.float32)], axis=1
    )
    again = pltpu.roll(wide, 3 * modes, 1)
    left = jnp.where(lane < 3 * modes, wide, jnp.where(lane < 5 * modes, again, 0.0))
    last = jnp.where(lane < modes, wide, 0.0)
    depth = LANES + 2 * LANES // 8
    columns = jnp.concatenate([left, last], axis=1)[:, 0:depth]
    gap = jnp.zeros((LANES - 5 * modes, panel_rows.shape[1]), jnp.float32)
    tail = jnp.zeros((depth - LANES - modes, panel_rows.shape[1]), jnp.float32)
    rows = jnp.concatenate([first] * 3 + [second] * 2 + [gap, third, tail], axis=0)
    return single_dot(columns.astype(jnp.bfloat16), rows.astype(jnp.bfloat16))


def plain_dot(left, right):
    return lax.dot_general(
        left,
        right,
        (((1,), (0,)), ((), ())),
        precision=HIGHEST,
        preferred_element_type=jnp.float32,
    )


def spread_row(strip, k):
    return jnp.broadcast_to(strip[k : k + 1, :], strip.shape)


def eliminate_pair(block, columns, pivots, iota, q, k):
    start = q * ROWS
    first, second = columns[start + k], columns[start + k + 1]
    corner, joint = spread_row(first[0], k), spread_row(first[0], k + 1)
    other_corner = spread_row(second[0], k + 1)
    minor = corner * other_corner - joint * joint
    inverse = pl.reciprocal(corner, approx=True)
    other_inverse = corner * pl.reciprocal(minor, approx=True)
    below = [column * inverse for column in first]
    second = [column - below[r] * joint for r, column in enumerate(second)]
    other_below = [column * other_inverse for column in second]
    below[0] = jnp.where(iota > k, below[0], 0.0)
    other_below[0] = jnp.where(iota > k + 1, other_below[0], 0.0)
    for j in range(start + k + 2, len(columns)):
        strip = j // ROWS - q
        head = spread_row(first[strip], j % ROWS)
        other_head = spread_row(second[strip], j % ROWS)
        columns[j] = [
            column - below[strip + r] * head - other_below[strip + r] * other_head
            for r, column in enumerate(columns[j])
        ]
    for t in range(len(block[q])):
        row = spread_row(block[q][t], k)
        for r, lower in enumerate(below):
            block[q + r][t] = block[q + r][t] - lower * row
        row = spread_row(block[q][t], k + 1)
        for r, lower in enumerate(other_below):
            block[q + r][t] = block[q + r][t] - lower * row
    return jnp.where(iota == k, corner, jnp.where(iota == k + 1, minor * inverse, pivots))


def factor_rows(blocks, tiles_per_part, first_row, turned):
    strip_count = len(blocks[0])
    iota = lax.broadcasted_iota(jnp.int32, (ROWS, LANES), 0)
    lane = lax.broadcasted_iota(jnp.int32, (ROWS, LANES), 1)
    blocks = [[list(strip) for strip in block] for block in blocks]
    at_once = len(blocks) <= PLANES_AT_ONCE
    held = [[] for _ in blocks]
    for q in range(strip_count):
        start = q * ROWS
        if q == 0 or not at_once:
            for b, block in enumerate(blocks):
                source = turned(b, block, q)
                for j in range(start, strip_count * ROWS if at_once else start + ROWS):
                    held[b].append(
                        [
                            jnp.broadcast_to(strip[:, j : j + 1], (ROWS, LANES))
                            for strip in source[j // ROWS - q :]
                        ]
                    )
        pivots = [jnp.zeros((ROWS, LANES), jnp.float32) for _ in blocks]
        for k in range(0, ROWS, 2):
            for b, block in enumerate(blocks):
                pivots[b] = eliminate_pair(block, held[b], pivots[b], iota, q, k)
        for b, block in enumerate(blocks):
            scale = lax.rsqrt(pivots[b])
            for t in range(len(block[q])):
                strip = block[q][t] * scale
                if t < tiles_per_part:
                    keep = lane + t * LANES >= iota + (first_row + start)
                    strip = jnp.where(keep, strip, 0.0)
                block[q][t] = strip
    return blocks


def eliminate_panel(grid_ref, planes, modes, order, part, lanes_used, panel, banded):
    per_part = part // LANES
    first_row = panel * modes
    static = isinstance(panel, int)
    if static:
        rows = pl.ds(first_row, modes)
    else:
        rows = pl.ds(pl.multiple_of(first_row, ROWS), modes)
    blocks = []
    for plane in planes:
        panel_rows = grid_ref[plane, rows, 0:lanes_used]
        blocks.append(
            [
                [
                    panel_rows[q * ROWS : (q + 1) * ROWS, t * LANES : (t + 1) * LANES]
                    for t in range(lanes_used // LANES)
                ]
                for q in range(modes // ROWS)
            ]
        )

    def turned(b, block, q):
        found = []
        for strip in block[q:]:
            if static and first_row // LANES == (first_row + modes - 1) // LANES:
                tile = strip[first_row // LANES]
                offset = first_row % LANES
                found.append(tile if offset == 0 else tile[:, offset : offset + modes])
            else:
                wide = jnp.concatenate(strip[:per_part], axis=1)
                found.append(pltpu.roll(wide, lax.rem(part - first_row, part), 1)[:, :LANES])
        return found

    blocks = factor_rows(blocks, per_part, first_row, turned)
    for plane, block in zip(planes, blocks):
        panel_rows = jnp.concatenate([jnp.concatenate(strip, axis=1) for strip in block], axis=0)
        grid_ref[plane, rows, 0:lanes_used] = panel_rows
        if static:
            below = (panel + 1) * modes
            end = min(below + modes, order) if banded else order
            if below < order:
                update = narrow_product(panel_rows, part, below, end)
                grid_ref[plane, below:end, 0:lanes_used] -= update
        else:
            lane = lax.broadcasted_iota(jnp.int32, (modes, part), 1)
            columns = jnp.where(lane >= first_row + modes, panel_rows[:, 0:part], 0.0)
            update = turned_dot(columns, panel_rows)[0:order]
            grid_ref[plane, :, 0:lanes_used] -= update


def eliminate_planes(grid_ref, planes, modes, order, part, lanes_used, banded=False):
    layers = order // modes
    if layers <= UNROLLED_LAYERS:
        for panel in range(layers):
            eliminate_panel(grid_ref, planes, modes, order, part, lanes_used, panel, banded)
    else:

        def one_panel(panel, carry):
            eliminate_panel(grid_ref, planes, modes, order, part, lanes_used, panel, banded)
            return carry

        lax.fori_loop(0, layers, one_panel, 0)


def update_partners(grid_ref, plane, distance, part, order, has_left):
    left, right = plane - distance, plane + distance
    both = grid_ref[plane, :, part : 3 * part]
    if part > order:
        spare = jnp.zeros((part - order, 2 * part), jnp.float32)
        both = jnp.concatenate([both, spare], axis=0)
    turned = [piece.astype(jnp.bfloat16) for piece in pieces_of(both.T)]
    held = [piece.astype(jnp.bfloat16) for piece in pieces_of(both)]
    held = jnp.concatenate([held[right] for _, right in PRODUCTS], axis=0)

    def product(rows):
        columns = jnp.concatenate([turned[left][rows] for left, _ in PRODUCTS], axis=1)
        return single_dot(columns, held)

    from_right = product(slice(part, part + order))
    grid_ref[right, :, 0:part] -= from_right[:, part : 2 * part]
    grid_ref[right, :, part : 2 * part] = -from_right[:, 0:part]

    def to_left():
        from_left = product(slice(0, order))
        grid_ref[left, :, 0:part] -= from_left[:, 0:part]
        grid_ref[left, :, 2 * part : 3 * part] = -from_left[:, part : 2 * part]

    if isinstance(has_left, bool):
        if has_left:
            to_left()
    else:
        pl.when(has_left)(to_left)


def unpack_tile(packed, modes):
    half = 3 * modes // 2
    upper = packed[:, 0 : 3 * modes]
    lower = jnp.concatenate(
        [packed[0:ROWS, 3 * modes : 3 * modes + half], packed[ROWS:, 3 * modes : 3 * modes + half]],
        axis=1,
    )
    return jnp.concatenate([upper, lower], axis=0)


def pack_tile(tile):
    modes = tile.shape[0]
    half = 3 * modes // 2
    top = modes - ROWS
    upper = tile[0:top]
    lower = jnp.concatenate([tile[top:, 0:half], tile[top:, half:]], axis=0)
    spare = jnp.zeros((top, LANES - 3 * modes - half), jnp.float32)
    return jnp.concatenate([upper, lower, spare], axis=1)


def factor_kernel(tiles_ref, after_ref, diag_ref, left_ref, right_ref, grid_ref, turned_ref):
    subs, layers, _, _ = tiles_ref.shape
    modes, order = diag_ref.shape
    part = grid_ref.shape[2] // 3
    unrolled = layers <= UNROLLED_LAYERS
    del after_ref
    lane = lax.broadcasted_iota(jnp.int32, (modes, part), 1)
    inside = [(lane >= j * modes) & (lane < (j + 1) * modes) for j in range(layers)]

    def place_tiles(s, before):
        tiles = [unpack_tile(tiles_ref[s, j], modes) for j in range(layers)]
        stacked = tiles
        if part > order:
            stacked = tiles + [jnp.zeros((part - order, tiles[0].shape[1]), jnp.float32)]
        turned = jnp.concatenate(stacked, axis=0).T
        for j, tile in enumerate(tiles):
            rows = slice(j * modes, (j + 1) * modes)
            own = jnp.where(inside[j], turned[0:modes], 0.0)
            if j + 1 < layers:
                own = jnp.where(inside[j + 1], turned[modes : 2 * modes], own)
            grid_ref[s, rows, 0:part] = own
            spare = jnp.zeros((modes, part - 3 * modes), jnp.float32)
            wide = jnp.concatenate([tile, spare], axis=1)
            shift = (j - 2) * modes % part
            down = pltpu.roll(wide, shift, 1) if shift else wide
            grid_ref[s, rows, part : 2 * part] = jnp.where(inside[j], down, 0.0)
            down = jnp.where(inside[j], turned[2 * modes : 3 * modes], 0.0)
            grid_ref[before, rows, 2 * part : 3 * part] = down

    place_tiles(0, subs - 1)
    if unrolled:
        for s in range(1, subs):
            place_tiles(s, s - 1)
    else:

        def place_one(s, carry):
            place_tiles(s, s - 1)
            return carry

        lax.fori_loop(1, subs, place_one, 0)

    distance = 1
    while distance < subs:
        if unrolled:
            planes = list(range(distance - 1, subs, 2 * distance))
            eliminate_planes(grid_ref, planes, modes, order, part, 3 * part, distance == 1)
            for plane in planes:
                update_partners(grid_ref, plane, distance, part, order, plane >= distance)
        else:

            def one_plane(index, carry, distance=distance):
                plane = distance - 1 + 2 * distance * index
                eliminate_planes(grid_ref, [plane], modes, order, part, 3 * part)
                update_partners(grid_ref, plane, distance, part, order, index > 0)
                return carry

            lax.fori_loop(0, subs // (2 * distance), one_plane, 0)
        distance *= 2
    eliminate_planes(grid_ref, [subs - 1], modes, order, part, part)

    sub_here, lay_here = lax.axis_index("sub"), lax.axis_index("layer")
    strip = pl.ds(pl.multiple_of(lay_here * modes, ROWS), modes)
    for k, out_ref in enumerate((diag_ref, left_ref, right_ref)):
        turned_ref[k] = grid_ref[sub_here, :, k * part : (k + 1) * part].T
        found = turned_ref[k, strip, :]
        out_ref[...] = found if k == 0 else jnp.where(sub_here < subs - 1, found, 0.0)


VMEM_BLOCK = pl.BlockSpec(memory_space=pltpu.VMEM)
SPARE_BYTES = 4 * 1024 * 1024


def kernel_params(shapes):
    held = sum(4 * math.prod(shape) for shape in shapes)
    return pltpu.CompilerParams(vmem_limit_bytes=min(2 * held + SPARE_BYTES, 60 * 1024 * 1024))


def factor_planes(plane_tiles, modes, after):
    subs, layers, _, _ = plane_tiles.shape
    order = layers * modes
    part = -(-order // LANES) * LANES
    strip = jax.ShapeDtypeStruct((modes, order), jnp.float32)
    scratch = ((subs, order, 3 * part), (3, part, order))
    return pl.pallas_call(
        factor_kernel,
        out_shape=(strip, strip, strip),
        in_specs=[VMEM_BLOCK, VMEM_BLOCK],
        out_specs=(VMEM_BLOCK, VMEM_BLOCK, VMEM_BLOCK),
        scratch_shapes=[pltpu.VMEM(shape, jnp.float32) for shape in scratch],
        compiler_params=kernel_params((plane_tiles.shape,) + scratch),
        name="factor_planes",
    )(plane_tiles, after)


def across_dot(left, right):
    return lax.dot_general(
        left,
        right,
        (((1,), (1,)), ((), ())),
        precision=HIGHEST,
        preferred_element_type=jnp.float32,
    )


def pick_kernel(
    vectors_in, lists_in, face_in, mass_in, inner_in,
    vectors_ref, lists_ref, face_ref, mass_ref, inner_ref, picked_ref, sub_ref, layer_ref, sems
):
    modes, row_count = vectors_ref.shape
    strips = modes // ROWS
    pairs = [(lists_in, lists_ref)]
    cut = row_count // CUTS
    for r in range(strips):
        for c in range(CUTS):
            piece = (pl.ds(r * ROWS, ROWS), pl.ds(c * cut, cut))
            pairs.append((vectors_in.at[piece], vectors_ref.at[piece]))
    pairs += [(face_in, face_ref), (mass_in, mass_ref), (inner_in, inner_ref)]
    copies = [pltpu.make_async_copy(a, b, sems.at[i]) for i, (a, b) in enumerate(pairs)]
    for copy in copies:
        copy.start()
    copies[0].wait()
    lists = []
    for k in range(4):
        rows = jnp.broadcast_to(lists_ref[k : k + 1, :], (ROWS, LANES))
        lists.append((rows // LANES, rows % LANES))
    for r in range(strips):
        for c in range(CUTS):
            copies[1 + r * CUTS + c].wait()
        strip = slice(r * ROWS, (r + 1) * ROWS)
        found = [jnp.zeros((ROWS, LANES), jnp.float32) for _ in range(4)]
        for c in range(row_count // LANES):
            tile = vectors_ref[strip, c * LANES : (c + 1) * LANES]
            for k, (tile_of, lane_of) in enumerate(lists):
                moved = jnp.take_along_axis(tile, lane_of, axis=1, mode="promise_in_bounds")
                found[k] = jnp.where(tile_of == c, moved, found[k])
        for k in range(4):
            picked_ref[k, strip] = found[k]
    for copy in copies[1 + strips * CUTS :]:
        copy.wait()
    for k, send_ref in ((0, sub_ref), (2, layer_ref)):
        send_ref[0:modes] = picked_ref[k]
        send_ref[modes:] = jnp.broadcast_to(face_ref[k // 2 : k // 2 + 1, :], (ROWS, LANES))


def own_kernel(
    vectors_ref, mass_ref, inner_ref, face_ref, picked_ref, base_ref, own_ref, *, subs, layers
):
    vectors = vectors_ref[...]
    row_count = vectors.shape[1]
    places = lax.broadcasted_iota(jnp.int32, (1, row_count), 1)
    base = mass_ref[...] * vectors
    for k, t in enumerate(STRIDES):
        edge_weight = jnp.where(places < row_count - t, inner_ref[k], 0.0)
        fluxes = edge_weight * (vectors - pltpu.roll(vectors, row_count - t, 1))
        base = base + fluxes - pltpu.roll(fluxes, t, 1)
    base_ref[...] = base
    own = across_dot(vectors, base)
    for k, axis, ends in ((0, "sub", subs - 1), (2, "layer", layers - 1)):
        springs = jnp.where(lax.axis_index(axis) < ends, face_ref[k // 2 : k // 2 + 1, :], 0.0)
        own = own + across_dot(picked_ref[k], springs * picked_ref[k])
    own_ref[...] = own


def tile_kernel(
    own_ref, picked_ref, sub_ref, layer_ref, copies_ref, sub_send_ref, layer_send_ref, *, row_count
):
    modes = own_ref.shape[0]
    inverse = 1.0 / row_count
    pairs = []
    for k, theirs_ref in ((1, sub_ref), (3, layer_ref)):
        mine = picked_ref[k]
        sprung = theirs_ref[modes : modes + 1] * mine
        stacked = jnp.concatenate([mine, theirs_ref[0:modes]], axis=0)
        pairs.append(across_dot(sprung, stacked))
    down, side = pairs
    diag_tile = (own_ref[...] + down[:, 0:modes] + side[:, 0:modes]) * inverse
    side_tile = -side[:, modes:] * inverse
    down_tile = -down[:, modes:] * inverse
    packed = pack_tile(jnp.concatenate([diag_tile, side_tile, down_tile], axis=1))
    for s in range(copies_ref.shape[0]):
        copies_ref[s] = packed
    sub_send_ref[...] = picked_ref[1]
    layer_send_ref[...] = picked_ref[3]


def scatter_kernel(
    base_ref, lists_ref, face_ref, picked_ref, before_sub_ref, after_sub_ref,
    before_layer_ref, after_layer_ref, applied_ref, token_ref, *, subs, layers
):
    modes, row_count = base_ref.shape
    width = 2 * LANES
    springs = [
        jnp.where(lax.axis_index("sub") < subs - 1, face_ref[0:1, :], 0.0),
        before_sub_ref[modes : modes + 1, :],
        jnp.where(lax.axis_index("layer") < layers - 1, face_ref[1:2, :], 0.0),
        before_layer_ref[modes : modes + 1, :],
    ]
    partners = [
        after_sub_ref[...],
        before_sub_ref[0:modes, :],
        after_layer_ref[...],
        before_layer_ref[0:modes, :],
    ]
    pulls = jnp.concatenate(
        [springs[k] * (picked_ref[k] - partners[k]) for k in range(4)], axis=1
    )
    rows = jnp.concatenate([lists_ref[k : k + 1, :] for k in range(4)], axis=1)
    block_of, lane_of = rows // width, rows % width
    lanes = lax.broadcasted_iota(jnp.int32, (width, rows.shape[1]), 0)
    onehot = jnp.where(lanes == lane_of, 1.0, 0.0).astype(jnp.bfloat16)
    total = None
    rest = pulls
    for _ in range(3):
        piece = rest.astype(jnp.bfloat16).astype(jnp.float32)
        rest = rest - piece
        spread = jnp.concatenate(
            [jnp.where(block_of == h, piece, 0.0) for h in range(row_count // width)], axis=0
        ).astype(jnp.bfloat16)
        moved = lax.dot_general(
            spread, onehot, (((1,), (1,)), ((), ())), preferred_element_type=jnp.float32
        )
        total = moved if total is None else total + moved
    for h in range(row_count // width):
        lanes = slice(h * width, (h + 1) * width)
        applied_ref[:, lanes] = base_ref[:, lanes] + total[h * modes : (h + 1) * modes]
    token_ref[...] = jnp.zeros_like(token_ref)


def local_call(body, outputs, operands, name):
    shapes = tuple(jax.ShapeDtypeStruct(shape, jnp.float32) for shape in outputs)
    return pl.pallas_call(
        body,
        out_shape=shapes,
        in_specs=[VMEM_BLOCK] * len(operands),
        out_specs=tuple(VMEM_BLOCK for _ in shapes),
        compiler_params=kernel_params([x.shape for x in operands] + list(outputs)),
        name=name,
    )(*operands)


def per_device(eigen_vectors, row_mass, inner_weight, face_weight, margin_rows):
    vectors = eigen_vectors[0, 0]
    row_lists = margin_rows[0, 0]
    face_springs = face_weight[0, 0]
    modes, row_count = vectors.shape
    width = row_lists.shape[-1]
    subs = lax.axis_size("sub")
    layers = lax.axis_size("layer")
    up_sub = [(i, i + 1) for i in range(subs - 1)]
    up_layer = [(i, i + 1) for i in range(layers - 1)]
    down_sub = [(i + 1, i) for i in range(subs - 1)]
    down_layer = [(i + 1, i) for i in range(layers - 1)]
    taken = (vectors, row_lists, face_springs, row_mass[0], inner_weight[0].reshape(-1, 1, row_count))
    held = [(x.shape, x.dtype) for x in taken]
    made = [(4, modes, width), (modes + ROWS, width), (modes + ROWS, width)]
    held += [(shape, jnp.float32) for shape in made]
    vectors, row_lists, face_springs, masses, interior, picked, sub_send, layer_send = pl.pallas_call(
        pick_kernel,
        out_shape=tuple(jax.ShapeDtypeStruct(*pair) for pair in held),
        in_specs=[pl.BlockSpec(memory_space=pltpu.HBM)] * len(taken),
        out_specs=(VMEM_BLOCK,) * len(held),
        scratch_shapes=[pltpu.SemaphoreType.DMA((len(taken) + CUTS * modes // ROWS - 1,))],
        compiler_params=kernel_params([shape for shape, _ in held]),
        name="pick_rows",
    )(*(pltpu.with_memory_space_constraint(x, pltpu.HBM) for x in taken))
    before_sub = lax.ppermute(sub_send, "sub", up_sub)
    before_layer = lax.ppermute(layer_send, "layer", up_layer)
    base, own = local_call(
        functools.partial(own_kernel, subs=subs, layers=layers),
        [(modes, row_count), (modes, modes)],
        (vectors, masses, interior, face_springs, picked),
        "own_rows",
    )
    copies, sub_send, layer_send = local_call(
        functools.partial(tile_kernel, row_count=row_count),
        [(subs * layers, modes - ROWS, LANES), (modes, width), (modes, width)],
        (own, picked, before_sub, before_layer),
        "coarse_tiles",
    )
    tiles = lax.all_to_all(copies, ("sub", "layer"), split_axis=0, concat_axis=0, tiled=True)
    after_sub = lax.ppermute(sub_send, "sub", down_sub)
    after_layer = lax.ppermute(layer_send, "layer", down_layer)
    applied, token = local_call(
        functools.partial(scatter_kernel, subs=subs, layers=layers),
        [(modes, row_count), (ROWS, LANES)],
        (base, row_lists, face_springs, picked, before_sub, after_sub, before_layer, after_layer),
        "spread_rows",
    )
    diag_strip, left_strip, right_strip = factor_planes(
        tiles.reshape(subs, layers, *tiles.shape[1:]), modes, token
    )
    return (applied[None, None], diag_strip[None], left_strip[None], right_strip[None])


def solution(mesh):
    in_specs = (
        P("sub", "layer", None, None),
        P("sub", "layer", None),
        P("sub", "layer", None, None),
        P("sub", "layer", None, None),
        P("sub", "layer", None, None),
    )
    out_specs = (
        P("sub", "layer", None, None),
        P("sub", "layer", None),
        P("sub", "layer", None),
        P("sub", "layer", None),
    )
    return jax.shard_map(
        per_device, mesh=mesh, in_specs=in_specs, out_specs=out_specs, check_vma=False
    )
```

```python
import functools
import math
import jax
import jax.numpy as jnp
from jax import lax
from jax.experimental import pallas as pl
from jax.experimental.pallas import tpu as pltpu
from jax.sharding import PartitionSpec as P

STRIDES = (1, 3, 27)
HIGHEST = lax.Precision.HIGHEST
LANES = 128
ROWS = 8
UNROLLED_LAYERS = 4
PLANES_AT_ONCE = 2
NARROW_DEPTH = LANES + LANES // 4


def turned_dot(left, right):
    return lax.dot_general(
        left,
        right,
        (((0,), (0,)), ((), ())),
        precision=HIGHEST,
        preferred_element_type=jnp.float32,
    )


PRODUCTS = ((0, 0), (1, 0), (2, 0), (0, 1), (1, 1), (0, 2))


def pieces_of(values):
    first = values.astype(jnp.bfloat16).astype(jnp.float32)
    rest = values - first
    second = rest.astype(jnp.bfloat16).astype(jnp.float32)
    return first, second, rest - second


def single_dot(left, right):
    return lax.dot_general(
        left, right, (((1,), (0,)), ((), ())), preferred_element_type=jnp.float32
    )


def narrow_columns(turned, modes):
    height = turned.shape[0]
    lane = lax.broadcasted_iota(jnp.int32, (height, LANES), 1)
    wide = jnp.concatenate([turned, jnp.zeros((height, LANES - 3 * modes), jnp.float32)], axis=1)
    again = pltpu.roll(wide, 3 * modes, 1)
    left = jnp.where(lane < 3 * modes, wide, jnp.where(lane < 5 * modes, again, 0.0))
    last = jnp.where(lane < modes, wide, 0.0)
    return jnp.concatenate([left, last], axis=1)[:, 0:NARROW_DEPTH].astype(jnp.bfloat16)


def narrow_rows(pieces):
    first, second, third = pieces
    modes, width = first.shape
    gap = jnp.zeros((LANES - 5 * modes, width), jnp.float32)
    tail = jnp.zeros((NARROW_DEPTH - LANES - modes, width), jnp.float32)
    rows = jnp.concatenate([first] * 3 + [second] * 2 + [gap, third, tail], axis=0)
    return rows.astype(jnp.bfloat16)


def plain_dot(left, right):
    return lax.dot_general(
        left,
        right,
        (((1,), (0,)), ((), ())),
        precision=HIGHEST,
        preferred_element_type=jnp.float32,
    )


def spread_row(strip, k):
    return jnp.broadcast_to(strip[k : k + 1, :], strip.shape)


def eliminate_pair(block, columns, pivots, iota, q, k):
    start = q * ROWS
    first, second = columns[start + k], columns[start + k + 1]
    corner, joint = spread_row(first[0], k), spread_row(first[0], k + 1)
    other_corner = spread_row(second[0], k + 1)
    minor = corner * other_corner - joint * joint
    inverse = pl.reciprocal(corner, approx=True)
    other_inverse = corner * pl.reciprocal(minor, approx=True)
    below = [column * inverse for column in first]
    second = [column - below[r] * joint for r, column in enumerate(second)]
    other_below = [column * other_inverse for column in second]
    below[0] = jnp.where(iota > k, below[0], 0.0)
    other_below[0] = jnp.where(iota > k + 1, other_below[0], 0.0)
    for j in range(start + k + 2, len(columns)):
        strip = j // ROWS - q
        head = spread_row(first[strip], j % ROWS)
        other_head = spread_row(second[strip], j % ROWS)
        columns[j] = [
            column - below[strip + r] * head - other_below[strip + r] * other_head
            for r, column in enumerate(columns[j])
        ]
    for t in range(len(block[q])):
        row = spread_row(block[q][t], k)
        for r, lower in enumerate(below):
            block[q + r][t] = block[q + r][t] - lower * row
        row = spread_row(block[q][t], k + 1)
        for r, lower in enumerate(other_below):
            block[q + r][t] = block[q + r][t] - lower * row
    return jnp.where(iota == k, corner, jnp.where(iota == k + 1, minor * inverse, pivots))


def factor_rows(blocks, tiles_per_part, first_row, turned):
    strip_count = len(blocks[0])
    iota = lax.broadcasted_iota(jnp.int32, (ROWS, LANES), 0)
    lane = lax.broadcasted_iota(jnp.int32, (ROWS, LANES), 1)
    blocks = [[list(strip) for strip in block] for block in blocks]
    at_once = len(blocks) <= PLANES_AT_ONCE
    held = [[] for _ in blocks]
    for q in range(strip_count):
        start = q * ROWS
        if q == 0 or not at_once:
            for b, block in enumerate(blocks):
                source = turned(b, block, q)
                for j in range(start, strip_count * ROWS if at_once else start + ROWS):
                    held[b].append(
                        [
                            jnp.broadcast_to(strip[:, j : j + 1], (ROWS, LANES))
                            for strip in source[j // ROWS - q :]
                        ]
                    )
        pivots = [jnp.zeros((ROWS, LANES), jnp.float32) for _ in blocks]
        for k in range(0, ROWS, 2):
            for b, block in enumerate(blocks):
                pivots[b] = eliminate_pair(block, held[b], pivots[b], iota, q, k)
        for b, block in enumerate(blocks):
            scale = lax.rsqrt(pivots[b])
            for t in range(len(block[q])):
                strip = block[q][t] * scale
                if t < tiles_per_part:
                    keep = lane + t * LANES >= iota + (first_row + start)
                    strip = jnp.where(keep, strip, 0.0)
                block[q][t] = strip
    return blocks


def eliminate_panel(grid_ref, planes, modes, order, part, lanes_used, panel, banded, distance):
    per_part = part // LANES
    first_row = panel * modes
    static = isinstance(panel, int)
    if static:
        rows = pl.ds(first_row, modes)
    else:
        rows = pl.ds(pl.multiple_of(first_row, ROWS), modes)
    blocks = []
    for plane in planes:
        panel_rows = grid_ref[plane, rows, 0:lanes_used]
        blocks.append(
            [
                [
                    panel_rows[q * ROWS : (q + 1) * ROWS, t * LANES : (t + 1) * LANES]
                    for t in range(lanes_used // LANES)
                ]
                for q in range(modes // ROWS)
            ]
        )

    def turned(b, block, q):
        found = []
        for strip in block[q:]:
            if static and first_row // LANES == (first_row + modes - 1) // LANES:
                tile = strip[first_row // LANES]
                offset = first_row % LANES
                found.append(tile if offset == 0 else tile[:, offset : offset + modes])
            else:
                wide = jnp.concatenate(strip[:per_part], axis=1)
                found.append(pltpu.roll(wide, lax.rem(part - first_row, part), 1)[:, :LANES])
        return found

    blocks = factor_rows(blocks, per_part, first_row, turned)
    for plane, block in zip(planes, blocks):
        panel_rows = jnp.concatenate([jnp.concatenate(strip, axis=1) for strip in block], axis=0)
        grid_ref[plane, rows, 0:lanes_used] = panel_rows
        if static:
            below = (panel + 1) * modes
            end = min(below + modes, order) if banded else order
            pieces = pieces_of(panel_rows)
            right = narrow_rows(pieces)
            stacked = jnp.concatenate(pieces, axis=0)
            if below < order:
                columns = narrow_columns(stacked[:, 0:part].T[below:end], modes)
                grid_ref[plane, below:end, 0:lanes_used] -= single_dot(columns, right)
            if distance:
                share_panel(grid_ref, plane, distance, stacked, right, modes, order, part, panel)
        else:
            lane = lax.broadcasted_iota(jnp.int32, (modes, part), 1)
            columns = jnp.where(lane >= first_row + modes, panel_rows[:, 0:part], 0.0)
            update = turned_dot(columns, panel_rows)[0:order]
            grid_ref[plane, :, 0:lanes_used] -= update


def eliminate_planes(
    grid_ref, planes, modes, order, part, lanes_used, banded=False, distance=0
):
    layers = order // modes
    if layers <= UNROLLED_LAYERS:
        for panel in range(layers):
            eliminate_panel(
                grid_ref, planes, modes, order, part, lanes_used, panel, banded, distance
            )
    else:

        def one_panel(panel, carry):
            eliminate_panel(grid_ref, planes, modes, order, part, lanes_used, panel, banded, 0)
            return carry

        lax.fori_loop(0, layers, one_panel, 0)


def share_panel(grid_ref, plane, distance, stacked, right, modes, order, part, panel):
    left_plane, right_plane = plane - distance, plane + distance
    turned = stacked[:, part : 3 * part].T
    both = right[:, part : 3 * part]

    def add(row_lanes, other, square, cross):
        found = single_dot(narrow_columns(turned[row_lanes : row_lanes + order], modes), both)
        grid_ref[other, :, 0:part] -= found[:, square : square + part]
        crossed = found[:, part - square : 2 * part - square]
        if panel == 0:
            grid_ref[other, :, cross : cross + part] = -crossed
        else:
            grid_ref[other, :, cross : cross + part] -= crossed

    add(part, right_plane, part, part)
    if left_plane >= 0:
        add(0, left_plane, 0, 2 * part)


def update_partners(grid_ref, plane, distance, part, order, has_left):
    left, right = plane - distance, plane + distance
    both = grid_ref[plane, :, part : 3 * part]
    if part > order:
        spare = jnp.zeros((part - order, 2 * part), jnp.float32)
        both = jnp.concatenate([both, spare], axis=0)
    turned = [piece.astype(jnp.bfloat16) for piece in pieces_of(both.T)]
    held = [piece.astype(jnp.bfloat16) for piece in pieces_of(both)]
    held = jnp.concatenate([held[right] for _, right in PRODUCTS], axis=0)

    def product(rows):
        columns = jnp.concatenate([turned[left][rows] for left, _ in PRODUCTS], axis=1)
        return single_dot(columns, held)

    from_right = product(slice(part, part + order))
    grid_ref[right, :, 0:part] -= from_right[:, part : 2 * part]
    grid_ref[right, :, part : 2 * part] = -from_right[:, 0:part]

    def to_left():
        from_left = product(slice(0, order))
        grid_ref[left, :, 0:part] -= from_left[:, 0:part]
        grid_ref[left, :, 2 * part : 3 * part] = -from_left[:, part : 2 * part]

    if isinstance(has_left, bool):
        if has_left:
            to_left()
    else:
        pl.when(has_left)(to_left)


def unpack_tile(packed, modes):
    half = 3 * modes // 2
    upper = packed[:, 0 : 3 * modes]
    lower = jnp.concatenate(
        [packed[0:ROWS, 3 * modes : 3 * modes + half], packed[ROWS:, 3 * modes : 3 * modes + half]],
        axis=1,
    )
    return jnp.concatenate([upper, lower], axis=0)


def pack_tile(tile):
    modes = tile.shape[0]
    half = 3 * modes // 2
    top = modes - ROWS
    upper = tile[0:top]
    lower = jnp.concatenate([tile[top:, 0:half], tile[top:, half:]], axis=0)
    spare = jnp.zeros((top, LANES - 3 * modes - half), jnp.float32)
    return jnp.concatenate([upper, lower, spare], axis=1)


def factor_kernel(tiles_ref, after_ref, diag_ref, left_ref, right_ref, grid_ref, turned_ref):
    subs, layers, _, _ = tiles_ref.shape
    modes, order = diag_ref.shape
    part = grid_ref.shape[2] // 3
    unrolled = layers <= UNROLLED_LAYERS
    del after_ref
    lane = lax.broadcasted_iota(jnp.int32, (modes, part), 1)
    inside = [(lane >= j * modes) & (lane < (j + 1) * modes) for j in range(layers)]

    def place_tiles(s, before):
        tiles = [unpack_tile(tiles_ref[s, j], modes) for j in range(layers)]
        stacked = tiles
        if part > order:
            stacked = tiles + [jnp.zeros((part - order, tiles[0].shape[1]), jnp.float32)]
        turned = jnp.concatenate(stacked, axis=0).T
        for j, tile in enumerate(tiles):
            rows = slice(j * modes, (j + 1) * modes)
            own = jnp.where(inside[j], turned[0:modes], 0.0)
            if j + 1 < layers:
                own = jnp.where(inside[j + 1], turned[modes : 2 * modes], own)
            grid_ref[s, rows, 0:part] = own
            spare = jnp.zeros((modes, part - 3 * modes), jnp.float32)
            wide = jnp.concatenate([tile, spare], axis=1)
            shift = (j - 2) * modes % part
            down = pltpu.roll(wide, shift, 1) if shift else wide
            grid_ref[s, rows, part : 2 * part] = jnp.where(inside[j], down, 0.0)
            down = jnp.where(inside[j], turned[2 * modes : 3 * modes], 0.0)
            grid_ref[before, rows, 2 * part : 3 * part] = down

    place_tiles(0, subs - 1)
    if unrolled:
        for s in range(1, subs):
            place_tiles(s, s - 1)
    else:

        def place_one(s, carry):
            place_tiles(s, s - 1)
            return carry

        lax.fori_loop(1, subs, place_one, 0)

    distance = 1
    while distance < subs:
        if unrolled:
            planes = list(range(distance - 1, subs, 2 * distance))
            share = distance if len(planes) <= PLANES_AT_ONCE else 0
            eliminate_planes(
                grid_ref, planes, modes, order, part, 3 * part, distance == 1, share
            )
            for plane in planes if not share else []:
                update_partners(grid_ref, plane, distance, part, order, plane >= distance)
        else:

            def one_plane(index, carry, distance=distance):
                plane = distance - 1 + 2 * distance * index
                eliminate_planes(grid_ref, [plane], modes, order, part, 3 * part)
                update_partners(grid_ref, plane, distance, part, order, index > 0)
                return carry

            lax.fori_loop(0, subs // (2 * distance), one_plane, 0)
        distance *= 2
    eliminate_planes(grid_ref, [subs - 1], modes, order, part, part)

    sub_here, lay_here = lax.axis_index("sub"), lax.axis_index("layer")
    strip = pl.ds(pl.multiple_of(lay_here * modes, ROWS), modes)
    for k, out_ref in enumerate((diag_ref, left_ref, right_ref)):
        turned_ref[k] = grid_ref[sub_here, :, k * part : (k + 1) * part].T
        found = turned_ref[k, strip, :]
        out_ref[...] = found if k == 0 else jnp.where(sub_here < subs - 1, found, 0.0)


VMEM_BLOCK = pl.BlockSpec(memory_space=pltpu.VMEM)
HBM_BLOCK = pl.BlockSpec(memory_space=pltpu.HBM)
SPARE_BYTES = 4 * 1024 * 1024


def kernel_params(shapes):
    held = sum(4 * math.prod(shape) for shape in shapes)
    return pltpu.CompilerParams(vmem_limit_bytes=min(2 * held + SPARE_BYTES, 60 * 1024 * 1024))


def factor_planes(plane_tiles, modes, after):
    subs, layers, _, _ = plane_tiles.shape
    order = layers * modes
    part = -(-order // LANES) * LANES
    strip = jax.ShapeDtypeStruct((modes, order), jnp.float32)
    scratch = ((subs, order, 3 * part), (3, part, order))
    return pl.pallas_call(
        factor_kernel,
        out_shape=(strip, strip, strip),
        in_specs=[VMEM_BLOCK, VMEM_BLOCK],
        out_specs=(VMEM_BLOCK, VMEM_BLOCK, VMEM_BLOCK),
        scratch_shapes=[pltpu.VMEM(shape, jnp.float32) for shape in scratch],
        compiler_params=kernel_params((plane_tiles.shape,) + scratch),
        name="factor_planes",
    )(plane_tiles, after)


def across_dot(left, right):
    return lax.dot_general(
        left,
        right,
        (((1,), (1,)), ((), ())),
        precision=HIGHEST,
        preferred_element_type=jnp.float32,
    )


def pick_lists(vectors_ref, lists_ref, chosen, strip):
    lists = []
    for k in chosen:
        rows = jnp.broadcast_to(lists_ref[k : k + 1, :], (ROWS, LANES))
        lists.append((rows // LANES, rows % LANES))
    found = [jnp.zeros((ROWS, LANES), jnp.float32) for _ in lists]
    for c in range(vectors_ref.shape[1] // LANES):
        tile = vectors_ref[strip, c * LANES : (c + 1) * LANES]
        for i, (tile_of, lane_of) in enumerate(lists):
            moved = jnp.take_along_axis(tile, lane_of, axis=1, mode="promise_in_bounds")
            found[i] = jnp.where(tile_of == c, moved, found[i])
    return found


def pick_kernel(
    vectors_in, lists_in, face_in, vectors_ref, lists_ref, face_ref, sub_ref, layer_ref, sems
):
    modes = vectors_ref.shape[0]
    strips = [slice(first, first + ROWS) for first in range(0, modes, ROWS)]
    pairs = [(lists_in, lists_ref)]
    pairs += [(vectors_in.at[pl.ds(s.start, ROWS)], vectors_ref.at[pl.ds(s.start, ROWS)]) for s in strips]
    pairs += [(face_in, face_ref)]
    copies = [pltpu.make_async_copy(a, b, sems.at[i]) for i, (a, b) in enumerate(pairs)]
    for copy in copies:
        copy.start()
    copies[0].wait()
    copies[-1].wait()
    for k, send_ref in ((0, sub_ref), (2, layer_ref)):
        send_ref[modes:] = jnp.broadcast_to(face_ref[k // 2 : k // 2 + 1, :], (ROWS, LANES))
    for copy, strip in zip(copies[1:], strips):
        copy.wait()
        sub_ref[strip], layer_ref[strip] = pick_lists(vectors_ref, lists_ref, (0, 2), strip)


def own_kernel(
    mass_in, inner_in, vectors_ref, lists_ref, face_ref, sub_ref, layer_ref,
    base_ref, own_ref, before_sub_ref, before_layer_ref, mass_ref, inner_ref, sems, *, subs, layers
):
    copies = [
        pltpu.make_async_copy(mass_in, mass_ref, sems.at[0]),
        pltpu.make_async_copy(inner_in, inner_ref, sems.at[1]),
    ]
    for copy in copies:
        copy.start()
    vectors = vectors_ref[...]
    modes, row_count = vectors.shape
    for first in range(0, modes, ROWS):
        strip = slice(first, first + ROWS)
        before_sub_ref[strip], before_layer_ref[strip] = pick_lists(
            vectors_ref, lists_ref, (1, 3), strip
        )
    for copy in copies:
        copy.wait()
    places = lax.broadcasted_iota(jnp.int32, (1, row_count), 1)
    base = mass_ref[...] * vectors
    for k, t in enumerate(STRIDES):
        edge_weight = jnp.where(places < row_count - t, inner_ref[k], 0.0)
        fluxes = edge_weight * (vectors - pltpu.roll(vectors, row_count - t, 1))
        base = base + fluxes - pltpu.roll(fluxes, t, 1)
    base_ref[...] = base
    own = across_dot(vectors, base)
    for k, axis, ends, send_ref in ((0, "sub", subs - 1, sub_ref), (1, "layer", layers - 1, layer_ref)):
        springs = jnp.where(lax.axis_index(axis) < ends, face_ref[k : k + 1, :], 0.0)
        picked = send_ref[0:modes]
        own = own + across_dot(picked, springs * picked)
    own_ref[...] = own


def tile_kernel(
    own_ref, mine_sub_ref, mine_layer_ref, sub_ref, layer_ref, copies_ref, layer_send_ref, *, row_count
):
    modes = own_ref.shape[0]
    inverse = 1.0 / row_count
    pairs = []
    for mine_ref, theirs_ref in ((mine_sub_ref, sub_ref), (mine_layer_ref, layer_ref)):
        mine = mine_ref[...]
        sprung = theirs_ref[modes : modes + 1] * mine
        stacked = jnp.concatenate([mine, theirs_ref[0:modes]], axis=0)
        pairs.append(across_dot(sprung, stacked))
    down, side = pairs
    diag_tile = (own_ref[...] + down[:, 0:modes] + side[:, 0:modes]) * inverse
    side_tile = -side[:, modes:] * inverse
    down_tile = -down[:, modes:] * inverse
    packed = pack_tile(jnp.concatenate([diag_tile, side_tile, down_tile], axis=1))
    for s in range(copies_ref.shape[0]):
        copies_ref[s] = packed
    layer_send_ref[...] = mine_layer_ref[...]


def scatter_kernel(
    base_ref, lists_ref, face_ref, up_sub_ref, down_sub_ref, up_layer_ref, down_layer_ref, before_sub_ref, after_sub_ref,
    before_layer_ref, after_layer_ref, applied_ref, token_ref, *, subs, layers
):
    modes, row_count = base_ref.shape
    width = 2 * LANES
    springs = [
        jnp.where(lax.axis_index("sub") < subs - 1, face_ref[0:1, :], 0.0),
        before_sub_ref[modes : modes + 1, :],
        jnp.where(lax.axis_index("layer") < layers - 1, face_ref[1:2, :], 0.0),
        before_layer_ref[modes : modes + 1, :],
    ]
    partners = [
        after_sub_ref[...],
        before_sub_ref[0:modes, :],
        after_layer_ref[...],
        before_layer_ref[0:modes, :],
    ]
    picked = [up_sub_ref[0:modes], down_sub_ref[...], up_layer_ref[0:modes], down_layer_ref[...]]
    pulls = jnp.concatenate([springs[k] * (picked[k] - partners[k]) for k in range(4)], axis=1)
    rows = jnp.concatenate([lists_ref[k : k + 1, :] for k in range(4)], axis=1)
    block_of, lane_of = rows // width, rows % width
    lanes = lax.broadcasted_iota(jnp.int32, (width, rows.shape[1]), 0)
    onehot = jnp.where(lanes == lane_of, 1.0, 0.0).astype(jnp.bfloat16)
    total = None
    rest = pulls
    for _ in range(3):
        piece = rest.astype(jnp.bfloat16).astype(jnp.float32)
        rest = rest - piece
        spread = jnp.concatenate(
            [jnp.where(block_of == h, piece, 0.0) for h in range(row_count // width)], axis=0
        ).astype(jnp.bfloat16)
        moved = lax.dot_general(
            spread, onehot, (((1,), (1,)), ((), ())), preferred_element_type=jnp.float32
        )
        total = moved if total is None else total + moved
    for h in range(row_count // width):
        lanes = slice(h * width, (h + 1) * width)
        applied_ref[:, lanes] = base_ref[:, lanes] + total[h * modes : (h + 1) * modes]
    token_ref[...] = jnp.zeros_like(token_ref)


def local_call(body, outputs, operands, name):
    shapes = tuple(jax.ShapeDtypeStruct(shape, jnp.float32) for shape in outputs)
    return pl.pallas_call(
        body,
        out_shape=shapes,
        in_specs=[VMEM_BLOCK] * len(operands),
        out_specs=tuple(VMEM_BLOCK for _ in shapes),
        compiler_params=kernel_params([x.shape for x in operands] + list(outputs)),
        name=name,
    )(*operands)


def per_device(eigen_vectors, row_mass, inner_weight, face_weight, margin_rows):
    vectors = eigen_vectors[0, 0]
    row_lists = margin_rows[0, 0]
    face_springs = face_weight[0, 0]
    modes, row_count = vectors.shape
    width = row_lists.shape[-1]
    subs = lax.axis_size("sub")
    layers = lax.axis_size("layer")
    up_sub = [(i, i + 1) for i in range(subs - 1)]
    up_layer = [(i, i + 1) for i in range(layers - 1)]
    down_sub = [(i + 1, i) for i in range(subs - 1)]
    down_layer = [(i + 1, i) for i in range(layers - 1)]
    def pinned(*arrays):
        return [pltpu.with_memory_space_constraint(x, pltpu.HBM) for x in arrays]

    def shaped(*shapes):
        return tuple(jax.ShapeDtypeStruct(shape, jnp.float32) for shape in shapes)

    taken = (vectors, row_lists, face_springs)
    held = tuple(jax.ShapeDtypeStruct(x.shape, x.dtype) for x in taken)
    held += shaped((modes + ROWS, width), (modes + ROWS, width))
    vectors, row_lists, face_springs, sub_send, layer_send = pl.pallas_call(
        pick_kernel,
        out_shape=held,
        in_specs=[HBM_BLOCK] * len(taken),
        out_specs=(VMEM_BLOCK,) * len(held),
        scratch_shapes=[pltpu.SemaphoreType.DMA((2 + modes // ROWS,))],
        compiler_params=kernel_params([x.shape for x in held]),
        name="pick_rows",
    )(*pinned(*taken))
    before_sub = lax.ppermute(sub_send, "sub", up_sub)
    before_layer = lax.ppermute(layer_send, "layer", up_layer)
    masses, interior = row_mass[0], inner_weight[0].reshape(-1, 1, row_count)
    made = shaped((modes, row_count), (modes, modes), (modes, width), (modes, width))
    base, own, picked_sub, picked_layer = pl.pallas_call(
        functools.partial(own_kernel, subs=subs, layers=layers),
        out_shape=made,
        in_specs=[HBM_BLOCK] * 2 + [VMEM_BLOCK] * len(held),
        out_specs=(VMEM_BLOCK,) * len(made),
        scratch_shapes=[
            pltpu.VMEM(masses.shape, jnp.float32),
            pltpu.VMEM(interior.shape, jnp.float32),
            pltpu.SemaphoreType.DMA((2,)),
        ],
        compiler_params=kernel_params([x.shape for x in held + made]),
        name="own_rows",
    )(*pinned(masses, interior), vectors, row_lists, face_springs, sub_send, layer_send)
    after_sub = lax.ppermute(picked_sub, "sub", down_sub)
    copies, after_send = local_call(
        functools.partial(tile_kernel, row_count=row_count),
        [(subs * layers, modes - ROWS, LANES), (modes, width)],
        (own, picked_sub, picked_layer, before_sub, before_layer),
        "coarse_tiles",
    )
    tiles = lax.all_to_all(copies, ("sub", "layer"), split_axis=0, concat_axis=0, tiled=True)
    after_layer = lax.ppermute(after_send, "layer", down_layer)
    applied, token = local_call(
        functools.partial(scatter_kernel, subs=subs, layers=layers),
        [(modes, row_count), (ROWS, LANES)],
        (base, row_lists, face_springs, sub_send, picked_sub, layer_send, picked_layer)
        + (before_sub, after_sub, before_layer, after_layer),
        "spread_rows",
    )
    diag_strip, left_strip, right_strip = factor_planes(
        tiles.reshape(subs, layers, *tiles.shape[1:]), modes, token
    )
    return (applied[None, None], diag_strip[None], left_strip[None], right_strip[None])


def solution(mesh):
    in_specs = (
        P("sub", "layer", None, None),
        P("sub", "layer", None),
        P("sub", "layer", None, None),
        P("sub", "layer", None, None),
        P("sub", "layer", None, None),
    )
    out_specs = (
        P("sub", "layer", None, None),
        P("sub", "layer", None),
        P("sub", "layer", None),
        P("sub", "layer", None),
    )
    return jax.shard_map(
        per_device, mesh=mesh, in_specs=in_specs, out_specs=out_specs, check_vma=False
    )
```

```python
import functools
import math
import jax
import jax.numpy as jnp
from jax import lax
from jax.experimental import pallas as pl
from jax.experimental.pallas import tpu as pltpu
from jax.sharding import PartitionSpec as P

STRIDES = (1, 3, 27)
HIGHEST = lax.Precision.HIGHEST
LANES = 128
ROWS = 8
UNROLLED_LAYERS = 4
PLANES_AT_ONCE = 2
NARROW_DEPTH = LANES + LANES // 4


def turned_dot(left, right):
    return lax.dot_general(
        left,
        right,
        (((0,), (0,)), ((), ())),
        precision=HIGHEST,
        preferred_element_type=jnp.float32,
    )


PRODUCTS = ((0, 0), (1, 0), (2, 0), (0, 1), (1, 1), (0, 2))


def pieces_of(values):
    first = values.astype(jnp.bfloat16).astype(jnp.float32)
    rest = values - first
    second = rest.astype(jnp.bfloat16).astype(jnp.float32)
    return first, second, rest - second


def single_dot(left, right):
    return lax.dot_general(
        left, right, (((1,), (0,)), ((), ())), preferred_element_type=jnp.float32
    )


def narrow_columns(turned, modes):
    height = turned.shape[0]
    lane = lax.broadcasted_iota(jnp.int32, (height, LANES), 1)
    wide = jnp.concatenate([turned, jnp.zeros((height, LANES - 3 * modes), jnp.float32)], axis=1)
    again = pltpu.roll(wide, 3 * modes, 1)
    left = jnp.where(lane < 3 * modes, wide, jnp.where(lane < 5 * modes, again, 0.0))
    last = jnp.where(lane < modes, wide, 0.0)
    return jnp.concatenate([left, last], axis=1)[:, 0:NARROW_DEPTH].astype(jnp.bfloat16)


def narrow_rows(pieces):
    first, second, third = pieces
    modes, width = first.shape
    gap = jnp.zeros((LANES - 5 * modes, width), jnp.float32)
    tail = jnp.zeros((NARROW_DEPTH - LANES - modes, width), jnp.float32)
    rows = jnp.concatenate([first] * 3 + [second] * 2 + [gap, third, tail], axis=0)
    return rows.astype(jnp.bfloat16)


def plain_dot(left, right):
    return lax.dot_general(
        left,
        right,
        (((1,), (0,)), ((), ())),
        precision=HIGHEST,
        preferred_element_type=jnp.float32,
    )


def spread_row(strip, k):
    return jnp.broadcast_to(strip[k : k + 1, :], strip.shape)


def eliminate_pair(block, columns, pivots, iota, q, k):
    start = q * ROWS
    first, second = columns[start + k], columns[start + k + 1]
    corner, joint = spread_row(first[0], k), spread_row(first[0], k + 1)
    other_corner = spread_row(second[0], k + 1)
    minor = corner * other_corner - joint * joint
    inverse = pl.reciprocal(corner, approx=True)
    other_inverse = corner * pl.reciprocal(minor, approx=True)
    below = [column * inverse for column in first]
    second = [column - below[r] * joint for r, column in enumerate(second)]
    other_below = [column * other_inverse for column in second]
    below[0] = jnp.where(iota > k, below[0], 0.0)
    other_below[0] = jnp.where(iota > k + 1, other_below[0], 0.0)
    for j in range(start + k + 2, len(columns)):
        strip = j // ROWS - q
        head = spread_row(first[strip], j % ROWS)
        other_head = spread_row(second[strip], j % ROWS)
        columns[j] = [
            column - below[strip + r] * head - other_below[strip + r] * other_head
            for r, column in enumerate(columns[j])
        ]
    for t in range(len(block[q])):
        row = spread_row(block[q][t], k)
        for r, lower in enumerate(below):
            block[q + r][t] = block[q + r][t] - lower * row
        row = spread_row(block[q][t], k + 1)
        for r, lower in enumerate(other_below):
            block[q + r][t] = block[q + r][t] - lower * row
    return jnp.where(iota == k, corner, jnp.where(iota == k + 1, minor * inverse, pivots))


def factor_rows(blocks, tiles_per_part, first_row, turned):
    strip_count = len(blocks[0])
    iota = lax.broadcasted_iota(jnp.int32, (ROWS, LANES), 0)
    lane = lax.broadcasted_iota(jnp.int32, (ROWS, LANES), 1)
    blocks = [[list(strip) for strip in block] for block in blocks]
    at_once = len(blocks) <= PLANES_AT_ONCE
    held = [[] for _ in blocks]
    for q in range(strip_count):
        start = q * ROWS
        if q == 0 or not at_once:
            for b, block in enumerate(blocks):
                source = turned(b, block, q)
                for j in range(start, strip_count * ROWS if at_once else start + ROWS):
                    held[b].append(
                        [
                            jnp.broadcast_to(strip[:, j : j + 1], (ROWS, LANES))
                            for strip in source[j // ROWS - q :]
                        ]
                    )
        pivots = [jnp.zeros((ROWS, LANES), jnp.float32) for _ in blocks]
        for k in range(0, ROWS, 2):
            for b, block in enumerate(blocks):
                pivots[b] = eliminate_pair(block, held[b], pivots[b], iota, q, k)
        for b, block in enumerate(blocks):
            scale = lax.rsqrt(pivots[b])
            for t in range(len(block[q])):
                strip = block[q][t] * scale
                if t < tiles_per_part:
                    keep = lane + t * LANES >= iota + (first_row + start)
                    strip = jnp.where(keep, strip, 0.0)
                block[q][t] = strip
    return blocks


def eliminate_panel(grid_ref, planes, modes, order, part, lanes_used, panel, banded):
    per_part = part // LANES
    first_row = panel * modes
    static = isinstance(panel, int)
    if static:
        rows = pl.ds(first_row, modes)
    else:
        rows = pl.ds(pl.multiple_of(first_row, ROWS), modes)
    blocks = []
    for plane in planes:
        panel_rows = grid_ref[plane, rows, 0:lanes_used]
        blocks.append(
            [
                [
                    panel_rows[q * ROWS : (q + 1) * ROWS, t * LANES : (t + 1) * LANES]
                    for t in range(lanes_used // LANES)
                ]
                for q in range(modes // ROWS)
            ]
        )

    def turned(b, block, q):
        found = []
        for strip in block[q:]:
            if static and first_row // LANES == (first_row + modes - 1) // LANES:
                tile = strip[first_row // LANES]
                offset = first_row % LANES
                found.append(tile if offset == 0 else tile[:, offset : offset + modes])
            else:
                wide = jnp.concatenate(strip[:per_part], axis=1)
                found.append(pltpu.roll(wide, lax.rem(part - first_row, part), 1)[:, :LANES])
        return found

    blocks = factor_rows(blocks, per_part, first_row, turned)
    for plane, block in zip(planes, blocks):
        panel_rows = jnp.concatenate([jnp.concatenate(strip, axis=1) for strip in block], axis=0)
        grid_ref[plane, rows, 0:lanes_used] = panel_rows
        if static:
            below = (panel + 1) * modes
            end = min(below + modes, order) if banded else order
            pieces = pieces_of(panel_rows)
            right = narrow_rows(pieces)
            stacked = jnp.concatenate(pieces, axis=0)
            if below < order:
                columns = narrow_columns(stacked[:, 0:part].T[below:end], modes)
                grid_ref[plane, below:end, 0:lanes_used] -= single_dot(columns, right)
        else:
            lane = lax.broadcasted_iota(jnp.int32, (modes, part), 1)
            columns = jnp.where(lane >= first_row + modes, panel_rows[:, 0:part], 0.0)
            update = turned_dot(columns, panel_rows)[0:order]
            grid_ref[plane, :, 0:lanes_used] -= update


def eliminate_planes(grid_ref, planes, modes, order, part, lanes_used, banded=False):
    layers = order // modes
    if layers <= UNROLLED_LAYERS:
        for panel in range(layers):
            eliminate_panel(grid_ref, planes, modes, order, part, lanes_used, panel, banded)
    else:

        def one_panel(panel, carry):
            eliminate_panel(grid_ref, planes, modes, order, part, lanes_used, panel, banded)
            return carry

        lax.fori_loop(0, layers, one_panel, 0)


def update_partners(grid_ref, plane, distance, part, order, has_left):
    left, right = plane - distance, plane + distance
    both = grid_ref[plane, :, part : 3 * part]
    if part > order:
        spare = jnp.zeros((part - order, 2 * part), jnp.float32)
        both = jnp.concatenate([both, spare], axis=0)
    turned = [piece.astype(jnp.bfloat16) for piece in pieces_of(both.T)]
    held = [piece.astype(jnp.bfloat16) for piece in pieces_of(both)]
    held = jnp.concatenate([held[right] for _, right in PRODUCTS], axis=0)

    def product(rows):
        columns = jnp.concatenate([turned[left][rows] for left, _ in PRODUCTS], axis=1)
        return single_dot(columns, held)

    from_right = product(slice(part, part + order))
    grid_ref[right, :, 0:part] -= from_right[:, part : 2 * part]
    grid_ref[right, :, part : 2 * part] = -from_right[:, 0:part]

    def to_left():
        from_left = product(slice(0, order))
        grid_ref[left, :, 0:part] -= from_left[:, 0:part]
        grid_ref[left, :, 2 * part : 3 * part] = -from_left[:, part : 2 * part]

    if isinstance(has_left, bool):
        if has_left:
            to_left()
    else:
        pl.when(has_left)(to_left)


def unpack_tile(packed, modes):
    half = 3 * modes // 2
    upper = packed[:, 0 : 3 * modes]
    lower = jnp.concatenate(
        [packed[0:ROWS, 3 * modes : 3 * modes + half], packed[ROWS:, 3 * modes : 3 * modes + half]],
        axis=1,
    )
    return jnp.concatenate([upper, lower], axis=0)


def pack_tile(tile):
    modes = tile.shape[0]
    half = 3 * modes // 2
    top = modes - ROWS
    upper = tile[0:top]
    lower = jnp.concatenate([tile[top:, 0:half], tile[top:, half:]], axis=0)
    spare = jnp.zeros((top, LANES - 3 * modes - half), jnp.float32)
    return jnp.concatenate([upper, lower, spare], axis=1)


def factor_kernel(tiles_ref, after_ref, diag_ref, left_ref, right_ref, grid_ref, turned_ref):
    subs, layers, _, _ = tiles_ref.shape
    modes, order = diag_ref.shape
    part = grid_ref.shape[2] // 3
    unrolled = layers <= UNROLLED_LAYERS
    del after_ref
    lane = lax.broadcasted_iota(jnp.int32, (modes, part), 1)
    inside = [(lane >= j * modes) & (lane < (j + 1) * modes) for j in range(layers)]

    def place_tiles(s, before):
        tiles = [unpack_tile(tiles_ref[s, j], modes) for j in range(layers)]
        stacked = tiles
        if part > order:
            stacked = tiles + [jnp.zeros((part - order, tiles[0].shape[1]), jnp.float32)]
        turned = jnp.concatenate(stacked, axis=0).T
        for j, tile in enumerate(tiles):
            rows = slice(j * modes, (j + 1) * modes)
            own = jnp.where(inside[j], turned[0:modes], 0.0)
            if j + 1 < layers:
                own = jnp.where(inside[j + 1], turned[modes : 2 * modes], own)
            grid_ref[s, rows, 0:part] = own
            spare = jnp.zeros((modes, part - 3 * modes), jnp.float32)
            wide = jnp.concatenate([tile, spare], axis=1)
            shift = (j - 2) * modes % part
            down = pltpu.roll(wide, shift, 1) if shift else wide
            grid_ref[s, rows, part : 2 * part] = jnp.where(inside[j], down, 0.0)
            down = jnp.where(inside[j], turned[2 * modes : 3 * modes], 0.0)
            grid_ref[before, rows, 2 * part : 3 * part] = down

    place_tiles(0, subs - 1)
    if unrolled:
        for s in range(1, subs):
            place_tiles(s, s - 1)
    else:

        def place_one(s, carry):
            place_tiles(s, s - 1)
            return carry

        lax.fori_loop(1, subs, place_one, 0)

    distance = 1
    while distance < subs:
        if unrolled:
            planes = list(range(distance - 1, subs, 2 * distance))
            eliminate_planes(grid_ref, planes, modes, order, part, 3 * part, distance == 1)
            for plane in planes:
                update_partners(grid_ref, plane, distance, part, order, plane >= distance)
        else:

            def one_plane(index, carry, distance=distance):
                plane = distance - 1 + 2 * distance * index
                eliminate_planes(grid_ref, [plane], modes, order, part, 3 * part)
                update_partners(grid_ref, plane, distance, part, order, index > 0)
                return carry

            lax.fori_loop(0, subs // (2 * distance), one_plane, 0)
        distance *= 2
    eliminate_planes(grid_ref, [subs - 1], modes, order, part, part)

    sub_here, lay_here = lax.axis_index("sub"), lax.axis_index("layer")
    strip = pl.ds(pl.multiple_of(lay_here * modes, ROWS), modes)
    for k, out_ref in enumerate((diag_ref, left_ref, right_ref)):
        turned_ref[k] = grid_ref[sub_here, :, k * part : (k + 1) * part].T
        found = turned_ref[k, strip, :]
        out_ref[...] = found if k == 0 else jnp.where(sub_here < subs - 1, found, 0.0)


VMEM_BLOCK = pl.BlockSpec(memory_space=pltpu.VMEM)
HBM_BLOCK = pl.BlockSpec(memory_space=pltpu.HBM)
SPARE_BYTES = 4 * 1024 * 1024


def kernel_params(shapes):
    held = sum(4 * math.prod(shape) for shape in shapes)
    return pltpu.CompilerParams(vmem_limit_bytes=min(2 * held + SPARE_BYTES, 60 * 1024 * 1024))


def factor_planes(plane_tiles, modes, after):
    subs, layers, _, _ = plane_tiles.shape
    order = layers * modes
    part = -(-order // LANES) * LANES
    strip = jax.ShapeDtypeStruct((modes, order), jnp.float32)
    scratch = ((subs, order, 3 * part), (3, part, order))
    return pl.pallas_call(
        factor_kernel,
        out_shape=(strip, strip, strip),
        in_specs=[VMEM_BLOCK, VMEM_BLOCK],
        out_specs=(VMEM_BLOCK, VMEM_BLOCK, VMEM_BLOCK),
        scratch_shapes=[pltpu.VMEM(shape, jnp.float32) for shape in scratch],
        compiler_params=kernel_params((plane_tiles.shape,) + scratch),
        name="factor_planes",
    )(plane_tiles, after)


def across_dot(left, right):
    rows, columns = left.shape[0], right.shape[0]

    def stacked(values):
        short = -3 * values.shape[0] % (2 * ROWS)
        spare = [jnp.zeros((short, values.shape[1]), jnp.float32)] if short else []
        return jnp.concatenate(list(pieces_of(values)) + spare, axis=0).astype(jnp.bfloat16)

    found = lax.dot_general(
        stacked(left),
        stacked(right),
        (((1,), (1,)), ((), ())),
        preferred_element_type=jnp.float32,
    )
    total = None
    for b in (2, 1, 0):
        column = found[:, b * columns : (b + 1) * columns]
        for a in (2, 1, 0):
            if (a, b) in PRODUCTS:
                block = column[a * rows : (a + 1) * rows]
                total = block if total is None else total + block
    return total


def pick_lists(vectors_ref, lists_ref, chosen, strip):
    lists = []
    for k in chosen:
        rows = jnp.broadcast_to(lists_ref[k : k + 1, :], (ROWS, LANES))
        lists.append((rows // LANES, rows % LANES))
    found = [jnp.zeros((ROWS, LANES), jnp.float32) for _ in lists]
    for c in range(vectors_ref.shape[1] // LANES):
        tile = vectors_ref[strip, c * LANES : (c + 1) * LANES]
        for i, (tile_of, lane_of) in enumerate(lists):
            moved = jnp.take_along_axis(tile, lane_of, axis=1, mode="promise_in_bounds")
            found[i] = jnp.where(tile_of == c, moved, found[i])
    return found


def pick_kernel(
    vectors_in, lists_in, face_in, vectors_ref, lists_ref, face_ref, layer_ref, sub_ref, sems
):
    modes = vectors_ref.shape[0]
    strips = [slice(first, first + ROWS) for first in range(0, modes, ROWS)]
    pairs = [(lists_in, lists_ref)]
    pairs += [(vectors_in.at[pl.ds(s.start, ROWS)], vectors_ref.at[pl.ds(s.start, ROWS)]) for s in strips]
    pairs += [(face_in, face_ref)]
    copies = [pltpu.make_async_copy(a, b, sems.at[i]) for i, (a, b) in enumerate(pairs)]
    for copy in copies:
        copy.start()
    copies[0].wait()
    copies[-1].wait()
    for k, send_ref in ((0, sub_ref), (2, layer_ref)):
        send_ref[modes:] = jnp.broadcast_to(face_ref[k // 2 : k // 2 + 1, :], (ROWS, LANES))
    for copy, strip in zip(copies[1:], strips):
        copy.wait()
        sub_ref[strip], layer_ref[strip] = pick_lists(vectors_ref, lists_ref, (0, 2), strip)


def own_kernel(
    mass_in, inner_in, vectors_ref, lists_ref, face_ref, sub_ref, layer_ref,
    base_ref, own_ref, before_sub_ref, before_layer_ref, mass_ref, inner_ref, sems, *, subs, layers
):
    copies = [
        pltpu.make_async_copy(mass_in, mass_ref, sems.at[0]),
        pltpu.make_async_copy(inner_in, inner_ref, sems.at[1]),
    ]
    for copy in copies:
        copy.start()
    vectors = vectors_ref[...]
    modes, row_count = vectors.shape
    for first in range(0, modes, ROWS):
        strip = slice(first, first + ROWS)
        before_sub_ref[strip], before_layer_ref[strip] = pick_lists(
            vectors_ref, lists_ref, (1, 3), strip
        )
    for copy in copies:
        copy.wait()
    places = lax.broadcasted_iota(jnp.int32, (1, row_count), 1)
    base = mass_ref[...] * vectors
    for k, t in enumerate(STRIDES):
        edge_weight = jnp.where(places < row_count - t, inner_ref[k], 0.0)
        fluxes = edge_weight * (vectors - pltpu.roll(vectors, row_count - t, 1))
        base = base + fluxes - pltpu.roll(fluxes, t, 1)
    base_ref[...] = base
    own = across_dot(vectors, base)
    for k, axis, ends, send_ref in ((0, "sub", subs - 1, sub_ref), (1, "layer", layers - 1, layer_ref)):
        springs = jnp.where(lax.axis_index(axis) < ends, face_ref[k : k + 1, :], 0.0)
        picked = send_ref[0:modes]
        own = own + across_dot(picked, springs * picked)
    own_ref[...] = own


def tile_kernel(
    own_ref, mine_layer_ref, mine_sub_ref, layer_ref, sub_ref, copies_ref, layer_send_ref, *, row_count
):
    modes = own_ref.shape[0]
    inverse = 1.0 / row_count
    pairs = []
    for mine_ref, theirs_ref in ((mine_sub_ref, sub_ref), (mine_layer_ref, layer_ref)):
        mine = mine_ref[...]
        sprung = theirs_ref[modes : modes + 1] * mine
        stacked = jnp.concatenate([mine, theirs_ref[0:modes]], axis=0)
        pairs.append(across_dot(sprung, stacked))
    down, side = pairs
    diag_tile = (own_ref[...] + down[:, 0:modes] + side[:, 0:modes]) * inverse
    side_tile = -side[:, modes:] * inverse
    down_tile = -down[:, modes:] * inverse
    packed = pack_tile(jnp.concatenate([diag_tile, side_tile, down_tile], axis=1))
    for s in range(copies_ref.shape[0]):
        copies_ref[s] = packed
    layer_send_ref[...] = mine_layer_ref[...]


def scatter_kernel(
    base_ref, lists_ref, face_ref, up_sub_ref, down_sub_ref, up_layer_ref, down_layer_ref, before_sub_ref, after_sub_ref,
    before_layer_ref, after_layer_ref, applied_ref, token_ref, *, subs, layers
):
    modes, row_count = base_ref.shape
    width = 2 * LANES
    springs = [
        jnp.where(lax.axis_index("sub") < subs - 1, face_ref[0:1, :], 0.0),
        before_sub_ref[modes : modes + 1, :],
        jnp.where(lax.axis_index("layer") < layers - 1, face_ref[1:2, :], 0.0),
        before_layer_ref[modes : modes + 1, :],
    ]
    partners = [
        after_sub_ref[...],
        before_sub_ref[0:modes, :],
        after_layer_ref[...],
        before_layer_ref[0:modes, :],
    ]
    picked = [up_sub_ref[0:modes], down_sub_ref[...], up_layer_ref[0:modes], down_layer_ref[...]]
    pulls = jnp.concatenate([springs[k] * (picked[k] - partners[k]) for k in range(4)], axis=1)
    rows = jnp.concatenate([lists_ref[k : k + 1, :] for k in range(4)], axis=1)
    block_of, lane_of = rows // width, rows % width
    lanes = lax.broadcasted_iota(jnp.int32, (width, rows.shape[1]), 0)
    onehot = jnp.where(lanes == lane_of, 1.0, 0.0).astype(jnp.bfloat16)
    total = None
    rest = pulls
    for _ in range(3):
        piece = rest.astype(jnp.bfloat16).astype(jnp.float32)
        rest = rest - piece
        spread = jnp.concatenate(
            [jnp.where(block_of == h, piece, 0.0) for h in range(row_count // width)], axis=0
        ).astype(jnp.bfloat16)
        moved = lax.dot_general(
            spread, onehot, (((1,), (1,)), ((), ())), preferred_element_type=jnp.float32
        )
        total = moved if total is None else total + moved
    for h in range(row_count // width):
        lanes = slice(h * width, (h + 1) * width)
        applied_ref[:, lanes] = base_ref[:, lanes] + total[h * modes : (h + 1) * modes]
    token_ref[...] = jnp.zeros_like(token_ref)


def local_call(body, outputs, operands, name):
    shapes = tuple(jax.ShapeDtypeStruct(shape, jnp.float32) for shape in outputs)
    return pl.pallas_call(
        body,
        out_shape=shapes,
        in_specs=[VMEM_BLOCK] * len(operands),
        out_specs=tuple(VMEM_BLOCK for _ in shapes),
        compiler_params=kernel_params([x.shape for x in operands] + list(outputs)),
        name=name,
    )(*operands)


def per_device(eigen_vectors, row_mass, inner_weight, face_weight, margin_rows):
    vectors = eigen_vectors[0, 0]
    row_lists = margin_rows[0, 0]
    face_springs = face_weight[0, 0]
    modes, row_count = vectors.shape
    width = row_lists.shape[-1]
    subs = lax.axis_size("sub")
    layers = lax.axis_size("layer")
    up_sub = [(i, i + 1) for i in range(subs - 1)]
    up_layer = [(i, i + 1) for i in range(layers - 1)]
    down_sub = [(i + 1, i) for i in range(subs - 1)]
    down_layer = [(i + 1, i) for i in range(layers - 1)]
    def pinned(*arrays):
        return [pltpu.with_memory_space_constraint(x, pltpu.HBM) for x in arrays]

    def shaped(*shapes):
        return tuple(jax.ShapeDtypeStruct(shape, jnp.float32) for shape in shapes)

    taken = (vectors, row_lists, face_springs)
    held = tuple(jax.ShapeDtypeStruct(x.shape, x.dtype) for x in taken)
    held += shaped((modes + ROWS, width), (modes + ROWS, width))
    vectors, row_lists, face_springs, layer_send, sub_send = pl.pallas_call(
        pick_kernel,
        out_shape=held,
        in_specs=[HBM_BLOCK] * len(taken),
        out_specs=(VMEM_BLOCK,) * len(held),
        scratch_shapes=[pltpu.SemaphoreType.DMA((2 + modes // ROWS,))],
        compiler_params=kernel_params([x.shape for x in held]),
        name="pick_rows",
    )(*pinned(*taken))
    before_layer = lax.ppermute(layer_send, "layer", up_layer)
    before_sub = lax.ppermute(sub_send, "sub", up_sub)
    masses, interior = row_mass[0], inner_weight[0].reshape(-1, 1, row_count)
    made = shaped((modes, row_count), (modes, modes), (modes, width), (modes, width))
    base, own, picked_sub, picked_layer = pl.pallas_call(
        functools.partial(own_kernel, subs=subs, layers=layers),
        out_shape=made,
        in_specs=[HBM_BLOCK] * 2 + [VMEM_BLOCK] * len(held),
        out_specs=(VMEM_BLOCK,) * len(made),
        scratch_shapes=[
            pltpu.VMEM(masses.shape, jnp.float32),
            pltpu.VMEM(interior.shape, jnp.float32),
            pltpu.SemaphoreType.DMA((2,)),
        ],
        compiler_params=kernel_params([x.shape for x in held + made]),
        name="own_rows",
    )(*pinned(masses, interior), vectors, row_lists, face_springs, sub_send, layer_send)
    after_sub = lax.ppermute(picked_sub, "sub", down_sub)
    copies, after_send = local_call(
        functools.partial(tile_kernel, row_count=row_count),
        [(subs * layers, modes - ROWS, LANES), (modes, width)],
        (own, picked_layer, picked_sub, before_layer, before_sub),
        "coarse_tiles",
    )
    tiles = lax.all_to_all(copies, ("sub", "layer"), split_axis=0, concat_axis=0, tiled=True)
    after_layer = lax.ppermute(after_send, "layer", down_layer)
    applied, token = local_call(
        functools.partial(scatter_kernel, subs=subs, layers=layers),
        [(modes, row_count), (ROWS, LANES)],
        (base, row_lists, face_springs, sub_send, picked_sub, layer_send, picked_layer)
        + (before_sub, after_sub, before_layer, after_layer),
        "spread_rows",
    )
    diag_strip, left_strip, right_strip = factor_planes(
        tiles.reshape(subs, layers, *tiles.shape[1:]), modes, token
    )
    return (applied[None, None], diag_strip[None], left_strip[None], right_strip[None])


def solution(mesh):
    in_specs = (
        P("sub", "layer", None, None),
        P("sub", "layer", None),
        P("sub", "layer", None, None),
        P("sub", "layer", None, None),
        P("sub", "layer", None, None),
    )
    out_specs = (
        P("sub", "layer", None, None),
        P("sub", "layer", None),
        P("sub", "layer", None),
        P("sub", "layer", None),
    )
    return jax.shard_map(
        per_device, mesh=mesh, in_specs=in_specs, out_specs=out_specs, check_vma=False
    )
```

```python
import functools
import math
import jax
import jax.numpy as jnp
from jax import lax
from jax.experimental import pallas as pl
from jax.experimental.pallas import tpu as pltpu
from jax.sharding import PartitionSpec as P

STRIDES = (1, 3, 27)
HIGHEST = lax.Precision.HIGHEST
LANES = 128
ROWS = 8
UNROLLED_LAYERS = 4
PLANES_AT_ONCE = 2
NARROW_DEPTH = LANES + LANES // 4


def turned_dot(left, right):
    return lax.dot_general(
        left,
        right,
        (((0,), (0,)), ((), ())),
        precision=HIGHEST,
        preferred_element_type=jnp.float32,
    )


PRODUCTS = ((0, 0), (1, 0), (2, 0), (0, 1), (1, 1), (0, 2))


def pieces_of(values):
    first = values.astype(jnp.bfloat16).astype(jnp.float32)
    rest = values - first
    second = rest.astype(jnp.bfloat16).astype(jnp.float32)
    return first, second, rest - second


def single_dot(left, right):
    return lax.dot_general(
        left, right, (((1,), (0,)), ((), ())), preferred_element_type=jnp.float32
    )


def narrow_columns(turned, modes):
    height = turned.shape[0]
    lane = lax.broadcasted_iota(jnp.int32, (height, LANES), 1)
    wide = jnp.concatenate([turned, jnp.zeros((height, LANES - 3 * modes), jnp.float32)], axis=1)
    again = pltpu.roll(wide, 3 * modes, 1)
    left = jnp.where(lane < 3 * modes, wide, jnp.where(lane < 5 * modes, again, 0.0))
    last = jnp.where(lane < modes, wide, 0.0)
    return jnp.concatenate([left, last], axis=1)[:, 0:NARROW_DEPTH].astype(jnp.bfloat16)


def narrow_rows(pieces):
    first, second, third = pieces
    modes, width = first.shape
    gap = jnp.zeros((LANES - 5 * modes, width), jnp.float32)
    tail = jnp.zeros((NARROW_DEPTH - LANES - modes, width), jnp.float32)
    rows = jnp.concatenate([first] * 3 + [second] * 2 + [gap, third, tail], axis=0)
    return rows.astype(jnp.bfloat16)


def plain_dot(left, right):
    return lax.dot_general(
        left,
        right,
        (((1,), (0,)), ((), ())),
        precision=HIGHEST,
        preferred_element_type=jnp.float32,
    )


def spread_row(strip, k):
    return jnp.broadcast_to(strip[k : k + 1, :], strip.shape)


def eliminate_pair(block, columns, pivots, iota, q, k):
    start = q * ROWS
    first, second = columns[start + k], columns[start + k + 1]
    corner, joint = spread_row(first[0], k), spread_row(first[0], k + 1)
    other_corner = spread_row(second[0], k + 1)
    minor = corner * other_corner - joint * joint
    inverse = pl.reciprocal(corner, approx=True)
    other_inverse = corner * pl.reciprocal(minor, approx=True)
    below = [column * inverse for column in first]
    second = [column - below[r] * joint for r, column in enumerate(second)]
    other_below = [column * other_inverse for column in second]
    below[0] = jnp.where(iota > k, below[0], 0.0)
    other_below[0] = jnp.where(iota > k + 1, other_below[0], 0.0)
    for j in range(start + k + 2, len(columns)):
        strip = j // ROWS - q
        head = spread_row(first[strip], j % ROWS)
        other_head = spread_row(second[strip], j % ROWS)
        columns[j] = [
            column - below[strip + r] * head - other_below[strip + r] * other_head
            for r, column in enumerate(columns[j])
        ]
    for t in range(len(block[q])):
        row = spread_row(block[q][t], k)
        for r, lower in enumerate(below):
            block[q + r][t] = block[q + r][t] - lower * row
        row = spread_row(block[q][t], k + 1)
        for r, lower in enumerate(other_below):
            block[q + r][t] = block[q + r][t] - lower * row
    return jnp.where(iota == k, corner, jnp.where(iota == k + 1, minor * inverse, pivots))


def factor_rows(blocks, tiles_per_part, first_row, turned):
    strip_count = len(blocks[0])
    iota = lax.broadcasted_iota(jnp.int32, (ROWS, LANES), 0)
    lane = lax.broadcasted_iota(jnp.int32, (ROWS, LANES), 1)
    blocks = [[list(strip) for strip in block] for block in blocks]
    at_once = len(blocks) <= PLANES_AT_ONCE
    held = [[] for _ in blocks]
    for q in range(strip_count):
        start = q * ROWS
        if q == 0 or not at_once:
            for b, block in enumerate(blocks):
                source = turned(b, block, q)
                for j in range(start, strip_count * ROWS if at_once else start + ROWS):
                    held[b].append(
                        [
                            jnp.broadcast_to(strip[:, j : j + 1], (ROWS, LANES))
                            for strip in source[j // ROWS - q :]
                        ]
                    )
        pivots = [jnp.zeros((ROWS, LANES), jnp.float32) for _ in blocks]
        for k in range(0, ROWS, 2):
            for b, block in enumerate(blocks):
                pivots[b] = eliminate_pair(block, held[b], pivots[b], iota, q, k)
        for b, block in enumerate(blocks):
            scale = lax.rsqrt(pivots[b])
            for t in range(len(block[q])):
                strip = block[q][t] * scale
                if t < tiles_per_part:
                    keep = lane + t * LANES >= iota + (first_row + start)
                    strip = jnp.where(keep, strip, 0.0)
                block[q][t] = strip
    return blocks


def eliminate_panel(grid_ref, planes, modes, order, part, lanes_used, panel, banded):
    per_part = part // LANES
    first_row = panel * modes
    static = isinstance(panel, int)
    if static:
        rows = pl.ds(first_row, modes)
    else:
        rows = pl.ds(pl.multiple_of(first_row, ROWS), modes)
    blocks = []
    for plane in planes:
        panel_rows = grid_ref[plane, rows, 0:lanes_used]
        blocks.append(
            [
                [
                    panel_rows[q * ROWS : (q + 1) * ROWS, t * LANES : (t + 1) * LANES]
                    for t in range(lanes_used // LANES)
                ]
                for q in range(modes // ROWS)
            ]
        )

    def turned(b, block, q):
        found = []
        for strip in block[q:]:
            if static and first_row // LANES == (first_row + modes - 1) // LANES:
                tile = strip[first_row // LANES]
                offset = first_row % LANES
                found.append(tile if offset == 0 else tile[:, offset : offset + modes])
            else:
                wide = jnp.concatenate(strip[:per_part], axis=1)
                found.append(pltpu.roll(wide, lax.rem(part - first_row, part), 1)[:, :LANES])
        return found

    blocks = factor_rows(blocks, per_part, first_row, turned)
    for plane, block in zip(planes, blocks):
        panel_rows = jnp.concatenate([jnp.concatenate(strip, axis=1) for strip in block], axis=0)
        grid_ref[plane, rows, 0:lanes_used] = panel_rows
        if static:
            below = (panel + 1) * modes
            end = min(below + modes, order) if banded else order
            pieces = pieces_of(panel_rows)
            right = narrow_rows(pieces)
            stacked = jnp.concatenate(pieces, axis=0)
            if below < order:
                columns = narrow_columns(stacked[:, 0:part].T[below:end], modes)
                grid_ref[plane, below:end, 0:lanes_used] -= single_dot(columns, right)
        else:
            lane = lax.broadcasted_iota(jnp.int32, (modes, part), 1)
            columns = jnp.where(lane >= first_row + modes, panel_rows[:, 0:part], 0.0)
            update = turned_dot(columns, panel_rows)[0:order]
            grid_ref[plane, :, 0:lanes_used] -= update


def eliminate_planes(grid_ref, planes, modes, order, part, lanes_used, banded=False):
    layers = order // modes
    if layers <= UNROLLED_LAYERS:
        for panel in range(layers):
            eliminate_panel(grid_ref, planes, modes, order, part, lanes_used, panel, banded)
    else:

        def one_panel(panel, carry):
            eliminate_panel(grid_ref, planes, modes, order, part, lanes_used, panel, banded)
            return carry

        lax.fori_loop(0, layers, one_panel, 0)


def update_partners(grid_ref, plane, distance, part, order, has_left):
    left, right = plane - distance, plane + distance
    both = grid_ref[plane, :, part : 3 * part]
    if part > order:
        spare = jnp.zeros((part - order, 2 * part), jnp.float32)
        both = jnp.concatenate([both, spare], axis=0)
    turned = [piece.astype(jnp.bfloat16) for piece in pieces_of(both.T)]
    held = [piece.astype(jnp.bfloat16) for piece in pieces_of(both)]
    held = jnp.concatenate([held[right] for _, right in PRODUCTS], axis=0)

    def product(rows):
        columns = jnp.concatenate([turned[left][rows] for left, _ in PRODUCTS], axis=1)
        return single_dot(columns, held)

    from_right = product(slice(part, part + order))
    grid_ref[right, :, 0:part] -= from_right[:, part : 2 * part]
    grid_ref[right, :, part : 2 * part] = -from_right[:, 0:part]

    def to_left():
        from_left = product(slice(0, order))
        grid_ref[left, :, 0:part] -= from_left[:, 0:part]
        grid_ref[left, :, 2 * part : 3 * part] = -from_left[:, part : 2 * part]

    if isinstance(has_left, bool):
        if has_left:
            to_left()
    else:
        pl.when(has_left)(to_left)


def unpack_tile(packed, modes):
    half = 3 * modes // 2
    upper = packed[:, 0 : 3 * modes]
    lower = jnp.concatenate(
        [packed[0:ROWS, 3 * modes : 3 * modes + half], packed[ROWS:, 3 * modes : 3 * modes + half]],
        axis=1,
    )
    return jnp.concatenate([upper, lower], axis=0)


def pack_tile(tile):
    modes = tile.shape[0]
    half = 3 * modes // 2
    top = modes - ROWS
    upper = tile[0:top]
    lower = jnp.concatenate([tile[top:, 0:half], tile[top:, half:]], axis=0)
    spare = jnp.zeros((top, LANES - 3 * modes - half), jnp.float32)
    return jnp.concatenate([upper, lower, spare], axis=1)


def factor_kernel(tiles_ref, after_ref, diag_ref, left_ref, right_ref, grid_ref, turned_ref):
    subs, layers, _, _ = tiles_ref.shape
    modes, order = diag_ref.shape
    part = grid_ref.shape[2] // 3
    unrolled = layers <= UNROLLED_LAYERS
    del after_ref
    lane = lax.broadcasted_iota(jnp.int32, (modes, part), 1)
    inside = [(lane >= j * modes) & (lane < (j + 1) * modes) for j in range(layers)]

    def place_tiles(s, before):
        tiles = [unpack_tile(tiles_ref[s, j], modes) for j in range(layers)]
        stacked = tiles
        if part > order:
            stacked = tiles + [jnp.zeros((part - order, tiles[0].shape[1]), jnp.float32)]
        turned = jnp.concatenate(stacked, axis=0).T
        for j, tile in enumerate(tiles):
            rows = slice(j * modes, (j + 1) * modes)
            own = jnp.where(inside[j], turned[0:modes], 0.0)
            if j + 1 < layers:
                own = jnp.where(inside[j + 1], turned[modes : 2 * modes], own)
            grid_ref[s, rows, 0:part] = own
            spare = jnp.zeros((modes, part - 3 * modes), jnp.float32)
            wide = jnp.concatenate([tile, spare], axis=1)
            shift = (j - 2) * modes % part
            down = pltpu.roll(wide, shift, 1) if shift else wide
            grid_ref[s, rows, part : 2 * part] = jnp.where(inside[j], down, 0.0)
            down = jnp.where(inside[j], turned[2 * modes : 3 * modes], 0.0)
            grid_ref[before, rows, 2 * part : 3 * part] = down

    place_tiles(0, subs - 1)
    if unrolled:
        for s in range(1, subs):
            place_tiles(s, s - 1)
    else:

        def place_one(s, carry):
            place_tiles(s, s - 1)
            return carry

        lax.fori_loop(1, subs, place_one, 0)

    sub_here, lay_here = lax.axis_index("sub"), lax.axis_index("layer")

    def one_level(distance):
        if unrolled:
            planes = list(range(distance - 1, subs, 2 * distance))
            eliminate_planes(grid_ref, planes, modes, order, part, 3 * part, distance == 1)
            for plane in planes:
                update_partners(grid_ref, plane, distance, part, order, plane >= distance)
        else:

            def one_plane(index, carry):
                plane = distance - 1 + 2 * distance * index
                eliminate_planes(grid_ref, [plane], modes, order, part, 3 * part)
                update_partners(grid_ref, plane, distance, part, order, index > 0)
                return carry

            lax.fori_loop(0, subs // (2 * distance), one_plane, 0)

    one_level(1)
    distance = 2
    while distance < subs:
        pl.when(lax.rem(sub_here + 1, distance) == 0)(functools.partial(one_level, distance))
        distance *= 2

    @pl.when(sub_here == subs - 1)
    def _():
        eliminate_planes(grid_ref, [subs - 1], modes, order, part, part)

    strip = pl.ds(pl.multiple_of(lay_here * modes, ROWS), modes)
    for k, out_ref in enumerate((diag_ref, left_ref, right_ref)):
        turned_ref[k] = grid_ref[sub_here, :, k * part : (k + 1) * part].T
        found = turned_ref[k, strip, :]
        out_ref[...] = found if k == 0 else jnp.where(sub_here < subs - 1, found, 0.0)


VMEM_BLOCK = pl.BlockSpec(memory_space=pltpu.VMEM)
HBM_BLOCK = pl.BlockSpec(memory_space=pltpu.HBM)
SPARE_BYTES = 4 * 1024 * 1024


def kernel_params(shapes):
    held = sum(4 * math.prod(shape) for shape in shapes)
    return pltpu.CompilerParams(vmem_limit_bytes=min(2 * held + SPARE_BYTES, 60 * 1024 * 1024))


def factor_planes(plane_tiles, modes, after):
    subs, layers, _, _ = plane_tiles.shape
    order = layers * modes
    part = -(-order // LANES) * LANES
    strip = jax.ShapeDtypeStruct((modes, order), jnp.float32)
    scratch = ((subs, order, 3 * part), (3, part, order))
    return pl.pallas_call(
        factor_kernel,
        out_shape=(strip, strip, strip),
        in_specs=[VMEM_BLOCK, VMEM_BLOCK],
        out_specs=(VMEM_BLOCK, VMEM_BLOCK, VMEM_BLOCK),
        scratch_shapes=[pltpu.VMEM(shape, jnp.float32) for shape in scratch],
        compiler_params=kernel_params((plane_tiles.shape,) + scratch),
        name="factor_planes",
    )(plane_tiles, after)


def across_dot(left, right):
    rows, columns = left.shape[0], right.shape[0]

    def stacked(values):
        short = -3 * values.shape[0] % (2 * ROWS)
        spare = [jnp.zeros((short, values.shape[1]), jnp.float32)] if short else []
        return jnp.concatenate(list(pieces_of(values)) + spare, axis=0).astype(jnp.bfloat16)

    found = lax.dot_general(
        stacked(left),
        stacked(right),
        (((1,), (1,)), ((), ())),
        preferred_element_type=jnp.float32,
    )
    total = None
    for b in (2, 1, 0):
        column = found[:, b * columns : (b + 1) * columns]
        for a in (2, 1, 0):
            if (a, b) in PRODUCTS:
                block = column[a * rows : (a + 1) * rows]
                total = block if total is None else total + block
    return total


def pick_lists(vectors_ref, lists_ref, chosen, strip):
    lists = []
    for k in chosen:
        rows = jnp.broadcast_to(lists_ref[k : k + 1, :], (ROWS, LANES))
        lists.append((rows // LANES, rows % LANES))
    found = [jnp.zeros((ROWS, LANES), jnp.float32) for _ in lists]
    for c in range(vectors_ref.shape[1] // LANES):
        tile = vectors_ref[strip, c * LANES : (c + 1) * LANES]
        for i, (tile_of, lane_of) in enumerate(lists):
            moved = jnp.take_along_axis(tile, lane_of, axis=1, mode="promise_in_bounds")
            found[i] = jnp.where(tile_of == c, moved, found[i])
    return found


def pick_kernel(
    vectors_in, lists_in, face_in, vectors_ref, lists_ref, face_ref, layer_ref, sub_ref, sems
):
    modes = vectors_ref.shape[0]
    strips = [slice(first, first + ROWS) for first in range(0, modes, ROWS)]
    pairs = [(lists_in, lists_ref)]
    pairs += [(vectors_in.at[pl.ds(s.start, ROWS)], vectors_ref.at[pl.ds(s.start, ROWS)]) for s in strips]
    pairs += [(face_in, face_ref)]
    copies = [pltpu.make_async_copy(a, b, sems.at[i]) for i, (a, b) in enumerate(pairs)]
    for copy in copies:
        copy.start()
    copies[0].wait()
    copies[-1].wait()
    for k, send_ref in ((0, sub_ref), (2, layer_ref)):
        send_ref[modes:] = jnp.broadcast_to(face_ref[k // 2 : k // 2 + 1, :], (ROWS, LANES))
    for copy, strip in zip(copies[1:], strips):
        copy.wait()
        sub_ref[strip], layer_ref[strip] = pick_lists(vectors_ref, lists_ref, (0, 2), strip)


def own_kernel(
    mass_in, inner_in, vectors_ref, lists_ref, face_ref, sub_ref, layer_ref,
    base_ref, own_ref, before_sub_ref, before_layer_ref, mass_ref, inner_ref, sems, *, subs, layers
):
    copies = [
        pltpu.make_async_copy(mass_in, mass_ref, sems.at[0]),
        pltpu.make_async_copy(inner_in, inner_ref, sems.at[1]),
    ]
    for copy in copies:
        copy.start()
    vectors = vectors_ref[...]
    modes, row_count = vectors.shape
    for first in range(0, modes, ROWS):
        strip = slice(first, first + ROWS)
        before_sub_ref[strip], before_layer_ref[strip] = pick_lists(
            vectors_ref, lists_ref, (1, 3), strip
        )
    for copy in copies:
        copy.wait()
    places = lax.broadcasted_iota(jnp.int32, (1, row_count), 1)
    base = mass_ref[...] * vectors
    for k, t in enumerate(STRIDES):
        edge_weight = jnp.where(places < row_count - t, inner_ref[k], 0.0)
        fluxes = edge_weight * (vectors - pltpu.roll(vectors, row_count - t, 1))
        base = base + fluxes - pltpu.roll(fluxes, t, 1)
    base_ref[...] = base
    own = across_dot(vectors, base)
    for k, axis, ends, send_ref in ((0, "sub", subs - 1, sub_ref), (1, "layer", layers - 1, layer_ref)):
        springs = jnp.where(lax.axis_index(axis) < ends, face_ref[k : k + 1, :], 0.0)
        picked = send_ref[0:modes]
        own = own + across_dot(picked, springs * picked)
    own_ref[...] = own


def tile_kernel(
    own_ref, mine_layer_ref, mine_sub_ref, layer_ref, sub_ref, copies_ref, layer_send_ref, *, row_count
):
    modes = own_ref.shape[0]
    inverse = 1.0 / row_count
    pairs = []
    for mine_ref, theirs_ref in ((mine_sub_ref, sub_ref), (mine_layer_ref, layer_ref)):
        mine = mine_ref[...]
        sprung = theirs_ref[modes : modes + 1] * mine
        stacked = jnp.concatenate([mine, theirs_ref[0:modes]], axis=0)
        pairs.append(across_dot(sprung, stacked))
    down, side = pairs
    diag_tile = (own_ref[...] + down[:, 0:modes] + side[:, 0:modes]) * inverse
    side_tile = -side[:, modes:] * inverse
    down_tile = -down[:, modes:] * inverse
    packed = pack_tile(jnp.concatenate([diag_tile, side_tile, down_tile], axis=1))
    for s in range(copies_ref.shape[0]):
        copies_ref[s] = packed
    layer_send_ref[...] = mine_layer_ref[...]


def scatter_kernel(
    base_ref, lists_ref, face_ref, up_sub_ref, down_sub_ref, up_layer_ref, down_layer_ref, before_sub_ref, after_sub_ref,
    before_layer_ref, after_layer_ref, applied_ref, token_ref, *, subs, layers
):
    modes, row_count = base_ref.shape
    width = 2 * LANES
    springs = [
        jnp.where(lax.axis_index("sub") < subs - 1, face_ref[0:1, :], 0.0),
        before_sub_ref[modes : modes + 1, :],
        jnp.where(lax.axis_index("layer") < layers - 1, face_ref[1:2, :], 0.0),
        before_layer_ref[modes : modes + 1, :],
    ]
    partners = [
        after_sub_ref[...],
        before_sub_ref[0:modes, :],
        after_layer_ref[...],
        before_layer_ref[0:modes, :],
    ]
    picked = [up_sub_ref[0:modes], down_sub_ref[...], up_layer_ref[0:modes], down_layer_ref[...]]
    pulls = jnp.concatenate([springs[k] * (picked[k] - partners[k]) for k in range(4)], axis=1)
    rows = jnp.concatenate([lists_ref[k : k + 1, :] for k in range(4)], axis=1)
    block_of, lane_of = rows // width, rows % width
    lanes = lax.broadcasted_iota(jnp.int32, (width, rows.shape[1]), 0)
    onehot = jnp.where(lanes == lane_of, 1.0, 0.0).astype(jnp.bfloat16)
    total = None
    rest = pulls
    for _ in range(3):
        piece = rest.astype(jnp.bfloat16).astype(jnp.float32)
        rest = rest - piece
        spread = jnp.concatenate(
            [jnp.where(block_of == h, piece, 0.0) for h in range(row_count // width)], axis=0
        ).astype(jnp.bfloat16)
        moved = lax.dot_general(
            spread, onehot, (((1,), (1,)), ((), ())), preferred_element_type=jnp.float32
        )
        total = moved if total is None else total + moved
    for h in range(row_count // width):
        lanes = slice(h * width, (h + 1) * width)
        applied_ref[:, lanes] = base_ref[:, lanes] + total[h * modes : (h + 1) * modes]
    token_ref[...] = jnp.zeros_like(token_ref)


def local_call(body, outputs, operands, name):
    shapes = tuple(jax.ShapeDtypeStruct(shape, jnp.float32) for shape in outputs)
    return pl.pallas_call(
        body,
        out_shape=shapes,
        in_specs=[VMEM_BLOCK] * len(operands),
        out_specs=tuple(VMEM_BLOCK for _ in shapes),
        compiler_params=kernel_params([x.shape for x in operands] + list(outputs)),
        name=name,
    )(*operands)


def per_device(eigen_vectors, row_mass, inner_weight, face_weight, margin_rows):
    vectors = eigen_vectors[0, 0]
    row_lists = margin_rows[0, 0]
    face_springs = face_weight[0, 0]
    modes, row_count = vectors.shape
    width = row_lists.shape[-1]
    subs = lax.axis_size("sub")
    layers = lax.axis_size("layer")
    up_sub = [(i, i + 1) for i in range(subs - 1)]
    up_layer = [(i, i + 1) for i in range(layers - 1)]
    down_sub = [(i + 1, i) for i in range(subs - 1)]
    down_layer = [(i + 1, i) for i in range(layers - 1)]
    def pinned(*arrays):
        return [pltpu.with_memory_space_constraint(x, pltpu.HBM) for x in arrays]

    def shaped(*shapes):
        return tuple(jax.ShapeDtypeStruct(shape, jnp.float32) for shape in shapes)

    taken = (vectors, row_lists, face_springs)
    held = tuple(jax.ShapeDtypeStruct(x.shape, x.dtype) for x in taken)
    held += shaped((modes + ROWS, width), (modes + ROWS, width))
    vectors, row_lists, face_springs, layer_send, sub_send = pl.pallas_call(
        pick_kernel,
        out_shape=held,
        in_specs=[HBM_BLOCK] * len(taken),
        out_specs=(VMEM_BLOCK,) * len(held),
        scratch_shapes=[pltpu.SemaphoreType.DMA((2 + modes // ROWS,))],
        compiler_params=kernel_params([x.shape for x in held]),
        name="pick_rows",
    )(*pinned(*taken))
    before_layer = lax.ppermute(layer_send, "layer", up_layer)
    before_sub = lax.ppermute(sub_send, "sub", up_sub)
    masses, interior = row_mass[0], inner_weight[0].reshape(-1, 1, row_count)
    made = shaped((modes, row_count), (modes, modes), (modes, width), (modes, width))
    base, own, picked_sub, picked_layer = pl.pallas_call(
        functools.partial(own_kernel, subs=subs, layers=layers),
        out_shape=made,
        in_specs=[HBM_BLOCK] * 2 + [VMEM_BLOCK] * len(held),
        out_specs=(VMEM_BLOCK,) * len(made),
        scratch_shapes=[
            pltpu.VMEM(masses.shape, jnp.float32),
            pltpu.VMEM(interior.shape, jnp.float32),
            pltpu.SemaphoreType.DMA((2,)),
        ],
        compiler_params=kernel_params([x.shape for x in held + made]),
        name="own_rows",
    )(*pinned(masses, interior), vectors, row_lists, face_springs, sub_send, layer_send)
    after_sub = lax.ppermute(picked_sub, "sub", down_sub)
    copies, after_send = local_call(
        functools.partial(tile_kernel, row_count=row_count),
        [(subs * layers, modes - ROWS, LANES), (modes, width)],
        (own, picked_layer, picked_sub, before_layer, before_sub),
        "coarse_tiles",
    )
    tiles = lax.all_to_all(copies, ("sub", "layer"), split_axis=0, concat_axis=0, tiled=True)
    after_layer = lax.ppermute(after_send, "layer", down_layer)
    applied, token = local_call(
        functools.partial(scatter_kernel, subs=subs, layers=layers),
        [(modes, row_count), (ROWS, LANES)],
        (base, row_lists, face_springs, sub_send, picked_sub, layer_send, picked_layer)
        + (before_sub, after_sub, before_layer, after_layer),
        "spread_rows",
    )
    diag_strip, left_strip, right_strip = factor_planes(
        tiles.reshape(subs, layers, *tiles.shape[1:]), modes, token
    )
    return (applied[None, None], diag_strip[None], left_strip[None], right_strip[None])


def solution(mesh):
    in_specs = (
        P("sub", "layer", None, None),
        P("sub", "layer", None),
        P("sub", "layer", None, None),
        P("sub", "layer", None, None),
        P("sub", "layer", None, None),
    )
    out_specs = (
        P("sub", "layer", None, None),
        P("sub", "layer", None),
        P("sub", "layer", None),
        P("sub", "layer", None),
    )
    return jax.shard_map(
        per_device, mesh=mesh, in_specs=in_specs, out_specs=out_specs, check_vma=False
    )
```

```python
import functools
import math
import jax
import jax.numpy as jnp
from jax import lax
from jax.experimental import pallas as pl
from jax.experimental.pallas import tpu as pltpu
from jax.sharding import PartitionSpec as P

STRIDES = (1, 3, 27)
HIGHEST = lax.Precision.HIGHEST
LANES = 128
ROWS = 8
UNROLLED_LAYERS = 4
PLANES_AT_ONCE = 2
NARROW_DEPTH = LANES + LANES // 4


def turned_dot(left, right):
    return lax.dot_general(
        left,
        right,
        (((0,), (0,)), ((), ())),
        precision=HIGHEST,
        preferred_element_type=jnp.float32,
    )


PRODUCTS = ((0, 0), (1, 0), (2, 0), (0, 1), (1, 1), (0, 2))


def pieces_of(values):
    first = values.astype(jnp.bfloat16).astype(jnp.float32)
    rest = values - first
    second = rest.astype(jnp.bfloat16).astype(jnp.float32)
    return first, second, rest - second


def single_dot(left, right):
    return lax.dot_general(
        left, right, (((1,), (0,)), ((), ())), preferred_element_type=jnp.float32
    )


def narrow_columns(turned, modes):
    height = turned.shape[0]
    lane = lax.broadcasted_iota(jnp.int32, (height, LANES), 1)
    wide = jnp.concatenate([turned, jnp.zeros((height, LANES - 3 * modes), jnp.float32)], axis=1)
    again = pltpu.roll(wide, 3 * modes, 1)
    left = jnp.where(lane < 3 * modes, wide, jnp.where(lane < 5 * modes, again, 0.0))
    last = jnp.where(lane < modes, wide, 0.0)
    return jnp.concatenate([left, last], axis=1)[:, 0:NARROW_DEPTH].astype(jnp.bfloat16)


def narrow_rows(pieces):
    first, second, third = pieces
    modes, width = first.shape
    gap = jnp.zeros((LANES - 5 * modes, width), jnp.float32)
    tail = jnp.zeros((NARROW_DEPTH - LANES - modes, width), jnp.float32)
    rows = jnp.concatenate([first] * 3 + [second] * 2 + [gap, third, tail], axis=0)
    return rows.astype(jnp.bfloat16)


def plain_dot(left, right):
    return lax.dot_general(
        left,
        right,
        (((1,), (0,)), ((), ())),
        precision=HIGHEST,
        preferred_element_type=jnp.float32,
    )


def spread_row(strip, k):
    return jnp.broadcast_to(strip[k : k + 1, :], strip.shape)


def eliminate_pair(block, columns, pivots, iota, q, k):
    start = q * ROWS
    first, second = columns[start + k], columns[start + k + 1]
    corner, joint = spread_row(first[0], k), spread_row(first[0], k + 1)
    other_corner = spread_row(second[0], k + 1)
    minor = corner * other_corner - joint * joint
    inverse = pl.reciprocal(corner, approx=True)
    other_inverse = corner * pl.reciprocal(minor, approx=True)
    below = [column * inverse for column in first]
    second = [column - below[r] * joint for r, column in enumerate(second)]
    other_below = [column * other_inverse for column in second]
    below[0] = jnp.where(iota > k, below[0], 0.0)
    other_below[0] = jnp.where(iota > k + 1, other_below[0], 0.0)
    for j in range(start + k + 2, len(columns)):
        strip = j // ROWS - q
        head = spread_row(first[strip], j % ROWS)
        other_head = spread_row(second[strip], j % ROWS)
        columns[j] = [
            column - below[strip + r] * head - other_below[strip + r] * other_head
            for r, column in enumerate(columns[j])
        ]
    for t in range(len(block[q])):
        row = spread_row(block[q][t], k)
        for r, lower in enumerate(below):
            block[q + r][t] = block[q + r][t] - lower * row
        row = spread_row(block[q][t], k + 1)
        for r, lower in enumerate(other_below):
            block[q + r][t] = block[q + r][t] - lower * row
    return jnp.where(iota == k, corner, jnp.where(iota == k + 1, minor * inverse, pivots))


def factor_rows(blocks, tiles_per_part, first_row, turned):
    strip_count = len(blocks[0])
    iota = lax.broadcasted_iota(jnp.int32, (ROWS, LANES), 0)
    lane = lax.broadcasted_iota(jnp.int32, (ROWS, LANES), 1)
    blocks = [[list(strip) for strip in block] for block in blocks]
    at_once = len(blocks) <= PLANES_AT_ONCE
    held = [[] for _ in blocks]
    for q in range(strip_count):
        start = q * ROWS
        if q == 0 or not at_once:
            for b, block in enumerate(blocks):
                source = turned(b, block, q)
                for j in range(start, strip_count * ROWS if at_once else start + ROWS):
                    held[b].append(
                        [
                            jnp.broadcast_to(strip[:, j : j + 1], (ROWS, LANES))
                            for strip in source[j // ROWS - q :]
                        ]
                    )
        pivots = [jnp.zeros((ROWS, LANES), jnp.float32) for _ in blocks]
        for k in range(0, ROWS, 2):
            for b, block in enumerate(blocks):
                pivots[b] = eliminate_pair(block, held[b], pivots[b], iota, q, k)
        for b, block in enumerate(blocks):
            scale = lax.rsqrt(pivots[b])
            for t in range(len(block[q])):
                strip = block[q][t] * scale
                if t < tiles_per_part:
                    keep = lane + t * LANES >= iota + (first_row + start)
                    strip = jnp.where(keep, strip, 0.0)
                block[q][t] = strip
    return blocks


def eliminate_panel(grid_ref, planes, modes, order, part, lanes_used, panel, banded):
    per_part = part // LANES
    first_row = panel * modes
    static = isinstance(panel, int)
    if static:
        rows = pl.ds(first_row, modes)
    else:
        rows = pl.ds(pl.multiple_of(first_row, ROWS), modes)
    blocks = []
    for plane in planes:
        panel_rows = grid_ref[plane, rows, 0:lanes_used]
        blocks.append(
            [
                [
                    panel_rows[q * ROWS : (q + 1) * ROWS, t * LANES : (t + 1) * LANES]
                    for t in range(lanes_used // LANES)
                ]
                for q in range(modes // ROWS)
            ]
        )

    def turned(b, block, q):
        found = []
        for strip in block[q:]:
            if static and first_row // LANES == (first_row + modes - 1) // LANES:
                tile = strip[first_row // LANES]
                offset = first_row % LANES
                found.append(tile if offset == 0 else tile[:, offset : offset + modes])
            else:
                wide = jnp.concatenate(strip[:per_part], axis=1)
                found.append(pltpu.roll(wide, lax.rem(part - first_row, part), 1)[:, :LANES])
        return found

    blocks = factor_rows(blocks, per_part, first_row, turned)
    for plane, block in zip(planes, blocks):
        panel_rows = jnp.concatenate([jnp.concatenate(strip, axis=1) for strip in block], axis=0)
        grid_ref[plane, rows, 0:lanes_used] = panel_rows
        if static:
            below = (panel + 1) * modes
            end = min(below + modes, order) if banded else order
            pieces = pieces_of(panel_rows)
            right = narrow_rows(pieces)
            stacked = jnp.concatenate(pieces, axis=0)
            if below < order:
                columns = narrow_columns(stacked[:, 0:part].T[below:end], modes)
                grid_ref[plane, below:end, 0:lanes_used] -= single_dot(columns, right)
        else:
            lane = lax.broadcasted_iota(jnp.int32, (modes, part), 1)
            columns = jnp.where(lane >= first_row + modes, panel_rows[:, 0:part], 0.0)
            update = turned_dot(columns, panel_rows)[0:order]
            grid_ref[plane, :, 0:lanes_used] -= update


def eliminate_planes(grid_ref, planes, modes, order, part, lanes_used, banded=False):
    layers = order // modes
    if layers <= UNROLLED_LAYERS:
        for panel in range(layers):
            eliminate_panel(grid_ref, planes, modes, order, part, lanes_used, panel, banded)
    else:

        def one_panel(panel, carry):
            eliminate_panel(grid_ref, planes, modes, order, part, lanes_used, panel, banded)
            return carry

        lax.fori_loop(0, layers, one_panel, 0)


def update_partners(grid_ref, plane, distance, part, order, has_left):
    left, right = plane - distance, plane + distance
    both = grid_ref[plane, :, part : 3 * part]
    if part > order:
        spare = jnp.zeros((part - order, 2 * part), jnp.float32)
        both = jnp.concatenate([both, spare], axis=0)
    turned = [piece.astype(jnp.bfloat16) for piece in pieces_of(both.T)]
    held = [piece.astype(jnp.bfloat16) for piece in pieces_of(both)]
    held = jnp.concatenate([held[right] for _, right in PRODUCTS], axis=0)

    def product(rows):
        columns = jnp.concatenate([turned[left][rows] for left, _ in PRODUCTS], axis=1)
        return single_dot(columns, held)

    from_right = product(slice(part, part + order))
    grid_ref[right, :, 0:part] -= from_right[:, part : 2 * part]
    grid_ref[right, :, part : 2 * part] = -from_right[:, 0:part]

    def to_left():
        from_left = product(slice(0, order))
        grid_ref[left, :, 0:part] -= from_left[:, 0:part]
        grid_ref[left, :, 2 * part : 3 * part] = -from_left[:, part : 2 * part]

    if isinstance(has_left, bool):
        if has_left:
            to_left()
    else:
        pl.when(has_left)(to_left)


def unpack_tile(packed, modes):
    half = 3 * modes // 2
    upper = packed[:, 0 : 3 * modes]
    lower = jnp.concatenate(
        [packed[0:ROWS, 3 * modes : 3 * modes + half], packed[ROWS:, 3 * modes : 3 * modes + half]],
        axis=1,
    )
    return jnp.concatenate([upper, lower], axis=0)


def pack_tile(tile):
    modes = tile.shape[0]
    half = 3 * modes // 2
    top = modes - ROWS
    upper = tile[0:top]
    lower = jnp.concatenate([tile[top:, 0:half], tile[top:, half:]], axis=0)
    spare = jnp.zeros((top, LANES - 3 * modes - half), jnp.float32)
    return jnp.concatenate([upper, lower, spare], axis=1)


def factor_kernel(tiles_ref, after_ref, diag_ref, left_ref, right_ref, grid_ref, turned_ref):
    subs, layers, _, _ = tiles_ref.shape
    modes, order = diag_ref.shape
    part = grid_ref.shape[2] // 3
    unrolled = layers <= UNROLLED_LAYERS
    del after_ref
    lane = lax.broadcasted_iota(jnp.int32, (modes, part), 1)
    inside = [(lane >= j * modes) & (lane < (j + 1) * modes) for j in range(layers)]

    def place_tiles(s, before):
        tiles = [unpack_tile(tiles_ref[s, j], modes) for j in range(layers)]
        stacked = tiles
        if part > order:
            stacked = tiles + [jnp.zeros((part - order, tiles[0].shape[1]), jnp.float32)]
        turned = jnp.concatenate(stacked, axis=0).T
        for j, tile in enumerate(tiles):
            rows = slice(j * modes, (j + 1) * modes)
            own = jnp.where(inside[j], turned[0:modes], 0.0)
            if j + 1 < layers:
                own = jnp.where(inside[j + 1], turned[modes : 2 * modes], own)
            grid_ref[s, rows, 0:part] = own
            spare = jnp.zeros((modes, part - 3 * modes), jnp.float32)
            wide = jnp.concatenate([tile, spare], axis=1)
            shift = (j - 2) * modes % part
            down = pltpu.roll(wide, shift, 1) if shift else wide
            grid_ref[s, rows, part : 2 * part] = jnp.where(inside[j], down, 0.0)
            down = jnp.where(inside[j], turned[2 * modes : 3 * modes], 0.0)
            grid_ref[before, rows, 2 * part : 3 * part] = down

    place_tiles(0, subs - 1)
    if unrolled:
        for s in range(1, subs):
            place_tiles(s, s - 1)
    else:

        def place_one(s, carry):
            place_tiles(s, s - 1)
            return carry

        lax.fori_loop(1, subs, place_one, 0)

    sub_here, lay_here = lax.axis_index("sub"), lax.axis_index("layer")

    def one_level(distance):
        if unrolled:
            planes = list(range(distance - 1, subs, 2 * distance))
            eliminate_planes(grid_ref, planes, modes, order, part, 3 * part, distance == 1)
            for plane in planes:
                update_partners(grid_ref, plane, distance, part, order, plane >= distance)
        else:

            def one_plane(index, carry):
                plane = distance - 1 + 2 * distance * index
                eliminate_planes(grid_ref, [plane], modes, order, part, 3 * part)
                update_partners(grid_ref, plane, distance, part, order, index > 0)
                return carry

            lax.fori_loop(0, subs // (2 * distance), one_plane, 0)

    one_level(1)
    if subs > 2:
        one_level(2)
    distance = 4
    while distance < subs:
        pl.when(lax.rem(sub_here + 1, distance) == 0)(functools.partial(one_level, distance))
        distance *= 2

    @pl.when(sub_here == subs - 1)
    def _():
        eliminate_planes(grid_ref, [subs - 1], modes, order, part, part)

    strip = pl.ds(pl.multiple_of(lay_here * modes, ROWS), modes)
    for k, out_ref in enumerate((diag_ref, left_ref, right_ref)):
        turned_ref[k] = grid_ref[sub_here, :, k * part : (k + 1) * part].T
        found = turned_ref[k, strip, :]
        out_ref[...] = found if k == 0 else jnp.where(sub_here < subs - 1, found, 0.0)


VMEM_BLOCK = pl.BlockSpec(memory_space=pltpu.VMEM)
HBM_BLOCK = pl.BlockSpec(memory_space=pltpu.HBM)
SPARE_BYTES = 4 * 1024 * 1024
WORK = 8 * 1024 * 1024


def kernel_params(shapes):
    held = sum(4 * math.prod(shape) for shape in shapes)
    return pltpu.CompilerParams(vmem_limit_bytes=min(2 * held + SPARE_BYTES, 60 * 1024 * 1024))


def factor_planes(plane_tiles, modes, after):
    subs, layers, _, _ = plane_tiles.shape
    order = layers * modes
    part = -(-order // LANES) * LANES
    strip = jax.ShapeDtypeStruct((modes, order), jnp.float32)
    scratch = ((subs, order, 3 * part), (3, part, order))
    return pl.pallas_call(
        factor_kernel,
        out_shape=(strip, strip, strip),
        in_specs=[VMEM_BLOCK, VMEM_BLOCK],
        out_specs=(VMEM_BLOCK, VMEM_BLOCK, VMEM_BLOCK),
        scratch_shapes=[pltpu.VMEM(shape, jnp.float32) for shape in scratch],
        compiler_params=kernel_params((plane_tiles.shape,) + scratch),
        name="factor_planes",
    )(plane_tiles, after)


def across_dot(left, right):
    rows, columns = left.shape[0], right.shape[0]

    def stacked(values):
        short = -3 * values.shape[0] % (2 * ROWS)
        spare = [jnp.zeros((short, values.shape[1]), jnp.float32)] if short else []
        return jnp.concatenate(list(pieces_of(values)) + spare, axis=0).astype(jnp.bfloat16)

    found = lax.dot_general(
        stacked(left),
        stacked(right),
        (((1,), (1,)), ((), ())),
        preferred_element_type=jnp.float32,
    )
    total = None
    for b in (2, 1, 0):
        column = found[:, b * columns : (b + 1) * columns]
        for a in (2, 1, 0):
            if (a, b) in PRODUCTS:
                block = column[a * rows : (a + 1) * rows]
                total = block if total is None else total + block
    return total


def pick_lists(vectors_ref, lists_ref, chosen, strip):
    lists = []
    for k in chosen:
        rows = jnp.broadcast_to(lists_ref[k : k + 1, :], (ROWS, LANES))
        lists.append((rows // LANES, rows % LANES))
    found = [jnp.zeros((ROWS, LANES), jnp.float32) for _ in lists]
    for c in range(vectors_ref.shape[1] // LANES):
        tile = vectors_ref[strip, c * LANES : (c + 1) * LANES]
        for i, (tile_of, lane_of) in enumerate(lists):
            moved = jnp.take_along_axis(tile, lane_of, axis=1, mode="promise_in_bounds")
            found[i] = jnp.where(tile_of == c, moved, found[i])
    return found


def mode_strips(modes):
    return [slice(first, first + ROWS) for first in range(0, modes, ROWS)]


def pick_kernel(
    vectors_in, lists_in, face_in, mass_in, inner_in,
    vectors_ref, lists_ref, face_ref, mass_ref, inner_ref, layer_ref, sub_ref, sems
):
    strips = mode_strips(vectors_ref.shape[0])
    pairs = [(lists_in, lists_ref)]
    for strip in strips:
        rows = pl.ds(strip.start, ROWS)
        pairs.append((vectors_in.at[rows], vectors_ref.at[rows]))
    pairs += [(face_in, face_ref), (mass_in, mass_ref), (inner_in, inner_ref)]
    copies = [pltpu.make_async_copy(a, b, sems.at[i]) for i, (a, b) in enumerate(pairs)]
    for copy in copies:
        copy.start()
    copies[0].wait()
    copies[1 + len(strips)].wait()
    for k, send_ref in ((1, layer_ref), (0, sub_ref)):
        send_ref[vectors_ref.shape[0] :] = jnp.broadcast_to(face_ref[k : k + 1, :], (ROWS, LANES))
    for copy, strip in zip(copies[1:], strips):
        copy.wait()
        layer_ref[strip], sub_ref[strip] = pick_lists(vectors_ref, lists_ref, (2, 0), strip)
    for copy in copies[2 + len(strips) :]:
        copy.wait()


def spread_weights(weights_ref, first, count, height):
    rows = [
        jnp.broadcast_to(weights_ref[first + c : first + c + 1, :], (ROWS, LANES))
        for c in range(count)
    ]
    wide = jnp.concatenate(rows, axis=1)
    return jnp.concatenate([wide] * (height // ROWS), axis=0)


def own_kernel(
    vectors_ref, lists_ref, face_ref, mass_ref, inner_ref, layer_ref, sub_ref, theirs_ref,
    base_ref, own_ref, side_ref, before_sub_ref, before_layer_ref, *, subs, layers
):
    vectors = vectors_ref[...]
    modes, row_count = vectors.shape
    tiles = row_count // LANES
    for strip in mode_strips(modes):
        before_sub_ref[strip], before_layer_ref[strip] = pick_lists(
            vectors_ref, lists_ref, (1, 3), strip
        )
    places = lax.broadcasted_iota(jnp.int32, (modes, row_count), 1)
    base = spread_weights(mass_ref, 0, tiles, modes) * vectors
    for k, t in enumerate(STRIDES):
        edge_weight = spread_weights(inner_ref, k * tiles, tiles, modes)
        edge_weight = jnp.where(places < row_count - t, edge_weight, 0.0)
        fluxes = edge_weight * (vectors - pltpu.roll(vectors, row_count - t, 1))
        base = base + fluxes - pltpu.roll(fluxes, t, 1)
    base_ref[...] = base
    own = across_dot(vectors, base)
    for k, axis, ends, send_ref in ((0, "sub", subs - 1, sub_ref), (1, "layer", layers - 1, layer_ref)):
        springs = jnp.where(lax.axis_index(axis) < ends, face_ref[k : k + 1, :], 0.0)
        picked = send_ref[0:modes]
        own = own + across_dot(picked, springs * picked)
    mine, theirs = before_layer_ref[...], theirs_ref[0:modes]
    sprung = theirs_ref[modes : modes + 1] * mine
    side = across_dot(sprung, jnp.concatenate([mine, theirs], axis=0))
    own_ref[...] = own + side[:, 0:modes]
    side_ref[...] = -side[:, modes:] * (1.0 / row_count)


def tile_kernel(
    own_ref, side_ref, mine_sub_ref, mine_layer_ref, sub_ref, copies_ref, layer_send_ref, *, row_count
):
    modes = own_ref.shape[0]
    inverse = 1.0 / row_count
    mine, theirs = mine_sub_ref[...], sub_ref[0:modes]
    sprung = sub_ref[modes : modes + 1] * mine
    down = across_dot(sprung, jnp.concatenate([mine, theirs], axis=0))
    diag_tile = (own_ref[...] + down[:, 0:modes]) * inverse
    side_tile = side_ref[...]
    down_tile = -down[:, modes:] * inverse
    packed = pack_tile(jnp.concatenate([diag_tile, side_tile, down_tile], axis=1))
    for s in range(copies_ref.shape[0]):
        copies_ref[s] = packed
    layer_send_ref[...] = mine_layer_ref[...]


def scatter_kernel(
    base_ref, lists_ref, face_ref, up_sub_ref, down_sub_ref, up_layer_ref, down_layer_ref, before_sub_ref, after_sub_ref,
    before_layer_ref, after_layer_ref, applied_ref, token_ref, *, subs, layers
):
    modes, row_count = base_ref.shape
    width = 2 * LANES
    springs = [
        jnp.where(lax.axis_index("sub") < subs - 1, face_ref[0:1, :], 0.0),
        before_sub_ref[modes : modes + 1, :],
        jnp.where(lax.axis_index("layer") < layers - 1, face_ref[1:2, :], 0.0),
        before_layer_ref[modes : modes + 1, :],
    ]
    partners = [
        after_sub_ref[...],
        before_sub_ref[0:modes, :],
        after_layer_ref[...],
        before_layer_ref[0:modes, :],
    ]
    picked = [up_sub_ref[0:modes], down_sub_ref[...], up_layer_ref[0:modes], down_layer_ref[...]]
    pulls = jnp.concatenate([springs[k] * (picked[k] - partners[k]) for k in range(4)], axis=1)
    rows = jnp.concatenate([lists_ref[k : k + 1, :] for k in range(4)], axis=1)
    block_of, lane_of = rows // width, rows % width
    lanes = lax.broadcasted_iota(jnp.int32, (width, rows.shape[1]), 0)
    onehot = jnp.where(lanes == lane_of, 1.0, 0.0).astype(jnp.bfloat16)
    total = None
    rest = pulls
    for _ in range(3):
        piece = rest.astype(jnp.bfloat16).astype(jnp.float32)
        rest = rest - piece
        spread = jnp.concatenate(
            [jnp.where(block_of == h, piece, 0.0) for h in range(row_count // width)], axis=0
        ).astype(jnp.bfloat16)
        moved = lax.dot_general(
            spread, onehot, (((1,), (1,)), ((), ())), preferred_element_type=jnp.float32
        )
        total = moved if total is None else total + moved
    for h in range(row_count // width):
        lanes = slice(h * width, (h + 1) * width)
        applied_ref[:, lanes] = base_ref[:, lanes] + total[h * modes : (h + 1) * modes]
    token_ref[...] = jnp.zeros_like(token_ref)


def local_call(body, outputs, operands, name, work=0):
    shapes = tuple(jax.ShapeDtypeStruct(shape, jnp.float32) for shape in outputs)
    return pl.pallas_call(
        body,
        out_shape=shapes,
        in_specs=[VMEM_BLOCK] * len(operands),
        out_specs=tuple(VMEM_BLOCK for _ in shapes),
        compiler_params=kernel_params([x.shape for x in operands] + list(outputs)),
        cost_estimate=pl.CostEstimate(flops=work, bytes_accessed=work, transcendentals=0),
        name=name,
    )(*operands)


def per_device(eigen_vectors, row_mass, inner_weight, face_weight, margin_rows):
    vectors = eigen_vectors[0, 0]
    row_lists = margin_rows[0, 0]
    face_springs = face_weight[0, 0]
    modes, row_count = vectors.shape
    width = row_lists.shape[-1]
    subs = lax.axis_size("sub")
    layers = lax.axis_size("layer")
    up_sub = [(i, i + 1) for i in range(subs - 1)]
    up_layer = [(i, i + 1) for i in range(layers - 1)]
    down_sub = [(i + 1, i) for i in range(subs - 1)]
    down_layer = [(i + 1, i) for i in range(layers - 1)]
    def pinned(*arrays):
        return [pltpu.with_memory_space_constraint(x, pltpu.HBM) for x in arrays]

    def shaped(*shapes):
        return tuple(jax.ShapeDtypeStruct(shape, jnp.float32) for shape in shapes)

    masses = row_mass.reshape(row_count // LANES, LANES)
    interior = inner_weight.reshape(-1, LANES)
    taken = (vectors, row_lists, face_springs, masses, interior)
    held = tuple(jax.ShapeDtypeStruct(x.shape, x.dtype) for x in taken)
    held += shaped((modes + ROWS, width), (modes + ROWS, width))
    vectors, row_lists, face_springs, masses, interior, layer_send, sub_send = pl.pallas_call(
        pick_kernel,
        out_shape=held,
        in_specs=[HBM_BLOCK] * len(taken),
        out_specs=(VMEM_BLOCK,) * len(held),
        scratch_shapes=[pltpu.SemaphoreType.DMA((4 + modes // ROWS,))],
        compiler_params=kernel_params([x.shape for x in held]),
        name="pick_rows",
    )(*pinned(*taken))
    before_layer = lax.ppermute(layer_send, "layer", up_layer)
    before_sub = lax.ppermute(sub_send, "sub", up_sub)
    base, own, side, picked_sub, picked_layer = local_call(
        functools.partial(own_kernel, subs=subs, layers=layers),
        [(modes, row_count), (modes, modes), (modes, modes), (modes, width), (modes, width)],
        (vectors, row_lists, face_springs, masses, interior, layer_send, sub_send, before_layer),
        "own_rows",
        WORK,
    )
    after_sub = lax.ppermute(picked_sub, "sub", down_sub)
    copies, after_send = local_call(
        functools.partial(tile_kernel, row_count=row_count),
        [(subs * layers, modes - ROWS, LANES), (modes, width)],
        (own, side, picked_sub, picked_layer, before_sub),
        "coarse_tiles",
    )
    tiles = lax.all_to_all(copies, ("sub", "layer"), split_axis=0, concat_axis=0, tiled=True)
    after_layer = lax.ppermute(after_send, "layer", down_layer)
    applied, token = local_call(
        functools.partial(scatter_kernel, subs=subs, layers=layers),
        [(modes, row_count), (ROWS, LANES)],
        (base, row_lists, face_springs, sub_send, picked_sub, layer_send, picked_layer)
        + (before_sub, after_sub, before_layer, after_layer),
        "spread_rows",
        WORK,
    )
    diag_strip, left_strip, right_strip = factor_planes(
        tiles.reshape(subs, layers, *tiles.shape[1:]), modes, token
    )
    return (applied[None, None], diag_strip[None], left_strip[None], right_strip[None])


def solution(mesh):
    in_specs = (
        P("sub", "layer", None, None),
        P("sub", "layer", None),
        P("sub", "layer", None, None),
        P("sub", "layer", None, None),
        P("sub", "layer", None, None),
    )
    out_specs = (
        P("sub", "layer", None, None),
        P("sub", "layer", None),
        P("sub", "layer", None),
        P("sub", "layer", None),
    )
    return jax.shard_map(
        per_device, mesh=mesh, in_specs=in_specs, out_specs=out_specs, check_vma=False
    )
```

```python
import functools
import math
import jax
import jax.numpy as jnp
from jax import lax
from jax.experimental import pallas as pl
from jax.experimental.pallas import tpu as pltpu
from jax.sharding import PartitionSpec as P

STRIDES = (1, 3, 27)
HIGHEST = lax.Precision.HIGHEST
LANES = 128
ROWS = 8
UNROLLED_LAYERS = 4
PLANES_AT_ONCE = 4
NARROW_DEPTH = LANES + LANES // 4


def turned_dot(left, right):
    return lax.dot_general(
        left,
        right,
        (((0,), (0,)), ((), ())),
        precision=HIGHEST,
        preferred_element_type=jnp.float32,
    )


PRODUCTS = ((0, 0), (1, 0), (2, 0), (0, 1), (1, 1), (0, 2))


def pieces_of(values):
    first = values.astype(jnp.bfloat16).astype(jnp.float32)
    rest = values - first
    second = rest.astype(jnp.bfloat16).astype(jnp.float32)
    return first, second, rest - second


def single_dot(left, right):
    return lax.dot_general(
        left, right, (((1,), (0,)), ((), ())), preferred_element_type=jnp.float32
    )


def narrow_columns(turned, modes):
    height = turned.shape[0]
    lane = lax.broadcasted_iota(jnp.int32, (height, LANES), 1)
    wide = jnp.concatenate([turned, jnp.zeros((height, LANES - 3 * modes), jnp.float32)], axis=1)
    again = pltpu.roll(wide, 3 * modes, 1)
    left = jnp.where(lane < 3 * modes, wide, jnp.where(lane < 5 * modes, again, 0.0))
    last = jnp.where(lane < modes, wide, 0.0)
    return jnp.concatenate([left, last], axis=1)[:, 0:NARROW_DEPTH].astype(jnp.bfloat16)


def narrow_rows(pieces):
    first, second, third = pieces
    modes, width = first.shape
    gap = jnp.zeros((LANES - 5 * modes, width), jnp.float32)
    tail = jnp.zeros((NARROW_DEPTH - LANES - modes, width), jnp.float32)
    rows = jnp.concatenate([first] * 3 + [second] * 2 + [gap, third, tail], axis=0)
    return rows.astype(jnp.bfloat16)


def plain_dot(left, right):
    return lax.dot_general(
        left,
        right,
        (((1,), (0,)), ((), ())),
        precision=HIGHEST,
        preferred_element_type=jnp.float32,
    )


def spread_row(strip, k):
    return jnp.broadcast_to(strip[k : k + 1, :], strip.shape)


def eliminate_pair(block, columns, pivots, iota, q, k):
    start = q * ROWS
    first, second = columns[start + k], columns[start + k + 1]
    corner, joint = spread_row(first[0], k), spread_row(first[0], k + 1)
    other_corner = spread_row(second[0], k + 1)
    minor = corner * other_corner - joint * joint
    inverse = pl.reciprocal(corner, approx=True)
    other_inverse = corner * pl.reciprocal(minor, approx=True)
    below = [column * inverse for column in first]
    second = [column - below[r] * joint for r, column in enumerate(second)]
    other_below = [column * other_inverse for column in second]
    below[0] = jnp.where(iota > k, below[0], 0.0)
    other_below[0] = jnp.where(iota > k + 1, other_below[0], 0.0)
    for j in range(start + k + 2, len(columns)):
        strip = j // ROWS - q
        head = spread_row(first[strip], j % ROWS)
        other_head = spread_row(second[strip], j % ROWS)
        columns[j] = [
            column - below[strip + r] * head - other_below[strip + r] * other_head
            for r, column in enumerate(columns[j])
        ]
    for t in range(len(block[q])):
        row = spread_row(block[q][t], k)
        for r, lower in enumerate(below):
            block[q + r][t] = block[q + r][t] - lower * row
        row = spread_row(block[q][t], k + 1)
        for r, lower in enumerate(other_below):
            block[q + r][t] = block[q + r][t] - lower * row
    return jnp.where(iota == k, corner, jnp.where(iota == k + 1, minor * inverse, pivots))


def factor_rows(blocks, tiles_per_part, first_row, turned):
    strip_count = len(blocks[0])
    iota = lax.broadcasted_iota(jnp.int32, (ROWS, LANES), 0)
    lane = lax.broadcasted_iota(jnp.int32, (ROWS, LANES), 1)
    blocks = [[list(strip) for strip in block] for block in blocks]
    at_once = len(blocks) <= PLANES_AT_ONCE
    held = [[] for _ in blocks]
    for q in range(strip_count):
        start = q * ROWS
        if q == 0 or not at_once:
            for b, block in enumerate(blocks):
                source = turned(b, block, q)
                for j in range(start, strip_count * ROWS if at_once else start + ROWS):
                    held[b].append(
                        [
                            jnp.broadcast_to(strip[:, j : j + 1], (ROWS, LANES))
                            for strip in source[j // ROWS - q :]
                        ]
                    )
        pivots = [jnp.zeros((ROWS, LANES), jnp.float32) for _ in blocks]
        for k in range(0, ROWS, 2):
            for b, block in enumerate(blocks):
                pivots[b] = eliminate_pair(block, held[b], pivots[b], iota, q, k)
        for b, block in enumerate(blocks):
            scale = lax.rsqrt(pivots[b])
            for t in range(len(block[q])):
                strip = block[q][t] * scale
                if t < tiles_per_part:
                    keep = lane + t * LANES >= iota + (first_row + start)
                    strip = jnp.where(keep, strip, 0.0)
                block[q][t] = strip
    return blocks


def eliminate_panel(grid_ref, planes, modes, order, part, lanes_used, panel, banded):
    per_part = part // LANES
    first_row = panel * modes
    static = isinstance(panel, int)
    if static:
        rows = pl.ds(first_row, modes)
    else:
        rows = pl.ds(pl.multiple_of(first_row, ROWS), modes)
    blocks = []
    for plane in planes:
        panel_rows = grid_ref[plane, rows, 0:lanes_used]
        blocks.append(
            [
                [
                    panel_rows[q * ROWS : (q + 1) * ROWS, t * LANES : (t + 1) * LANES]
                    for t in range(lanes_used // LANES)
                ]
                for q in range(modes // ROWS)
            ]
        )

    def turned(b, block, q):
        found = []
        for strip in block[q:]:
            if static and first_row // LANES == (first_row + modes - 1) // LANES:
                tile = strip[first_row // LANES]
                offset = first_row % LANES
                found.append(tile if offset == 0 else tile[:, offset : offset + modes])
            else:
                wide = jnp.concatenate(strip[:per_part], axis=1)
                found.append(pltpu.roll(wide, lax.rem(part - first_row, part), 1)[:, :LANES])
        return found

    blocks = factor_rows(blocks, per_part, first_row, turned)
    for plane, block in zip(planes, blocks):
        panel_rows = jnp.concatenate([jnp.concatenate(strip, axis=1) for strip in block], axis=0)
        grid_ref[plane, rows, 0:lanes_used] = panel_rows
        if static:
            below = (panel + 1) * modes
            end = min(below + modes, order) if banded else order
            pieces = pieces_of(panel_rows)
            right = narrow_rows(pieces)
            stacked = jnp.concatenate(pieces, axis=0)
            if below < order:
                columns = narrow_columns(stacked[:, 0:part].T[below:end], modes)
                grid_ref[plane, below:end, 0:lanes_used] -= single_dot(columns, right)
        else:
            lane = lax.broadcasted_iota(jnp.int32, (modes, part), 1)
            columns = jnp.where(lane >= first_row + modes, panel_rows[:, 0:part], 0.0)
            update = turned_dot(columns, panel_rows)[0:order]
            grid_ref[plane, :, 0:lanes_used] -= update


def eliminate_planes(grid_ref, planes, modes, order, part, lanes_used, banded=False):
    layers = order // modes
    if layers <= UNROLLED_LAYERS:
        for panel in range(layers):
            eliminate_panel(grid_ref, planes, modes, order, part, lanes_used, panel, banded)
    else:

        def one_panel(panel, carry):
            eliminate_panel(grid_ref, planes, modes, order, part, lanes_used, panel, banded)
            return carry

        lax.fori_loop(0, layers, one_panel, 0)


def update_partners(grid_ref, plane, distance, part, order, has_left):
    left, right = plane - distance, plane + distance
    both = grid_ref[plane, :, part : 3 * part]
    if part > order:
        spare = jnp.zeros((part - order, 2 * part), jnp.float32)
        both = jnp.concatenate([both, spare], axis=0)
    turned = [piece.astype(jnp.bfloat16) for piece in pieces_of(both.T)]
    held = [piece.astype(jnp.bfloat16) for piece in pieces_of(both)]
    held = jnp.concatenate([held[right] for _, right in PRODUCTS], axis=0)

    def product(rows):
        columns = jnp.concatenate([turned[left][rows] for left, _ in PRODUCTS], axis=1)
        return single_dot(columns, held)

    from_right = product(slice(part, part + order))
    grid_ref[right, :, 0:part] -= from_right[:, part : 2 * part]
    grid_ref[right, :, part : 2 * part] = -from_right[:, 0:part]

    def to_left():
        from_left = product(slice(0, order))
        grid_ref[left, :, 0:part] -= from_left[:, 0:part]
        grid_ref[left, :, 2 * part : 3 * part] = -from_left[:, part : 2 * part]

    if isinstance(has_left, bool):
        if has_left:
            to_left()
    else:
        pl.when(has_left)(to_left)


def unpack_tile(packed, modes):
    half = 3 * modes // 2
    upper = packed[:, 0 : 3 * modes]
    lower = jnp.concatenate(
        [packed[0:ROWS, 3 * modes : 3 * modes + half], packed[ROWS:, 3 * modes : 3 * modes + half]],
        axis=1,
    )
    return jnp.concatenate([upper, lower], axis=0)


def pack_tile(tile):
    modes = tile.shape[0]
    half = 3 * modes // 2
    top = modes - ROWS
    upper = tile[0:top]
    lower = jnp.concatenate([tile[top:, 0:half], tile[top:, half:]], axis=0)
    spare = jnp.zeros((top, LANES - 3 * modes - half), jnp.float32)
    return jnp.concatenate([upper, lower, spare], axis=1)


def factor_kernel(tiles_ref, after_ref, diag_ref, left_ref, right_ref, grid_ref, turned_ref):
    subs, layers, _, _ = tiles_ref.shape
    modes, order = diag_ref.shape
    part = grid_ref.shape[2] // 3
    unrolled = layers <= UNROLLED_LAYERS
    del after_ref
    lane = lax.broadcasted_iota(jnp.int32, (modes, part), 1)
    inside = [(lane >= j * modes) & (lane < (j + 1) * modes) for j in range(layers)]

    def place_tiles(s, before):
        tiles = [unpack_tile(tiles_ref[s, j], modes) for j in range(layers)]
        stacked = tiles
        if part > order:
            stacked = tiles + [jnp.zeros((part - order, tiles[0].shape[1]), jnp.float32)]
        turned = jnp.concatenate(stacked, axis=0).T
        for j, tile in enumerate(tiles):
            rows = slice(j * modes, (j + 1) * modes)
            own = jnp.where(inside[j], turned[0:modes], 0.0)
            if j + 1 < layers:
                own = jnp.where(inside[j + 1], turned[modes : 2 * modes], own)
            grid_ref[s, rows, 0:part] = own
            spare = jnp.zeros((modes, part - 3 * modes), jnp.float32)
            wide = jnp.concatenate([tile, spare], axis=1)
            shift = (j - 2) * modes % part
            down = pltpu.roll(wide, shift, 1) if shift else wide
            grid_ref[s, rows, part : 2 * part] = jnp.where(inside[j], down, 0.0)
            down = jnp.where(inside[j], turned[2 * modes : 3 * modes], 0.0)
            grid_ref[before, rows, 2 * part : 3 * part] = down

    place_tiles(0, subs - 1)
    if unrolled:
        for s in range(1, subs):
            place_tiles(s, s - 1)
    else:

        def place_one(s, carry):
            place_tiles(s, s - 1)
            return carry

        lax.fori_loop(1, subs, place_one, 0)

    sub_here, lay_here = lax.axis_index("sub"), lax.axis_index("layer")

    def one_level(distance):
        if unrolled:
            planes = list(range(distance - 1, subs, 2 * distance))
            eliminate_planes(grid_ref, planes, modes, order, part, 3 * part, distance == 1)
            for plane in planes:
                update_partners(grid_ref, plane, distance, part, order, plane >= distance)
        else:

            def one_plane(index, carry):
                plane = distance - 1 + 2 * distance * index
                eliminate_planes(grid_ref, [plane], modes, order, part, 3 * part)
                update_partners(grid_ref, plane, distance, part, order, index > 0)
                return carry

            lax.fori_loop(0, subs // (2 * distance), one_plane, 0)

    one_level(1)
    if subs > 2:
        one_level(2)
    distance = 4
    while distance < subs:
        pl.when(lax.rem(sub_here + 1, distance) == 0)(functools.partial(one_level, distance))
        distance *= 2

    @pl.when(sub_here == subs - 1)
    def _():
        eliminate_planes(grid_ref, [subs - 1], modes, order, part, part)

    strip = pl.ds(pl.multiple_of(lay_here * modes, ROWS), modes)
    for k, out_ref in enumerate((diag_ref, left_ref, right_ref)):
        turned_ref[k] = grid_ref[sub_here, :, k * part : (k + 1) * part].T
        found = turned_ref[k, strip, :]
        out_ref[...] = found if k == 0 else jnp.where(sub_here < subs - 1, found, 0.0)


VMEM_BLOCK = pl.BlockSpec(memory_space=pltpu.VMEM)
HBM_BLOCK = pl.BlockSpec(memory_space=pltpu.HBM)
SPARE_BYTES = 4 * 1024 * 1024
WORK = 8 * 1024 * 1024


def kernel_params(shapes):
    held = sum(4 * math.prod(shape) for shape in shapes)
    return pltpu.CompilerParams(vmem_limit_bytes=min(2 * held + SPARE_BYTES, 60 * 1024 * 1024))


def factor_planes(plane_tiles, modes, after):
    subs, layers, _, _ = plane_tiles.shape
    order = layers * modes
    part = -(-order // LANES) * LANES
    strip = jax.ShapeDtypeStruct((modes, order), jnp.float32)
    scratch = ((subs, order, 3 * part), (3, part, order))
    return pl.pallas_call(
        factor_kernel,
        out_shape=(strip, strip, strip),
        in_specs=[VMEM_BLOCK, VMEM_BLOCK],
        out_specs=(VMEM_BLOCK, VMEM_BLOCK, VMEM_BLOCK),
        scratch_shapes=[pltpu.VMEM(shape, jnp.float32) for shape in scratch],
        compiler_params=kernel_params((plane_tiles.shape,) + scratch),
        name="factor_planes",
    )(plane_tiles, after)


def across_dot(left, right):
    rows, columns = left.shape[0], right.shape[0]

    def stacked(values):
        short = -3 * values.shape[0] % (2 * ROWS)
        spare = [jnp.zeros((short, values.shape[1]), jnp.float32)] if short else []
        return jnp.concatenate(list(pieces_of(values)) + spare, axis=0).astype(jnp.bfloat16)

    found = lax.dot_general(
        stacked(left),
        stacked(right),
        (((1,), (1,)), ((), ())),
        preferred_element_type=jnp.float32,
    )
    total = None
    for b in (2, 1, 0):
        column = found[:, b * columns : (b + 1) * columns]
        for a in (2, 1, 0):
            if (a, b) in PRODUCTS:
                block = column[a * rows : (a + 1) * rows]
                total = block if total is None else total + block
    return total


def pick_lists(vectors_ref, lists_ref, chosen, strip):
    lists = []
    for k in chosen:
        rows = jnp.broadcast_to(lists_ref[k : k + 1, :], (ROWS, LANES))
        lists.append((rows // LANES, rows % LANES))
    found = [jnp.zeros((ROWS, LANES), jnp.float32) for _ in lists]
    for c in range(vectors_ref.shape[1] // LANES):
        tile = vectors_ref[strip, c * LANES : (c + 1) * LANES]
        for i, (tile_of, lane_of) in enumerate(lists):
            moved = jnp.take_along_axis(tile, lane_of, axis=1, mode="promise_in_bounds")
            found[i] = jnp.where(tile_of == c, moved, found[i])
    return found


def mode_strips(modes):
    return [slice(first, first + ROWS) for first in range(0, modes, ROWS)]


def pick_kernel(
    vectors_in, lists_in, face_in, mass_in, inner_in,
    vectors_ref, lists_ref, face_ref, mass_ref, inner_ref, layer_ref, sub_ref, sems
):
    strips = mode_strips(vectors_ref.shape[0])
    pairs = [(lists_in, lists_ref)]
    for strip in strips:
        rows = pl.ds(strip.start, ROWS)
        pairs.append((vectors_in.at[rows], vectors_ref.at[rows]))
    pairs += [(face_in, face_ref), (mass_in, mass_ref), (inner_in, inner_ref)]
    copies = [pltpu.make_async_copy(a, b, sems.at[i]) for i, (a, b) in enumerate(pairs)]
    for copy in copies:
        copy.start()
    copies[0].wait()
    copies[1 + len(strips)].wait()
    for k, send_ref in ((1, layer_ref), (0, sub_ref)):
        send_ref[vectors_ref.shape[0] :] = jnp.broadcast_to(face_ref[k : k + 1, :], (ROWS, LANES))
    for copy, strip in zip(copies[1:], strips):
        copy.wait()
        layer_ref[strip], sub_ref[strip] = pick_lists(vectors_ref, lists_ref, (2, 0), strip)
    for copy in copies[2 + len(strips) :]:
        copy.wait()


def spread_weights(weights_ref, first, count, height):
    rows = [
        jnp.broadcast_to(weights_ref[first + c : first + c + 1, :], (ROWS, LANES))
        for c in range(count)
    ]
    wide = jnp.concatenate(rows, axis=1)
    return jnp.concatenate([wide] * (height // ROWS), axis=0)


def own_kernel(
    vectors_ref, lists_ref, face_ref, mass_ref, inner_ref, layer_ref, sub_ref, theirs_ref,
    base_ref, own_ref, side_ref, before_sub_ref, before_layer_ref, *, subs, layers
):
    vectors = vectors_ref[...]
    modes, row_count = vectors.shape
    tiles = row_count // LANES
    for strip in mode_strips(modes):
        before_sub_ref[strip], before_layer_ref[strip] = pick_lists(
            vectors_ref, lists_ref, (1, 3), strip
        )
    places = lax.broadcasted_iota(jnp.int32, (modes, row_count), 1)
    base = spread_weights(mass_ref, 0, tiles, modes) * vectors
    for k, t in enumerate(STRIDES):
        edge_weight = spread_weights(inner_ref, k * tiles, tiles, modes)
        edge_weight = jnp.where(places < row_count - t, edge_weight, 0.0)
        fluxes = edge_weight * (vectors - pltpu.roll(vectors, row_count - t, 1))
        base = base + fluxes - pltpu.roll(fluxes, t, 1)
    base_ref[...] = base
    own = across_dot(vectors, base)
    for k, axis, ends, send_ref in ((0, "sub", subs - 1, sub_ref), (1, "layer", layers - 1, layer_ref)):
        springs = jnp.where(lax.axis_index(axis) < ends, face_ref[k : k + 1, :], 0.0)
        picked = send_ref[0:modes]
        own = own + across_dot(picked, springs * picked)
    mine, theirs = before_layer_ref[...], theirs_ref[0:modes]
    sprung = theirs_ref[modes : modes + 1] * mine
    side = across_dot(sprung, jnp.concatenate([mine, theirs], axis=0))
    own_ref[...] = own + side[:, 0:modes]
    side_ref[...] = -side[:, modes:] * (1.0 / row_count)


def tile_kernel(
    own_ref, side_ref, mine_sub_ref, sub_ref, copies_ref, sub_send_ref, *, row_count
):
    modes = own_ref.shape[0]
    inverse = 1.0 / row_count
    mine, theirs = mine_sub_ref[...], sub_ref[0:modes]
    sprung = sub_ref[modes : modes + 1] * mine
    down = across_dot(sprung, jnp.concatenate([mine, theirs], axis=0))
    diag_tile = (own_ref[...] + down[:, 0:modes]) * inverse
    side_tile = side_ref[...]
    down_tile = -down[:, modes:] * inverse
    packed = pack_tile(jnp.concatenate([diag_tile, side_tile, down_tile], axis=1))
    for s in range(copies_ref.shape[0]):
        copies_ref[s] = packed
    sub_send_ref[...] = mine_sub_ref[...]


def scatter_kernel(
    base_ref, lists_ref, face_ref, up_sub_ref, down_sub_ref, up_layer_ref, down_layer_ref, before_sub_ref, after_sub_ref,
    before_layer_ref, after_layer_ref, applied_ref, token_ref, *, subs, layers
):
    modes, row_count = base_ref.shape
    width = 2 * LANES
    springs = [
        jnp.where(lax.axis_index("sub") < subs - 1, face_ref[0:1, :], 0.0),
        before_sub_ref[modes : modes + 1, :],
        jnp.where(lax.axis_index("layer") < layers - 1, face_ref[1:2, :], 0.0),
        before_layer_ref[modes : modes + 1, :],
    ]
    partners = [
        after_sub_ref[...],
        before_sub_ref[0:modes, :],
        after_layer_ref[...],
        before_layer_ref[0:modes, :],
    ]
    picked = [up_sub_ref[0:modes], down_sub_ref[...], up_layer_ref[0:modes], down_layer_ref[...]]
    pulls = jnp.concatenate([springs[k] * (picked[k] - partners[k]) for k in range(4)], axis=1)
    rows = jnp.concatenate([lists_ref[k : k + 1, :] for k in range(4)], axis=1)
    block_of, lane_of = rows // width, rows % width
    lanes = lax.broadcasted_iota(jnp.int32, (width, rows.shape[1]), 0)
    onehot = jnp.where(lanes == lane_of, 1.0, 0.0).astype(jnp.bfloat16)
    total = None
    rest = pulls
    for _ in range(3):
        piece = rest.astype(jnp.bfloat16).astype(jnp.float32)
        rest = rest - piece
        spread = jnp.concatenate(
            [jnp.where(block_of == h, piece, 0.0) for h in range(row_count // width)], axis=0
        ).astype(jnp.bfloat16)
        moved = lax.dot_general(
            spread, onehot, (((1,), (1,)), ((), ())), preferred_element_type=jnp.float32
        )
        total = moved if total is None else total + moved
    for h in range(row_count // width):
        lanes = slice(h * width, (h + 1) * width)
        applied_ref[:, lanes] = base_ref[:, lanes] + total[h * modes : (h + 1) * modes]
    token_ref[...] = jnp.zeros_like(token_ref)


def local_call(body, outputs, operands, name, work=0):
    shapes = tuple(jax.ShapeDtypeStruct(shape, jnp.float32) for shape in outputs)
    return pl.pallas_call(
        body,
        out_shape=shapes,
        in_specs=[VMEM_BLOCK] * len(operands),
        out_specs=tuple(VMEM_BLOCK for _ in shapes),
        compiler_params=kernel_params([x.shape for x in operands] + list(outputs)),
        cost_estimate=pl.CostEstimate(flops=work, bytes_accessed=work, transcendentals=0),
        name=name,
    )(*operands)


def per_device(eigen_vectors, row_mass, inner_weight, face_weight, margin_rows):
    vectors = eigen_vectors[0, 0]
    row_lists = margin_rows[0, 0]
    face_springs = face_weight[0, 0]
    modes, row_count = vectors.shape
    width = row_lists.shape[-1]
    subs = lax.axis_size("sub")
    layers = lax.axis_size("layer")
    up_sub = [(i, i + 1) for i in range(subs - 1)]
    up_layer = [(i, i + 1) for i in range(layers - 1)]
    down_sub = [(i + 1, i) for i in range(subs - 1)]
    down_layer = [(i + 1, i) for i in range(layers - 1)]
    def pinned(*arrays):
        return [pltpu.with_memory_space_constraint(x, pltpu.HBM) for x in arrays]

    def shaped(*shapes):
        return tuple(jax.ShapeDtypeStruct(shape, jnp.float32) for shape in shapes)

    masses = row_mass.reshape(row_count // LANES, LANES)
    interior = inner_weight.reshape(-1, LANES)
    taken = (vectors, row_lists, face_springs, masses, interior)
    held = tuple(jax.ShapeDtypeStruct(x.shape, x.dtype) for x in taken)
    held += shaped((modes + ROWS, width), (modes + ROWS, width))
    vectors, row_lists, face_springs, masses, interior, layer_send, sub_send = pl.pallas_call(
        pick_kernel,
        out_shape=held,
        in_specs=[HBM_BLOCK] * len(taken),
        out_specs=(VMEM_BLOCK,) * len(held),
        scratch_shapes=[pltpu.SemaphoreType.DMA((4 + modes // ROWS,))],
        compiler_params=kernel_params([x.shape for x in held]),
        name="pick_rows",
    )(*pinned(*taken))
    before_layer = lax.ppermute(layer_send, "layer", up_layer)
    before_sub = lax.ppermute(sub_send, "sub", up_sub)
    base, own, side, picked_sub, picked_layer = local_call(
        functools.partial(own_kernel, subs=subs, layers=layers),
        [(modes, row_count), (modes, modes), (modes, modes), (modes, width), (modes, width)],
        (vectors, row_lists, face_springs, masses, interior, layer_send, sub_send, before_layer),
        "own_rows",
        WORK,
    )
    after_layer = lax.ppermute(picked_layer, "layer", down_layer)
    copies, after_send = local_call(
        functools.partial(tile_kernel, row_count=row_count),
        [(subs * layers, modes - ROWS, LANES), (modes, width)],
        (own, side, picked_sub, before_sub),
        "coarse_tiles",
    )
    tiles = lax.all_to_all(copies, ("sub", "layer"), split_axis=0, concat_axis=0, tiled=True)
    after_sub = lax.ppermute(after_send, "sub", down_sub)
    applied, token = local_call(
        functools.partial(scatter_kernel, subs=subs, layers=layers),
        [(modes, row_count), (ROWS, LANES)],
        (base, row_lists, face_springs, sub_send, picked_sub, layer_send, picked_layer)
        + (before_sub, after_sub, before_layer, after_layer),
        "spread_rows",
        WORK,
    )
    diag_strip, left_strip, right_strip = factor_planes(
        tiles.reshape(subs, layers, *tiles.shape[1:]), modes, token
    )
    return (applied[None, None], diag_strip[None], left_strip[None], right_strip[None])


def solution(mesh):
    in_specs = (
        P("sub", "layer", None, None),
        P("sub", "layer", None),
        P("sub", "layer", None, None),
        P("sub", "layer", None, None),
        P("sub", "layer", None, None),
    )
    out_specs = (
        P("sub", "layer", None, None),
        P("sub", "layer", None),
        P("sub", "layer", None),
        P("sub", "layer", None),
    )
    return jax.shard_map(
        per_device, mesh=mesh, in_specs=in_specs, out_specs=out_specs, check_vma=False
    )
```

```python
import functools
import math
import jax
import jax.numpy as jnp
from jax import lax
from jax.experimental import pallas as pl
from jax.experimental.pallas import tpu as pltpu
from jax.sharding import PartitionSpec as P

STRIDES = (1, 3, 27)
HIGHEST = lax.Precision.HIGHEST
LANES = 128
ROWS = 8
UNROLLED_LAYERS = 4
PLANES_AT_ONCE = 1
NARROW_DEPTH = LANES + LANES // 4


def turned_dot(left, right):
    return lax.dot_general(
        left,
        right,
        (((0,), (0,)), ((), ())),
        precision=HIGHEST,
        preferred_element_type=jnp.float32,
    )


PRODUCTS = ((0, 0), (1, 0), (2, 0), (0, 1), (1, 1), (0, 2))


def pieces_of(values):
    first = values.astype(jnp.bfloat16).astype(jnp.float32)
    rest = values - first
    second = rest.astype(jnp.bfloat16).astype(jnp.float32)
    return first, second, rest - second


def single_dot(left, right):
    return lax.dot_general(
        left, right, (((1,), (0,)), ((), ())), preferred_element_type=jnp.float32
    )


def narrow_columns(turned, modes):
    height = turned.shape[0]
    lane = lax.broadcasted_iota(jnp.int32, (height, LANES), 1)
    wide = jnp.concatenate([turned, jnp.zeros((height, LANES - 3 * modes), jnp.float32)], axis=1)
    again = pltpu.roll(wide, 3 * modes, 1)
    left = jnp.where(lane < 3 * modes, wide, jnp.where(lane < 5 * modes, again, 0.0))
    last = jnp.where(lane < modes, wide, 0.0)
    return jnp.concatenate([left, last], axis=1)[:, 0:NARROW_DEPTH].astype(jnp.bfloat16)


def narrow_rows(pieces):
    first, second, third = pieces
    modes, width = first.shape
    gap = jnp.zeros((LANES - 5 * modes, width), jnp.float32)
    tail = jnp.zeros((NARROW_DEPTH - LANES - modes, width), jnp.float32)
    rows = jnp.concatenate([first] * 3 + [second] * 2 + [gap, third, tail], axis=0)
    return rows.astype(jnp.bfloat16)


def plain_dot(left, right):
    return lax.dot_general(
        left,
        right,
        (((1,), (0,)), ((), ())),
        precision=HIGHEST,
        preferred_element_type=jnp.float32,
    )


def spread_row(strip, k):
    return jnp.broadcast_to(strip[k : k + 1, :], strip.shape)


def eliminate_pair(block, columns, pivots, iota, q, k):
    start = q * ROWS
    first, second = columns[start + k], columns[start + k + 1]
    corner, joint = spread_row(first[0], k), spread_row(first[0], k + 1)
    other_corner = spread_row(second[0], k + 1)
    minor = corner * other_corner - joint * joint
    inverse = pl.reciprocal(corner, approx=True)
    other_inverse = corner * pl.reciprocal(minor, approx=True)
    below = [column * inverse for column in first]
    second = [column - below[r] * joint for r, column in enumerate(second)]
    other_below = [column * other_inverse for column in second]
    below[0] = jnp.where(iota > k, below[0], 0.0)
    other_below[0] = jnp.where(iota > k + 1, other_below[0], 0.0)
    for j in range(start + k + 2, len(columns)):
        strip = j // ROWS - q
        head = spread_row(first[strip], j % ROWS)
        other_head = spread_row(second[strip], j % ROWS)
        columns[j] = [
            column - below[strip + r] * head - other_below[strip + r] * other_head
            for r, column in enumerate(columns[j])
        ]
    for t in range(len(block[q])):
        row = spread_row(block[q][t], k)
        for r, lower in enumerate(below):
            block[q + r][t] = block[q + r][t] - lower * row
        row = spread_row(block[q][t], k + 1)
        for r, lower in enumerate(other_below):
            block[q + r][t] = block[q + r][t] - lower * row
    return jnp.where(iota == k, corner, jnp.where(iota == k + 1, minor * inverse, pivots))


def factor_rows(blocks, tiles_per_part, first_row, turned):
    strip_count = len(blocks[0])
    iota = lax.broadcasted_iota(jnp.int32, (ROWS, LANES), 0)
    lane = lax.broadcasted_iota(jnp.int32, (ROWS, LANES), 1)
    blocks = [[list(strip) for strip in block] for block in blocks]
    at_once = len(blocks) <= PLANES_AT_ONCE
    held = [[] for _ in blocks]
    for q in range(strip_count):
        start = q * ROWS
        if q == 0 or not at_once:
            for b, block in enumerate(blocks):
                source = turned(b, block, q)
                for j in range(start, strip_count * ROWS if at_once else start + ROWS):
                    held[b].append(
                        [
                            jnp.broadcast_to(strip[:, j : j + 1], (ROWS, LANES))
                            for strip in source[j // ROWS - q :]
                        ]
                    )
        pivots = [jnp.zeros((ROWS, LANES), jnp.float32) for _ in blocks]
        for k in range(0, ROWS, 2):
            for b, block in enumerate(blocks):
                pivots[b] = eliminate_pair(block, held[b], pivots[b], iota, q, k)
        for b, block in enumerate(blocks):
            scale = lax.rsqrt(pivots[b])
            for t in range(len(block[q])):
                strip = block[q][t] * scale
                if t < tiles_per_part:
                    keep = lane + t * LANES >= iota + (first_row + start)
                    strip = jnp.where(keep, strip, 0.0)
                block[q][t] = strip
    return blocks


def eliminate_panel(grid_ref, planes, modes, order, part, lanes_used, panel, banded):
    per_part = part // LANES
    first_row = panel * modes
    static = isinstance(panel, int)
    if static:
        rows = pl.ds(first_row, modes)
    else:
        rows = pl.ds(pl.multiple_of(first_row, ROWS), modes)
    blocks = []
    for plane in planes:
        panel_rows = grid_ref[plane, rows, 0:lanes_used]
        blocks.append(
            [
                [
                    panel_rows[q * ROWS : (q + 1) * ROWS, t * LANES : (t + 1) * LANES]
                    for t in range(lanes_used // LANES)
                ]
                for q in range(modes // ROWS)
            ]
        )

    def turned(b, block, q):
        found = []
        for strip in block[q:]:
            if static and first_row // LANES == (first_row + modes - 1) // LANES:
                tile = strip[first_row // LANES]
                offset = first_row % LANES
                found.append(tile if offset == 0 else tile[:, offset : offset + modes])
            else:
                wide = jnp.concatenate(strip[:per_part], axis=1)
                found.append(pltpu.roll(wide, lax.rem(part - first_row, part), 1)[:, :LANES])
        return found

    blocks = factor_rows(blocks, per_part, first_row, turned)
    for plane, block in zip(planes, blocks):
        panel_rows = jnp.concatenate([jnp.concatenate(strip, axis=1) for strip in block], axis=0)
        grid_ref[plane, rows, 0:lanes_used] = panel_rows
        if static:
            below = (panel + 1) * modes
            end = min(below + modes, order) if banded else order
            pieces = pieces_of(panel_rows)
            right = narrow_rows(pieces)
            stacked = jnp.concatenate(pieces, axis=0)
            if below < order:
                columns = narrow_columns(stacked[:, 0:part].T[below:end], modes)
                grid_ref[plane, below:end, 0:lanes_used] -= single_dot(columns, right)
        else:
            lane = lax.broadcasted_iota(jnp.int32, (modes, part), 1)
            columns = jnp.where(lane >= first_row + modes, panel_rows[:, 0:part], 0.0)
            update = turned_dot(columns, panel_rows)[0:order]
            grid_ref[plane, :, 0:lanes_used] -= update


def eliminate_planes(grid_ref, planes, modes, order, part, lanes_used, banded=False):
    layers = order // modes
    if layers <= UNROLLED_LAYERS:
        for panel in range(layers):
            eliminate_panel(grid_ref, planes, modes, order, part, lanes_used, panel, banded)
    else:

        def one_panel(panel, carry):
            eliminate_panel(grid_ref, planes, modes, order, part, lanes_used, panel, banded)
            return carry

        lax.fori_loop(0, layers, one_panel, 0)


def update_partners(grid_ref, plane, distance, part, order, has_left):
    left, right = plane - distance, plane + distance
    both = grid_ref[plane, :, part : 3 * part]
    if part > order:
        spare = jnp.zeros((part - order, 2 * part), jnp.float32)
        both = jnp.concatenate([both, spare], axis=0)
    turned = [piece.astype(jnp.bfloat16) for piece in pieces_of(both.T)]
    held = [piece.astype(jnp.bfloat16) for piece in pieces_of(both)]
    held = jnp.concatenate([held[right] for _, right in PRODUCTS], axis=0)

    def product(rows):
        columns = jnp.concatenate([turned[left][rows] for left, _ in PRODUCTS], axis=1)
        return single_dot(columns, held)

    from_right = product(slice(part, part + order))
    grid_ref[right, :, 0:part] -= from_right[:, part : 2 * part]
    grid_ref[right, :, part : 2 * part] = -from_right[:, 0:part]

    def to_left():
        from_left = product(slice(0, order))
        grid_ref[left, :, 0:part] -= from_left[:, 0:part]
        grid_ref[left, :, 2 * part : 3 * part] = -from_left[:, part : 2 * part]

    if isinstance(has_left, bool):
        if has_left:
            to_left()
    else:
        pl.when(has_left)(to_left)


def unpack_tile(packed, modes):
    half = 3 * modes // 2
    upper = packed[:, 0 : 3 * modes]
    lower = jnp.concatenate(
        [packed[0:ROWS, 3 * modes : 3 * modes + half], packed[ROWS:, 3 * modes : 3 * modes + half]],
        axis=1,
    )
    return jnp.concatenate([upper, lower], axis=0)


def pack_tile(tile):
    modes = tile.shape[0]
    half = 3 * modes // 2
    top = modes - ROWS
    upper = tile[0:top]
    lower = jnp.concatenate([tile[top:, 0:half], tile[top:, half:]], axis=0)
    spare = jnp.zeros((top, LANES - 3 * modes - half), jnp.float32)
    return jnp.concatenate([upper, lower, spare], axis=1)


def factor_kernel(tiles_ref, after_ref, diag_ref, left_ref, right_ref, grid_ref, turned_ref):
    subs, layers, _, _ = tiles_ref.shape
    modes, order = diag_ref.shape
    part = grid_ref.shape[2] // 3
    unrolled = layers <= UNROLLED_LAYERS
    del after_ref
    lane = lax.broadcasted_iota(jnp.int32, (modes, part), 1)
    inside = [(lane >= j * modes) & (lane < (j + 1) * modes) for j in range(layers)]

    def place_tiles(s, before):
        tiles = [unpack_tile(tiles_ref[s, j], modes) for j in range(layers)]
        stacked = tiles
        if part > order:
            stacked = tiles + [jnp.zeros((part - order, tiles[0].shape[1]), jnp.float32)]
        turned = jnp.concatenate(stacked, axis=0).T
        for j, tile in enumerate(tiles):
            rows = slice(j * modes, (j + 1) * modes)
            own = jnp.where(inside[j], turned[0:modes], 0.0)
            if j + 1 < layers:
                own = jnp.where(inside[j + 1], turned[modes : 2 * modes], own)
            grid_ref[s, rows, 0:part] = own
            spare = jnp.zeros((modes, part - 3 * modes), jnp.float32)
            wide = jnp.concatenate([tile, spare], axis=1)
            shift = (j - 2) * modes % part
            down = pltpu.roll(wide, shift, 1) if shift else wide
            grid_ref[s, rows, part : 2 * part] = jnp.where(inside[j], down, 0.0)
            down = jnp.where(inside[j], turned[2 * modes : 3 * modes], 0.0)
            grid_ref[before, rows, 2 * part : 3 * part] = down

    place_tiles(0, subs - 1)
    if unrolled:
        for s in range(1, subs):
            place_tiles(s, s - 1)
    else:

        def place_one(s, carry):
            place_tiles(s, s - 1)
            return carry

        lax.fori_loop(1, subs, place_one, 0)

    sub_here, lay_here = lax.axis_index("sub"), lax.axis_index("layer")

    def one_level(distance):
        if unrolled:
            planes = list(range(distance - 1, subs, 2 * distance))
            eliminate_planes(grid_ref, planes, modes, order, part, 3 * part, distance == 1)
            for plane in planes:
                update_partners(grid_ref, plane, distance, part, order, plane >= distance)
        else:

            def one_plane(index, carry):
                plane = distance - 1 + 2 * distance * index
                eliminate_planes(grid_ref, [plane], modes, order, part, 3 * part)
                update_partners(grid_ref, plane, distance, part, order, index > 0)
                return carry

            lax.fori_loop(0, subs // (2 * distance), one_plane, 0)

    one_level(1)
    if subs > 2:
        one_level(2)
    distance = 4
    while distance < subs:
        pl.when(lax.rem(sub_here + 1, distance) == 0)(functools.partial(one_level, distance))
        distance *= 2

    @pl.when(sub_here == subs - 1)
    def _():
        eliminate_planes(grid_ref, [subs - 1], modes, order, part, part)

    strip = pl.ds(pl.multiple_of(lay_here * modes, ROWS), modes)
    for k, out_ref in enumerate((diag_ref, left_ref, right_ref)):
        turned_ref[k] = grid_ref[sub_here, :, k * part : (k + 1) * part].T
        found = turned_ref[k, strip, :]
        out_ref[...] = found if k == 0 else jnp.where(sub_here < subs - 1, found, 0.0)


VMEM_BLOCK = pl.BlockSpec(memory_space=pltpu.VMEM)
HBM_BLOCK = pl.BlockSpec(memory_space=pltpu.HBM)
SPARE_BYTES = 4 * 1024 * 1024
WORK = 8 * 1024 * 1024


def kernel_params(shapes):
    held = sum(4 * math.prod(shape) for shape in shapes)
    return pltpu.CompilerParams(vmem_limit_bytes=min(2 * held + SPARE_BYTES, 60 * 1024 * 1024))


def factor_planes(plane_tiles, modes, after):
    subs, layers, _, _ = plane_tiles.shape
    order = layers * modes
    part = -(-order // LANES) * LANES
    strip = jax.ShapeDtypeStruct((modes, order), jnp.float32)
    scratch = ((subs, order, 3 * part), (3, part, order))
    return pl.pallas_call(
        factor_kernel,
        out_shape=(strip, strip, strip),
        in_specs=[VMEM_BLOCK, VMEM_BLOCK],
        out_specs=(VMEM_BLOCK, VMEM_BLOCK, VMEM_BLOCK),
        scratch_shapes=[pltpu.VMEM(shape, jnp.float32) for shape in scratch],
        compiler_params=kernel_params((plane_tiles.shape,) + scratch),
        name="factor_planes",
    )(plane_tiles, after)


def across_dot(left, right):
    rows, columns = left.shape[0], right.shape[0]

    def stacked(values):
        short = -3 * values.shape[0] % (2 * ROWS)
        spare = [jnp.zeros((short, values.shape[1]), jnp.float32)] if short else []
        return jnp.concatenate(list(pieces_of(values)) + spare, axis=0).astype(jnp.bfloat16)

    found = lax.dot_general(
        stacked(left),
        stacked(right),
        (((1,), (1,)), ((), ())),
        preferred_element_type=jnp.float32,
    )
    total = None
    for b in (2, 1, 0):
        column = found[:, b * columns : (b + 1) * columns]
        for a in (2, 1, 0):
            if (a, b) in PRODUCTS:
                block = column[a * rows : (a + 1) * rows]
                total = block if total is None else total + block
    return total


def pick_lists(vectors_ref, lists_ref, chosen, strip):
    lists = []
    for k in chosen:
        rows = jnp.broadcast_to(lists_ref[k : k + 1, :], (ROWS, LANES))
        lists.append((rows // LANES, rows % LANES))
    found = [jnp.zeros((ROWS, LANES), jnp.float32) for _ in lists]
    for c in range(vectors_ref.shape[1] // LANES):
        tile = vectors_ref[strip, c * LANES : (c + 1) * LANES]
        for i, (tile_of, lane_of) in enumerate(lists):
            moved = jnp.take_along_axis(tile, lane_of, axis=1, mode="promise_in_bounds")
            found[i] = jnp.where(tile_of == c, moved, found[i])
    return found


def mode_strips(modes):
    return [slice(first, first + ROWS) for first in range(0, modes, ROWS)]


def pick_kernel(
    vectors_in, lists_in, face_in, mass_in, inner_in,
    vectors_ref, lists_ref, face_ref, mass_ref, inner_ref, layer_ref, sub_ref, sems
):
    strips = mode_strips(vectors_ref.shape[0])
    pairs = [(lists_in, lists_ref)]
    for strip in strips:
        rows = pl.ds(strip.start, ROWS)
        pairs.append((vectors_in.at[rows], vectors_ref.at[rows]))
    pairs += [(face_in, face_ref), (mass_in, mass_ref), (inner_in, inner_ref)]
    copies = [pltpu.make_async_copy(a, b, sems.at[i]) for i, (a, b) in enumerate(pairs)]
    for copy in copies:
        copy.start()
    copies[0].wait()
    copies[1 + len(strips)].wait()
    for k, send_ref in ((1, layer_ref), (0, sub_ref)):
        send_ref[vectors_ref.shape[0] :] = jnp.broadcast_to(face_ref[k : k + 1, :], (ROWS, LANES))
    for copy, strip in zip(copies[1:], strips):
        copy.wait()
        layer_ref[strip], sub_ref[strip] = pick_lists(vectors_ref, lists_ref, (2, 0), strip)
    for copy in copies[2 + len(strips) :]:
        copy.wait()


def spread_weights(weights_ref, first, count, height):
    rows = [
        jnp.broadcast_to(weights_ref[first + c : first + c + 1, :], (ROWS, LANES))
        for c in range(count)
    ]
    wide = jnp.concatenate(rows, axis=1)
    return jnp.concatenate([wide] * (height // ROWS), axis=0)


def own_kernel(
    vectors_ref, lists_ref, face_ref, mass_ref, inner_ref, layer_ref, sub_ref, theirs_ref,
    base_ref, own_ref, side_ref, before_sub_ref, before_layer_ref, *, subs, layers
):
    vectors = vectors_ref[...]
    modes, row_count = vectors.shape
    tiles = row_count // LANES
    for strip in mode_strips(modes):
        before_sub_ref[strip], before_layer_ref[strip] = pick_lists(
            vectors_ref, lists_ref, (1, 3), strip
        )
    places = lax.broadcasted_iota(jnp.int32, (modes, row_count), 1)
    base = spread_weights(mass_ref, 0, tiles, modes) * vectors
    for k, t in enumerate(STRIDES):
        edge_weight = spread_weights(inner_ref, k * tiles, tiles, modes)
        edge_weight = jnp.where(places < row_count - t, edge_weight, 0.0)
        fluxes = edge_weight * (vectors - pltpu.roll(vectors, row_count - t, 1))
        base = base + fluxes - pltpu.roll(fluxes, t, 1)
    base_ref[...] = base
    own = across_dot(vectors, base)
    for k, axis, ends, send_ref in ((0, "sub", subs - 1, sub_ref), (1, "layer", layers - 1, layer_ref)):
        springs = jnp.where(lax.axis_index(axis) < ends, face_ref[k : k + 1, :], 0.0)
        picked = send_ref[0:modes]
        own = own + across_dot(picked, springs * picked)
    mine, theirs = before_layer_ref[...], theirs_ref[0:modes]
    sprung = theirs_ref[modes : modes + 1] * mine
    side = across_dot(sprung, jnp.concatenate([mine, theirs], axis=0))
    own_ref[...] = own + side[:, 0:modes]
    side_ref[...] = -side[:, modes:] * (1.0 / row_count)


def tile_kernel(
    own_ref, side_ref, mine_sub_ref, sub_ref, copies_ref, sub_send_ref, *, row_count
):
    modes = own_ref.shape[0]
    inverse = 1.0 / row_count
    mine, theirs = mine_sub_ref[...], sub_ref[0:modes]
    sprung = sub_ref[modes : modes + 1] * mine
    down = across_dot(sprung, jnp.concatenate([mine, theirs], axis=0))
    diag_tile = (own_ref[...] + down[:, 0:modes]) * inverse
    side_tile = side_ref[...]
    down_tile = -down[:, modes:] * inverse
    packed = pack_tile(jnp.concatenate([diag_tile, side_tile, down_tile], axis=1))
    for s in range(copies_ref.shape[0]):
        copies_ref[s] = packed
    sub_send_ref[...] = mine_sub_ref[...]


def scatter_kernel(
    base_ref, lists_ref, face_ref, up_sub_ref, down_sub_ref, up_layer_ref, down_layer_ref, before_sub_ref, after_sub_ref,
    before_layer_ref, after_layer_ref, applied_ref, token_ref, *, subs, layers
):
    modes, row_count = base_ref.shape
    width = 2 * LANES
    springs = [
        jnp.where(lax.axis_index("sub") < subs - 1, face_ref[0:1, :], 0.0),
        before_sub_ref[modes : modes + 1, :],
        jnp.where(lax.axis_index("layer") < layers - 1, face_ref[1:2, :], 0.0),
        before_layer_ref[modes : modes + 1, :],
    ]
    partners = [
        after_sub_ref[...],
        before_sub_ref[0:modes, :],
        after_layer_ref[...],
        before_layer_ref[0:modes, :],
    ]
    picked = [up_sub_ref[0:modes], down_sub_ref[...], up_layer_ref[0:modes], down_layer_ref[...]]
    pulls = jnp.concatenate([springs[k] * (picked[k] - partners[k]) for k in range(4)], axis=1)
    rows = jnp.concatenate([lists_ref[k : k + 1, :] for k in range(4)], axis=1)
    block_of, lane_of = rows // width, rows % width
    lanes = lax.broadcasted_iota(jnp.int32, (width, rows.shape[1]), 0)
    onehot = jnp.where(lanes == lane_of, 1.0, 0.0).astype(jnp.bfloat16)
    total = None
    rest = pulls
    for _ in range(3):
        piece = rest.astype(jnp.bfloat16).astype(jnp.float32)
        rest = rest - piece
        spread = jnp.concatenate(
            [jnp.where(block_of == h, piece, 0.0) for h in range(row_count // width)], axis=0
        ).astype(jnp.bfloat16)
        moved = lax.dot_general(
            spread, onehot, (((1,), (1,)), ((), ())), preferred_element_type=jnp.float32
        )
        total = moved if total is None else total + moved
    for h in range(row_count // width):
        lanes = slice(h * width, (h + 1) * width)
        applied_ref[:, lanes] = base_ref[:, lanes] + total[h * modes : (h + 1) * modes]
    token_ref[...] = jnp.zeros_like(token_ref)


def local_call(body, outputs, operands, name, work=0):
    shapes = tuple(jax.ShapeDtypeStruct(shape, jnp.float32) for shape in outputs)
    return pl.pallas_call(
        body,
        out_shape=shapes,
        in_specs=[VMEM_BLOCK] * len(operands),
        out_specs=tuple(VMEM_BLOCK for _ in shapes),
        compiler_params=kernel_params([x.shape for x in operands] + list(outputs)),
        cost_estimate=pl.CostEstimate(flops=work, bytes_accessed=work, transcendentals=0),
        name=name,
    )(*operands)


def per_device(eigen_vectors, row_mass, inner_weight, face_weight, margin_rows):
    vectors = eigen_vectors[0, 0]
    row_lists = margin_rows[0, 0]
    face_springs = face_weight[0, 0]
    modes, row_count = vectors.shape
    width = row_lists.shape[-1]
    subs = lax.axis_size("sub")
    layers = lax.axis_size("layer")
    up_sub = [(i, i + 1) for i in range(subs - 1)]
    up_layer = [(i, i + 1) for i in range(layers - 1)]
    down_sub = [(i + 1, i) for i in range(subs - 1)]
    down_layer = [(i + 1, i) for i in range(layers - 1)]
    def pinned(*arrays):
        return [pltpu.with_memory_space_constraint(x, pltpu.HBM) for x in arrays]

    def shaped(*shapes):
        return tuple(jax.ShapeDtypeStruct(shape, jnp.float32) for shape in shapes)

    masses = row_mass.reshape(row_count // LANES, LANES)
    interior = inner_weight.reshape(-1, LANES)
    taken = (vectors, row_lists, face_springs, masses, interior)
    held = tuple(jax.ShapeDtypeStruct(x.shape, x.dtype) for x in taken)
    held += shaped((modes + ROWS, width), (modes + ROWS, width))
    vectors, row_lists, face_springs, masses, interior, layer_send, sub_send = pl.pallas_call(
        pick_kernel,
        out_shape=held,
        in_specs=[HBM_BLOCK] * len(taken),
        out_specs=(VMEM_BLOCK,) * len(held),
        scratch_shapes=[pltpu.SemaphoreType.DMA((4 + modes // ROWS,))],
        compiler_params=kernel_params([x.shape for x in held]),
        name="pick_rows",
    )(*pinned(*taken))
    before_layer = lax.ppermute(layer_send, "layer", up_layer)
    before_sub = lax.ppermute(sub_send, "sub", up_sub)
    base, own, side, picked_sub, picked_layer = local_call(
        functools.partial(own_kernel, subs=subs, layers=layers),
        [(modes, row_count), (modes, modes), (modes, modes), (modes, width), (modes, width)],
        (vectors, row_lists, face_springs, masses, interior, layer_send, sub_send, before_layer),
        "own_rows",
        WORK,
    )
    after_layer = lax.ppermute(picked_layer, "layer", down_layer)
    copies, after_send = local_call(
        functools.partial(tile_kernel, row_count=row_count),
        [(subs * layers, modes - ROWS, LANES), (modes, width)],
        (own, side, picked_sub, before_sub),
        "coarse_tiles",
    )
    tiles = lax.all_to_all(copies, ("sub", "layer"), split_axis=0, concat_axis=0, tiled=True)
    after_sub = lax.ppermute(after_send, "sub", down_sub)
    applied, token = local_call(
        functools.partial(scatter_kernel, subs=subs, layers=layers),
        [(modes, row_count), (ROWS, LANES)],
        (base, row_lists, face_springs, sub_send, picked_sub, layer_send, picked_layer)
        + (before_sub, after_sub, before_layer, after_layer),
        "spread_rows",
        WORK,
    )
    diag_strip, left_strip, right_strip = factor_planes(
        tiles.reshape(subs, layers, *tiles.shape[1:]), modes, token
    )
    return (applied[None, None], diag_strip[None], left_strip[None], right_strip[None])


def solution(mesh):
    in_specs = (
        P("sub", "layer", None, None),
        P("sub", "layer", None),
        P("sub", "layer", None, None),
        P("sub", "layer", None, None),
        P("sub", "layer", None, None),
    )
    out_specs = (
        P("sub", "layer", None, None),
        P("sub", "layer", None),
        P("sub", "layer", None),
        P("sub", "layer", None),
    )
    return jax.shard_map(
        per_device, mesh=mesh, in_specs=in_specs, out_specs=out_specs, check_vma=False
    )
```

```python
import functools
import math
import jax
import jax.numpy as jnp
from jax import lax
from jax.experimental import pallas as pl
from jax.experimental.pallas import tpu as pltpu
from jax.sharding import PartitionSpec as P

STRIDES = (1, 3, 27)
HIGHEST = lax.Precision.HIGHEST
LANES = 128
ROWS = 8
UNROLLED_LAYERS = 4
PLANES_AT_ONCE = 1


def turned_dot(left, right):
    return lax.dot_general(
        left,
        right,
        (((0,), (0,)), ((), ())),
        precision=HIGHEST,
        preferred_element_type=jnp.float32,
    )


PRODUCTS = ((0, 0), (1, 0), (2, 0), (0, 1), (1, 1), (0, 2))


def pieces_of(values):
    first = values.astype(jnp.bfloat16).astype(jnp.float32)
    rest = values - first
    second = rest.astype(jnp.bfloat16).astype(jnp.float32)
    return first, second, rest - second


def single_dot(left, right):
    return lax.dot_general(
        left, right, (((1,), (0,)), ((), ())), preferred_element_type=jnp.float32
    )


def plain_dot(left, right):
    return lax.dot_general(
        left,
        right,
        (((1,), (0,)), ((), ())),
        precision=HIGHEST,
        preferred_element_type=jnp.float32,
    )


def spread_row(strip, k):
    return jnp.broadcast_to(strip[k : k + 1, :], strip.shape)


def eliminate_pair(block, columns, pivots, iota, q, k):
    start = q * ROWS
    first, second = columns[start + k], columns[start + k + 1]
    corner, joint = spread_row(first[0], k), spread_row(first[0], k + 1)
    other_corner = spread_row(second[0], k + 1)
    minor = corner * other_corner - joint * joint
    inverse = pl.reciprocal(corner, approx=True)
    other_inverse = corner * pl.reciprocal(minor, approx=True)
    below = [column * inverse for column in first]
    second = [column - below[r] * joint for r, column in enumerate(second)]
    other_below = [column * other_inverse for column in second]
    below[0] = jnp.where(iota > k, below[0], 0.0)
    other_below[0] = jnp.where(iota > k + 1, other_below[0], 0.0)
    for j in range(start + k + 2, len(columns)):
        strip = j // ROWS - q
        head = spread_row(first[strip], j % ROWS)
        other_head = spread_row(second[strip], j % ROWS)
        columns[j] = [
            column - below[strip + r] * head - other_below[strip + r] * other_head
            for r, column in enumerate(columns[j])
        ]
    for t in range(len(block[q])):
        row = spread_row(block[q][t], k)
        for r, lower in enumerate(below):
            block[q + r][t] = block[q + r][t] - lower * row
        row = spread_row(block[q][t], k + 1)
        for r, lower in enumerate(other_below):
            block[q + r][t] = block[q + r][t] - lower * row
    return jnp.where(iota == k, corner, jnp.where(iota == k + 1, minor * inverse, pivots))


def factor_rows(blocks, tiles_per_part, first_row, turned):
    strip_count = len(blocks[0])
    iota = lax.broadcasted_iota(jnp.int32, (ROWS, LANES), 0)
    lane = lax.broadcasted_iota(jnp.int32, (ROWS, LANES), 1)
    blocks = [[list(strip) for strip in block] for block in blocks]
    at_once = len(blocks) <= PLANES_AT_ONCE
    held = [[] for _ in blocks]
    for q in range(strip_count):
        start = q * ROWS
        if q == 0 or not at_once:
            for b, block in enumerate(blocks):
                source = turned(b, block, q)
                for j in range(start, strip_count * ROWS if at_once else start + ROWS):
                    held[b].append(
                        [
                            jnp.broadcast_to(strip[:, j : j + 1], (ROWS, LANES))
                            for strip in source[j // ROWS - q :]
                        ]
                    )
        pivots = [jnp.zeros((ROWS, LANES), jnp.float32) for _ in blocks]
        for k in range(0, ROWS, 2):
            for b, block in enumerate(blocks):
                pivots[b] = eliminate_pair(block, held[b], pivots[b], iota, q, k)
        for b, block in enumerate(blocks):
            scale = lax.rsqrt(pivots[b])
            for t in range(len(block[q])):
                strip = block[q][t] * scale
                if t < tiles_per_part:
                    keep = lane + t * LANES >= iota + (first_row + start)
                    strip = jnp.where(keep, strip, 0.0)
                block[q][t] = strip
    return blocks


def eliminate_panel(grid_ref, planes, modes, order, part, lanes_used, panel, banded):
    per_part = part // LANES
    first_row = panel * modes
    static = isinstance(panel, int)
    if static:
        rows = pl.ds(first_row, modes)
    else:
        rows = pl.ds(pl.multiple_of(first_row, ROWS), modes)
    blocks = []
    for plane in planes:
        panel_rows = grid_ref[plane, rows, 0:lanes_used]
        blocks.append(
            [
                [
                    panel_rows[q * ROWS : (q + 1) * ROWS, t * LANES : (t + 1) * LANES]
                    for t in range(lanes_used // LANES)
                ]
                for q in range(modes // ROWS)
            ]
        )

    def turned(b, block, q):
        found = []
        for strip in block[q:]:
            if static and first_row // LANES == (first_row + modes - 1) // LANES:
                tile = strip[first_row // LANES]
                offset = first_row % LANES
                found.append(tile if offset == 0 else tile[:, offset : offset + modes])
            else:
                wide = jnp.concatenate(strip[:per_part], axis=1)
                found.append(pltpu.roll(wide, lax.rem(part - first_row, part), 1)[:, :LANES])
        return found

    blocks = factor_rows(blocks, per_part, first_row, turned)
    for plane, block in zip(planes, blocks):
        panel_rows = jnp.concatenate([jnp.concatenate(strip, axis=1) for strip in block], axis=0)
        grid_ref[plane, rows, 0:lanes_used] = panel_rows
        if static:
            below = (panel + 1) * modes
            end = min(below + modes, order) if banded else order
            if below < order:
                columns = panel_rows[:, 0:part].T[below:end]
                grid_ref[plane, below:end, 0:lanes_used] -= plain_dot(columns, panel_rows)
        else:
            lane = lax.broadcasted_iota(jnp.int32, (modes, part), 1)
            columns = jnp.where(lane >= first_row + modes, panel_rows[:, 0:part], 0.0)
            update = turned_dot(columns, panel_rows)[0:order]
            grid_ref[plane, :, 0:lanes_used] -= update


def eliminate_planes(grid_ref, planes, modes, order, part, lanes_used, banded=False):
    layers = order // modes
    if layers <= UNROLLED_LAYERS:
        for panel in range(layers):
            eliminate_panel(grid_ref, planes, modes, order, part, lanes_used, panel, banded)
    else:

        def one_panel(panel, carry):
            eliminate_panel(grid_ref, planes, modes, order, part, lanes_used, panel, banded)
            return carry

        lax.fori_loop(0, layers, one_panel, 0)


def update_partners(grid_ref, plane, distance, part, order, has_left):
    left, right = plane - distance, plane + distance
    both = grid_ref[plane, :, part : 3 * part]
    if part > order:
        spare = jnp.zeros((part - order, 2 * part), jnp.float32)
        both = jnp.concatenate([both, spare], axis=0)
    turned = [piece.astype(jnp.bfloat16) for piece in pieces_of(both.T)]
    held = [piece.astype(jnp.bfloat16) for piece in pieces_of(both)]
    held = jnp.concatenate([held[right] for _, right in PRODUCTS], axis=0)

    def product(rows):
        columns = jnp.concatenate([turned[left][rows] for left, _ in PRODUCTS], axis=1)
        return single_dot(columns, held)

    from_right = product(slice(part, part + order))
    grid_ref[right, :, 0:part] -= from_right[:, part : 2 * part]
    grid_ref[right, :, part : 2 * part] = -from_right[:, 0:part]

    def to_left():
        from_left = product(slice(0, order))
        grid_ref[left, :, 0:part] -= from_left[:, 0:part]
        grid_ref[left, :, 2 * part : 3 * part] = -from_left[:, part : 2 * part]

    if isinstance(has_left, bool):
        if has_left:
            to_left()
    else:
        pl.when(has_left)(to_left)


def unpack_tile(packed, modes):
    half = 3 * modes // 2
    upper = packed[:, 0 : 3 * modes]
    lower = jnp.concatenate(
        [packed[0:ROWS, 3 * modes : 3 * modes + half], packed[ROWS:, 3 * modes : 3 * modes + half]],
        axis=1,
    )
    return jnp.concatenate([upper, lower], axis=0)


def pack_tile(tile):
    modes = tile.shape[0]
    half = 3 * modes // 2
    top = modes - ROWS
    upper = tile[0:top]
    lower = jnp.concatenate([tile[top:, 0:half], tile[top:, half:]], axis=0)
    spare = jnp.zeros((top, LANES - 3 * modes - half), jnp.float32)
    return jnp.concatenate([upper, lower, spare], axis=1)


def factor_kernel(tiles_ref, after_ref, diag_ref, left_ref, right_ref, grid_ref, turned_ref):
    subs, layers, _, _ = tiles_ref.shape
    modes, order = diag_ref.shape
    part = grid_ref.shape[2] // 3
    unrolled = layers <= UNROLLED_LAYERS
    del after_ref
    lane = lax.broadcasted_iota(jnp.int32, (modes, part), 1)
    inside = [(lane >= j * modes) & (lane < (j + 1) * modes) for j in range(layers)]

    def place_tiles(s, before):
        tiles = [unpack_tile(tiles_ref[s, j], modes) for j in range(layers)]
        stacked = tiles
        if part > order:
            stacked = tiles + [jnp.zeros((part - order, tiles[0].shape[1]), jnp.float32)]
        turned = jnp.concatenate(stacked, axis=0).T
        for j, tile in enumerate(tiles):
            rows = slice(j * modes, (j + 1) * modes)
            own = jnp.where(inside[j], turned[0:modes], 0.0)
            if j + 1 < layers:
                own = jnp.where(inside[j + 1], turned[modes : 2 * modes], own)
            grid_ref[s, rows, 0:part] = own
            spare = jnp.zeros((modes, part - 3 * modes), jnp.float32)
            wide = jnp.concatenate([tile, spare], axis=1)
            shift = (j - 2) * modes % part
            down = pltpu.roll(wide, shift, 1) if shift else wide
            grid_ref[s, rows, part : 2 * part] = jnp.where(inside[j], down, 0.0)
            down = jnp.where(inside[j], turned[2 * modes : 3 * modes], 0.0)
            grid_ref[before, rows, 2 * part : 3 * part] = down

    place_tiles(0, subs - 1)
    if unrolled:
        for s in range(1, subs):
            place_tiles(s, s - 1)
    else:

        def place_one(s, carry):
            place_tiles(s, s - 1)
            return carry

        lax.fori_loop(1, subs, place_one, 0)

    sub_here, lay_here = lax.axis_index("sub"), lax.axis_index("layer")

    def one_level(distance):
        if unrolled:
            planes = list(range(distance - 1, subs, 2 * distance))
            eliminate_planes(grid_ref, planes, modes, order, part, 3 * part, distance == 1)
            for plane in planes:
                update_partners(grid_ref, plane, distance, part, order, plane >= distance)
        else:

            def one_plane(index, carry):
                plane = distance - 1 + 2 * distance * index
                eliminate_planes(grid_ref, [plane], modes, order, part, 3 * part)
                update_partners(grid_ref, plane, distance, part, order, index > 0)
                return carry

            lax.fori_loop(0, subs // (2 * distance), one_plane, 0)

    one_level(1)
    if subs > 2:
        one_level(2)
    distance = 4
    while distance < subs:
        pl.when(lax.rem(sub_here + 1, distance) == 0)(functools.partial(one_level, distance))
        distance *= 2

    @pl.when(sub_here == subs - 1)
    def _():
        eliminate_planes(grid_ref, [subs - 1], modes, order, part, part)

    strip = pl.ds(pl.multiple_of(lay_here * modes, ROWS), modes)
    for k, out_ref in enumerate((diag_ref, left_ref, right_ref)):
        turned_ref[k] = grid_ref[sub_here, :, k * part : (k + 1) * part].T
        found = turned_ref[k, strip, :]
        out_ref[...] = found if k == 0 else jnp.where(sub_here < subs - 1, found, 0.0)


VMEM_BLOCK = pl.BlockSpec(memory_space=pltpu.VMEM)
HBM_BLOCK = pl.BlockSpec(memory_space=pltpu.HBM)
SPARE_BYTES = 4 * 1024 * 1024
WORK = 8 * 1024 * 1024


def kernel_params(shapes):
    held = sum(4 * math.prod(shape) for shape in shapes)
    return pltpu.CompilerParams(vmem_limit_bytes=min(2 * held + SPARE_BYTES, 60 * 1024 * 1024))


def factor_planes(plane_tiles, modes, after):
    subs, layers, _, _ = plane_tiles.shape
    order = layers * modes
    part = -(-order // LANES) * LANES
    strip = jax.ShapeDtypeStruct((modes, order), jnp.float32)
    scratch = ((subs, order, 3 * part), (3, part, order))
    return pl.pallas_call(
        factor_kernel,
        out_shape=(strip, strip, strip),
        in_specs=[VMEM_BLOCK, VMEM_BLOCK],
        out_specs=(VMEM_BLOCK, VMEM_BLOCK, VMEM_BLOCK),
        scratch_shapes=[pltpu.VMEM(shape, jnp.float32) for shape in scratch],
        compiler_params=kernel_params((plane_tiles.shape,) + scratch),
        name="factor_planes",
    )(plane_tiles, after)


def across_dot(left, right):
    rows, columns = left.shape[0], right.shape[0]

    def stacked(values):
        short = -3 * values.shape[0] % (2 * ROWS)
        spare = [jnp.zeros((short, values.shape[1]), jnp.float32)] if short else []
        return jnp.concatenate(list(pieces_of(values)) + spare, axis=0).astype(jnp.bfloat16)

    found = lax.dot_general(
        stacked(left),
        stacked(right),
        (((1,), (1,)), ((), ())),
        preferred_element_type=jnp.float32,
    )
    total = None
    for b in (2, 1, 0):
        column = found[:, b * columns : (b + 1) * columns]
        for a in (2, 1, 0):
            if (a, b) in PRODUCTS:
                block = column[a * rows : (a + 1) * rows]
                total = block if total is None else total + block
    return total


def pick_lists(vectors_ref, lists_ref, chosen, strip):
    lists = []
    for k in chosen:
        rows = jnp.broadcast_to(lists_ref[k : k + 1, :], (ROWS, LANES))
        lists.append((rows // LANES, rows % LANES))
    found = [jnp.zeros((ROWS, LANES), jnp.float32) for _ in lists]
    for c in range(vectors_ref.shape[1] // LANES):
        tile = vectors_ref[strip, c * LANES : (c + 1) * LANES]
        for i, (tile_of, lane_of) in enumerate(lists):
            moved = jnp.take_along_axis(tile, lane_of, axis=1, mode="promise_in_bounds")
            found[i] = jnp.where(tile_of == c, moved, found[i])
    return found


def mode_strips(modes):
    return [slice(first, first + ROWS) for first in range(0, modes, ROWS)]


def pick_kernel(
    vectors_in, lists_in, face_in, mass_in, inner_in,
    vectors_ref, lists_ref, face_ref, mass_ref, inner_ref, layer_ref, sub_ref, sems
):
    strips = mode_strips(vectors_ref.shape[0])
    pairs = [(lists_in, lists_ref)]
    for strip in strips:
        rows = pl.ds(strip.start, ROWS)
        pairs.append((vectors_in.at[rows], vectors_ref.at[rows]))
    pairs += [(face_in, face_ref), (mass_in, mass_ref), (inner_in, inner_ref)]
    copies = [pltpu.make_async_copy(a, b, sems.at[i]) for i, (a, b) in enumerate(pairs)]
    for copy in copies:
        copy.start()
    copies[0].wait()
    copies[1 + len(strips)].wait()
    for k, send_ref in ((1, layer_ref), (0, sub_ref)):
        send_ref[vectors_ref.shape[0] :] = jnp.broadcast_to(face_ref[k : k + 1, :], (ROWS, LANES))
    for copy, strip in zip(copies[1:], strips):
        copy.wait()
        layer_ref[strip], sub_ref[strip] = pick_lists(vectors_ref, lists_ref, (2, 0), strip)
    for copy in copies[2 + len(strips) :]:
        copy.wait()


def spread_weights(weights_ref, first, count, height):
    rows = [
        jnp.broadcast_to(weights_ref[first + c : first + c + 1, :], (ROWS, LANES))
        for c in range(count)
    ]
    wide = jnp.concatenate(rows, axis=1)
    return jnp.concatenate([wide] * (height // ROWS), axis=0)


def own_kernel(
    vectors_ref, lists_ref, face_ref, mass_ref, inner_ref, layer_ref, sub_ref, theirs_ref,
    base_ref, own_ref, side_ref, before_sub_ref, before_layer_ref, *, subs, layers
):
    vectors = vectors_ref[...]
    modes, row_count = vectors.shape
    tiles = row_count // LANES
    for strip in mode_strips(modes):
        before_sub_ref[strip], before_layer_ref[strip] = pick_lists(
            vectors_ref, lists_ref, (1, 3), strip
        )
    places = lax.broadcasted_iota(jnp.int32, (modes, row_count), 1)
    base = spread_weights(mass_ref, 0, tiles, modes) * vectors
    for k, t in enumerate(STRIDES):
        edge_weight = spread_weights(inner_ref, k * tiles, tiles, modes)
        edge_weight = jnp.where(places < row_count - t, edge_weight, 0.0)
        fluxes = edge_weight * (vectors - pltpu.roll(vectors, row_count - t, 1))
        base = base + fluxes - pltpu.roll(fluxes, t, 1)
    base_ref[...] = base
    own = across_dot(vectors, base)
    for k, axis, ends, send_ref in ((0, "sub", subs - 1, sub_ref), (1, "layer", layers - 1, layer_ref)):
        springs = jnp.where(lax.axis_index(axis) < ends, face_ref[k : k + 1, :], 0.0)
        picked = send_ref[0:modes]
        own = own + across_dot(picked, springs * picked)
    mine, theirs = before_layer_ref[...], theirs_ref[0:modes]
    sprung = theirs_ref[modes : modes + 1] * mine
    side = across_dot(sprung, jnp.concatenate([mine, theirs], axis=0))
    own_ref[...] = own + side[:, 0:modes]
    side_ref[...] = -side[:, modes:] * (1.0 / row_count)


def tile_kernel(
    own_ref, side_ref, mine_sub_ref, sub_ref, copies_ref, sub_send_ref, *, row_count
):
    modes = own_ref.shape[0]
    inverse = 1.0 / row_count
    mine, theirs = mine_sub_ref[...], sub_ref[0:modes]
    sprung = sub_ref[modes : modes + 1] * mine
    down = across_dot(sprung, jnp.concatenate([mine, theirs], axis=0))
    diag_tile = (own_ref[...] + down[:, 0:modes]) * inverse
    side_tile = side_ref[...]
    down_tile = -down[:, modes:] * inverse
    packed = pack_tile(jnp.concatenate([diag_tile, side_tile, down_tile], axis=1))
    for s in range(copies_ref.shape[0]):
        copies_ref[s] = packed
    sub_send_ref[...] = mine_sub_ref[...]


def scatter_kernel(
    base_ref, lists_ref, face_ref, up_sub_ref, down_sub_ref, up_layer_ref, down_layer_ref, before_sub_ref, after_sub_ref,
    before_layer_ref, after_layer_ref, applied_ref, token_ref, *, subs, layers
):
    modes, row_count = base_ref.shape
    width = 2 * LANES
    springs = [
        jnp.where(lax.axis_index("sub") < subs - 1, face_ref[0:1, :], 0.0),
        before_sub_ref[modes : modes + 1, :],
        jnp.where(lax.axis_index("layer") < layers - 1, face_ref[1:2, :], 0.0),
        before_layer_ref[modes : modes + 1, :],
    ]
    partners = [
        after_sub_ref[...],
        before_sub_ref[0:modes, :],
        after_layer_ref[...],
        before_layer_ref[0:modes, :],
    ]
    picked = [up_sub_ref[0:modes], down_sub_ref[...], up_layer_ref[0:modes], down_layer_ref[...]]
    pulls = jnp.concatenate([springs[k] * (picked[k] - partners[k]) for k in range(4)], axis=1)
    rows = jnp.concatenate([lists_ref[k : k + 1, :] for k in range(4)], axis=1)
    block_of, lane_of = rows // width, rows % width
    lanes = lax.broadcasted_iota(jnp.int32, (width, rows.shape[1]), 0)
    onehot = jnp.where(lanes == lane_of, 1.0, 0.0).astype(jnp.bfloat16)
    total = None
    rest = pulls
    for _ in range(3):
        piece = rest.astype(jnp.bfloat16).astype(jnp.float32)
        rest = rest - piece
        spread = jnp.concatenate(
            [jnp.where(block_of == h, piece, 0.0) for h in range(row_count // width)], axis=0
        ).astype(jnp.bfloat16)
        moved = lax.dot_general(
            spread, onehot, (((1,), (1,)), ((), ())), preferred_element_type=jnp.float32
        )
        total = moved if total is None else total + moved
    for h in range(row_count // width):
        lanes = slice(h * width, (h + 1) * width)
        applied_ref[:, lanes] = base_ref[:, lanes] + total[h * modes : (h + 1) * modes]
    token_ref[...] = jnp.zeros_like(token_ref)


def local_call(body, outputs, operands, name, work=0):
    shapes = tuple(jax.ShapeDtypeStruct(shape, jnp.float32) for shape in outputs)
    return pl.pallas_call(
        body,
        out_shape=shapes,
        in_specs=[VMEM_BLOCK] * len(operands),
        out_specs=tuple(VMEM_BLOCK for _ in shapes),
        compiler_params=kernel_params([x.shape for x in operands] + list(outputs)),
        cost_estimate=pl.CostEstimate(flops=work, bytes_accessed=work, transcendentals=0),
        name=name,
    )(*operands)


def per_device(eigen_vectors, row_mass, inner_weight, face_weight, margin_rows):
    vectors = eigen_vectors[0, 0]
    row_lists = margin_rows[0, 0]
    face_springs = face_weight[0, 0]
    modes, row_count = vectors.shape
    width = row_lists.shape[-1]
    subs = lax.axis_size("sub")
    layers = lax.axis_size("layer")
    up_sub = [(i, i + 1) for i in range(subs - 1)]
    up_layer = [(i, i + 1) for i in range(layers - 1)]
    down_sub = [(i + 1, i) for i in range(subs - 1)]
    down_layer = [(i + 1, i) for i in range(layers - 1)]
    def pinned(*arrays):
        return [pltpu.with_memory_space_constraint(x, pltpu.HBM) for x in arrays]

    def shaped(*shapes):
        return tuple(jax.ShapeDtypeStruct(shape, jnp.float32) for shape in shapes)

    masses = row_mass.reshape(row_count // LANES, LANES)
    interior = inner_weight.reshape(-1, LANES)
    taken = (vectors, row_lists, face_springs, masses, interior)
    held = tuple(jax.ShapeDtypeStruct(x.shape, x.dtype) for x in taken)
    held += shaped((modes + ROWS, width), (modes + ROWS, width))
    vectors, row_lists, face_springs, masses, interior, layer_send, sub_send = pl.pallas_call(
        pick_kernel,
        out_shape=held,
        in_specs=[HBM_BLOCK] * len(taken),
        out_specs=(VMEM_BLOCK,) * len(held),
        scratch_shapes=[pltpu.SemaphoreType.DMA((4 + modes // ROWS,))],
        compiler_params=kernel_params([x.shape for x in held]),
        name="pick_rows",
    )(*pinned(*taken))
    before_layer = lax.ppermute(layer_send, "layer", up_layer)
    before_sub = lax.ppermute(sub_send, "sub", up_sub)
    base, own, side, picked_sub, picked_layer = local_call(
        functools.partial(own_kernel, subs=subs, layers=layers),
        [(modes, row_count), (modes, modes), (modes, modes), (modes, width), (modes, width)],
        (vectors, row_lists, face_springs, masses, interior, layer_send, sub_send, before_layer),
        "own_rows",
        WORK,
    )
    after_layer = lax.ppermute(picked_layer, "layer", down_layer)
    copies, after_send = local_call(
        functools.partial(tile_kernel, row_count=row_count),
        [(subs * layers, modes - ROWS, LANES), (modes, width)],
        (own, side, picked_sub, before_sub),
        "coarse_tiles",
    )
    tiles = lax.all_to_all(copies, ("sub", "layer"), split_axis=0, concat_axis=0, tiled=True)
    after_sub = lax.ppermute(after_send, "sub", down_sub)
    applied, token = local_call(
        functools.partial(scatter_kernel, subs=subs, layers=layers),
        [(modes, row_count), (ROWS, LANES)],
        (base, row_lists, face_springs, sub_send, picked_sub, layer_send, picked_layer)
        + (before_sub, after_sub, before_layer, after_layer),
        "spread_rows",
        WORK,
    )
    diag_strip, left_strip, right_strip = factor_planes(
        tiles.reshape(subs, layers, *tiles.shape[1:]), modes, token
    )
    return (applied[None, None], diag_strip[None], left_strip[None], right_strip[None])


def solution(mesh):
    in_specs = (
        P("sub", "layer", None, None),
        P("sub", "layer", None),
        P("sub", "layer", None, None),
        P("sub", "layer", None, None),
        P("sub", "layer", None, None),
    )
    out_specs = (
        P("sub", "layer", None, None),
        P("sub", "layer", None),
        P("sub", "layer", None),
        P("sub", "layer", None),
    )
    return jax.shard_map(
        per_device, mesh=mesh, in_specs=in_specs, out_specs=out_specs, check_vma=False
    )
```

```python
import functools
import math
import jax
import jax.numpy as jnp
from jax import lax
from jax.experimental import pallas as pl
from jax.experimental.pallas import tpu as pltpu
from jax.sharding import PartitionSpec as P

STRIDES = (1, 3, 27)
HIGHEST = lax.Precision.HIGHEST
LANES = 128
ROWS = 8
UNROLLED_LAYERS = 4
PLANES_AT_ONCE = 0
NARROW_DEPTH = LANES + LANES // 4


def turned_dot(left, right):
    return lax.dot_general(
        left,
        right,
        (((0,), (0,)), ((), ())),
        precision=HIGHEST,
        preferred_element_type=jnp.float32,
    )


PRODUCTS = ((0, 0), (1, 0), (2, 0), (0, 1), (1, 1), (0, 2))


def pieces_of(values):
    first = values.astype(jnp.bfloat16).astype(jnp.float32)
    rest = values - first
    second = rest.astype(jnp.bfloat16).astype(jnp.float32)
    return first, second, rest - second


def single_dot(left, right):
    return lax.dot_general(
        left, right, (((1,), (0,)), ((), ())), preferred_element_type=jnp.float32
    )


def narrow_columns(turned, modes):
    height = turned.shape[0]
    lane = lax.broadcasted_iota(jnp.int32, (height, LANES), 1)
    wide = jnp.concatenate([turned, jnp.zeros((height, LANES - 3 * modes), jnp.float32)], axis=1)
    again = pltpu.roll(wide, 3 * modes, 1)
    left = jnp.where(lane < 3 * modes, wide, jnp.where(lane < 5 * modes, again, 0.0))
    last = jnp.where(lane < modes, wide, 0.0)
    return jnp.concatenate([left, last], axis=1)[:, 0:NARROW_DEPTH].astype(jnp.bfloat16)


def narrow_rows(pieces):
    first, second, third = pieces
    modes, width = first.shape
    gap = jnp.zeros((LANES - 5 * modes, width), jnp.float32)
    tail = jnp.zeros((NARROW_DEPTH - LANES - modes, width), jnp.float32)
    rows = jnp.concatenate([first] * 3 + [second] * 2 + [gap, third, tail], axis=0)
    return rows.astype(jnp.bfloat16)


def plain_dot(left, right):
    return lax.dot_general(
        left,
        right,
        (((1,), (0,)), ((), ())),
        precision=HIGHEST,
        preferred_element_type=jnp.float32,
    )


def spread_row(strip, k):
    return jnp.broadcast_to(strip[k : k + 1, :], strip.shape)


def eliminate_pair(block, columns, pivots, iota, q, k):
    start = q * ROWS
    first, second = columns[start + k], columns[start + k + 1]
    corner, joint = spread_row(first[0], k), spread_row(first[0], k + 1)
    other_corner = spread_row(second[0], k + 1)
    minor = corner * other_corner - joint * joint
    inverse = pl.reciprocal(corner, approx=True)
    other_inverse = corner * pl.reciprocal(minor, approx=True)
    below = [column * inverse for column in first]
    second = [column - below[r] * joint for r, column in enumerate(second)]
    other_below = [column * other_inverse for column in second]
    below[0] = jnp.where(iota > k, below[0], 0.0)
    other_below[0] = jnp.where(iota > k + 1, other_below[0], 0.0)
    for j in range(start + k + 2, len(columns)):
        strip = j // ROWS - q
        head = spread_row(first[strip], j % ROWS)
        other_head = spread_row(second[strip], j % ROWS)
        columns[j] = [
            column - below[strip + r] * head - other_below[strip + r] * other_head
            for r, column in enumerate(columns[j])
        ]
    for t in range(len(block[q])):
        row = spread_row(block[q][t], k)
        for r, lower in enumerate(below):
            block[q + r][t] = block[q + r][t] - lower * row
        row = spread_row(block[q][t], k + 1)
        for r, lower in enumerate(other_below):
            block[q + r][t] = block[q + r][t] - lower * row
    return jnp.where(iota == k, corner, jnp.where(iota == k + 1, minor * inverse, pivots))


def factor_rows(blocks, tiles_per_part, first_row, turned):
    strip_count = len(blocks[0])
    iota = lax.broadcasted_iota(jnp.int32, (ROWS, LANES), 0)
    lane = lax.broadcasted_iota(jnp.int32, (ROWS, LANES), 1)
    blocks = [[list(strip) for strip in block] for block in blocks]
    at_once = len(blocks) <= PLANES_AT_ONCE
    held = [[] for _ in blocks]
    for q in range(strip_count):
        start = q * ROWS
        if q == 0 or not at_once:
            for b, block in enumerate(blocks):
                source = turned(b, block, q)
                for j in range(start, strip_count * ROWS if at_once else start + ROWS):
                    held[b].append(
                        [
                            jnp.broadcast_to(strip[:, j : j + 1], (ROWS, LANES))
                            for strip in source[j // ROWS - q :]
                        ]
                    )
        pivots = [jnp.zeros((ROWS, LANES), jnp.float32) for _ in blocks]
        for k in range(0, ROWS, 2):
            for b, block in enumerate(blocks):
                pivots[b] = eliminate_pair(block, held[b], pivots[b], iota, q, k)
        for b, block in enumerate(blocks):
            scale = lax.rsqrt(pivots[b])
            for t in range(len(block[q])):
                strip = block[q][t] * scale
                if t < tiles_per_part:
                    keep = lane + t * LANES >= iota + (first_row + start)
                    strip = jnp.where(keep, strip, 0.0)
                block[q][t] = strip
    return blocks


def eliminate_panel(grid_ref, planes, modes, order, part, lanes_used, panel, banded):
    per_part = part // LANES
    first_row = panel * modes
    static = isinstance(panel, int)
    if static:
        rows = pl.ds(first_row, modes)
    else:
        rows = pl.ds(pl.multiple_of(first_row, ROWS), modes)
    blocks = []
    for plane in planes:
        panel_rows = grid_ref[plane, rows, 0:lanes_used]
        blocks.append(
            [
                [
                    panel_rows[q * ROWS : (q + 1) * ROWS, t * LANES : (t + 1) * LANES]
                    for t in range(lanes_used // LANES)
                ]
                for q in range(modes // ROWS)
            ]
        )

    def turned(b, block, q):
        found = []
        for strip in block[q:]:
            if static and first_row // LANES == (first_row + modes - 1) // LANES:
                tile = strip[first_row // LANES]
                offset = first_row % LANES
                found.append(tile if offset == 0 else tile[:, offset : offset + modes])
            else:
                wide = jnp.concatenate(strip[:per_part], axis=1)
                found.append(pltpu.roll(wide, lax.rem(part - first_row, part), 1)[:, :LANES])
        return found

    blocks = factor_rows(blocks, per_part, first_row, turned)
    for plane, block in zip(planes, blocks):
        panel_rows = jnp.concatenate([jnp.concatenate(strip, axis=1) for strip in block], axis=0)
        grid_ref[plane, rows, 0:lanes_used] = panel_rows
        if static:
            below = (panel + 1) * modes
            end = min(below + modes, order) if banded else order
            pieces = pieces_of(panel_rows)
            right = narrow_rows(pieces)
            stacked = jnp.concatenate(pieces, axis=0)
            if below < order:
                columns = narrow_columns(stacked[:, 0:part].T[below:end], modes)
                grid_ref[plane, below:end, 0:lanes_used] -= single_dot(columns, right)
        else:
            lane = lax.broadcasted_iota(jnp.int32, (modes, part), 1)
            columns = jnp.where(lane >= first_row + modes, panel_rows[:, 0:part], 0.0)
            update = turned_dot(columns, panel_rows)[0:order]
            grid_ref[plane, :, 0:lanes_used] -= update


def eliminate_planes(grid_ref, planes, modes, order, part, lanes_used, banded=False):
    layers = order // modes
    if layers <= UNROLLED_LAYERS:
        for panel in range(layers):
            eliminate_panel(grid_ref, planes, modes, order, part, lanes_used, panel, banded)
    else:

        def one_panel(panel, carry):
            eliminate_panel(grid_ref, planes, modes, order, part, lanes_used, panel, banded)
            return carry

        lax.fori_loop(0, layers, one_panel, 0)


def update_partners(grid_ref, plane, distance, part, order, has_left):
    left, right = plane - distance, plane + distance
    both = grid_ref[plane, :, part : 3 * part]
    if part > order:
        spare = jnp.zeros((part - order, 2 * part), jnp.float32)
        both = jnp.concatenate([both, spare], axis=0)
    turned = [piece.astype(jnp.bfloat16) for piece in pieces_of(both.T)]
    held = [piece.astype(jnp.bfloat16) for piece in pieces_of(both)]
    held = jnp.concatenate([held[right] for _, right in PRODUCTS], axis=0)

    def product(rows):
        columns = jnp.concatenate([turned[left][rows] for left, _ in PRODUCTS], axis=1)
        return single_dot(columns, held)

    from_right = product(slice(part, part + order))
    grid_ref[right, :, 0:part] -= from_right[:, part : 2 * part]
    grid_ref[right, :, part : 2 * part] = -from_right[:, 0:part]

    def to_left():
        from_left = product(slice(0, order))
        grid_ref[left, :, 0:part] -= from_left[:, 0:part]
        grid_ref[left, :, 2 * part : 3 * part] = -from_left[:, part : 2 * part]

    if isinstance(has_left, bool):
        if has_left:
            to_left()
    else:
        pl.when(has_left)(to_left)


def unpack_tile(packed, modes):
    half = 3 * modes // 2
    upper = packed[:, 0 : 3 * modes]
    lower = jnp.concatenate(
        [packed[0:ROWS, 3 * modes : 3 * modes + half], packed[ROWS:, 3 * modes : 3 * modes + half]],
        axis=1,
    )
    return jnp.concatenate([upper, lower], axis=0)


def pack_tile(tile):
    modes = tile.shape[0]
    half = 3 * modes // 2
    top = modes - ROWS
    upper = tile[0:top]
    lower = jnp.concatenate([tile[top:, 0:half], tile[top:, half:]], axis=0)
    spare = jnp.zeros((top, LANES - 3 * modes - half), jnp.float32)
    return jnp.concatenate([upper, lower, spare], axis=1)


def factor_kernel(tiles_ref, after_ref, diag_ref, left_ref, right_ref, grid_ref, turned_ref):
    subs, layers, _, _ = tiles_ref.shape
    modes, order = diag_ref.shape
    part = grid_ref.shape[2] // 3
    unrolled = layers <= UNROLLED_LAYERS
    del after_ref
    lane = lax.broadcasted_iota(jnp.int32, (modes, part), 1)
    inside = [(lane >= j * modes) & (lane < (j + 1) * modes) for j in range(layers)]

    def place_tiles(s, before):
        tiles = [unpack_tile(tiles_ref[s, j], modes) for j in range(layers)]
        stacked = tiles
        if part > order:
            stacked = tiles + [jnp.zeros((part - order, tiles[0].shape[1]), jnp.float32)]
        turned = jnp.concatenate(stacked, axis=0).T
        for j, tile in enumerate(tiles):
            rows = slice(j * modes, (j + 1) * modes)
            own = jnp.where(inside[j], turned[0:modes], 0.0)
            if j + 1 < layers:
                own = jnp.where(inside[j + 1], turned[modes : 2 * modes], own)
            grid_ref[s, rows, 0:part] = own
            spare = jnp.zeros((modes, part - 3 * modes), jnp.float32)
            wide = jnp.concatenate([tile, spare], axis=1)
            shift = (j - 2) * modes % part
            down = pltpu.roll(wide, shift, 1) if shift else wide
            grid_ref[s, rows, part : 2 * part] = jnp.where(inside[j], down, 0.0)
            down = jnp.where(inside[j], turned[2 * modes : 3 * modes], 0.0)
            grid_ref[before, rows, 2 * part : 3 * part] = down

    place_tiles(0, subs - 1)
    if unrolled:
        for s in range(1, subs):
            place_tiles(s, s - 1)
    else:

        def place_one(s, carry):
            place_tiles(s, s - 1)
            return carry

        lax.fori_loop(1, subs, place_one, 0)

    sub_here, lay_here = lax.axis_index("sub"), lax.axis_index("layer")

    def one_level(distance):
        if unrolled:
            planes = list(range(distance - 1, subs, 2 * distance))
            eliminate_planes(grid_ref, planes, modes, order, part, 3 * part, distance == 1)
            for plane in planes:
                update_partners(grid_ref, plane, distance, part, order, plane >= distance)
        else:

            def one_plane(index, carry):
                plane = distance - 1 + 2 * distance * index
                eliminate_planes(grid_ref, [plane], modes, order, part, 3 * part)
                update_partners(grid_ref, plane, distance, part, order, index > 0)
                return carry

            lax.fori_loop(0, subs // (2 * distance), one_plane, 0)

    one_level(1)
    if subs > 2:
        one_level(2)
    distance = 4
    while distance < subs:
        pl.when(lax.rem(sub_here + 1, distance) == 0)(functools.partial(one_level, distance))
        distance *= 2

    @pl.when(sub_here == subs - 1)
    def _():
        eliminate_planes(grid_ref, [subs - 1], modes, order, part, part)

    strip = pl.ds(pl.multiple_of(lay_here * modes, ROWS), modes)
    for k, out_ref in enumerate((diag_ref, left_ref, right_ref)):
        turned_ref[k] = grid_ref[sub_here, :, k * part : (k + 1) * part].T
        found = turned_ref[k, strip, :]
        out_ref[...] = found if k == 0 else jnp.where(sub_here < subs - 1, found, 0.0)


VMEM_BLOCK = pl.BlockSpec(memory_space=pltpu.VMEM)
HBM_BLOCK = pl.BlockSpec(memory_space=pltpu.HBM)
SPARE_BYTES = 4 * 1024 * 1024
WORK = 8 * 1024 * 1024


def kernel_params(shapes):
    held = sum(4 * math.prod(shape) for shape in shapes)
    return pltpu.CompilerParams(vmem_limit_bytes=min(2 * held + SPARE_BYTES, 60 * 1024 * 1024))


def factor_planes(plane_tiles, modes, after):
    subs, layers, _, _ = plane_tiles.shape
    order = layers * modes
    part = -(-order // LANES) * LANES
    strip = jax.ShapeDtypeStruct((modes, order), jnp.float32)
    scratch = ((subs, order, 3 * part), (3, part, order))
    return pl.pallas_call(
        factor_kernel,
        out_shape=(strip, strip, strip),
        in_specs=[VMEM_BLOCK, VMEM_BLOCK],
        out_specs=(VMEM_BLOCK, VMEM_BLOCK, VMEM_BLOCK),
        scratch_shapes=[pltpu.VMEM(shape, jnp.float32) for shape in scratch],
        compiler_params=kernel_params((plane_tiles.shape,) + scratch),
        name="factor_planes",
    )(plane_tiles, after)


def across_dot(left, right):
    rows, columns = left.shape[0], right.shape[0]

    def stacked(values):
        short = -3 * values.shape[0] % (2 * ROWS)
        spare = [jnp.zeros((short, values.shape[1]), jnp.float32)] if short else []
        return jnp.concatenate(list(pieces_of(values)) + spare, axis=0).astype(jnp.bfloat16)

    found = lax.dot_general(
        stacked(left),
        stacked(right),
        (((1,), (1,)), ((), ())),
        preferred_element_type=jnp.float32,
    )
    total = None
    for b in (2, 1, 0):
        column = found[:, b * columns : (b + 1) * columns]
        for a in (2, 1, 0):
            if (a, b) in PRODUCTS:
                block = column[a * rows : (a + 1) * rows]
                total = block if total is None else total + block
    return total


def pick_lists(vectors_ref, lists_ref, chosen, strip):
    lists = []
    for k in chosen:
        rows = jnp.broadcast_to(lists_ref[k : k + 1, :], (ROWS, LANES))
        lists.append((rows // LANES, rows % LANES))
    found = [jnp.zeros((ROWS, LANES), jnp.float32) for _ in lists]
    for c in range(vectors_ref.shape[1] // LANES):
        tile = vectors_ref[strip, c * LANES : (c + 1) * LANES]
        for i, (tile_of, lane_of) in enumerate(lists):
            moved = jnp.take_along_axis(tile, lane_of, axis=1, mode="promise_in_bounds")
            found[i] = jnp.where(tile_of == c, moved, found[i])
    return found


def mode_strips(modes):
    return [slice(first, first + ROWS) for first in range(0, modes, ROWS)]


def pick_kernel(
    vectors_in, lists_in, face_in, mass_in, inner_in,
    vectors_ref, lists_ref, face_ref, mass_ref, inner_ref, layer_ref, sub_ref, sems
):
    strips = mode_strips(vectors_ref.shape[0])
    pairs = [(lists_in, lists_ref)]
    for strip in strips:
        rows = pl.ds(strip.start, ROWS)
        pairs.append((vectors_in.at[rows], vectors_ref.at[rows]))
    pairs += [(face_in, face_ref), (mass_in, mass_ref), (inner_in, inner_ref)]
    copies = [pltpu.make_async_copy(a, b, sems.at[i]) for i, (a, b) in enumerate(pairs)]
    for copy in copies:
        copy.start()
    copies[0].wait()
    copies[1 + len(strips)].wait()
    for k, send_ref in ((1, layer_ref), (0, sub_ref)):
        send_ref[vectors_ref.shape[0] :] = jnp.broadcast_to(face_ref[k : k + 1, :], (ROWS, LANES))
    for copy, strip in zip(copies[1:], strips):
        copy.wait()
        layer_ref[strip], sub_ref[strip] = pick_lists(vectors_ref, lists_ref, (2, 0), strip)
    for copy in copies[2 + len(strips) :]:
        copy.wait()


def spread_weights(weights_ref, first, count, height):
    rows = [
        jnp.broadcast_to(weights_ref[first + c : first + c + 1, :], (ROWS, LANES))
        for c in range(count)
    ]
    wide = jnp.concatenate(rows, axis=1)
    return jnp.concatenate([wide] * (height // ROWS), axis=0)


def own_kernel(
    vectors_ref, lists_ref, face_ref, mass_ref, inner_ref, layer_ref, sub_ref, theirs_ref,
    base_ref, own_ref, side_ref, before_sub_ref, before_layer_ref, *, subs, layers
):
    vectors = vectors_ref[...]
    modes, row_count = vectors.shape
    tiles = row_count // LANES
    for strip in mode_strips(modes):
        before_sub_ref[strip], before_layer_ref[strip] = pick_lists(
            vectors_ref, lists_ref, (1, 3), strip
        )
    places = lax.broadcasted_iota(jnp.int32, (modes, row_count), 1)
    base = spread_weights(mass_ref, 0, tiles, modes) * vectors
    for k, t in enumerate(STRIDES):
        edge_weight = spread_weights(inner_ref, k * tiles, tiles, modes)
        edge_weight = jnp.where(places < row_count - t, edge_weight, 0.0)
        fluxes = edge_weight * (vectors - pltpu.roll(vectors, row_count - t, 1))
        base = base + fluxes - pltpu.roll(fluxes, t, 1)
    base_ref[...] = base
    own = across_dot(vectors, base)
    for k, axis, ends, send_ref in ((0, "sub", subs - 1, sub_ref), (1, "layer", layers - 1, layer_ref)):
        springs = jnp.where(lax.axis_index(axis) < ends, face_ref[k : k + 1, :], 0.0)
        picked = send_ref[0:modes]
        own = own + across_dot(picked, springs * picked)
    mine, theirs = before_layer_ref[...], theirs_ref[0:modes]
    sprung = theirs_ref[modes : modes + 1] * mine
    side = across_dot(sprung, jnp.concatenate([mine, theirs], axis=0))
    own_ref[...] = own + side[:, 0:modes]
    side_ref[...] = -side[:, modes:] * (1.0 / row_count)


def tile_kernel(
    own_ref, side_ref, mine_sub_ref, sub_ref, copies_ref, sub_send_ref, *, row_count
):
    modes = own_ref.shape[0]
    inverse = 1.0 / row_count
    mine, theirs = mine_sub_ref[...], sub_ref[0:modes]
    sprung = sub_ref[modes : modes + 1] * mine
    down = across_dot(sprung, jnp.concatenate([mine, theirs], axis=0))
    diag_tile = (own_ref[...] + down[:, 0:modes]) * inverse
    side_tile = side_ref[...]
    down_tile = -down[:, modes:] * inverse
    packed = pack_tile(jnp.concatenate([diag_tile, side_tile, down_tile], axis=1))
    for s in range(copies_ref.shape[0]):
        copies_ref[s] = packed
    sub_send_ref[...] = mine_sub_ref[...]


def scatter_kernel(
    base_ref, lists_ref, face_ref, up_sub_ref, down_sub_ref, up_layer_ref, down_layer_ref, before_sub_ref, after_sub_ref,
    before_layer_ref, after_layer_ref, applied_ref, token_ref, *, subs, layers
):
    modes, row_count = base_ref.shape
    width = 2 * LANES
    springs = [
        jnp.where(lax.axis_index("sub") < subs - 1, face_ref[0:1, :], 0.0),
        before_sub_ref[modes : modes + 1, :],
        jnp.where(lax.axis_index("layer") < layers - 1, face_ref[1:2, :], 0.0),
        before_layer_ref[modes : modes + 1, :],
    ]
    partners = [
        after_sub_ref[...],
        before_sub_ref[0:modes, :],
        after_layer_ref[...],
        before_layer_ref[0:modes, :],
    ]
    picked = [up_sub_ref[0:modes], down_sub_ref[...], up_layer_ref[0:modes], down_layer_ref[...]]
    pulls = jnp.concatenate([springs[k] * (picked[k] - partners[k]) for k in range(4)], axis=1)
    rows = jnp.concatenate([lists_ref[k : k + 1, :] for k in range(4)], axis=1)
    block_of, lane_of = rows // width, rows % width
    lanes = lax.broadcasted_iota(jnp.int32, (width, rows.shape[1]), 0)
    onehot = jnp.where(lanes == lane_of, 1.0, 0.0).astype(jnp.bfloat16)
    total = None
    rest = pulls
    for _ in range(3):
        piece = rest.astype(jnp.bfloat16).astype(jnp.float32)
        rest = rest - piece
        spread = jnp.concatenate(
            [jnp.where(block_of == h, piece, 0.0) for h in range(row_count // width)], axis=0
        ).astype(jnp.bfloat16)
        moved = lax.dot_general(
            spread, onehot, (((1,), (1,)), ((), ())), preferred_element_type=jnp.float32
        )
        total = moved if total is None else total + moved
    for h in range(row_count // width):
        lanes = slice(h * width, (h + 1) * width)
        applied_ref[:, lanes] = base_ref[:, lanes] + total[h * modes : (h + 1) * modes]
    token_ref[...] = jnp.zeros_like(token_ref)


def local_call(body, outputs, operands, name, work=0):
    shapes = tuple(jax.ShapeDtypeStruct(shape, jnp.float32) for shape in outputs)
    return pl.pallas_call(
        body,
        out_shape=shapes,
        in_specs=[VMEM_BLOCK] * len(operands),
        out_specs=tuple(VMEM_BLOCK for _ in shapes),
        compiler_params=kernel_params([x.shape for x in operands] + list(outputs)),
        cost_estimate=pl.CostEstimate(flops=work, bytes_accessed=work, transcendentals=0),
        name=name,
    )(*operands)


def per_device(eigen_vectors, row_mass, inner_weight, face_weight, margin_rows):
    vectors = eigen_vectors[0, 0]
    row_lists = margin_rows[0, 0]
    face_springs = face_weight[0, 0]
    modes, row_count = vectors.shape
    width = row_lists.shape[-1]
    subs = lax.axis_size("sub")
    layers = lax.axis_size("layer")
    up_sub = [(i, i + 1) for i in range(subs - 1)]
    up_layer = [(i, i + 1) for i in range(layers - 1)]
    down_sub = [(i + 1, i) for i in range(subs - 1)]
    down_layer = [(i + 1, i) for i in range(layers - 1)]
    def pinned(*arrays):
        return [pltpu.with_memory_space_constraint(x, pltpu.HBM) for x in arrays]

    def shaped(*shapes):
        return tuple(jax.ShapeDtypeStruct(shape, jnp.float32) for shape in shapes)

    masses = row_mass.reshape(row_count // LANES, LANES)
    interior = inner_weight.reshape(-1, LANES)
    taken = (vectors, row_lists, face_springs, masses, interior)
    held = tuple(jax.ShapeDtypeStruct(x.shape, x.dtype) for x in taken)
    held += shaped((modes + ROWS, width), (modes + ROWS, width))
    vectors, row_lists, face_springs, masses, interior, layer_send, sub_send = pl.pallas_call(
        pick_kernel,
        out_shape=held,
        in_specs=[HBM_BLOCK] * len(taken),
        out_specs=(VMEM_BLOCK,) * len(held),
        scratch_shapes=[pltpu.SemaphoreType.DMA((4 + modes // ROWS,))],
        compiler_params=kernel_params([x.shape for x in held]),
        name="pick_rows",
    )(*pinned(*taken))
    before_layer = lax.ppermute(layer_send, "layer", up_layer)
    before_sub = lax.ppermute(sub_send, "sub", up_sub)
    base, own, side, picked_sub, picked_layer = local_call(
        functools.partial(own_kernel, subs=subs, layers=layers),
        [(modes, row_count), (modes, modes), (modes, modes), (modes, width), (modes, width)],
        (vectors, row_lists, face_springs, masses, interior, layer_send, sub_send, before_layer),
        "own_rows",
        WORK,
    )
    after_layer = lax.ppermute(picked_layer, "layer", down_layer)
    copies, after_send = local_call(
        functools.partial(tile_kernel, row_count=row_count),
        [(subs * layers, modes - ROWS, LANES), (modes, width)],
        (own, side, picked_sub, before_sub),
        "coarse_tiles",
    )
    tiles = lax.all_to_all(copies, ("sub", "layer"), split_axis=0, concat_axis=0, tiled=True)
    after_sub = lax.ppermute(after_send, "sub", down_sub)
    applied, token = local_call(
        functools.partial(scatter_kernel, subs=subs, layers=layers),
        [(modes, row_count), (ROWS, LANES)],
        (base, row_lists, face_springs, sub_send, picked_sub, layer_send, picked_layer)
        + (before_sub, after_sub, before_layer, after_layer),
        "spread_rows",
        WORK,
    )
    diag_strip, left_strip, right_strip = factor_planes(
        tiles.reshape(subs, layers, *tiles.shape[1:]), modes, token
    )
    return (applied[None, None], diag_strip[None], left_strip[None], right_strip[None])


def solution(mesh):
    in_specs = (
        P("sub", "layer", None, None),
        P("sub", "layer", None),
        P("sub", "layer", None, None),
        P("sub", "layer", None, None),
        P("sub", "layer", None, None),
    )
    out_specs = (
        P("sub", "layer", None, None),
        P("sub", "layer", None),
        P("sub", "layer", None),
        P("sub", "layer", None),
    )
    return jax.shard_map(
        per_device, mesh=mesh, in_specs=in_specs, out_specs=out_specs, check_vma=False
    )
```
